32 devices in a mesh: row: 4 (over y, x), col: 8 (over z, core).
Axes of the slice: x: 2, y: 2, z: 4, core: 2. Of those that a mesh axis runs over, the one named last changes fastest.
Arguments:
- image: bfloat16 [128, 256, 180], P('row', 'col'), may hold values from -6 to 6
- norm1_gain: float32 [180], replicated, may hold values from 0.5 to 1.5
- norm2_gain: float32 [180], replicated, may hold values from 0.5 to 1.5
- qkv_weight: bfloat16 [180, 540], replicated, may hold values from -2 to 2
- proj_weight: bfloat16 [180, 180], replicated, may hold values from -0.4375 to 0.4375
- rel_table: float32 [961, 6], replicated, may hold values from -4 to 4
- conv_weight: bfloat16 [3, 3, 180, 180], replicated, may hold values from -0.15625 to 0.15625
- fc1_weight: bfloat16 [180, 360], replicated, may hold values from -0.4375 to 0.4375
- fc2_weight: bfloat16 [360, 180], replicated, may hold values from -0.3125 to 0.3125
Outputs:
- mixed_out: bfloat16 [128, 256, 180], P('row', 'col')
The draws below stay inside these ranges and needn't reach their ends.
All inputs are finite; a program needn't handle non-finite values.
Results may differ from the reference program's by a relative error of at most 0.012.
The reference program's roundings to bfloat16 on the way count: a program that leaves them out, or rounds other values in their place, can miss the bound.
Values may be sent and summed in bfloat16 or wider, within the bound.
No kernel may reach another device: no remote copies, remote signals or barrier semaphores. Data moves between devices by JAX's collectives and lax.ppermute only.
A program may use at most 128 MiB of HBM per device.

```python
import jax
import jax.numpy as jnp
from jax import lax

DIM = 180
HEADS = 6
MLP_HID = 360
WIN = 16
SHIFT = 8
NROWS = 128
NCOLS = 256


def draw_qkv_weight(key, part):
    key = jax.random.fold_in(key, 7)
    values = jax.random.normal(key, (DIM, 3 * DIM), jnp.float32) * DIM ** (-0.5)
    return jnp.clip(values, -2.0, 2.0).astype(jnp.bfloat16)


def steps_of(key, shape, cuts, least, top_value):
    gain, own = 1.0, jax.random.fold_in(key, 6)
    for dim, parts in cuts:
        draws = jnp.exp(jax.random.uniform(jax.random.fold_in(own, dim), (parts,), jnp.float32, least / len(cuts), top_value / len(cuts)))
        gain = gain * jnp.repeat(draws, shape[dim] // parts).reshape([-1 if axis == dim else 1 for axis in range(len(shape))])
    return gain


def gaussian(rng, shape, scale, reach, shards=(), kind=jnp.bfloat16):
    drawn = jax.random.normal(rng, shape, jnp.float32) * scale
    if len(shards) > 0:
        drawn = steps_of(rng, shape, shards, -0.22, 0.18) * drawn
    return jnp.clip(drawn, min=-reach, max=reach).astype(kind)


def setup_inputs(seed: int = 0) -> dict:
    splits = jax.random.split(jax.random.key(seed), 10)
    return {
        "image": gaussian(splits[0], (NROWS, NCOLS, DIM), 1.0, 6.0, ((0, 4), (1, 8))),
        "norm1_gain": jnp.clip(1.0 + 0.1 * jax.random.normal(splits[1], (DIM,), jnp.float32), 0.5, 1.5),
        "norm2_gain": jnp.clip(1.0 + 0.1 * jax.random.normal(splits[2], (DIM,), jnp.float32), 0.5, 1.5),
        "qkv_weight": draw_qkv_weight(jax.random.fold_in(splits[9], 71), 0),
        "proj_weight": gaussian(splits[4], (DIM, DIM), DIM ** -0.5, 0.4375),
        "rel_table": gaussian(splits[5], ((2 * WIN - 1) * (2 * WIN - 1), HEADS), 1.0, 4.0, (), jnp.float32),
        "conv_weight": gaussian(splits[6], (3, 3, DIM, DIM), (9 * DIM) ** -0.5, 0.15625),
        "fc1_weight": gaussian(splits[7], (DIM, MLP_HID), DIM ** -0.5, 0.4375),
        "fc2_weight": gaussian(splits[8], (MLP_HID, DIM), MLP_HID ** -0.5, 0.3125),
    }


def layer_norm(values, norm_gain):
    centre = lax.optimization_barrier(jnp.mean(values, axis=-1, keepdims=True))
    spread = lax.optimization_barrier(jnp.mean((values - centre) ** 2, axis=-1, keepdims=True))
    return (values - centre) * lax.rsqrt(spread + 1e-05) * norm_gain

def to_windows(field):
    rows_n, cols_n = (field.shape[0], field.shape[1])
    shaped = field.reshape(rows_n // WIN, WIN, cols_n // WIN, WIN, field.shape[2])
    return shaped.transpose(0, 2, 1, 3, 4).reshape(-1, WIN * WIN, field.shape[2])

def from_windows(windowed, rows_n, cols_n):
    shaped = windowed.reshape(rows_n // WIN, cols_n // WIN, WIN, WIN, windowed.shape[2])
    return shaped.transpose(0, 2, 1, 3, 4).reshape(rows_n, cols_n, windowed.shape[2])

def region(position, extent):
    return (position >= extent - WIN).astype(jnp.int32) + (position >= extent - WIN // 2).astype(jnp.int32)

def position_bias(rel_table):
    coords = jnp.arange(WIN * WIN, dtype=jnp.int32)
    pos_y = coords // WIN
    pos_x = coords % WIN
    offsets = (pos_y[:, None] - pos_y[None, :] + WIN - 1) * (2 * WIN - 1) + (pos_x[:, None] - pos_x[None, :] + WIN - 1)
    return jnp.take(rel_table, offsets, axis=0).transpose(2, 0, 1)

def attend(windowed, win_labels, qkv_weight, proj_weight, pos_bias):
    count_win, pixels, channels = windowed.shape
    head_dim = channels // HEADS
    qkv_rows = jnp.dot(windowed.reshape(-1, channels), qkv_weight, preferred_element_type=jnp.float32)
    qkv_rows = qkv_rows.astype(jnp.bfloat16).reshape(count_win, pixels, 3, HEADS, head_dim)
    queries = qkv_rows[:, :, 0].astype(jnp.float32)
    keys_all = qkv_rows[:, :, 1].astype(jnp.float32)
    values_all = qkv_rows[:, :, 2].astype(jnp.float32)
    scores = jnp.einsum('wphd,wqhd->whpq', queries, keys_all) * head_dim ** (-0.5) + pos_bias[None]
    same_region = win_labels[:, :, None] == win_labels[:, None, :]
    scores = jnp.where(same_region[:, None], scores, -1000000000.0)
    scores = scores - lax.optimization_barrier(jnp.max(scores, axis=-1, keepdims=True))
    exp_scores = jnp.exp(scores)
    soft_weights = (exp_scores / lax.optimization_barrier(jnp.sum(exp_scores, axis=-1, keepdims=True))).astype(jnp.bfloat16)
    heads_out = jnp.einsum('whpq,wqhd->wphd', soft_weights.astype(jnp.float32), values_all).astype(jnp.bfloat16)
    heads_out = heads_out.reshape(count_win * pixels, channels)
    projected = jnp.dot(heads_out, proj_weight, preferred_element_type=jnp.float32).astype(jnp.bfloat16)
    return projected.reshape(count_win, pixels, channels)

def block_tail(state, attended, conv_sum, norm2_gain, fc1_weight, fc2_weight):
    channels = state.shape[-1]
    state1 = state.astype(jnp.float32) + attended.astype(jnp.float32) + conv_sum
    normed2 = layer_norm(state1, norm2_gain).astype(jnp.bfloat16).reshape(-1, channels)
    hidden = jax.nn.gelu(jnp.dot(normed2, fc1_weight, preferred_element_type=jnp.float32), approximate=False).astype(jnp.bfloat16)
    mlp_out = jnp.dot(hidden, fc2_weight, preferred_element_type=jnp.float32).reshape(state1.shape)
    return (state1 + mlp_out).astype(jnp.bfloat16)

def reference(image, norm1_gain, norm2_gain, qkv_weight, proj_weight, rel_table, conv_weight, fc1_weight, fc2_weight):
    channels = image.shape[-1]
    normed1 = layer_norm(image.astype(jnp.float32), norm1_gain).astype(jnp.bfloat16)
    shifted = jnp.roll(normed1, (-SHIFT, -SHIFT), (0, 1))
    row_labels = region(jnp.arange(NROWS, dtype=jnp.int32), NROWS)
    col_labels = region(jnp.arange(NCOLS, dtype=jnp.int32), NCOLS)
    labels = row_labels[:, None] * 3 + col_labels[None, :]
    pos_bias = position_bias(rel_table)
    strips = shifted.reshape(NROWS // WIN, WIN, NCOLS, channels)
    label_strips = labels.reshape(NROWS // WIN, WIN, NCOLS)

    def one_strip(strip_args):
        strip, strip_labels = strip_args
        windowed = to_windows(strip)
        win_labels = to_windows(strip_labels[:, :, None])[:, :, 0]
        return from_windows(attend(windowed, win_labels, qkv_weight, proj_weight, pos_bias), WIN, NCOLS)
    attended = lax.map(one_strip, (strips, label_strips)).reshape(NROWS, NCOLS, channels)
    attended = jnp.roll(attended, (SHIFT, SHIFT), (0, 1))
    padded = jnp.pad(normed1, ((1, 1), (1, 1), (0, 0)))
    image_strips = image.reshape(NROWS // WIN, WIN, NCOLS, channels)
    attended_strips = attended.reshape(NROWS // WIN, WIN, NCOLS, channels)

    def tail_strip(strip_args):
        strip_index, state, attended_part = strip_args
        slab_rows = lax.dynamic_slice_in_dim(padded, strip_index * WIN, WIN + 2, 0)
        conv_sum = jnp.zeros((WIN * NCOLS, channels), jnp.float32)
        for row_tap in range(3):
            for col_tap in range(3):
                piece = slab_rows[row_tap:row_tap + WIN, col_tap:col_tap + NCOLS].reshape(-1, channels)
                conv_sum = conv_sum + jnp.dot(piece, conv_weight[row_tap, col_tap], preferred_element_type=jnp.float32)
        conv_sum = conv_sum.reshape(WIN, NCOLS, channels)
        return block_tail(state, attended_part, conv_sum, norm2_gain, fc1_weight, fc2_weight)
    strip_ids = jnp.arange(NROWS // WIN, dtype=jnp.int32)
    mixed_out = lax.map(tail_strip, (strip_ids, image_strips, attended_strips))
    return mixed_out.reshape(NROWS, NCOLS, channels)
```

```python
import functools
import math

import jax
import jax.numpy as jnp
from jax import lax
from jax.experimental import pallas as pl
from jax.experimental.pallas import tpu as pltpu
from jax.sharding import PartitionSpec as P

HEADS = 6
WIN = 16
SHIFT = 8
LANES = 256
F32 = jnp.float32
BF16 = jnp.bfloat16
LOG2E = math.log2(math.e)
MASKED = -4.0e9


def layer_norm(values, norm_gain):
    centre = jnp.mean(values, axis=-1, keepdims=True)
    values = values - centre
    spread = jnp.mean(values * values, axis=-1, keepdims=True)
    return values * lax.rsqrt(spread + 1e-05) * norm_gain


def dot(a, b):
    return jnp.dot(a, b, preferred_element_type=F32)


def dot_nt(a, b):
    return lax.dot_general(a, b, (((1,), (1,)), ((), ())), preferred_element_type=F32)


def one_hot(condition):
    return jnp.where(condition, 1.0, 0.0).astype(BF16)


def expand_bias(table_ref, padded, strip, bias):
    span = 2 * WIN - 1
    padded[...] = jnp.zeros_like(padded)
    padded[0:HEADS, 0 : span * span] = table_ref[...] * LOG2E
    table = padded[...]
    width = padded.shape[1]
    shifted = jnp.concatenate(
        [table if px == 0 else pltpu.roll(table, width - px, 1) for px in range(WIN)], axis=0
    )
    high = shifted.astype(BF16)
    low = (shifted - high.astype(F32)).astype(BF16)
    entry = lax.broadcasted_iota(jnp.int32, (width, 512), 0)
    place = lax.broadcasted_iota(jnp.int32, (1, 512), 1)
    wanted = (2 * WIN - 2 - lax.div(place, WIN)) * span + WIN - 1 - lax.rem(place, WIN)
    picked = dot(jnp.concatenate([high, low], axis=0), one_hot(entry == wanted))
    half = 8 * WIN
    picked = picked[:half] + picked[half:]
    for tile in range(4):
        strip[tile] = picked[:, 128 * tile : 128 * (tile + 1)]
    for head in range(HEADS):
        rows = jnp.concatenate(
            [strip[tile, pl.ds(head, WIN, stride=8), :] for tile in range(4)], axis=1
        )
        for turn in range(8):
            rolled = rows if turn == 0 else pltpu.roll(rows, 512 - 16 * turn, 1)
            bias[head, 15 - turn] = rolled[:, 0:256]
            bias[head, 7 - turn] = rolled[:, 128:384]


def kernel(
    image_ref, top_ref, bottom_ref, left_ref, right_ref, gain1_ref, gain2_ref,
    qkv_ref, proj_ref, table_ref, conv_ref, fc1_ref, fc2_ref, out_ref,
    normed, kv, query, heads, bias, shifted, padded, strip, wq, wkv, wp, wc,
):
    rows, cols, channels = image_ref.shape
    head_dim = channels // HEADS
    row, col = lax.axis_index("row"), lax.axis_index("col")
    last_row, last_col = lax.axis_size("row") - 1, lax.axis_size("col") - 1
    lane = lax.broadcasted_iota(jnp.int32, (1, LANES), 1)
    flag_lane, one_lane = channels, channels + 1

    expand_bias(table_ref, padded, strip, bias)

    for ref in (wq, wkv, wp, wc):
        ref[...] = jnp.zeros_like(ref)
    special = lax.broadcasted_iota(jnp.int32, (16, LANES), 0) + 176
    lanes16 = lax.broadcasted_iota(jnp.int32, (16, LANES), 1)
    wq[176:192, :] = one_hot((special == one_lane) & (lanes16 == flag_lane))
    wkv[176:192, 0:LANES] = jnp.where(
        (special == flag_lane) & (lanes16 == flag_lane), MASKED, 0.0
    ).astype(BF16)
    wkv[176:192, LANES:] = one_hot(
        (special == one_lane) & (lanes16 >= channels) & (lanes16 < channels + HEADS)
    )
    wq[0:channels, 0:channels] = qkv_ref[:, 0:channels]
    wkv[0:channels, 0:channels] = qkv_ref[:, channels : 2 * channels]
    wkv[0:channels, LANES : LANES + channels] = qkv_ref[:, 2 * channels :]
    wp[0:channels, :] = proj_ref[...]
    for row_tap in range(3):
        for col_tap in range(3):
            wc[row_tap, col_tap, 0:channels, :] = conv_ref[row_tap, col_tap]

    half = lane[:, LANES // 2 :]
    one_mark = jnp.where(half == one_lane, 1.0, 0.0)
    flag_mark = jnp.where(half == flag_lane, 1.0, 0.0)
    outside_r = [(row == 0).astype(F32), 0.0, (row == last_row).astype(F32)]
    outside_c = [(col == 0).astype(F32), 0.0, (col == last_col).astype(F32)]
    spans_r = [(0, SHIFT), (SHIFT, SHIFT + rows), (SHIFT + rows, 2 * SHIFT + rows)]
    spans_c = [(0, SHIFT), (SHIFT, SHIFT + cols), (SHIFT + cols, 2 * SHIFT + cols)]
    for (r0, r1), out_r in zip(spans_r, outside_r):
        for (c0, c1), out_c in zip(spans_c, outside_c):
            mark = one_mark + flag_mark * (out_r + out_c)
            normed[r0:r1, c0:c1, LANES // 2 :] = jnp.broadcast_to(
                mark[None], (r1 - r0, c1 - c0, LANES // 2)
            )
    gain1 = gain1_ref[...]
    for r in range(0, rows, 8):
        normed[SHIFT + r : SHIFT + r + 8, SHIFT : SHIFT + cols, 0:channels] = layer_norm(
            image_ref[r : r + 8].astype(F32), gain1
        )
    for r0, ref in ((0, top_ref), (SHIFT + rows, bottom_ref)):
        normed[r0 : r0 + SHIFT, SHIFT : SHIFT + cols, 0:channels] = layer_norm(
            ref[...].astype(F32), gain1
        )
    for c0, ref in ((0, left_ref), (SHIFT + cols, right_ref)):
        for r in range(0, rows + 2 * SHIFT, WIN):
            normed[r : r + WIN, c0 : c0 + SHIFT, 0:channels] = layer_norm(
                ref[r : r + WIN].astype(F32), gain1
            )

    scale = head_dim**-0.5 * LOG2E
    for r in range(0, rows, 8):
        pixels = normed[SHIFT + r : SHIFT + r + 8, SHIFT : SHIFT + cols, :].astype(BF16)
        query[r : r + 8] = (dot(pixels.reshape(-1, LANES), wq[...]) * scale).reshape(8, cols, LANES)
    wide = cols + 2 * SHIFT
    for r in range(0, rows + 2 * SHIFT, 8):
        pixels = normed[r : r + 8].astype(BF16).reshape(-1, LANES)
        kv[r : r + 8] = dot(pixels, wkv[...]).astype(BF16).reshape(8, wide, 2 * LANES)

    def spans(extent):
        cuts = []
        for window in range((extent + 2 * SHIFT) // WIN):
            start = max(window * WIN, SHIFT)
            stop = min((window + 1) * WIN, extent + SHIFT)
            cuts.append((window * WIN, start, stop))
        return cuts

    own = [(lane >= h * head_dim) & (lane < (h + 1) * head_dim) for h in range(HEADS)]
    for key_r, r0, r1 in spans(rows):
        for key_c, c0, c1 in spans(cols):
            pair = kv[key_r : key_r + WIN, key_c : key_c + WIN, :].reshape(WIN * WIN, 2 * LANES)
            keys, values = pair[:, :LANES], pair[:, LANES:]
            step = max(8, 128 // (c1 - c0))
            for q0 in range(r0, r1, step):
                q1 = min(q0 + step, r1)
                count = (q1 - q0) * (c1 - c0)
                part = query[q0 - SHIFT : q1 - SHIFT, c0 - SHIFT : c1 - SHIFT, :]
                part = part.reshape(count, LANES)
                stacked = jnp.concatenate(
                    [
                        jnp.where(own[h] | (lane == flag_lane), part, 0.0).astype(BF16)
                        for h in range(HEADS)
                    ],
                    axis=0,
                )
                scores = dot_nt(stacked, keys).reshape(HEADS, count, WIN * WIN)
                part_bias = bias[:, q0 - key_r : q1 - key_r, c0 - key_c : c1 - key_c, :]
                scores = scores + part_bias.reshape(HEADS, count, WIN * WIN)
                scores = scores - jnp.max(scores, axis=-1, keepdims=True)
                soft = jnp.exp2(scores).astype(BF16).reshape(HEADS * count, WIN * WIN)
                mixed = dot(soft, values)
                result = mixed[0:count]
                for h in range(1, HEADS):
                    mine = own[h] | (lane == channels + h)
                    result = jnp.where(mine, mixed[h * count : (h + 1) * count], result)
                heads[q0 - SHIFT : q1 - SHIFT, c0 - SHIFT : c1 - SHIFT, :] = result.reshape(
                    q1 - q0, c1 - c0, LANES
                )

    for tap in range(3):
        for r in range(0, rows + 2, 8):
            stop = min(r + 8, rows + 2)
            shifted[tap, r:stop] = normed[
                SHIFT - 1 + r : SHIFT - 1 + stop, SHIFT - 1 + tap : SHIFT - 1 + tap + cols, :
            ].astype(BF16)

    @pl.when(row == 0)
    def _():
        shifted[:, 0] = jnp.zeros_like(shifted[:, 0])

    @pl.when(row == last_row)
    def _():
        shifted[:, rows + 1] = jnp.zeros_like(shifted[:, rows + 1])

    @pl.when(col == 0)
    def _():
        edge = lax.broadcasted_iota(jnp.int32, (1, cols, LANES), 1) == 0
        shifted[0] = jnp.where(edge, 0.0, shifted[0].astype(F32)).astype(BF16)

    @pl.when(col == last_col)
    def _():
        edge = lax.broadcasted_iota(jnp.int32, (1, cols, LANES), 1) == cols - 1
        shifted[2] = jnp.where(edge, 0.0, shifted[2].astype(F32)).astype(BF16)

    sum_row = lax.broadcasted_iota(jnp.int32, (LANES // 2, LANES), 0) + LANES // 2 - channels
    lane_wide = lax.broadcasted_iota(jnp.int32, (LANES // 2, LANES), 1)
    spread = one_hot(
        (sum_row >= 0) & (lane_wide >= sum_row * head_dim) & (lane_wide < (sum_row + 1) * head_dim)
        & (lane_wide < channels)
    )
    is_sum = (half >= channels) & (half < channels + HEADS)
    gain2 = gain2_ref[...]
    band = 8
    for r in range(0, rows, band):
        raw = heads[r : r + band].reshape(band * cols, LANES)
        inverse = jnp.where(is_sum, 1.0 / raw[:, LANES // 2 :], 0.0)
        high = inverse.astype(BF16)
        low = (inverse - high.astype(F32)).astype(BF16)
        heads_out = (raw * (dot(high, spread) + dot(low, spread))).astype(BF16)
        attended = dot(heads_out, wp[...]).astype(BF16).astype(F32)
        conv_sum = None
        for row_tap in range(3):
            for col_tap in range(3):
                piece = shifted[col_tap, r + row_tap : r + row_tap + band].reshape(-1, LANES)
                term = dot(piece, wc[row_tap, col_tap])
                conv_sum = term if conv_sum is None else conv_sum + term
        state1 = image_ref[r : r + band].astype(F32).reshape(-1, channels) + attended + conv_sum
        normed2 = layer_norm(state1, gain2).astype(BF16)
        hidden = dot(normed2, fc1_ref[...])
        hidden = (0.5 * hidden * (1.0 + lax.erf(hidden * math.sqrt(0.5)))).astype(BF16)
        mixed_out = state1 + dot_nt(hidden, fc2_ref[...])
        out_ref[r : r + band] = mixed_out.astype(BF16).reshape(band, cols, channels)


def neighbour(block, axis, step):
    count = lax.axis_size(axis)
    return lax.ppermute(block, axis, [(i, (i + step) % count) for i in range(count)])


def on_device(
    image, norm1_gain, norm2_gain, qkv_weight, proj_weight, rel_table, conv_weight, fc1_weight,
    fc2_weight,
):
    rows, cols, channels = image.shape
    top = neighbour(image[rows - SHIFT :], "row", 1)
    bottom = neighbour(image[:SHIFT], "row", -1)
    tall = jnp.concatenate([top, image, bottom], axis=0)
    left = neighbour(tall[:, cols - SHIFT :], "col", 1)
    right = neighbour(tall[:, :SHIFT], "col", -1)
    tall_rows, wide_cols = rows + 2 * SHIFT, cols + 2 * SHIFT
    vmem = pl.BlockSpec(memory_space=pltpu.VMEM)
    return pl.pallas_call(
        kernel,
        out_shape=jax.ShapeDtypeStruct(image.shape, BF16),
        in_specs=[vmem] * 13,
        out_specs=vmem,
        scratch_shapes=[
            pltpu.VMEM((tall_rows, wide_cols, LANES), F32),
            pltpu.VMEM((tall_rows, wide_cols, 2 * LANES), BF16),
            pltpu.VMEM((rows, cols, LANES), F32),
            pltpu.VMEM((rows, cols, LANES), F32),
            pltpu.VMEM((HEADS, WIN, WIN, WIN * WIN), F32),
            pltpu.VMEM((3, rows + 2, cols, LANES), BF16),
            pltpu.VMEM((8, 1024), F32),
            pltpu.VMEM((4, 8 * WIN, 128), F32),
            pltpu.VMEM((LANES, LANES), BF16),
            pltpu.VMEM((LANES, 2 * LANES), BF16),
            pltpu.VMEM((LANES, channels), BF16),
            pltpu.VMEM((3, 3, LANES, channels), BF16),
        ],
        compiler_params=pltpu.CompilerParams(vmem_limit_bytes=48 * 1024 * 1024),
        name="block",
    )(
        image, top, bottom, left, right, norm1_gain[None], norm2_gain[None],
        qkv_weight, proj_weight, rel_table.T, conv_weight, fc1_weight, fc2_weight.T,
    )


def solution(mesh):
    placed = (P("row", "col", None), P(), P(), P(), P(), P(), P(), P(), P())
    return jax.shard_map(
        on_device, mesh=mesh, in_specs=placed, out_specs=P("row", "col", None), check_vma=False
    )
```

```python
import functools
import math

import jax
import jax.numpy as jnp
from jax import lax
from jax.experimental import pallas as pl
from jax.experimental.pallas import tpu as pltpu
from jax.sharding import PartitionSpec as P

HEADS = 6
WIN = 16
SHIFT = 8
LANES = 256
HALF = LANES // 2
F32 = jnp.float32
BF16 = jnp.bfloat16
LOG2E = math.log2(math.e)
MASKED = -4.0e9


def layer_norm(values, norm_gain):
    centre = jnp.mean(values, axis=-1, keepdims=True)
    values = values - centre
    spread = jnp.mean(values * values, axis=-1, keepdims=True)
    return values * lax.rsqrt(spread + 1e-05) * norm_gain


def dot(a, b):
    return jnp.dot(a, b, preferred_element_type=F32)


def dot_nt(a, b):
    return lax.dot_general(a, b, (((1,), (1,)), ((), ())), preferred_element_type=F32)


def one_hot(condition):
    return jnp.where(condition, 1.0, 0.0).astype(BF16)


def lanes_of(width=LANES):
    return lax.broadcasted_iota(jnp.int32, (1, width), 1)


def mark_lanes(ref, place, shape, channels, outside):
    half = lanes_of()[:, HALF:]
    mark = jnp.where(half == channels + 1, 1.0, 0.0) + jnp.where(half == channels, outside, 0.0)
    ref[(*place, slice(HALF, LANES))] = jnp.broadcast_to(mark[None], (*shape, HALF))


def expand_bias(table_ref, padded, strip, bias):
    span = 2 * WIN - 1
    padded[...] = jnp.zeros_like(padded)
    padded[0:HEADS, 0 : span * span] = table_ref[...] * LOG2E
    table = padded[...]
    width = padded.shape[1]
    shifted = jnp.concatenate(
        [table if px == 0 else pltpu.roll(table, width - px, 1) for px in range(WIN)], axis=0
    )
    high = shifted.astype(BF16)
    low = (shifted - high.astype(F32)).astype(BF16)
    entry = lax.broadcasted_iota(jnp.int32, (width, 512), 0)
    place = lax.broadcasted_iota(jnp.int32, (1, 512), 1)
    wanted = (2 * WIN - 2 - lax.div(place, WIN)) * span + WIN - 1 - lax.rem(place, WIN)
    picked = dot(jnp.concatenate([high, low], axis=0), one_hot(entry == wanted))
    half = 8 * WIN
    picked = picked[:half] + picked[half:]
    for tile in range(4):
        strip[tile] = picked[:, 128 * tile : 128 * (tile + 1)]
    for head in range(HEADS):
        rows = jnp.concatenate(
            [strip[tile, pl.ds(head, WIN, stride=8), :] for tile in range(4)], axis=1
        )
        for turn in range(8):
            rolled = rows if turn == 0 else pltpu.roll(rows, 512 - 16 * turn, 1)
            bias[head, 15 - turn] = rolled[:, 0:256]
            bias[head, 7 - turn] = rolled[:, 128:384]


def own_kernel(
    image_ref, gain1_ref, qkv_ref, proj_ref, table_ref, conv_ref,
    bias, normed, q_mid, q_left, q_right, kv_mid, wkv, wp, wc,
    padded, strip, wq,
):
    rows, cols, channels = image_ref.shape
    head_dim = channels // HEADS
    flag_lane, one_lane = channels, channels + 1
    expand_bias(table_ref, padded, strip, bias)

    for ref in (wq, wkv, wp, wc):
        ref[...] = jnp.zeros_like(ref)
    special = lax.broadcasted_iota(jnp.int32, (16, LANES), 0) + 176
    lanes16 = lax.broadcasted_iota(jnp.int32, (16, LANES), 1)
    wq[176:192, :] = one_hot((special == one_lane) & (lanes16 == flag_lane))
    wkv[176:192, 0:LANES] = jnp.where(
        (special == flag_lane) & (lanes16 == flag_lane), MASKED, 0.0
    ).astype(BF16)
    wkv[176:192, LANES:] = one_hot(
        (special == one_lane) & (lanes16 >= channels) & (lanes16 < channels + HEADS)
    )
    wq[0:channels, 0:channels] = qkv_ref[:, 0:channels]
    wkv[0:channels, 0:channels] = qkv_ref[:, channels : 2 * channels]
    wkv[0:channels, LANES : LANES + channels] = qkv_ref[:, 2 * channels :]
    wp[0:channels, :] = proj_ref[...]
    for row_tap in range(3):
        for col_tap in range(3):
            wc[row_tap, col_tap, 0:channels, :] = conv_ref[row_tap, col_tap]

    mark_lanes(normed, (slice(0, rows), slice(0, cols)), (rows, cols), channels, 0.0)
    gain1 = gain1_ref[...]
    for r in range(0, rows, 8):
        normed[r : r + 8, :, 0:channels] = layer_norm(image_ref[r : r + 8].astype(F32), gain1)

    scale = head_dim**-0.5 * LOG2E
    for r in range(0, rows, 8):
        pixels = normed[r : r + 8].astype(BF16).reshape(-1, LANES)
        q = (dot(pixels, wq[...]) * scale).reshape(8, cols, LANES)
        q_left[r : r + 8] = q[:, :SHIFT]
        q_mid[r : r + 8] = q[:, SHIFT : cols - SHIFT]
        q_right[r : r + 8] = q[:, cols - SHIFT :]
        middle = normed[r : r + 8, SHIFT : cols - SHIFT].astype(BF16).reshape(-1, LANES)
        kv = dot(middle, wkv[...]).astype(BF16)
        kv_mid[r : r + 8] = kv.reshape(8, cols - 2 * SHIFT, 2 * LANES)


def attend(part, pair, part_bias, head_dim, channels):
    lane = lanes_of()
    keys, values = pair[:, :LANES], pair[:, LANES:]
    count = part.shape[0]
    own = [(lane >= h * head_dim) & (lane < (h + 1) * head_dim) for h in range(HEADS)]
    stacked = jnp.concatenate(
        [jnp.where(own[h] | (lane == channels), part, 0.0).astype(BF16) for h in range(HEADS)],
        axis=0,
    )
    scores = dot_nt(stacked, keys).reshape(HEADS, count, WIN * WIN)
    scores = scores + part_bias.reshape(HEADS, count, WIN * WIN)
    scores = scores - jnp.max(scores, axis=-1, keepdims=True)
    soft = jnp.exp2(scores).astype(BF16).reshape(HEADS * count, WIN * WIN)
    mixed = dot(soft, values)
    result = mixed[0:count]
    for h in range(1, HEADS):
        mine = own[h] | (lane == channels + h)
        result = jnp.where(mine, mixed[h * count : (h + 1) * count], result)
    return result


def finish(raw, pieces, image, wp, wc, gain2, fc1, fc2, channels):
    head_dim = channels // HEADS
    half = lanes_of()[:, HALF:]
    sum_row = lax.broadcasted_iota(jnp.int32, (HALF, LANES), 0) + HALF - channels
    lane_wide = lax.broadcasted_iota(jnp.int32, (HALF, LANES), 1)
    spread = one_hot(
        (sum_row >= 0) & (lane_wide >= sum_row * head_dim) & (lane_wide < (sum_row + 1) * head_dim)
        & (lane_wide < channels)
    )
    is_sum = (half >= channels) & (half < channels + HEADS)
    inverse = jnp.where(is_sum, 1.0 / raw[:, HALF:], 0.0)
    high = inverse.astype(BF16)
    low = (inverse - high.astype(F32)).astype(BF16)
    heads_out = (raw * (dot(high, spread) + dot(low, spread))).astype(BF16)
    attended = dot(heads_out, wp[...]).astype(BF16).astype(F32)
    conv_sum = None
    for row_tap in range(3):
        for col_tap in range(3):
            term = dot(pieces(row_tap, col_tap), wc[row_tap, col_tap])
            conv_sum = term if conv_sum is None else conv_sum + term
    state1 = image + attended + conv_sum
    normed2 = layer_norm(state1, gain2).astype(BF16)
    hidden = dot(normed2, fc1[...])
    hidden = (0.5 * hidden * (1.0 + lax.erf(hidden * math.sqrt(0.5)))).astype(BF16)
    return state1 + dot_nt(hidden, fc2[...])


def middle_kernel(
    image_ref, top_ref, bottom_ref, gain1_ref, gain2_ref, fc1_ref, fc2_ref,
    bias, normed, q_mid, kv_mid, wkv, wp, wc, out_ref,
    bands, shifted, heads,
):
    rows, cols, channels = image_ref.shape
    head_dim = channels // HEADS
    wide = cols - 2 * SHIFT
    row, last_row = lax.axis_index("row"), lax.axis_size("row") - 1
    gain1 = gain1_ref[...]
    kv_band = []
    for i, (ref, edge) in enumerate(((top_ref, 0), (bottom_ref, last_row))):
        mark_lanes(
            bands, (i, slice(0, SHIFT), slice(0, cols)), (SHIFT, cols), channels, (row == edge).astype(F32)
        )
        bands[i, :, :, 0:channels] = layer_norm(ref[...].astype(F32), gain1)
        pixels = bands[i, :, SHIFT : cols - SHIFT].astype(BF16).reshape(-1, LANES)
        kv_band.append(dot(pixels, wkv[...]).astype(BF16))

    for window in range(rows // WIN + 1):
        start, stop = max(window * WIN - SHIFT, 0), min((window + 1) * WIN - SHIFT, rows)
        first = start - (window * WIN - SHIFT)
        pair = kv_mid[start:stop].reshape(-1, 2 * LANES)
        if window == 0:
            pair = jnp.concatenate([kv_band[0], pair], axis=0)
        if window == rows // WIN:
            pair = jnp.concatenate([pair, kv_band[1]], axis=0)
        for r in range(start, stop, SHIFT):
            part_bias = bias[:, first + r - start : first + r - start + SHIFT]
            part = q_mid[r : r + SHIFT].reshape(-1, LANES)
            result = attend(part, pair, part_bias, head_dim, channels)
            heads[r : r + SHIFT] = result.reshape(SHIFT, wide, LANES)

    for tap in range(3):
        c0 = SHIFT - 1 + tap
        shifted[tap, 0] = bands[0, SHIFT - 1, c0 : c0 + wide].astype(BF16)
        for r in range(0, rows, 8):
            shifted[tap, 1 + r : 9 + r] = normed[r : r + 8, c0 : c0 + wide].astype(BF16)
        shifted[tap, 1 + rows] = bands[1, 0, c0 : c0 + wide].astype(BF16)

    gain2 = gain2_ref[...]
    band = 16
    for r in range(0, rows, band):
        image = image_ref[r : r + band].astype(F32)[:, SHIFT : cols - SHIFT].reshape(-1, channels)
        raw = heads[r : r + band].reshape(-1, LANES)

        def pieces(row_tap, col_tap):
            return shifted[col_tap, r + row_tap : r + row_tap + band].reshape(-1, LANES)

        mixed = finish(raw, pieces, image, wp, wc, gain2, fc1_ref, fc2_ref, channels)
        out_ref[r : r + band] = mixed.reshape(band, wide, channels)


def side_kernel(
    image_ref, top_ref, bottom_ref, left_ref, right_ref, gain1_ref, gain2_ref, fc1_ref, fc2_ref,
    bias, normed, q_left, q_right, wkv, wp, wc, middle_ref, out_ref,
    side, kv, shifted, heads,
):
    rows, cols, channels = image_ref.shape
    head_dim = channels // HEADS
    tall = rows + 2 * SHIFT
    row, last_row = lax.axis_index("row"), lax.axis_size("row") - 1
    col, last_col = lax.axis_index("col"), lax.axis_size("col") - 1
    gain1 = gain1_ref[...]
    out_row = [(row == 0).astype(F32), (row == last_row).astype(F32)]
    out_col = [(col == 0).astype(F32), (col == last_col).astype(F32)]
    for s, (ref, halo, own, c0) in enumerate(
        ((left_ref, 0, SHIFT, 0), (right_ref, 2 * SHIFT, 0, cols - 2 * SHIFT))
    ):
        mark_lanes(side, (s, slice(0, SHIFT), slice(halo, halo + SHIFT)), (SHIFT, SHIFT), channels,
                   out_col[s] + out_row[0])
        mark_lanes(side, (s, slice(SHIFT, SHIFT + rows), slice(halo, halo + SHIFT)), (rows, SHIFT), channels,
                   out_col[s])
        mark_lanes(side, (s, slice(SHIFT + rows, tall), slice(halo, halo + SHIFT)), (SHIFT, SHIFT), channels,
                   out_col[s] + out_row[1])
        for r in range(0, tall, WIN):
            side[s, r : r + WIN, halo : halo + SHIFT, 0:channels] = layer_norm(
                ref[r : r + WIN].astype(F32), gain1
            )
        for i, (r0, band_ref) in enumerate(((0, top_ref), (SHIFT + rows, bottom_ref))):
            values = band_ref[...].astype(F32)[:, c0 : c0 + 2 * SHIFT]
            mark_lanes(side, (s, slice(r0, r0 + SHIFT), slice(own, own + 2 * SHIFT)), (SHIFT, 2 * SHIFT),
                       channels, out_row[i])
            side[s, r0 : r0 + SHIFT, own : own + 2 * SHIFT, 0:channels] = layer_norm(values, gain1)
        side[s, SHIFT : SHIFT + rows, own : own + 2 * SHIFT] = normed[:, c0 : c0 + 2 * SHIFT]

        k0 = 0 if s == 0 else SHIFT
        for r in range(0, tall, WIN):
            pixels = side[s, r : r + WIN, k0 : k0 + WIN].astype(BF16).reshape(-1, LANES)
            kv[s, r : r + WIN] = dot(pixels, wkv[...]).astype(BF16).reshape(WIN, WIN, 2 * LANES)

    for s, q_ref in enumerate((q_left, q_right)):
        px = SHIFT if s == 0 else 0
        for window in range(rows // WIN + 1):
            start, stop = max(window * WIN - SHIFT, 0), min((window + 1) * WIN - SHIFT, rows)
            first = start - (window * WIN - SHIFT)
            pair = kv[s, window * WIN : (window + 1) * WIN].reshape(-1, 2 * LANES)
            part_bias = bias[:, first : first + stop - start, px : px + SHIFT]
            part = q_ref[start:stop].reshape(-1, LANES)
            result = attend(part, pair, part_bias, head_dim, channels)
            heads[s, start:stop] = result.reshape(stop - start, SHIFT, LANES)

    for s in range(2):
        for tap in range(3):
            c0 = (SHIFT if s == 0 else SHIFT) - 1 + tap
            for r in range(0, rows + 2, 8):
                stop = min(r + 8, rows + 2)
                shifted[tap, s, r:stop] = side[s, SHIFT - 1 + r : SHIFT - 1 + stop, c0 : c0 + SHIFT]

    gain2 = gain2_ref[...]
    band = 16
    for r in range(0, rows, band):
        whole = image_ref[r : r + band].astype(F32)
        image = jnp.concatenate(
            [whole[:, :SHIFT].reshape(-1, channels), whole[:, cols - SHIFT :].reshape(-1, channels)], axis=0
        )
        raw = heads[:, r : r + band].reshape(-1, LANES)

        def pieces(row_tap, col_tap):
            piece = shifted[col_tap, :, r + row_tap : r + row_tap + band]
            return piece.reshape(-1, LANES).astype(BF16)

        mixed = finish(raw, pieces, image, wp, wc, gain2, fc1_ref, fc2_ref, channels)
        mixed = mixed.reshape(2, band, SHIFT, channels)
        whole = jnp.concatenate([mixed[0], middle_ref[r : r + band], mixed[1]], axis=1)
        out_ref[r : r + band] = whole.astype(BF16)


def from_neighbour(block, axis, step):
    count = lax.axis_size(axis)
    pairs = [(i, i + step) for i in range(count) if 0 <= i + step < count]
    return lax.ppermute(block, axis, pairs)


def call(kernel, name, outs, scratch, flops, operands):
    vmem = pl.BlockSpec(memory_space=pltpu.VMEM)
    return pl.pallas_call(
        kernel,
        out_shape=[jax.ShapeDtypeStruct(shape, kind) for shape, kind in outs],
        in_specs=[vmem] * len(operands),
        out_specs=[vmem] * len(outs),
        scratch_shapes=[pltpu.VMEM(shape, kind) for shape, kind in scratch],
        cost_estimate=pl.CostEstimate(flops=flops, bytes_accessed=4_000_000, transcendentals=1_000_000),
        compiler_params=pltpu.CompilerParams(vmem_limit_bytes=24 * 1024 * 1024),
        name=name,
    )(*operands)


def on_device(
    image, norm1_gain, norm2_gain, qkv_weight, proj_weight, rel_table, conv_weight, fc1_weight,
    fc2_weight,
):
    rows, cols, channels = image.shape
    tall, wide = rows + 2 * SHIFT, cols - 2 * SHIFT
    gain1, gain2, fc2 = norm1_gain[None], norm2_gain[None], fc2_weight.T
    top = from_neighbour(image[rows - SHIFT :], "row", 1)
    bottom = from_neighbour(image[:SHIFT], "row", -1)
    bias, normed, q_mid, q_left, q_right, kv_mid, wkv, wp, wc = call(
        own_kernel,
        "own_tile",
        [
            ((HEADS, WIN, WIN, WIN * WIN), F32),
            ((rows, cols, LANES), F32),
            ((rows, wide, LANES), F32),
            ((rows, SHIFT, LANES), F32),
            ((rows, SHIFT, LANES), F32),
            ((rows, wide, 2 * LANES), BF16),
            ((LANES, 2 * LANES), BF16),
            ((LANES, channels), BF16),
            ((3, 3, LANES, channels), BF16),
        ],
        [((8, 1024), F32), ((4, 8 * WIN, 128), F32), ((LANES, LANES), BF16)],
        2_000_000_000,
        (image, gain1, qkv_weight, proj_weight, rel_table.T, conv_weight),
    )
    left_part = jnp.concatenate([top[:, cols - SHIFT :], image[:, cols - SHIFT :], bottom[:, cols - SHIFT :]])
    right_part = jnp.concatenate([top[:, :SHIFT], image[:, :SHIFT], bottom[:, :SHIFT]])
    left = from_neighbour(left_part, "col", 1)
    right = from_neighbour(right_part, "col", -1)
    (middle,) = call(
        middle_kernel,
        "middle_columns",
        [((rows, wide, channels), F32)],
        [
            ((2, SHIFT, cols, LANES), F32),
            ((3, rows + 2, wide, LANES), BF16),
            ((rows, wide, LANES), F32),
        ],
        2_000_000_000,
        (image, top, bottom, gain1, gain2, fc1_weight, fc2, bias, normed, q_mid, kv_mid, wkv, wp, wc),
    )
    (out,) = call(
        side_kernel,
        "side_columns",
        [(image.shape, BF16)],
        [
            ((2, tall, 3 * SHIFT, LANES), F32),
            ((2, tall, WIN, 2 * LANES), BF16),
            ((3, 2, rows + 2, SHIFT, LANES), F32),
            ((2, rows, SHIFT, LANES), F32),
        ],
        2_000_000_000,
        (image, top, bottom, left, right, gain1, gain2, fc1_weight, fc2, bias, normed, q_left, q_right,
         wkv, wp, wc, middle),
    )
    return out


def solution(mesh):
    placed = (P("row", "col", None), P(), P(), P(), P(), P(), P(), P(), P())
    return jax.shard_map(
        on_device, mesh=mesh, in_specs=placed, out_specs=P("row", "col", None), check_vma=False
    )
```

```python
import functools
import math

import jax
import jax.numpy as jnp
from jax import lax
from jax.experimental import pallas as pl
from jax.experimental.pallas import tpu as pltpu
from jax.sharding import PartitionSpec as P

HEADS = 6
WIN = 16
SHIFT = 8
LANES = 256
HALF = LANES // 2
F32 = jnp.float32
BF16 = jnp.bfloat16
LOG2E = math.log2(math.e)
MASKED = -4.0e9


def layer_norm(values, norm_gain):
    centre = jnp.mean(values, axis=-1, keepdims=True)
    values = values - centre
    spread = jnp.mean(values * values, axis=-1, keepdims=True)
    return values * lax.rsqrt(spread + 1e-05) * norm_gain


def dot(a, b):
    return jnp.dot(a, b, preferred_element_type=F32)


def dot_nt(a, b):
    return lax.dot_general(a, b, (((1,), (1,)), ((), ())), preferred_element_type=F32)


def one_hot(condition):
    return jnp.where(condition, 1.0, 0.0).astype(BF16)


def gelu(x):
    size = jnp.abs(x)
    t = 1.0 / (1.0 + (0.3275911 * math.sqrt(0.5)) * size)
    poly = 0.5 * 1.061405429
    for factor in (-1.453152027, 1.421413741, -0.284496736, 0.254829592):
        poly = poly * t + 0.5 * factor
    tail = poly * t * jnp.exp2(size * size * (-0.5 * LOG2E))
    return jnp.maximum(x, 0.0) - size * tail


def lanes_of(width=LANES):
    return lax.broadcasted_iota(jnp.int32, (1, width), 1)


def mark_lanes(ref, place, shape, channels, outside):
    half = lanes_of()[:, HALF:]
    mark = jnp.where(half == channels + 1, 1.0, 0.0) + jnp.where(half == channels, outside, 0.0)
    ref[(*place, slice(HALF, LANES))] = jnp.broadcast_to(mark[None], (*shape, HALF))


def expand_bias(table_ref, padded, strip, bias):
    span = 2 * WIN - 1
    padded[...] = jnp.zeros_like(padded)
    padded[0:HEADS, 0 : span * span] = table_ref[...] * LOG2E
    table = padded[...]
    width = padded.shape[1]
    shifted = jnp.concatenate(
        [table if px == 0 else pltpu.roll(table, width - px, 1) for px in range(WIN)], axis=0
    )
    high = shifted.astype(BF16)
    low = (shifted - high.astype(F32)).astype(BF16)
    entry = lax.broadcasted_iota(jnp.int32, (width, 512), 0)
    place = lax.broadcasted_iota(jnp.int32, (1, 512), 1)
    wanted = (2 * WIN - 2 - lax.div(place, WIN)) * span + WIN - 1 - lax.rem(place, WIN)
    picked = dot(jnp.concatenate([high, low], axis=0), one_hot(entry == wanted))
    half = 8 * WIN
    picked = picked[:half] + picked[half:]
    for tile in range(4):
        strip[tile] = picked[:, 128 * tile : 128 * (tile + 1)]
    for head in range(HEADS):
        rows = jnp.concatenate(
            [strip[tile, pl.ds(head, WIN, stride=8), :] for tile in range(4)], axis=1
        )
        for turn in range(8):
            rolled = rows if turn == 0 else pltpu.roll(rows, 512 - 16 * turn, 1)
            bias[head, 15 - turn] = rolled[:, 0:256]
            bias[head, 7 - turn] = rolled[:, 128:384]


def own_kernel(
    image_hbm, gain1_ref, qkv_hbm, proj_hbm, table_hbm, conv_hbm,
    bias, normed, q_mid, q_left, q_right, kv_mid, wkv, wp, wc, first_cols, last_cols,
    padded, strip, wq, table_ref, image_ref, qkv_ref, proj_ref, conv_ref, sems,
):
    rows, cols, channels = image_ref.shape
    head_dim = channels // HEADS
    flag_lane, one_lane = channels, channels + 1
    fetches = [
        pltpu.make_async_copy(source, target, sems.at[i])
        for i, (source, target) in enumerate(
            ((table_hbm, table_ref), (image_hbm, image_ref), (qkv_hbm, qkv_ref),
             (proj_hbm, proj_ref), (conv_hbm, conv_ref))
        )
    ]
    for fetch in fetches:
        fetch.start()
    fetches[0].wait()
    expand_bias(table_ref, padded, strip, bias)
    for fetch in fetches[1:]:
        fetch.wait()
    first_cols[...] = image_ref[...].astype(F32)[:, :SHIFT].astype(BF16)
    last_cols[...] = image_ref[...].astype(F32)[:, cols - SHIFT :].astype(BF16)

    for ref in (wq, wkv, wp, wc):
        ref[...] = jnp.zeros_like(ref)
    special = lax.broadcasted_iota(jnp.int32, (16, LANES), 0) + 176
    lanes16 = lax.broadcasted_iota(jnp.int32, (16, LANES), 1)
    wq[176:192, :] = one_hot((special == one_lane) & (lanes16 == flag_lane))
    wkv[176:192, 0:LANES] = jnp.where(
        (special == flag_lane) & (lanes16 == flag_lane), MASKED, 0.0
    ).astype(BF16)
    wkv[176:192, LANES:] = one_hot(
        (special == one_lane) & (lanes16 >= channels) & (lanes16 < channels + HEADS)
    )
    wq[0:channels, 0:channels] = qkv_ref[:, 0:channels]
    wkv[0:channels, 0:channels] = qkv_ref[:, channels : 2 * channels]
    wkv[0:channels, LANES : LANES + channels] = qkv_ref[:, 2 * channels :]
    wp[0:channels, :] = proj_ref[...]
    for row_tap in range(3):
        for col_tap in range(3):
            tap = (3 * row_tap + col_tap) * LANES
            wc[tap : tap + channels, :] = conv_ref[row_tap, col_tap]

    mark_lanes(normed, (slice(0, rows), slice(0, cols)), (rows, cols), channels, 0.0)
    gain1 = gain1_ref[...]
    for r in range(0, rows, 8):
        normed[r : r + 8, :, 0:channels] = layer_norm(image_ref[r : r + 8].astype(F32), gain1)

    scale = head_dim**-0.5 * LOG2E
    for r in range(0, rows, 8):
        pixels = normed[r : r + 8].astype(BF16).reshape(-1, LANES)
        q = (dot(pixels, wq[...]) * scale).reshape(8, cols, LANES)
        q_left[r : r + 8] = q[:, :SHIFT]
        q_mid[r : r + 8] = q[:, SHIFT : cols - SHIFT]
        q_right[r : r + 8] = q[:, cols - SHIFT :]
        middle = normed[r : r + 8, SHIFT : cols - SHIFT].astype(BF16).reshape(-1, LANES)
        kv = dot(middle, wkv[...]).astype(BF16)
        kv_mid[r : r + 8] = kv.reshape(8, cols - 2 * SHIFT, 2 * LANES)


def attend(part, pair, part_bias, head_dim, channels):
    lane = lanes_of()
    keys, values = pair[:, :LANES], pair[:, LANES:]
    count = part.shape[0]
    own = [(lane >= h * head_dim) & (lane < (h + 1) * head_dim) for h in range(HEADS)]
    stacked = jnp.concatenate(
        [jnp.where(own[h] | (lane == channels), part, 0.0).astype(BF16) for h in range(HEADS)],
        axis=0,
    )
    scores = dot_nt(stacked, keys).reshape(HEADS, count, WIN * WIN)
    scores = scores + part_bias.reshape(HEADS, count, WIN * WIN)
    scores = scores - jnp.max(scores, axis=-1, keepdims=True)
    soft = jnp.exp2(scores).astype(BF16).reshape(HEADS * count, WIN * WIN)
    mixed = dot(soft, values)
    result = mixed[0:count]
    for h in range(1, HEADS):
        mine = own[h] | (lane == channels + h)
        result = jnp.where(mine, mixed[h * count : (h + 1) * count], result)
    return result


def finish(raw, pieces, image, wp, wc, gain2, fc1, fc2, channels):
    head_dim = channels // HEADS
    half = lanes_of()[:, HALF:]
    sum_row = lax.broadcasted_iota(jnp.int32, (HALF, LANES), 0) + HALF - channels
    lane_wide = lax.broadcasted_iota(jnp.int32, (HALF, LANES), 1)
    spread = one_hot(
        (sum_row >= 0) & (lane_wide >= sum_row * head_dim) & (lane_wide < (sum_row + 1) * head_dim)
        & (lane_wide < channels)
    )
    is_sum = (half >= channels) & (half < channels + HEADS)
    inverse = jnp.where(is_sum, 1.0 / raw[:, HALF:], 0.0)
    high = inverse.astype(BF16)
    low = (inverse - high.astype(F32)).astype(BF16)
    heads_out = (raw * (dot(high, spread) + dot(low, spread))).astype(BF16)
    attended = dot(heads_out, wp[...]).astype(BF16).astype(F32)
    taps = [pieces(row_tap, col_tap) for row_tap in range(3) for col_tap in range(3)]
    conv_sum = dot(jnp.concatenate(taps, axis=1), wc[...])
    state1 = image + attended + conv_sum
    normed2 = layer_norm(state1, gain2).astype(BF16)
    hidden = dot(normed2, fc1[...])
    hidden = gelu(hidden).astype(BF16)
    return state1 + dot_nt(hidden, fc2[...])


def middle_kernel(
    image_ref, top_ref, bottom_ref, gain1_ref, gain2_ref, fc1_ref, fc2_ref,
    bias, normed, q_mid, kv_mid, wkv, wp, wc, out_ref,
    bands, shifted, heads,
):
    rows, cols, channels = image_ref.shape
    head_dim = channels // HEADS
    wide = cols - 2 * SHIFT
    row, last_row = lax.axis_index("row"), lax.axis_size("row") - 1
    gain1 = gain1_ref[...]
    kv_band = []
    for i, (ref, edge) in enumerate(((top_ref, 0), (bottom_ref, last_row))):
        mark_lanes(
            bands, (i, slice(0, SHIFT), slice(0, cols)), (SHIFT, cols), channels, (row == edge).astype(F32)
        )
        bands[i, :, :, 0:channels] = layer_norm(ref[...].astype(F32), gain1)
        pixels = bands[i, :, SHIFT : cols - SHIFT].astype(BF16).reshape(-1, LANES)
        kv_band.append(dot(pixels, wkv[...]).astype(BF16))

    for window in range(rows // WIN + 1):
        start, stop = max(window * WIN - SHIFT, 0), min((window + 1) * WIN - SHIFT, rows)
        first = start - (window * WIN - SHIFT)
        pair = kv_mid[start:stop].reshape(-1, 2 * LANES)
        if window == 0:
            pair = jnp.concatenate([kv_band[0], pair], axis=0)
        if window == rows // WIN:
            pair = jnp.concatenate([pair, kv_band[1]], axis=0)
        for r in range(start, stop, SHIFT):
            part_bias = bias[:, first + r - start : first + r - start + SHIFT]
            part = q_mid[r : r + SHIFT].reshape(-1, LANES)
            result = attend(part, pair, part_bias, head_dim, channels)
            heads[r : r + SHIFT] = result.reshape(SHIFT, wide, LANES)

    for tap in range(3):
        c0 = SHIFT - 1 + tap
        shifted[tap, 0] = bands[0, SHIFT - 1, c0 : c0 + wide].astype(BF16)
        for r in range(0, rows, 8):
            shifted[tap, 1 + r : 9 + r] = normed[r : r + 8, c0 : c0 + wide].astype(BF16)
        shifted[tap, 1 + rows] = bands[1, 0, c0 : c0 + wide].astype(BF16)

    gain2 = gain2_ref[...]
    band = 16
    for r in range(0, rows, band):
        image = image_ref[r : r + band].astype(F32)[:, SHIFT : cols - SHIFT].reshape(-1, channels)
        raw = heads[r : r + band].reshape(-1, LANES)

        def pieces(row_tap, col_tap):
            return shifted[col_tap, r + row_tap : r + row_tap + band].reshape(-1, LANES)

        mixed = finish(raw, pieces, image, wp, wc, gain2, fc1_ref, fc2_ref, channels)
        out_ref[r : r + band] = mixed.reshape(band, wide, channels)


def side_kernel(
    image_ref, top_ref, bottom_ref, left_ref, right_ref, gain1_ref, gain2_ref, fc1_ref, fc2_ref,
    bias, normed, q_left, q_right, wkv, wp, wc, middle_ref, out_ref,
    side, kv, shifted, heads,
):
    rows, cols, channels = image_ref.shape
    head_dim = channels // HEADS
    tall = rows + 2 * SHIFT
    row, last_row = lax.axis_index("row"), lax.axis_size("row") - 1
    col, last_col = lax.axis_index("col"), lax.axis_size("col") - 1
    gain1 = gain1_ref[...]
    out_row = [(row == 0).astype(F32), (row == last_row).astype(F32)]
    out_col = [(col == 0).astype(F32), (col == last_col).astype(F32)]
    for s, (ref, halo, own, c0) in enumerate(
        ((left_ref, 0, SHIFT, 0), (right_ref, 2 * SHIFT, 0, cols - 2 * SHIFT))
    ):
        mark_lanes(side, (s, slice(0, SHIFT), slice(halo, halo + SHIFT)), (SHIFT, SHIFT), channels,
                   out_col[s] + out_row[0])
        mark_lanes(side, (s, slice(SHIFT, SHIFT + rows), slice(halo, halo + SHIFT)), (rows, SHIFT), channels,
                   out_col[s])
        mark_lanes(side, (s, slice(SHIFT + rows, tall), slice(halo, halo + SHIFT)), (SHIFT, SHIFT), channels,
                   out_col[s] + out_row[1])
        for r in range(0, tall, WIN):
            side[s, r : r + WIN, halo : halo + SHIFT, 0:channels] = layer_norm(
                ref[r : r + WIN].astype(F32), gain1
            )
        for i, (r0, band_ref) in enumerate(((0, top_ref), (SHIFT + rows, bottom_ref))):
            values = band_ref[...].astype(F32)[:, c0 : c0 + 2 * SHIFT]
            mark_lanes(side, (s, slice(r0, r0 + SHIFT), slice(own, own + 2 * SHIFT)), (SHIFT, 2 * SHIFT),
                       channels, out_row[i])
            side[s, r0 : r0 + SHIFT, own : own + 2 * SHIFT, 0:channels] = layer_norm(values, gain1)
        side[s, SHIFT : SHIFT + rows, own : own + 2 * SHIFT] = normed[:, c0 : c0 + 2 * SHIFT]

        k0 = 0 if s == 0 else SHIFT
        for r in range(0, tall, WIN):
            pixels = side[s, r : r + WIN, k0 : k0 + WIN].astype(BF16).reshape(-1, LANES)
            kv[s, r : r + WIN] = dot(pixels, wkv[...]).astype(BF16).reshape(WIN, WIN, 2 * LANES)

    for s, q_ref in enumerate((q_left, q_right)):
        px = SHIFT if s == 0 else 0
        for window in range(rows // WIN + 1):
            start, stop = max(window * WIN - SHIFT, 0), min((window + 1) * WIN - SHIFT, rows)
            first = start - (window * WIN - SHIFT)
            pair = kv[s, window * WIN : (window + 1) * WIN].reshape(-1, 2 * LANES)
            part_bias = bias[:, first : first + stop - start, px : px + SHIFT]
            part = q_ref[start:stop].reshape(-1, LANES)
            result = attend(part, pair, part_bias, head_dim, channels)
            heads[s, start:stop] = result.reshape(stop - start, SHIFT, LANES)

    for s in range(2):
        for tap in range(3):
            c0 = (SHIFT if s == 0 else SHIFT) - 1 + tap
            for r in range(0, rows + 2, 8):
                stop = min(r + 8, rows + 2)
                shifted[tap, s, r:stop] = side[s, SHIFT - 1 + r : SHIFT - 1 + stop, c0 : c0 + SHIFT]

    gain2 = gain2_ref[...]
    band = 16
    for r in range(0, rows, band):
        whole = image_ref[r : r + band].astype(F32)
        image = jnp.concatenate(
            [whole[:, :SHIFT].reshape(-1, channels), whole[:, cols - SHIFT :].reshape(-1, channels)], axis=0
        )
        raw = heads[:, r : r + band].reshape(-1, LANES)

        def pieces(row_tap, col_tap):
            piece = shifted[col_tap, :, r + row_tap : r + row_tap + band]
            return piece.reshape(-1, LANES).astype(BF16)

        mixed = finish(raw, pieces, image, wp, wc, gain2, fc1_ref, fc2_ref, channels)
        mixed = mixed.reshape(2, band, SHIFT, channels)
        whole = jnp.concatenate([mixed[0], middle_ref[r : r + band], mixed[1]], axis=1)
        out_ref[r : r + band] = whole.astype(BF16)


def swap(low, high, axis):
    count, place = lax.axis_size(axis), lax.axis_index(axis)
    even = lax.rem(place, 2) == 0

    def pairs(first):
        after = {i: i + 1 for i in range(first, count - 1, 2)}
        before = {j: i for i, j in after.items()}
        return [(i, after.get(i, before.get(i, i))) for i in range(count)]

    one = lax.ppermute(jnp.where(even, high, low), axis, pairs(0))
    other = lax.ppermute(jnp.where(even, low, high), axis, pairs(1))
    zero = jnp.zeros_like(one)
    before = jnp.where(place == 0, zero, jnp.where(even, other, one))
    after = jnp.where(place == count - 1, zero, jnp.where(even, one, other))
    return before, after


def call(kernel, name, outs, scratch, flops, operands, in_hbm=()):
    vmem = pl.BlockSpec(memory_space=pltpu.VMEM)
    hbm = pl.BlockSpec(memory_space=pltpu.HBM)
    return pl.pallas_call(
        kernel,
        out_shape=[jax.ShapeDtypeStruct(shape, kind) for shape, kind in outs],
        in_specs=[hbm if i in in_hbm else vmem for i in range(len(operands))],
        out_specs=[vmem] * len(outs),
        scratch_shapes=[pltpu.VMEM(*s) if isinstance(s, tuple) else s for s in scratch],
        cost_estimate=pl.CostEstimate(flops=flops, bytes_accessed=4_000_000, transcendentals=1_000_000),
        compiler_params=pltpu.CompilerParams(vmem_limit_bytes=24 * 1024 * 1024),
        name=name,
    )(*operands)


def on_device(
    image, norm1_gain, norm2_gain, qkv_weight, proj_weight, rel_table, conv_weight, fc1_weight,
    fc2_weight,
):
    rows, cols, channels = image.shape
    tall, wide = rows + 2 * SHIFT, cols - 2 * SHIFT
    gain1, gain2, fc2 = norm1_gain[None], norm2_gain[None], fc2_weight.T
    top, bottom = swap(image[:SHIFT], image[rows - SHIFT :], "row")
    bias, normed, q_mid, q_left, q_right, kv_mid, wkv, wp, wc, first_cols, last_cols = call(
        own_kernel,
        "own_tile",
        [
            ((HEADS, WIN, WIN, WIN * WIN), F32),
            ((rows, cols, LANES), F32),
            ((rows, wide, LANES), F32),
            ((rows, SHIFT, LANES), F32),
            ((rows, SHIFT, LANES), F32),
            ((rows, wide, 2 * LANES), BF16),
            ((LANES, 2 * LANES), BF16),
            ((LANES, channels), BF16),
            ((9 * LANES, channels), BF16),
            ((rows, SHIFT, channels), BF16),
            ((rows, SHIFT, channels), BF16),
        ],
        [
            ((8, 1024), F32), ((4, 8 * WIN, 128), F32), ((LANES, LANES), BF16),
            (rel_table.T.shape, F32), (image.shape, BF16), (qkv_weight.shape, BF16),
            (proj_weight.shape, BF16), (conv_weight.shape, BF16), pltpu.SemaphoreType.DMA((5,)),
        ],
        2_000_000_000,
        (image, gain1, qkv_weight, proj_weight, rel_table.T, conv_weight),
        (0, 2, 3, 4, 5),
    )
    first_part = jnp.concatenate([top[:, :SHIFT], first_cols, bottom[:, :SHIFT]])
    last_part = jnp.concatenate([top[:, cols - SHIFT :], last_cols, bottom[:, cols - SHIFT :]])
    left, right = swap(first_part, last_part, "col")
    (middle,) = call(
        middle_kernel,
        "middle_columns",
        [((rows, wide, channels), F32)],
        [
            ((2, SHIFT, cols, LANES), F32),
            ((3, rows + 2, wide, LANES), BF16),
            ((rows, wide, LANES), F32),
        ],
        2_000_000_000,
        (image, top, bottom, gain1, gain2, fc1_weight, fc2, bias, normed, q_mid, kv_mid, wkv, wp, wc),
    )
    (out,) = call(
        side_kernel,
        "side_columns",
        [(image.shape, BF16)],
        [
            ((2, tall, 3 * SHIFT, LANES), F32),
            ((2, tall, WIN, 2 * LANES), BF16),
            ((3, 2, rows + 2, SHIFT, LANES), F32),
            ((2, rows, SHIFT, LANES), F32),
        ],
        2_000_000_000,
        (image, top, bottom, left, right, gain1, gain2, fc1_weight, fc2, bias, normed, q_left, q_right,
         wkv, wp, wc, middle),
    )
    return out


def solution(mesh):
    placed = (P("row", "col", None), P(), P(), P(), P(), P(), P(), P(), P())
    return jax.shard_map(
        on_device, mesh=mesh, in_specs=placed, out_specs=P("row", "col", None), check_vma=False
    )
```

```python
import functools
import math

import jax
import jax.numpy as jnp
from jax import lax
from jax.experimental import pallas as pl
from jax.experimental.pallas import tpu as pltpu
from jax.sharding import PartitionSpec as P

HEADS = 6
WIN = 16
SHIFT = 8
LANES = 256
HALF = LANES // 2
F32 = jnp.float32
BF16 = jnp.bfloat16
LOG2E = math.log2(math.e)
MASKED = -4.0e9


def layer_norm(values, norm_gain):
    centre = jnp.mean(values, axis=-1, keepdims=True)
    values = values - centre
    spread = jnp.mean(values * values, axis=-1, keepdims=True)
    return values * lax.rsqrt(spread + 1e-05) * norm_gain


def dot(a, b):
    return jnp.dot(a, b, preferred_element_type=F32)


def dot_nt(a, b):
    return lax.dot_general(a, b, (((1,), (1,)), ((), ())), preferred_element_type=F32)


def one_hot(condition):
    return jnp.where(condition, 1.0, 0.0).astype(BF16)


def gelu(x):
    size = jnp.abs(x)
    t = 1.0 / (1.0 + (0.3275911 * math.sqrt(0.5)) * size)
    poly = 0.5 * 1.061405429
    for factor in (-1.453152027, 1.421413741, -0.284496736, 0.254829592):
        poly = poly * t + 0.5 * factor
    tail = poly * t * jnp.exp2(size * size * (-0.5 * LOG2E))
    return jnp.maximum(x, 0.0) - size * tail


def lanes_of(width=LANES):
    return lax.broadcasted_iota(jnp.int32, (1, width), 1)


def mark_lanes(ref, place, shape, channels, outside):
    half = lanes_of()[:, HALF:]
    mark = jnp.where(half == channels + 1, 1.0, 0.0) + jnp.where(half == channels, outside, 0.0)
    ref[(*place, slice(HALF, LANES))] = jnp.broadcast_to(mark[None], (*shape, HALF))


def expand_bias(table_ref, padded, strip, bias):
    span = 2 * WIN - 1
    padded[...] = jnp.zeros_like(padded)
    padded[0:HEADS, 0 : span * span] = table_ref[...] * LOG2E
    table = padded[...]
    width = padded.shape[1]
    shifted = jnp.concatenate(
        [table if px == 0 else pltpu.roll(table, width - px, 1) for px in range(WIN)], axis=0
    )
    high = shifted.astype(BF16)
    low = (shifted - high.astype(F32)).astype(BF16)
    entry = lax.broadcasted_iota(jnp.int32, (width, 512), 0)
    place = lax.broadcasted_iota(jnp.int32, (1, 512), 1)
    wanted = (2 * WIN - 2 - lax.div(place, WIN)) * span + WIN - 1 - lax.rem(place, WIN)
    picked = dot(jnp.concatenate([high, low], axis=0), one_hot(entry == wanted))
    half = 8 * WIN
    picked = picked[:half] + picked[half:]
    for tile in range(4):
        strip[tile] = picked[:, 128 * tile : 128 * (tile + 1)]
    for head in range(HEADS):
        rows = jnp.concatenate(
            [strip[tile, pl.ds(head, WIN, stride=8), :] for tile in range(4)], axis=1
        )
        for turn in range(8):
            rolled = rows if turn == 0 else pltpu.roll(rows, 512 - 16 * turn, 1)
            bias[head, 15 - turn] = rolled[:, 0:256]
            bias[head, 7 - turn] = rolled[:, 128:384]


def own_kernel(
    image_hbm, gain1_hbm, qkv_hbm, proj_hbm, table_hbm, conv_hbm,
    bias, normed, q_mid, q_left, q_right, kv_mid, wkv, wp, wc, first_cols, last_cols,
    padded, strip, wq, table_ref, image_ref, gain1_ref, qkv_ref, proj_ref, conv_ref, sems,
):
    rows, cols, channels = image_ref.shape
    head_dim = channels // HEADS
    flag_lane, one_lane = channels, channels + 1
    fetches = [
        pltpu.make_async_copy(source, target, sems.at[i])
        for i, (source, target) in enumerate(
            ((table_hbm, table_ref), (image_hbm, image_ref), (gain1_hbm, gain1_ref), (qkv_hbm, qkv_ref),
             (proj_hbm, proj_ref), (conv_hbm, conv_ref))
        )
    ]
    for fetch in fetches:
        fetch.start()
    fetches[0].wait()
    expand_bias(table_ref, padded, strip, bias)
    for fetch in fetches[1:]:
        fetch.wait()
    first_cols[...] = image_ref[...].astype(F32)[:, :SHIFT].astype(BF16)
    last_cols[...] = image_ref[...].astype(F32)[:, cols - SHIFT :].astype(BF16)

    for ref in (wq, wkv, wp, wc):
        ref[...] = jnp.zeros_like(ref)
    special = lax.broadcasted_iota(jnp.int32, (16, LANES), 0) + 176
    lanes16 = lax.broadcasted_iota(jnp.int32, (16, LANES), 1)
    wq[176:192, :] = one_hot((special == one_lane) & (lanes16 == flag_lane))
    wkv[176:192, 0:LANES] = jnp.where(
        (special == flag_lane) & (lanes16 == flag_lane), MASKED, 0.0
    ).astype(BF16)
    wkv[176:192, LANES:] = one_hot(
        (special == one_lane) & (lanes16 >= channels) & (lanes16 < channels + HEADS)
    )
    wq[0:channels, 0:channels] = qkv_ref[:, 0:channels]
    wkv[0:channels, 0:channels] = qkv_ref[:, channels : 2 * channels]
    wkv[0:channels, LANES : LANES + channels] = qkv_ref[:, 2 * channels :]
    wp[0:channels, :] = proj_ref[...]
    for row_tap in range(3):
        for col_tap in range(3):
            tap = (3 * row_tap + col_tap) * LANES
            wc[tap : tap + channels, :] = conv_ref[row_tap, col_tap]

    mark_lanes(normed, (slice(0, rows), slice(0, cols)), (rows, cols), channels, 0.0)
    gain1 = gain1_ref[...]
    for r in range(0, rows, 8):
        normed[r : r + 8, :, 0:channels] = layer_norm(image_ref[r : r + 8].astype(F32), gain1)

    scale = head_dim**-0.5 * LOG2E
    for r in range(0, rows, 8):
        pixels = normed[r : r + 8].astype(BF16).reshape(-1, LANES)
        q = (dot(pixels, wq[...]) * scale).reshape(8, cols, LANES)
        q_left[r : r + 8] = q[:, :SHIFT]
        q_mid[r : r + 8] = q[:, SHIFT : cols - SHIFT]
        q_right[r : r + 8] = q[:, cols - SHIFT :]
        middle = normed[r : r + 8, SHIFT : cols - SHIFT].astype(BF16).reshape(-1, LANES)
        kv = dot(middle, wkv[...]).astype(BF16)
        kv_mid[r : r + 8] = kv.reshape(8, cols - 2 * SHIFT, 2 * LANES)


def attend(part, pair, part_bias, head_dim, channels):
    lane = lanes_of()
    keys, values = pair[:, :LANES], pair[:, LANES:]
    count = part.shape[0]
    own = [(lane >= h * head_dim) & (lane < (h + 1) * head_dim) for h in range(HEADS)]
    stacked = jnp.concatenate(
        [jnp.where(own[h] | (lane == channels), part, 0.0).astype(BF16) for h in range(HEADS)],
        axis=0,
    )
    scores = dot_nt(stacked, keys).reshape(HEADS, count, WIN * WIN)
    scores = scores + part_bias.reshape(HEADS, count, WIN * WIN)
    scores = scores - jnp.max(scores, axis=-1, keepdims=True)
    soft = jnp.exp2(scores).astype(BF16).reshape(HEADS * count, WIN * WIN)
    mixed = dot(soft, values)
    result = mixed[0:count]
    for h in range(1, HEADS):
        mine = own[h] | (lane == channels + h)
        result = jnp.where(mine, mixed[h * count : (h + 1) * count], result)
    return result


def finish(raw, pieces, image, wp, wc, gain2, fc1, fc2, channels):
    head_dim = channels // HEADS
    half = lanes_of()[:, HALF:]
    sum_row = lax.broadcasted_iota(jnp.int32, (HALF, LANES), 0) + HALF - channels
    lane_wide = lax.broadcasted_iota(jnp.int32, (HALF, LANES), 1)
    spread = one_hot(
        (sum_row >= 0) & (lane_wide >= sum_row * head_dim) & (lane_wide < (sum_row + 1) * head_dim)
        & (lane_wide < channels)
    )
    is_sum = (half >= channels) & (half < channels + HEADS)
    inverse = jnp.where(is_sum, 1.0 / raw[:, HALF:], 0.0)
    high = inverse.astype(BF16)
    low = (inverse - high.astype(F32)).astype(BF16)
    heads_out = (raw * (dot(high, spread) + dot(low, spread))).astype(BF16)
    attended = dot(heads_out, wp[...]).astype(BF16).astype(F32)
    taps = [pieces(row_tap, col_tap) for row_tap in range(3) for col_tap in range(3)]
    conv_sum = dot(jnp.concatenate(taps, axis=1), wc[...])
    state1 = image + attended + conv_sum
    normed2 = layer_norm(state1, gain2).astype(BF16)
    hidden = dot(normed2, fc1[...])
    hidden = gelu(hidden).astype(BF16)
    return state1 + dot_nt(hidden, fc2[...])


def middle_kernel(
    image_ref, top_ref, bottom_ref, gain1_ref, gain2_ref, fc1_ref, fc2_ref,
    bias, normed, q_mid, kv_mid, wkv, wp, wc, out_ref,
    bands, shifted, heads,
):
    rows, cols, channels = image_ref.shape
    head_dim = channels // HEADS
    wide = cols - 2 * SHIFT
    row, last_row = lax.axis_index("row"), lax.axis_size("row") - 1
    gain1 = gain1_ref[...]
    kv_band = []
    for i, (ref, edge) in enumerate(((top_ref, 0), (bottom_ref, last_row))):
        mark_lanes(
            bands, (i, slice(0, SHIFT), slice(0, cols)), (SHIFT, cols), channels, (row == edge).astype(F32)
        )
        inside = gain1 * (row != edge).astype(F32)
        bands[i, :, :, 0:channels] = layer_norm(ref[...].astype(F32), inside)
        pixels = bands[i, :, SHIFT : cols - SHIFT].astype(BF16).reshape(-1, LANES)
        kv_band.append(dot(pixels, wkv[...]).astype(BF16))

    for window in range(rows // WIN + 1):
        start, stop = max(window * WIN - SHIFT, 0), min((window + 1) * WIN - SHIFT, rows)
        first = start - (window * WIN - SHIFT)
        pair = kv_mid[start:stop].reshape(-1, 2 * LANES)
        if window == 0:
            pair = jnp.concatenate([kv_band[0], pair], axis=0)
        if window == rows // WIN:
            pair = jnp.concatenate([pair, kv_band[1]], axis=0)
        for r in range(start, stop, SHIFT):
            part_bias = bias[:, first + r - start : first + r - start + SHIFT]
            part = q_mid[r : r + SHIFT].reshape(-1, LANES)
            result = attend(part, pair, part_bias, head_dim, channels)
            heads[r : r + SHIFT] = result.reshape(SHIFT, wide, LANES)

    for tap in range(3):
        c0 = SHIFT - 1 + tap
        shifted[tap, 0] = bands[0, SHIFT - 1, c0 : c0 + wide].astype(BF16)
        for r in range(0, rows, 8):
            shifted[tap, 1 + r : 9 + r] = normed[r : r + 8, c0 : c0 + wide].astype(BF16)
        shifted[tap, 1 + rows] = bands[1, 0, c0 : c0 + wide].astype(BF16)

    gain2 = gain2_ref[...]
    band = 16
    for r in range(0, rows, band):
        image = image_ref[r : r + band].astype(F32)[:, SHIFT : cols - SHIFT].reshape(-1, channels)
        raw = heads[r : r + band].reshape(-1, LANES)

        def pieces(row_tap, col_tap):
            return shifted[col_tap, r + row_tap : r + row_tap + band].reshape(-1, LANES)

        mixed = finish(raw, pieces, image, wp, wc, gain2, fc1_ref, fc2_ref, channels)
        out_ref[r : r + band] = mixed.reshape(band, wide, channels)


def side_kernel(
    image_ref, top_ref, bottom_ref, left_ref, right_ref, gain1_ref, gain2_ref, fc1_ref, fc2_ref,
    bias, normed, q_left, q_right, wkv, wp, wc, middle_ref, out_ref,
    side, kv, shifted, heads,
):
    rows, cols, channels = image_ref.shape
    head_dim = channels // HEADS
    tall = rows + 2 * SHIFT
    row, last_row = lax.axis_index("row"), lax.axis_size("row") - 1
    col, last_col = lax.axis_index("col"), lax.axis_size("col") - 1
    gain1 = gain1_ref[...]
    out_row = [(row == 0).astype(F32), (row == last_row).astype(F32)]
    out_col = [(col == 0).astype(F32), (col == last_col).astype(F32)]
    for s, (ref, halo, own, c0) in enumerate(
        ((left_ref, 0, SHIFT, 0), (right_ref, 2 * SHIFT, 0, cols - 2 * SHIFT))
    ):
        mark_lanes(side, (s, slice(0, SHIFT), slice(halo, halo + SHIFT)), (SHIFT, SHIFT), channels,
                   out_col[s] + out_row[0])
        mark_lanes(side, (s, slice(SHIFT, SHIFT + rows), slice(halo, halo + SHIFT)), (rows, SHIFT), channels,
                   out_col[s])
        mark_lanes(side, (s, slice(SHIFT + rows, tall), slice(halo, halo + SHIFT)), (SHIFT, SHIFT), channels,
                   out_col[s] + out_row[1])
        for r in range(0, tall, SHIFT):
            inside = gain1 * (1.0 - out_col[s])
            if r == 0:
                inside = inside * (1.0 - out_row[0])
            if r == tall - SHIFT:
                inside = inside * (1.0 - out_row[1])
            side[s, r : r + SHIFT, halo : halo + SHIFT, 0:channels] = layer_norm(
                ref[r : r + SHIFT].astype(F32), inside
            )
        for i, (r0, band_ref) in enumerate(((0, top_ref), (SHIFT + rows, bottom_ref))):
            values = band_ref[...].astype(F32)[:, c0 : c0 + 2 * SHIFT]
            mark_lanes(side, (s, slice(r0, r0 + SHIFT), slice(own, own + 2 * SHIFT)), (SHIFT, 2 * SHIFT),
                       channels, out_row[i])
            side[s, r0 : r0 + SHIFT, own : own + 2 * SHIFT, 0:channels] = layer_norm(
                values, gain1 * (1.0 - out_row[i])
            )
        side[s, SHIFT : SHIFT + rows, own : own + 2 * SHIFT] = normed[:, c0 : c0 + 2 * SHIFT]

        k0 = 0 if s == 0 else SHIFT
        for r in range(0, tall, WIN):
            pixels = side[s, r : r + WIN, k0 : k0 + WIN].astype(BF16).reshape(-1, LANES)
            kv[s, r : r + WIN] = dot(pixels, wkv[...]).astype(BF16).reshape(WIN, WIN, 2 * LANES)

    for s, q_ref in enumerate((q_left, q_right)):
        px = SHIFT if s == 0 else 0
        for window in range(rows // WIN + 1):
            start, stop = max(window * WIN - SHIFT, 0), min((window + 1) * WIN - SHIFT, rows)
            first = start - (window * WIN - SHIFT)
            pair = kv[s, window * WIN : (window + 1) * WIN].reshape(-1, 2 * LANES)
            part_bias = bias[:, first : first + stop - start, px : px + SHIFT]
            part = q_ref[start:stop].reshape(-1, LANES)
            result = attend(part, pair, part_bias, head_dim, channels)
            heads[s, start:stop] = result.reshape(stop - start, SHIFT, LANES)

    for s in range(2):
        for tap in range(3):
            c0 = (SHIFT if s == 0 else SHIFT) - 1 + tap
            for r in range(0, rows + 2, 8):
                stop = min(r + 8, rows + 2)
                shifted[tap, s, r:stop] = side[s, SHIFT - 1 + r : SHIFT - 1 + stop, c0 : c0 + SHIFT]

    gain2 = gain2_ref[...]
    band = 16
    for r in range(0, rows, band):
        whole = image_ref[r : r + band].astype(F32)
        image = jnp.concatenate(
            [whole[:, :SHIFT].reshape(-1, channels), whole[:, cols - SHIFT :].reshape(-1, channels)], axis=0
        )
        raw = heads[:, r : r + band].reshape(-1, LANES)

        def pieces(row_tap, col_tap):
            piece = shifted[col_tap, :, r + row_tap : r + row_tap + band]
            return piece.reshape(-1, LANES).astype(BF16)

        mixed = finish(raw, pieces, image, wp, wc, gain2, fc1_ref, fc2_ref, channels)
        mixed = mixed.reshape(2, band, SHIFT, channels)
        whole = jnp.concatenate([mixed[0], middle_ref[r : r + band], mixed[1]], axis=1)
        out_ref[r : r + band] = whole.astype(BF16)


def exchange(low, high, axis):
    count = lax.axis_size(axis)
    before = lax.ppermute(high, axis, [(i, (i + 1) % count) for i in range(count)])
    after = lax.ppermute(low, axis, [((i + 1) % count, i) for i in range(count)])
    return before, after


def call(kernel, name, outs, scratch, flops, operands, in_hbm=()):
    vmem = pl.BlockSpec(memory_space=pltpu.VMEM)
    hbm = pl.BlockSpec(memory_space=pltpu.HBM)
    return pl.pallas_call(
        kernel,
        out_shape=[out if isinstance(out, jax.ShapeDtypeStruct) else pltpu.VMEM(*out) for out in outs],
        in_specs=[hbm if i in in_hbm else vmem for i in range(len(operands))],
        out_specs=[vmem] * len(outs),
        scratch_shapes=[pltpu.VMEM(*s) if isinstance(s, tuple) else s for s in scratch],
        cost_estimate=pl.CostEstimate(flops=flops, bytes_accessed=4_000_000, transcendentals=1_000_000),
        compiler_params=pltpu.CompilerParams(vmem_limit_bytes=24 * 1024 * 1024),
        name=name,
    )(*[pltpu.with_memory_space_constraint(x, pltpu.HBM) if i in in_hbm else x for i, x in enumerate(operands)])


def on_device(
    image, norm1_gain, norm2_gain, qkv_weight, proj_weight, rel_table, conv_weight, fc1_weight,
    fc2_weight,
):
    rows, cols, channels = image.shape
    tall, wide = rows + 2 * SHIFT, cols - 2 * SHIFT
    gain1, gain2, fc2 = norm1_gain[None], norm2_gain[None], fc2_weight.T
    top, bottom = exchange(image[:SHIFT], image[rows - SHIFT :], "row")
    bias, normed, q_mid, q_left, q_right, kv_mid, wkv, wp, wc, first_cols, last_cols = call(
        own_kernel,
        "own_tile",
        [
            ((HEADS, WIN, WIN, WIN * WIN), F32),
            ((rows, cols, LANES), F32),
            ((rows, wide, LANES), F32),
            ((rows, SHIFT, LANES), F32),
            ((rows, SHIFT, LANES), F32),
            ((rows, wide, 2 * LANES), BF16),
            ((LANES, 2 * LANES), BF16),
            ((LANES, channels), BF16),
            ((9 * LANES, channels), BF16),
            ((rows, SHIFT, channels), BF16),
            ((rows, SHIFT, channels), BF16),
        ],
        [
            ((8, 1024), F32), ((4, 8 * WIN, 128), F32), ((LANES, LANES), BF16),
            (rel_table.T.shape, F32), (image.shape, BF16), (gain1.shape, F32), (qkv_weight.shape, BF16),
            (proj_weight.shape, BF16), (conv_weight.shape, BF16), pltpu.SemaphoreType.DMA((6,)),
        ],
        2_000_000_000,
        (image, gain1, qkv_weight, proj_weight, rel_table.T, conv_weight),
        (0, 1, 2, 3, 4, 5),
    )
    first_part = jnp.concatenate([top[:, :SHIFT], first_cols, bottom[:, :SHIFT]])
    last_part = jnp.concatenate([top[:, cols - SHIFT :], last_cols, bottom[:, cols - SHIFT :]])
    left, right = exchange(first_part, last_part, "col")
    (middle,) = call(
        middle_kernel,
        "middle_columns",
        [((rows, wide, channels), F32)],
        [
            ((2, SHIFT, cols, LANES), F32),
            ((3, rows + 2, wide, LANES), BF16),
            ((rows, wide, LANES), F32),
        ],
        2_000_000_000,
        (image, top, bottom, gain1, gain2, fc1_weight, fc2, bias, normed, q_mid, kv_mid, wkv, wp, wc),
    )
    (out,) = call(
        side_kernel,
        "side_columns",
        [jax.ShapeDtypeStruct(image.shape, BF16)],
        [
            ((2, tall, 3 * SHIFT, LANES), F32),
            ((2, tall, WIN, 2 * LANES), BF16),
            ((3, 2, rows + 2, SHIFT, LANES), F32),
            ((2, rows, SHIFT, LANES), F32),
        ],
        2_000_000_000,
        (image, top, bottom, left, right, gain1, gain2, fc1_weight, fc2, bias, normed, q_left, q_right,
         wkv, wp, wc, middle),
    )
    return out


def solution(mesh):
    placed = (P("row", "col", None), P(), P(), P(), P(), P(), P(), P(), P())
    return jax.shard_map(
        on_device, mesh=mesh, in_specs=placed, out_specs=P("row", "col", None), check_vma=False
    )
```

```python
import functools
import math

import jax
import jax.numpy as jnp
from jax import lax
from jax.experimental import pallas as pl
from jax.experimental.pallas import tpu as pltpu
from jax.sharding import PartitionSpec as P

HEADS = 6
WIN = 16
SHIFT = 8
LANES = 256
HALF = LANES // 2
F32 = jnp.float32
BF16 = jnp.bfloat16
LOG2E = math.log2(math.e)
MASKED = -4.0e9


def layer_norm(values, norm_gain):
    centre = jnp.mean(values, axis=-1, keepdims=True)
    values = values - centre
    spread = jnp.mean(values * values, axis=-1, keepdims=True)
    return values * lax.rsqrt(spread + 1e-05) * norm_gain


def dot(a, b):
    return jnp.dot(a, b, preferred_element_type=F32)


def dot_nt(a, b):
    return lax.dot_general(a, b, (((1,), (1,)), ((), ())), preferred_element_type=F32)


def one_hot(condition):
    return jnp.where(condition, 1.0, 0.0).astype(BF16)


def gelu(x):
    size = jnp.abs(x)
    t = 1.0 / (1.0 + (0.3275911 * math.sqrt(0.5)) * size)
    poly = 0.5 * 1.061405429
    for factor in (-1.453152027, 1.421413741, -0.284496736, 0.254829592):
        poly = poly * t + 0.5 * factor
    tail = poly * t * jnp.exp2(size * size * (-0.5 * LOG2E))
    return jnp.maximum(x, 0.0) - size * tail


def lanes_of(width=LANES):
    return lax.broadcasted_iota(jnp.int32, (1, width), 1)


def mark_lanes(ref, place, shape, channels, outside):
    half = lanes_of()[:, HALF:]
    mark = jnp.where(half == channels + 1, 1.0, 0.0) + jnp.where(half == channels, outside, 0.0)
    ref[(*place, slice(HALF, LANES))] = jnp.broadcast_to(mark[None], (*shape, HALF))


def expand_bias(table_ref, padded, strip, bias):
    span = 2 * WIN - 1
    padded[...] = jnp.zeros_like(padded)
    padded[0:HEADS, 0 : span * span] = table_ref[...] * LOG2E
    table = padded[...]
    width = padded.shape[1]
    shifted = jnp.concatenate(
        [table if px == 0 else pltpu.roll(table, width - px, 1) for px in range(WIN)], axis=0
    )
    high = shifted.astype(BF16)
    low = (shifted - high.astype(F32)).astype(BF16)
    entry = lax.broadcasted_iota(jnp.int32, (width, 512), 0)
    place = lax.broadcasted_iota(jnp.int32, (1, 512), 1)
    wanted = (2 * WIN - 2 - lax.div(place, WIN)) * span + WIN - 1 - lax.rem(place, WIN)
    picked = dot(jnp.concatenate([high, low], axis=0), one_hot(entry == wanted))
    half = 8 * WIN
    picked = picked[:half] + picked[half:]
    for tile in range(4):
        strip[tile] = picked[:, 128 * tile : 128 * (tile + 1)]
    for head in range(HEADS):
        rows = jnp.concatenate(
            [strip[tile, pl.ds(head, WIN, stride=8), :] for tile in range(4)], axis=1
        )
        for turn in range(8):
            rolled = rows if turn == 0 else pltpu.roll(rows, 512 - 16 * turn, 1)
            bias[head, 15 - turn] = rolled[:, 0:256]
            bias[head, 7 - turn] = rolled[:, 128:384]


def own_kernel(
    image_hbm, gain1_hbm, qkv_hbm, proj_hbm, table_hbm, conv_hbm,
    bias, normed, q_mid, q_left, q_right, kv_mid, wkv, wp, wc, first_cols, last_cols,
    padded, strip, wq, table_ref, image_ref, gain1_ref, qkv_ref, proj_ref, conv_ref, sems,
):
    rows, cols, channels = image_ref.shape
    head_dim = channels // HEADS
    flag_lane, one_lane = channels, channels + 1
    fetches = [
        pltpu.make_async_copy(source, target, sems.at[i])
        for i, (source, target) in enumerate(
            ((table_hbm, table_ref), (image_hbm, image_ref), (gain1_hbm, gain1_ref), (qkv_hbm, qkv_ref),
             (proj_hbm, proj_ref), (conv_hbm, conv_ref))
        )
    ]
    for fetch in fetches:
        fetch.start()
    fetches[0].wait()
    expand_bias(table_ref, padded, strip, bias)
    for fetch in fetches[1:]:
        fetch.wait()
    first_cols[...] = image_ref[...].astype(F32)[:, :SHIFT].astype(BF16)
    last_cols[...] = image_ref[...].astype(F32)[:, cols - SHIFT :].astype(BF16)

    for ref in (wq, wkv, wp, wc):
        ref[...] = jnp.zeros_like(ref)
    special = lax.broadcasted_iota(jnp.int32, (16, LANES), 0) + 176
    lanes16 = lax.broadcasted_iota(jnp.int32, (16, LANES), 1)
    wq[176:192, :] = one_hot((special == one_lane) & (lanes16 == flag_lane))
    wkv[176:192, 0:LANES] = jnp.where(
        (special == flag_lane) & (lanes16 == flag_lane), MASKED, 0.0
    ).astype(BF16)
    wkv[176:192, LANES:] = one_hot(
        (special == one_lane) & (lanes16 >= channels) & (lanes16 < channels + HEADS)
    )
    wq[0:channels, 0:channels] = qkv_ref[:, 0:channels]
    wkv[0:channels, 0:channels] = qkv_ref[:, channels : 2 * channels]
    wkv[0:channels, LANES : LANES + channels] = qkv_ref[:, 2 * channels :]
    wp[0:channels, :] = proj_ref[...]
    for row_tap in range(3):
        for col_tap in range(3):
            tap = (3 * row_tap + col_tap) * LANES
            wc[tap : tap + channels, :] = conv_ref[row_tap, col_tap]

    mark_lanes(normed, (slice(0, rows), slice(0, cols)), (rows, cols), channels, 0.0)
    gain1 = gain1_ref[...]
    for r in range(0, rows, 8):
        normed[r : r + 8, :, 0:channels] = layer_norm(image_ref[r : r + 8].astype(F32), gain1)

    scale = head_dim**-0.5 * LOG2E
    for r in range(0, rows, 8):
        pixels = normed[r : r + 8].astype(BF16).reshape(-1, LANES)
        q = (dot(pixels, wq[...]) * scale).reshape(8, cols, LANES)
        q_left[r : r + 8] = q[:, :SHIFT]
        q_mid[r : r + 8] = q[:, SHIFT : cols - SHIFT]
        q_right[r : r + 8] = q[:, cols - SHIFT :]
        middle = normed[r : r + 8, SHIFT : cols - SHIFT].astype(BF16).reshape(-1, LANES)
        kv = dot(middle, wkv[...]).astype(BF16)
        kv_mid[r : r + 8] = kv.reshape(8, cols - 2 * SHIFT, 2 * LANES)


def attend(part, pair, part_bias, head_dim, channels):
    lane = lanes_of()
    keys, values = pair[:, :LANES], pair[:, LANES:]
    count = part.shape[0]
    own = [(lane >= h * head_dim) & (lane < (h + 1) * head_dim) for h in range(HEADS)]
    stacked = jnp.concatenate(
        [jnp.where(own[h] | (lane == channels), part, 0.0).astype(BF16) for h in range(HEADS)],
        axis=0,
    )
    scores = dot_nt(stacked, keys).reshape(HEADS, count, WIN * WIN)
    scores = scores + part_bias.reshape(HEADS, count, WIN * WIN)
    scores = scores - jnp.max(scores, axis=-1, keepdims=True)
    soft = jnp.exp2(scores).astype(BF16).reshape(HEADS * count, WIN * WIN)
    mixed = dot(soft, values)
    result = mixed[0:count]
    for h in range(1, HEADS):
        mine = own[h] | (lane == channels + h)
        result = jnp.where(mine, mixed[h * count : (h + 1) * count], result)
    return result


def finish(raw, pieces, image, wp, wc, gain2, fc1, fc2, channels):
    head_dim = channels // HEADS
    half = lanes_of()[:, HALF:]
    sum_row = lax.broadcasted_iota(jnp.int32, (HALF, LANES), 0) + HALF - channels
    lane_wide = lax.broadcasted_iota(jnp.int32, (HALF, LANES), 1)
    spread = one_hot(
        (sum_row >= 0) & (lane_wide >= sum_row * head_dim) & (lane_wide < (sum_row + 1) * head_dim)
        & (lane_wide < channels)
    )
    is_sum = (half >= channels) & (half < channels + HEADS)
    inverse = jnp.where(is_sum, 1.0 / raw[:, HALF:], 0.0)
    high = inverse.astype(BF16)
    low = (inverse - high.astype(F32)).astype(BF16)
    heads_out = (raw * (dot(high, spread) + dot(low, spread))).astype(BF16)
    attended = dot(heads_out, wp[...]).astype(BF16).astype(F32)
    taps = [pieces(row_tap, col_tap) for row_tap in range(3) for col_tap in range(3)]
    conv_sum = dot(jnp.concatenate(taps, axis=1), wc[...])
    state1 = image + attended + conv_sum
    normed2 = layer_norm(state1, gain2).astype(BF16)
    hidden = dot(normed2, fc1[...])
    hidden = gelu(hidden).astype(BF16)
    return state1 + dot_nt(hidden, fc2[...])


def middle_kernel(
    image_ref, top_ref, bottom_ref, gain1_ref, gain2_ref, fc1_ref, fc2_ref,
    bias, normed, q_mid, kv_mid, wkv, wp, wc, out_ref,
    bands, shifted, heads,
):
    rows, cols, channels = image_ref.shape
    head_dim = channels // HEADS
    wide = cols - 2 * SHIFT
    row, last_row = lax.axis_index("row"), lax.axis_size("row") - 1
    gain1 = gain1_ref[...]
    kv_band = []
    for i, (ref, edge) in enumerate(((top_ref, 0), (bottom_ref, last_row))):
        mark_lanes(
            bands, (i, slice(0, SHIFT), slice(0, cols)), (SHIFT, cols), channels, (row == edge).astype(F32)
        )
        inside = gain1 * (row != edge).astype(F32)
        bands[i, :, :, 0:channels] = layer_norm(ref[...].astype(F32), inside)
        pixels = bands[i, :, SHIFT : cols - SHIFT].astype(BF16).reshape(-1, LANES)
        kv_band.append(dot(pixels, wkv[...]).astype(BF16))

    for window in range(rows // WIN + 1):
        start, stop = max(window * WIN - SHIFT, 0), min((window + 1) * WIN - SHIFT, rows)
        first = start - (window * WIN - SHIFT)
        pair = kv_mid[start:stop].reshape(-1, 2 * LANES)
        if window == 0:
            pair = jnp.concatenate([kv_band[0], pair], axis=0)
        if window == rows // WIN:
            pair = jnp.concatenate([pair, kv_band[1]], axis=0)
        for r in range(start, stop, SHIFT):
            part_bias = bias[:, first + r - start : first + r - start + SHIFT]
            part = q_mid[r : r + SHIFT].reshape(-1, LANES)
            result = attend(part, pair, part_bias, head_dim, channels)
            heads[r : r + SHIFT] = result.reshape(SHIFT, wide, LANES)

    for tap in range(3):
        c0 = SHIFT - 1 + tap
        shifted[tap, 0] = bands[0, SHIFT - 1, c0 : c0 + wide].astype(BF16)
        for r in range(0, rows, 8):
            shifted[tap, 1 + r : 9 + r] = normed[r : r + 8, c0 : c0 + wide].astype(BF16)
        shifted[tap, 1 + rows] = bands[1, 0, c0 : c0 + wide].astype(BF16)

    gain2 = gain2_ref[...]
    band = 16
    for r in range(0, rows, band):
        image = image_ref[r : r + band].astype(F32)[:, SHIFT : cols - SHIFT].reshape(-1, channels)
        raw = heads[r : r + band].reshape(-1, LANES)

        def pieces(row_tap, col_tap):
            return shifted[col_tap, r + row_tap : r + row_tap + band].reshape(-1, LANES)

        mixed = finish(raw, pieces, image, wp, wc, gain2, fc1_ref, fc2_ref, channels)
        out_ref[r : r + band] = mixed.reshape(band, wide, channels)


def side_kernel(
    image_ref, top_ref, bottom_ref, left_ref, right_ref, gain1_ref, gain2_ref, fc1_ref, fc2_ref,
    bias, normed, q_left, q_right, wkv, wp, wc, middle_ref, out_ref,
    side, kv, shifted, heads,
):
    rows, cols, channels = image_ref.shape
    head_dim = channels // HEADS
    tall = rows + 2 * SHIFT
    row, last_row = lax.axis_index("row"), lax.axis_size("row") - 1
    col, last_col = lax.axis_index("col"), lax.axis_size("col") - 1
    gain1 = gain1_ref[...]
    out_row = [(row == 0).astype(F32), (row == last_row).astype(F32)]
    out_col = [(col == 0).astype(F32), (col == last_col).astype(F32)]
    for s, (ref, halo, own, c0) in enumerate(
        ((left_ref, 0, SHIFT, 0), (right_ref, 2 * SHIFT, 0, cols - 2 * SHIFT))
    ):
        mark_lanes(side, (s, slice(0, SHIFT), slice(halo, halo + SHIFT)), (SHIFT, SHIFT), channels,
                   out_col[s] + out_row[0])
        mark_lanes(side, (s, slice(SHIFT, SHIFT + rows), slice(halo, halo + SHIFT)), (rows, SHIFT), channels,
                   out_col[s])
        mark_lanes(side, (s, slice(SHIFT + rows, tall), slice(halo, halo + SHIFT)), (SHIFT, SHIFT), channels,
                   out_col[s] + out_row[1])
        for r in range(0, tall, SHIFT):
            inside = gain1 * (1.0 - out_col[s])
            if r == 0:
                inside = inside * (1.0 - out_row[0])
            if r == tall - SHIFT:
                inside = inside * (1.0 - out_row[1])
            side[s, r : r + SHIFT, halo : halo + SHIFT, 0:channels] = layer_norm(
                ref[r : r + SHIFT].astype(F32), inside
            )
        for i, (r0, band_ref) in enumerate(((0, top_ref), (SHIFT + rows, bottom_ref))):
            values = band_ref[...].astype(F32)[:, c0 : c0 + 2 * SHIFT]
            mark_lanes(side, (s, slice(r0, r0 + SHIFT), slice(own, own + 2 * SHIFT)), (SHIFT, 2 * SHIFT),
                       channels, out_row[i])
            side[s, r0 : r0 + SHIFT, own : own + 2 * SHIFT, 0:channels] = layer_norm(
                values, gain1 * (1.0 - out_row[i])
            )
        side[s, SHIFT : SHIFT + rows, own : own + 2 * SHIFT] = normed[:, c0 : c0 + 2 * SHIFT]

        k0 = 0 if s == 0 else SHIFT
        for r in range(0, tall, WIN):
            pixels = side[s, r : r + WIN, k0 : k0 + WIN].astype(BF16).reshape(-1, LANES)
            kv[s, r : r + WIN] = dot(pixels, wkv[...]).astype(BF16).reshape(WIN, WIN, 2 * LANES)

    for s, q_ref in enumerate((q_left, q_right)):
        px = SHIFT if s == 0 else 0
        for window in range(rows // WIN + 1):
            start, stop = max(window * WIN - SHIFT, 0), min((window + 1) * WIN - SHIFT, rows)
            first = start - (window * WIN - SHIFT)
            pair = kv[s, window * WIN : (window + 1) * WIN].reshape(-1, 2 * LANES)
            part_bias = bias[:, first : first + stop - start, px : px + SHIFT]
            part = q_ref[start:stop].reshape(-1, LANES)
            result = attend(part, pair, part_bias, head_dim, channels)
            heads[s, start:stop] = result.reshape(stop - start, SHIFT, LANES)

    for s in range(2):
        for tap in range(3):
            c0 = (SHIFT if s == 0 else SHIFT) - 1 + tap
            for r in range(0, rows + 2, 8):
                stop = min(r + 8, rows + 2)
                shifted[tap, s, r:stop] = side[s, SHIFT - 1 + r : SHIFT - 1 + stop, c0 : c0 + SHIFT]

    gain2 = gain2_ref[...]
    band = 16
    for r in range(0, rows, band):
        whole = image_ref[r : r + band].astype(F32)
        image = jnp.concatenate(
            [whole[:, :SHIFT].reshape(-1, channels), whole[:, cols - SHIFT :].reshape(-1, channels)], axis=0
        )
        raw = heads[:, r : r + band].reshape(-1, LANES)

        def pieces(row_tap, col_tap):
            piece = shifted[col_tap, :, r + row_tap : r + row_tap + band]
            return piece.reshape(-1, LANES).astype(BF16)

        mixed = finish(raw, pieces, image, wp, wc, gain2, fc1_ref, fc2_ref, channels)
        mixed = mixed.reshape(2, band, SHIFT, channels)
        whole = jnp.concatenate([mixed[0], middle_ref[r : r + band], mixed[1]], axis=1)
        out_ref[r : r + band] = whole.astype(BF16)


def exchange(low, high, axis):
    count, place = lax.axis_size(axis), lax.axis_index(axis)
    even = lax.rem(place, 2) == 0
    inner = [[i, i + 1] for i in range(0, count, 2)]
    outer = [[i, (i + 1) % count] for i in range(1, count, 2)]
    one = lax.all_gather(jnp.where(even, high, low), axis, axis_index_groups=inner)
    other = lax.all_gather(jnp.where(even, low, high), axis, axis_index_groups=outer)
    before = jnp.where(even, other[0], one[0])
    after = jnp.where(even, one[1], other[1])
    return before, after


def call(kernel, name, outs, scratch, flops, operands, in_hbm=()):
    vmem = pl.BlockSpec(memory_space=pltpu.VMEM)
    hbm = pl.BlockSpec(memory_space=pltpu.HBM)
    return pl.pallas_call(
        kernel,
        out_shape=[out if isinstance(out, jax.ShapeDtypeStruct) else pltpu.VMEM(*out) for out in outs],
        in_specs=[hbm if i in in_hbm else vmem for i in range(len(operands))],
        out_specs=[vmem] * len(outs),
        scratch_shapes=[pltpu.VMEM(*s) if isinstance(s, tuple) else s for s in scratch],
        cost_estimate=pl.CostEstimate(flops=flops, bytes_accessed=4_000_000, transcendentals=1_000_000),
        compiler_params=pltpu.CompilerParams(vmem_limit_bytes=24 * 1024 * 1024),
        name=name,
    )(*[pltpu.with_memory_space_constraint(x, pltpu.HBM) if i in in_hbm else x for i, x in enumerate(operands)])


def on_device(
    image, norm1_gain, norm2_gain, qkv_weight, proj_weight, rel_table, conv_weight, fc1_weight,
    fc2_weight,
):
    rows, cols, channels = image.shape
    tall, wide = rows + 2 * SHIFT, cols - 2 * SHIFT
    gain1, gain2, fc2 = norm1_gain[None], norm2_gain[None], fc2_weight.T
    top, bottom = exchange(image[:SHIFT], image[rows - SHIFT :], "row")
    bias, normed, q_mid, q_left, q_right, kv_mid, wkv, wp, wc, first_cols, last_cols = call(
        own_kernel,
        "own_tile",
        [
            ((HEADS, WIN, WIN, WIN * WIN), F32),
            ((rows, cols, LANES), F32),
            ((rows, wide, LANES), F32),
            ((rows, SHIFT, LANES), F32),
            ((rows, SHIFT, LANES), F32),
            ((rows, wide, 2 * LANES), BF16),
            ((LANES, 2 * LANES), BF16),
            ((LANES, channels), BF16),
            ((9 * LANES, channels), BF16),
            ((rows, SHIFT, channels), BF16),
            ((rows, SHIFT, channels), BF16),
        ],
        [
            ((8, 1024), F32), ((4, 8 * WIN, 128), F32), ((LANES, LANES), BF16),
            (rel_table.T.shape, F32), (image.shape, BF16), (gain1.shape, F32), (qkv_weight.shape, BF16),
            (proj_weight.shape, BF16), (conv_weight.shape, BF16), pltpu.SemaphoreType.DMA((6,)),
        ],
        2_000_000_000,
        (image, gain1, qkv_weight, proj_weight, rel_table.T, conv_weight),
        (0, 1, 2, 3, 4, 5),
    )
    first_part = jnp.concatenate([top[:, :SHIFT], first_cols, bottom[:, :SHIFT]])
    last_part = jnp.concatenate([top[:, cols - SHIFT :], last_cols, bottom[:, cols - SHIFT :]])
    left, right = exchange(first_part, last_part, "col")
    (middle,) = call(
        middle_kernel,
        "middle_columns",
        [((rows, wide, channels), F32)],
        [
            ((2, SHIFT, cols, LANES), F32),
            ((3, rows + 2, wide, LANES), BF16),
            ((rows, wide, LANES), F32),
        ],
        2_000_000_000,
        (image, top, bottom, gain1, gain2, fc1_weight, fc2, bias, normed, q_mid, kv_mid, wkv, wp, wc),
    )
    (out,) = call(
        side_kernel,
        "side_columns",
        [jax.ShapeDtypeStruct(image.shape, BF16)],
        [
            ((2, tall, 3 * SHIFT, LANES), F32),
            ((2, tall, WIN, 2 * LANES), BF16),
            ((3, 2, rows + 2, SHIFT, LANES), F32),
            ((2, rows, SHIFT, LANES), F32),
        ],
        2_000_000_000,
        (image, top, bottom, left, right, gain1, gain2, fc1_weight, fc2, bias, normed, q_left, q_right,
         wkv, wp, wc, middle),
    )
    return out


def solution(mesh):
    placed = (P("row", "col", None), P(), P(), P(), P(), P(), P(), P(), P())
    return jax.shard_map(
        on_device, mesh=mesh, in_specs=placed, out_specs=P("row", "col", None), check_vma=False
    )
```

```python
import math

import jax
import jax.numpy as jnp
from jax import lax
from jax.experimental import pallas as pl
from jax.experimental.pallas import tpu as pltpu
from jax.sharding import PartitionSpec as P

HEADS = 6
WIN = 16
SHIFT = 8
SIDE = 8
AREA = SIDE * SIDE
LANES = 256
HALF = LANES // 2
F32 = jnp.float32
BF16 = jnp.bfloat16
LOG2E = math.log2(math.e)
MASKED = -4.0e9


def layer_norm(values, norm_gain):
    centre = jnp.mean(values, axis=-1, keepdims=True)
    values = values - centre
    spread = jnp.mean(values * values, axis=-1, keepdims=True)
    return values * lax.rsqrt(spread + 1e-05) * norm_gain


def dot(a, b):
    return jnp.dot(a, b, preferred_element_type=F32)


def dot_nt(a, b):
    return lax.dot_general(a, b, (((1,), (1,)), ((), ())), preferred_element_type=F32)


def one_hot(condition):
    return jnp.where(condition, 1.0, 0.0).astype(BF16)


def gelu(x):
    size = jnp.abs(x)
    t = 1.0 / (1.0 + (0.3275911 * math.sqrt(0.5)) * size)
    poly = 0.5 * 1.061405429
    for factor in (-1.453152027, 1.421413741, -0.284496736, 0.254829592):
        poly = poly * t + 0.5 * factor
    tail = poly * t * jnp.exp2(size * size * (-0.5 * LOG2E))
    return jnp.maximum(x, 0.0) - size * tail


def lanes_of(width=LANES):
    return lax.broadcasted_iota(jnp.int32, (1, width), 1)


def marks(channels, outside):
    half = lanes_of()[:, HALF:]
    return jnp.where(half == channels + 1, 1.0, 0.0) + jnp.where(half == channels, outside, 0.0)


def expand_bias(table_ref, padded, strip, bias):
    span = 2 * WIN - 1
    padded[...] = jnp.zeros_like(padded)
    padded[0:HEADS, 0 : span * span] = table_ref[...] * LOG2E
    table = padded[...]
    width = padded.shape[1]
    shifted = jnp.concatenate(
        [table if px == 0 else pltpu.roll(table, width - px, 1) for px in range(WIN)], axis=0
    )
    high = shifted.astype(BF16)
    low = (shifted - high.astype(F32)).astype(BF16)
    entry = lax.broadcasted_iota(jnp.int32, (width, 512), 0)
    place = lax.broadcasted_iota(jnp.int32, (1, 512), 1)
    column = lax.div(place, 256) * SIDE + lax.rem(place, SIDE)
    wanted = (span - 1 - lax.div(lax.rem(place, 256), SIDE)) * span + WIN - 1 - column
    picked = dot(jnp.concatenate([high, low], axis=0), one_hot(entry == wanted))
    half = 8 * WIN
    picked = picked[:half] + picked[half:]
    for tile in range(4):
        strip[tile] = picked[:, 128 * tile : 128 * (tile + 1)]
    for head in range(HEADS):
        for half in range(2):
            rows = jnp.concatenate(
                [strip[2 * half + t, pl.ds(head, WIN, stride=8), :] for t in range(2)], axis=1
            )
            for py in range(WIN):
                start = (WIN - 1 - py) * SIDE
                rolled = (rows if start == 0 else pltpu.roll(rows, 256 - start, 1))[:, 0:128]
                lanes = slice(128 * half, 128 * (half + 1))
                place = slice(py % SIDE * SIDE, (py % SIDE + 1) * SIDE)
                bias[head, py // SIDE, 0, place, lanes] = rolled[:SIDE]
                bias[head, py // SIDE, 1, place, lanes] = rolled[SIDE:]


def scores_of(blocks, keys, head_dim, channels):
    lane = lanes_of()
    part = jnp.concatenate(blocks, axis=0)
    own = [(lane >= h * head_dim) & (lane < (h + 1) * head_dim) for h in range(HEADS)]
    stacked = jnp.concatenate(
        [jnp.where(own[h] | (lane == channels), part, 0.0).astype(BF16) for h in range(HEADS)],
        axis=0,
    )
    return dot_nt(stacked, keys)


def mix(scores, part_bias, values, head_dim, channels):
    lane = lanes_of()
    count = scores.shape[0] // HEADS
    scores = scores.reshape(HEADS, count, WIN * WIN) + part_bias
    scores = scores - jnp.max(scores, axis=-1, keepdims=True)
    soft = jnp.exp2(scores).astype(BF16).reshape(HEADS * count, WIN * WIN)
    mixed = dot(soft, values)
    result = mixed[0:count]
    for h in range(1, HEADS):
        mine = (lane >= h * head_dim) & (lane < (h + 1) * head_dim) | (lane == channels + h)
        result = jnp.where(mine, mixed[h * count : (h + 1) * count], result)
    return result


def attention(units, bias, head_dim, channels):
    def scores_at(unit):
        return scores_of(unit[0], unit[2][:, :LANES], head_dim, channels)

    results = []
    ahead = scores_at(units[0])
    for i, unit in enumerate(units):
        scores, ahead = ahead, scores_at(units[i + 1]) if i + 1 < len(units) else None
        part_bias = jnp.concatenate([bias[:, hy, hx] for hy, hx in unit[1]], axis=1)
        results.append(mix(scores, part_bias, unit[2][:, LANES:], head_dim, channels))
    return results


def spread_matrix(channels):
    head_dim = channels // HEADS
    sum_row = lax.broadcasted_iota(jnp.int32, (HALF, LANES), 0) + HALF - channels
    lane_wide = lax.broadcasted_iota(jnp.int32, (HALF, LANES), 1)
    return one_hot(
        (sum_row >= 0) & (lane_wide >= sum_row * head_dim) & (lane_wide < (sum_row + 1) * head_dim)
        & (lane_wide < channels)
    )


def finish(raw, base, spread, wp, gain2, fc1, fc2, channels):
    half = lanes_of()[:, HALF:]
    is_sum = (half >= channels) & (half < channels + HEADS)
    inverse = jnp.where(is_sum, 1.0 / raw[:, HALF:], 0.0)
    high = inverse.astype(BF16)
    low = (inverse - high.astype(F32)).astype(BF16)
    heads_out = (raw * (dot(high, spread) + dot(low, spread))).astype(BF16)
    state1 = base + dot(heads_out, wp[...]).astype(BF16).astype(F32)
    normed2 = layer_norm(state1, gain2).astype(BF16)
    hidden = gelu(dot(normed2, fc1[...])).astype(BF16)
    return state1 + dot_nt(hidden, fc2[...])


def own_kernel(
    image_hbm, gain1_hbm, gain2_hbm, qkv_hbm, proj_hbm, table_hbm, conv_hbm, fc1_hbm, fc2_hbm,
    bias, query, kv, base, wkv, wp, wc, out_mid,
    padded, strip, wq, normed, shifted,
    table_ref, image_ref, gain1_ref, gain2_ref, qkv_ref, proj_ref, conv_ref, fc1_ref, fc2_ref, sems,
):
    rows, cols, channels = image_ref.shape
    head_dim = channels // HEADS
    flag_lane, one_lane = channels, channels + 1
    blocks_r, blocks_c = rows // SIDE, cols // SIDE
    fetches = [
        pltpu.make_async_copy(source, target, sems.at[i])
        for i, (source, target) in enumerate(
            ((table_hbm, table_ref), (image_hbm, image_ref), (gain1_hbm, gain1_ref), (qkv_hbm, qkv_ref),
             (proj_hbm, proj_ref), (conv_hbm, conv_ref), (gain2_hbm, gain2_ref), (fc1_hbm, fc1_ref),
             (fc2_hbm, fc2_ref))
        )
    ]
    for fetch in fetches:
        fetch.start()

    for ref in (wq, wkv, wp, wc):
        ref[...] = jnp.zeros_like(ref)
    special = lax.broadcasted_iota(jnp.int32, (16, LANES), 0) + 176
    lanes16 = lax.broadcasted_iota(jnp.int32, (16, LANES), 1)
    wq[176:192, :] = one_hot((special == one_lane) & (lanes16 == flag_lane))
    wkv[176:192, 0:LANES] = jnp.where(
        (special == flag_lane) & (lanes16 == flag_lane), MASKED, 0.0
    ).astype(BF16)
    wkv[176:192, LANES:] = one_hot(
        (special == one_lane) & (lanes16 >= channels) & (lanes16 < channels + HEADS)
    )
    normed[...] = jnp.zeros_like(normed)
    normed[1 : 1 + rows, SHIFT : SHIFT + cols, HALF:] = jnp.broadcast_to(
        marks(channels, 0.0)[None], (rows, cols, HALF)
    )

    fetches[0].wait()
    expand_bias(table_ref, padded, strip, bias)
    for fetch in fetches[1:]:
        fetch.wait()
    wq[0:channels, 0:channels] = qkv_ref[:, 0:channels]
    wkv[0:channels, 0:channels] = qkv_ref[:, channels : 2 * channels]
    wkv[0:channels, LANES : LANES + channels] = qkv_ref[:, 2 * channels :]
    wp[0:channels, :] = proj_ref[...]
    for tap in range(9):
        wc[tap * LANES : tap * LANES + channels, :] = conv_ref[tap // 3, tap % 3]

    gain1 = gain1_ref[...]
    scale = head_dim**-0.5 * LOG2E
    for br in range(blocks_r):
        r = br * SIDE
        inner = (slice(1 + r, 1 + r + SIDE), slice(SHIFT, SHIFT + cols))
        normed[(*inner, slice(0, channels))] = layer_norm(image_ref[r : r + SIDE].astype(F32), gain1)
        pixels = normed[inner].astype(BF16).reshape(-1, LANES)
        q = (dot(pixels, wq[...]) * scale).reshape(SIDE, cols, LANES)
        both = dot(pixels, wkv[...]).reshape(SIDE, cols, 2 * LANES)
        for bc in range(blocks_c):
            part = slice(bc * SIDE, (bc + 1) * SIDE)
            query[br, bc] = q[:, part].reshape(AREA, LANES)
            kv[br, bc] = both[:, part].reshape(AREA, 2 * LANES).astype(BF16)

    middle = [(1, 1), (2, 1), (1, 2), (2, 2)]
    pair = jnp.concatenate([kv[at] for at in middle], axis=0)
    units = [
        ([query[1, 1], query[1, 2]], [(0, 0), (0, 1)], pair),
        ([query[2, 1], query[2, 2]], [(1, 0), (1, 1)], pair),
    ]
    mixed = attention(units, bias, head_dim, channels)

    for tap in range(3):
        c0 = SHIFT - 1 + tap
        for r in range(0, rows + 2, SIDE):
            stop = min(r + SIDE, rows + 2)
            shifted[tap, r:stop] = normed[r:stop, c0 : c0 + cols].astype(BF16)
    for br in range(blocks_r):
        r = br * SIDE
        taps = [
            shifted[tap % 3, r + tap // 3 : r + tap // 3 + SIDE].reshape(-1, LANES) for tap in range(9)
        ]
        summed = dot(jnp.concatenate(taps, axis=1), wc[...]).reshape(SIDE, cols, channels)
        summed = summed + image_ref[r : r + SIDE].astype(F32)
        for bc in range(blocks_c):
            base[br, bc] = summed[:, bc * SIDE : (bc + 1) * SIDE].reshape(AREA, channels)

    own_base = jnp.concatenate([base[at] for at in ((1, 1), (1, 2), (2, 1), (2, 2))], axis=0)
    out_mid[...] = finish(
        jnp.concatenate(mixed, axis=0), own_base, spread_matrix(channels), wp, gain2_ref[...], fc1_ref,
        fc2_ref, channels,
    )


def edge_kernel(
    top_ref, bottom_ref, left_ref, right_ref, gain1_ref, gain2_ref, fc1_ref, fc2_ref,
    bias, query, kv, base, wkv, wp, wc,
    kv_edge, fixes, out_edge,
    bands_r, bands_c,
):
    cols, channels = top_ref.shape[1:]
    rows = left_ref.shape[0]
    head_dim = channels // HEADS
    row, last_row = lax.axis_index("row"), lax.axis_size("row") - 1
    col, last_col = lax.axis_index("col"), lax.axis_size("col") - 1
    gain1 = gain1_ref[...]
    outside = [(row == 0).astype(F32), (row == last_row).astype(F32),
               (col == 0).astype(F32), (col == last_col).astype(F32)]

    bands_r[...] = jnp.zeros_like(bands_r)
    bands_c[...] = jnp.zeros_like(bands_c)
    for i, ref in enumerate((top_ref, bottom_ref, left_ref, right_ref)):
        mark = jnp.broadcast_to(marks(channels, outside[i])[None], (*ref.shape[:2], HALF))
        values = layer_norm(ref[...].astype(F32), gain1 * (1.0 - outside[i]))
        if i < 2:
            bands_r[i, :, SHIFT : SHIFT + cols, HALF:] = mark
            bands_r[i, :, SHIFT : SHIFT + cols, 0:channels] = values
            pixels = bands_r[i, :, SHIFT : SHIFT + cols]
            count = cols // SIDE
            blocks = [pixels[:, b * SIDE : (b + 1) * SIDE].reshape(AREA, LANES) for b in range(count)]
        else:
            bands_c[i - 2, 1 : 1 + rows, :, HALF:] = mark
            bands_c[i - 2, 1 : 1 + rows, :, 0:channels] = values
            count = rows // SIDE
            pixels = bands_c[i - 2, 1 : 1 + rows]
            blocks = [pixels.reshape(-1, LANES)]
        both = dot(jnp.concatenate(blocks, axis=0).astype(BF16), wkv[...]).astype(BF16)
        kv_edge[i] = both.reshape(count, AREA, 2 * LANES)

    keys = [
        [kv_edge[0, 1], kv[0, 1], kv_edge[0, 2], kv[0, 2]],
        [kv[3, 1], kv_edge[1, 1], kv[3, 2], kv_edge[1, 2]],
        [kv_edge[2, 1], kv_edge[2, 2], kv[1, 0], kv[2, 0]],
        [kv[1, 3], kv[2, 3], kv_edge[3, 1], kv_edge[3, 2]],
    ]
    places = [((0, 1), (0, 2)), ((3, 1), (3, 2)), ((1, 0), (2, 0)), ((1, 3), (2, 3))]
    quadrants = [((1, 0), (1, 1)), ((0, 0), (0, 1)), ((0, 1), (1, 1)), ((0, 0), (1, 0))]
    units = [
        ([query[at] for at in places[i]], quadrants[i], jnp.concatenate(keys[i], axis=0))
        for i in range(4)
    ]
    mixed = attention(units, bias, head_dim, channels)

    for i, (taps, source) in enumerate((((0, 1, 2), SHIFT - 1), ((6, 7, 8), 0))):
        pieces = [bands_r[i, source, SHIFT - 1 + t : SHIFT - 1 + t + cols] for t in range(3)]
        weights = jnp.concatenate([wc[t * LANES : (t + 1) * LANES] for t in taps], axis=0)
        fixes[i] = dot(jnp.concatenate(pieces, axis=1).astype(BF16), weights)
    for i, (taps, source) in enumerate((((0, 3, 6), SHIFT - 1), ((2, 5, 8), 0))):
        pieces = [bands_c[i, t : t + rows, source] for t in range(3)]
        weights = jnp.concatenate([wc[t * LANES : (t + 1) * LANES] for t in taps], axis=0)
        fixes[2 + i] = dot(jnp.concatenate(pieces, axis=1).astype(BF16), weights)

    gain2, spread = gain2_ref[...], spread_matrix(channels)
    for group in range(2):
        raw = jnp.concatenate([mixed[2 * group], mixed[2 * group + 1]], axis=0)
        parts = [
            corrected(base, fixes, at, channels)
            for at in (*places[2 * group], *places[2 * group + 1])
        ]
        out_edge[group] = finish(
            raw, jnp.concatenate(parts, axis=0), spread, wp, gain2, fc1_ref, fc2_ref, channels
        )


def corrected(base, fixes, at, channels):
    br, bc = at
    block = base[at].reshape(SIDE, SIDE, channels)
    y = lax.broadcasted_iota(jnp.int32, (SIDE, SIDE, 1), 0)
    x = lax.broadcasted_iota(jnp.int32, (SIDE, SIDE, 1), 1)
    if br in (0, 3):
        fix = fixes[0 if br == 0 else 1, bc * SIDE : (bc + 1) * SIDE]
        block = block + jnp.where(y == (0 if br == 0 else SIDE - 1), fix[None], 0.0)
    if bc in (0, 3):
        fix = fixes[2 if bc == 0 else 3, br * SIDE : (br + 1) * SIDE]
        block = block + jnp.where(x == (0 if bc == 0 else SIDE - 1), fix[:, None], 0.0)
    return block.reshape(AREA, channels)


def corner_kernel(
    left_ref, right_ref, gain1_ref, gain2_ref, fc1_ref, fc2_ref,
    bias, query, kv, base, wkv, wp, wc, kv_edge, fixes, out_mid, out_edge,
    out_ref,
    normed,
):
    channels = left_ref.shape[2]
    head_dim = channels // HEADS
    row, last_row = lax.axis_index("row"), lax.axis_size("row") - 1
    col, last_col = lax.axis_index("col"), lax.axis_size("col") - 1
    gain1 = gain1_ref[...]
    out_row = [(row == 0).astype(F32), (row == last_row).astype(F32)]
    out_col = [(col == 0).astype(F32), (col == last_col).astype(F32)]
    for i in range(4):
        ref = (left_ref, right_ref)[i % 2]
        inside = (1.0 - out_row[i // 2]) * (1.0 - out_col[i % 2])
        mark = marks(channels, out_row[i // 2] + out_col[i % 2])
        normed[i, :, HALF:] = jnp.broadcast_to(mark, (AREA, HALF))
        values = ref[i // 2 * SIDE : (i // 2 + 1) * SIDE].astype(F32)
        normed[i, :, 0:channels] = layer_norm(values.reshape(AREA, channels), gain1 * inside)
    corner = dot(normed[...].reshape(-1, LANES).astype(BF16), wkv[...]).astype(BF16)
    corner = [corner[i * AREA : (i + 1) * AREA] for i in range(4)]
    keys = [
        [corner[0], kv_edge[2, 0], kv_edge[0, 0], kv[0, 0]],
        [kv_edge[0, 3], kv[0, 3], corner[1], kv_edge[3, 0]],
        [kv_edge[2, 3], corner[2], kv[3, 0], kv_edge[1, 0]],
        [kv[3, 3], kv_edge[1, 3], kv_edge[3, 3], corner[3]],
    ]
    places = [(0, 0), (0, 3), (3, 0), (3, 3)]
    quadrants = [(1, 1), (1, 0), (0, 1), (0, 0)]
    units = [
        ([query[places[i]]], [quadrants[i]], jnp.concatenate(keys[i], axis=0)) for i in range(4)
    ]
    mixed = attention(units, bias, head_dim, channels)

    parts = []
    for i, (tap, y, x) in enumerate(((0, 7, 7), (2, 7, 0), (6, 0, 7), (8, 0, 0))):
        start = y * SIDE
        term = dot(normed[i, start : start + SIDE].astype(BF16), wc[tap * LANES : (tap + 1) * LANES])
        term = term[x : x + 1]
        pixel = lax.broadcasted_iota(jnp.int32, (AREA, 1), 0)
        at = (SIDE - 1 - y) * SIDE + SIDE - 1 - x
        block = corrected(base, fixes, places[i], channels)
        parts.append(block + jnp.where(pixel == at, term, 0.0))
    out_corner = finish(
        jnp.concatenate(mixed, axis=0), jnp.concatenate(parts, axis=0), spread_matrix(channels), wp,
        gain2_ref[...], fc1_ref, fc2_ref, channels,
    )

    def piece(source, i):
        return source[i * AREA : (i + 1) * AREA].reshape(SIDE, SIDE, channels)

    bands = [
        [piece(out_corner, 0), piece(out_edge.at[0], 0), piece(out_edge.at[0], 1), piece(out_corner, 1)],
        [piece(out_edge.at[1], 0), piece(out_mid, 0), piece(out_mid, 1), piece(out_edge.at[1], 2)],
        [piece(out_edge.at[1], 1), piece(out_mid, 2), piece(out_mid, 3), piece(out_edge.at[1], 3)],
        [piece(out_corner, 2), piece(out_edge.at[0], 2), piece(out_edge.at[0], 3), piece(out_corner, 3)],
    ]
    for br, band in enumerate(bands):
        out_ref[br * SIDE : (br + 1) * SIDE] = jnp.concatenate(band, axis=1).astype(BF16)


def exchange(low, high, axis):
    count = lax.axis_size(axis)
    before = lax.ppermute(high, axis, [(i, (i + 1) % count) for i in range(count)])
    after = lax.ppermute(low, axis, [((i + 1) % count, i) for i in range(count)])
    return before, after


def call(kernel, name, outs, scratch, flops, operands, in_hbm=()):
    vmem = pl.BlockSpec(memory_space=pltpu.VMEM)
    hbm = pl.BlockSpec(memory_space=pltpu.HBM)
    return pl.pallas_call(
        kernel,
        out_shape=[out if isinstance(out, jax.ShapeDtypeStruct) else pltpu.VMEM(*out) for out in outs],
        in_specs=[hbm if i in in_hbm else vmem for i in range(len(operands))],
        out_specs=[vmem] * len(outs),
        scratch_shapes=[pltpu.VMEM(*s) if isinstance(s, tuple) else s for s in scratch],
        cost_estimate=pl.CostEstimate(flops=flops, bytes_accessed=4_000_000, transcendentals=1_000_000),
        compiler_params=pltpu.CompilerParams(vmem_limit_bytes=24 * 1024 * 1024),
        name=name,
    )(*[pltpu.with_memory_space_constraint(x, pltpu.HBM) if i in in_hbm else x for i, x in enumerate(operands)])


def on_device(
    image, norm1_gain, norm2_gain, qkv_weight, proj_weight, rel_table, conv_weight, fc1_weight,
    fc2_weight,
):
    rows, cols, channels = image.shape
    blocks_r, blocks_c = rows // SIDE, cols // SIDE
    gain1, gain2, fc2, table = norm1_gain[None], norm2_gain[None], fc2_weight.T, rel_table.T
    top, bottom = exchange(image[:SHIFT], image[rows - SHIFT :], "row")
    left, right = exchange(image[:, :SHIFT], image[:, cols - SHIFT :], "col")
    fetched = (table, image, gain1, gain2, qkv_weight, proj_weight, conv_weight, fc1_weight, fc2)
    bias, query, kv, base, wkv, wp, wc, out_mid = call(
        own_kernel,
        "own_tile",
        [
            ((HEADS, 2, 2, AREA, WIN * WIN), F32),
            ((blocks_r, blocks_c, AREA, LANES), F32),
            ((blocks_r, blocks_c, AREA, 2 * LANES), BF16),
            ((blocks_r, blocks_c, AREA, channels), F32),
            ((LANES, 2 * LANES), BF16),
            ((LANES, channels), BF16),
            ((9 * LANES, channels), BF16),
            ((4 * AREA, channels), F32),
        ],
        [
            ((8, 1024), F32),
            ((4, 8 * WIN, 128), F32),
            ((LANES, LANES), BF16),
            ((rows + 2, cols + 2 * SHIFT, LANES), F32),
            ((3, rows + 2, cols, LANES), BF16),
            *[(x.shape, x.dtype) for x in fetched],
            pltpu.SemaphoreType.DMA((len(fetched),)),
        ],
        2_000_000_000,
        (image, gain1, gain2, qkv_weight, proj_weight, table, conv_weight, fc1_weight, fc2),
        range(9),
    )
    first = jnp.concatenate([top[:, :SHIFT], bottom[:, :SHIFT]])
    last = jnp.concatenate([top[:, cols - SHIFT :], bottom[:, cols - SHIFT :]])
    left_corner, right_corner = exchange(first, last, "col")
    kv_edge, fixes, out_edge = call(
        edge_kernel,
        "edge_windows",
        [
            ((4, blocks_c, AREA, 2 * LANES), BF16),
            ((4, cols, channels), F32),
            ((2, 4 * AREA, channels), F32),
        ],
        [((2, SHIFT, cols + 2 * SHIFT, LANES), F32), ((2, rows + 2, SHIFT, LANES), F32)],
        2_000_000_000,
        (top, bottom, left, right, gain1, gain2, fc1_weight, fc2, bias, query, kv, base, wkv, wp, wc),
    )
    (out,) = call(
        corner_kernel,
        "corner_windows",
        [jax.ShapeDtypeStruct(image.shape, BF16)],
        [((4, AREA, LANES), F32)],
        1_000_000_000,
        (left_corner, right_corner, gain1, gain2, fc1_weight, fc2, bias, query, kv, base, wkv, wp, wc,
         kv_edge, fixes, out_mid, out_edge),
    )
    return out


def solution(mesh):
    placed = (P("row", "col", None), P(), P(), P(), P(), P(), P(), P(), P())
    return jax.shard_map(
        on_device, mesh=mesh, in_specs=placed, out_specs=P("row", "col", None), check_vma=False
    )
```

```python
import math

import jax
import jax.numpy as jnp
from jax import lax
from jax.experimental import pallas as pl
from jax.experimental.pallas import tpu as pltpu
from jax.sharding import PartitionSpec as P

HEADS = 6
WIN = 16
SHIFT = 8
SIDE = 8
AREA = SIDE * SIDE
LANES = 256
HALF = LANES // 2
F32 = jnp.float32
BF16 = jnp.bfloat16
LOG2E = math.log2(math.e)
MASKED = -4.0e9


def layer_norm(values, norm_gain):
    centre = jnp.mean(values, axis=-1, keepdims=True)
    values = values - centre
    spread = jnp.mean(values * values, axis=-1, keepdims=True)
    return values * lax.rsqrt(spread + 1e-05) * norm_gain


def dot(a, b):
    return jnp.dot(a, b, preferred_element_type=F32)


def dot_nt(a, b):
    return lax.dot_general(a, b, (((1,), (1,)), ((), ())), preferred_element_type=F32)


def one_hot(condition):
    return jnp.where(condition, 1.0, 0.0).astype(BF16)


def gelu(x):
    size = jnp.abs(x)
    t = 1.0 / (1.0 + (0.3275911 * math.sqrt(0.5)) * size)
    poly = 0.5 * 1.061405429
    for factor in (-1.453152027, 1.421413741, -0.284496736, 0.254829592):
        poly = poly * t + 0.5 * factor
    tail = poly * t * jnp.exp2(size * size * (-0.5 * LOG2E))
    return jnp.maximum(x, 0.0) - size * tail


def lanes_of(width=LANES):
    return lax.broadcasted_iota(jnp.int32, (1, width), 1)


def marks(channels, outside):
    half = lanes_of()[:, HALF:]
    return jnp.where(half == channels + 1, 1.0, 0.0) + jnp.where(half == channels, outside, 0.0)


def expand_bias(table_ref, padded, strip, bias):
    span = 2 * WIN - 1
    padded[...] = jnp.zeros_like(padded)
    padded[0:HEADS, 0 : span * span] = table_ref[...] * LOG2E
    table = padded[...]
    width = padded.shape[1]
    shifted = jnp.concatenate(
        [table if px == 0 else pltpu.roll(table, width - px, 1) for px in range(WIN)], axis=0
    )
    high = shifted.astype(BF16)
    low = (shifted - high.astype(F32)).astype(BF16)
    entry = lax.broadcasted_iota(jnp.int32, (width, 512), 0)
    place = lax.broadcasted_iota(jnp.int32, (1, 512), 1)
    column = lax.div(place, 256) * SIDE + lax.rem(place, SIDE)
    wanted = (span - 1 - lax.div(lax.rem(place, 256), SIDE)) * span + WIN - 1 - column
    picked = dot(jnp.concatenate([high, low], axis=0), one_hot(entry == wanted))
    half = 8 * WIN
    picked = picked[:half] + picked[half:]
    for tile in range(4):
        strip[tile] = picked[:, 128 * tile : 128 * (tile + 1)]
    for head in range(HEADS):
        for half in range(2):
            rows = jnp.concatenate(
                [strip[2 * half + t, pl.ds(head, WIN, stride=8), :] for t in range(2)], axis=1
            )
            for py in range(WIN):
                start = (WIN - 1 - py) * SIDE
                rolled = (rows if start == 0 else pltpu.roll(rows, 256 - start, 1))[:, 0:128]
                lanes = slice(128 * half, 128 * (half + 1))
                place = slice(py % SIDE * SIDE, (py % SIDE + 1) * SIDE)
                bias[head, py // SIDE, 0, place, lanes] = rolled[:SIDE]
                bias[head, py // SIDE, 1, place, lanes] = rolled[SIDE:]


def scores_of(blocks, keys, head_dim, channels):
    lane = lanes_of()
    part = jnp.concatenate(blocks, axis=0)
    own = [(lane >= h * head_dim) & (lane < (h + 1) * head_dim) for h in range(HEADS)]
    stacked = jnp.concatenate(
        [part * one_hot(own[h] | (lane == channels)) for h in range(HEADS)], axis=0
    )
    return dot_nt(stacked, keys)


def mix(scores, part_bias, values, head_dim, channels):
    lane = lanes_of()
    count = scores.shape[0] // HEADS
    scores = scores.reshape(HEADS, count, WIN * WIN) + part_bias
    scores = scores - jnp.max(scores, axis=-1, keepdims=True)
    soft = jnp.exp2(scores).astype(BF16).reshape(HEADS * count, WIN * WIN)
    mixed = dot(soft, values)
    result = mixed[0:count]
    for h in range(1, HEADS):
        mine = (lane >= h * head_dim) & (lane < (h + 1) * head_dim) | (lane == channels + h)
        result = jnp.where(mine, mixed[h * count : (h + 1) * count], result)
    return result


def attention(units, bias, head_dim, channels):
    def scores_at(unit):
        return scores_of(unit[0], unit[2][:, :LANES], head_dim, channels)

    results = []
    ahead = scores_at(units[0])
    for i, unit in enumerate(units):
        scores, ahead = ahead, scores_at(units[i + 1]) if i + 1 < len(units) else None
        part_bias = jnp.concatenate([bias[:, hy, hx] for hy, hx in unit[1]], axis=1)
        results.append(mix(scores, part_bias, unit[2][:, LANES:], head_dim, channels))
    return results


def spread_matrix(channels):
    head_dim = channels // HEADS
    sum_row = lax.broadcasted_iota(jnp.int32, (HALF, LANES), 0) + HALF - channels
    lane_wide = lax.broadcasted_iota(jnp.int32, (HALF, LANES), 1)
    return one_hot(
        (sum_row >= 0) & (lane_wide >= sum_row * head_dim) & (lane_wide < (sum_row + 1) * head_dim)
        & (lane_wide < channels)
    )


def finish(raw, base, spread, wp, gain2, fc1, fc2, channels):
    half = lanes_of()[:, HALF:]
    is_sum = (half >= channels) & (half < channels + HEADS)
    inverse = jnp.where(is_sum, 1.0 / raw[:, HALF:], 0.0)
    high = inverse.astype(BF16)
    low = (inverse - high.astype(F32)).astype(BF16)
    heads_out = (raw * (dot(high, spread) + dot(low, spread))).astype(BF16)
    state1 = base + dot(heads_out, wp[...]).astype(BF16).astype(F32)
    normed2 = layer_norm(state1, gain2).astype(BF16)
    hidden = gelu(dot(normed2, fc1[...])).astype(BF16)
    return state1 + dot_nt(hidden, fc2[...])


def cut_kernel(image_hbm, image_ref, top, bottom, left, right, sem):
    rows, cols, _ = image_ref.shape
    fetch = pltpu.make_async_copy(image_hbm, image_ref, sem)
    fetch.start()
    fetch.wait()
    top[...] = image_ref[:SHIFT]
    bottom[...] = image_ref[rows - SHIFT :]
    for r in range(0, rows, SIDE):
        band = image_ref[r : r + SIDE].astype(F32)
        left[r : r + SIDE] = band[:, :SHIFT].astype(BF16)
        right[r : r + SIDE] = band[:, cols - SHIFT :].astype(BF16)


def own_kernel(
    image_ref, gain1_hbm, gain2_hbm, qkv_hbm, proj_hbm, table_hbm, conv_hbm, fc1_hbm, fc2_hbm,
    bias, query, kv, base, wkv, wp, wc, out_mid,
    padded, strip, wq, normed, shifted,
    table_ref, gain1_ref, gain2_ref, qkv_ref, proj_ref, conv_ref, fc1_ref, fc2_ref, sems,
):
    rows, cols, channels = image_ref.shape
    head_dim = channels // HEADS
    flag_lane, one_lane = channels, channels + 1
    blocks_r, blocks_c = rows // SIDE, cols // SIDE
    fetches = [
        pltpu.make_async_copy(source, target, sems.at[i])
        for i, (source, target) in enumerate(
            ((gain1_hbm, gain1_ref), (qkv_hbm, qkv_ref), (table_hbm, table_ref), (proj_hbm, proj_ref),
             (conv_hbm, conv_ref), (gain2_hbm, gain2_ref), (fc1_hbm, fc1_ref), (fc2_hbm, fc2_ref))
        )
    ]
    for fetch in fetches:
        fetch.start()

    for ref in (wq, wkv, wp, wc):
        ref[...] = jnp.zeros_like(ref)
    special = lax.broadcasted_iota(jnp.int32, (16, LANES), 0) + 176
    lanes16 = lax.broadcasted_iota(jnp.int32, (16, LANES), 1)
    wq[176:192, :] = one_hot((special == one_lane) & (lanes16 == flag_lane))
    wkv[176:192, 0:LANES] = jnp.where(
        (special == flag_lane) & (lanes16 == flag_lane), MASKED, 0.0
    ).astype(BF16)
    wkv[176:192, LANES:] = one_hot(
        (special == one_lane) & (lanes16 >= channels) & (lanes16 < channels + HEADS)
    )
    normed[...] = jnp.zeros_like(normed)
    normed[1 : 1 + rows, SHIFT : SHIFT + cols, HALF:] = jnp.broadcast_to(
        marks(channels, 0.0)[None], (rows, cols, HALF)
    )

    fetches[0].wait()
    gain1 = gain1_ref[...]
    for r in range(0, rows, SIDE):
        inner = (slice(1 + r, 1 + r + SIDE), slice(SHIFT, SHIFT + cols))
        normed[(*inner, slice(0, channels))] = layer_norm(image_ref[r : r + SIDE].astype(F32), gain1)

    for fetch in fetches[1:]:
        fetch.wait()
    wq[0:channels, 0:channels] = qkv_ref[:, 0:channels]
    wkv[0:channels, 0:channels] = qkv_ref[:, channels : 2 * channels]
    wkv[0:channels, LANES : LANES + channels] = qkv_ref[:, 2 * channels :]
    wp[0:channels, :] = proj_ref[...]
    for tap in range(9):
        wc[tap * LANES : tap * LANES + channels, :] = conv_ref[tap // 3, tap % 3]

    scale = head_dim**-0.5 * LOG2E
    for r in range(0, rows, 2 * SIDE):
        inner = (slice(1 + r, 1 + r + 2 * SIDE), slice(SHIFT, SHIFT + cols))
        pixels = normed[inner].astype(BF16).reshape(-1, LANES)
        q = (dot(pixels, wq[...]) * scale).reshape(2 * SIDE, cols, LANES)
        both = dot(pixels, wkv[...]).reshape(2 * SIDE, cols, 2 * LANES)
        for i in range(2):
            for bc in range(blocks_c):
                part = (slice(i * SIDE, (i + 1) * SIDE), slice(bc * SIDE, (bc + 1) * SIDE))
                query[r // SIDE + i, bc] = q[part].reshape(AREA, LANES).astype(BF16)
                kv[r // SIDE + i, bc] = both[part].reshape(AREA, 2 * LANES).astype(BF16)
    expand_bias(table_ref, padded, strip, bias)

    middle = [(1, 1), (2, 1), (1, 2), (2, 2)]
    pair = jnp.concatenate([kv[at] for at in middle], axis=0)
    units = [
        ([query[1, 1], query[1, 2]], [(0, 0), (0, 1)], pair),
        ([query[2, 1], query[2, 2]], [(1, 0), (1, 1)], pair),
    ]
    mixed = attention(units, bias, head_dim, channels)

    for tap in range(3):
        c0 = SHIFT - 1 + tap
        for r in range(0, rows + 2, SIDE):
            stop = min(r + SIDE, rows + 2)
            shifted[tap, r:stop] = normed[r:stop, c0 : c0 + cols].astype(BF16)
    for r in range(0, rows, 2 * SIDE):
        taps = [
            shifted[tap % 3, r + tap // 3 : r + tap // 3 + 2 * SIDE].reshape(-1, LANES)
            for tap in range(9)
        ]
        summed = dot(jnp.concatenate(taps, axis=1), wc[...]).reshape(2 * SIDE, cols, channels)
        summed = summed + image_ref[r : r + 2 * SIDE].astype(F32)
        for i in range(2):
            for bc in range(blocks_c):
                part = (slice(i * SIDE, (i + 1) * SIDE), slice(bc * SIDE, (bc + 1) * SIDE))
                base[r // SIDE + i, bc] = summed[part].reshape(AREA, channels)

    own_base = jnp.concatenate([base[at] for at in ((1, 1), (1, 2), (2, 1), (2, 2))], axis=0)
    out_mid[...] = finish(
        jnp.concatenate(mixed, axis=0), own_base, spread_matrix(channels), wp, gain2_ref[...], fc1_ref,
        fc2_ref, channels,
    )


def edge_kernel(
    top_ref, bottom_ref, left_ref, right_ref, gain1_ref, gain2_ref, fc1_ref, fc2_ref,
    bias, query, kv, base, wkv, wp, wc,
    kv_edge, fixes, out_edge,
    bands_r, bands_c,
):
    cols, channels = top_ref.shape[1:]
    rows = left_ref.shape[0]
    head_dim = channels // HEADS
    row, last_row = lax.axis_index("row"), lax.axis_size("row") - 1
    col, last_col = lax.axis_index("col"), lax.axis_size("col") - 1
    gain1 = gain1_ref[...]
    outside = [(row == 0).astype(F32), (row == last_row).astype(F32),
               (col == 0).astype(F32), (col == last_col).astype(F32)]

    bands_r[...] = jnp.zeros_like(bands_r)
    bands_c[...] = jnp.zeros_like(bands_c)
    for i, ref in enumerate((top_ref, bottom_ref, left_ref, right_ref)):
        mark = jnp.broadcast_to(marks(channels, outside[i])[None], (*ref.shape[:2], HALF))
        values = layer_norm(ref[...].astype(F32), gain1 * (1.0 - outside[i]))
        if i < 2:
            bands_r[i, :, SHIFT : SHIFT + cols, HALF:] = mark
            bands_r[i, :, SHIFT : SHIFT + cols, 0:channels] = values
            pixels = bands_r[i, :, SHIFT : SHIFT + cols]
            count = cols // SIDE
            blocks = [pixels[:, b * SIDE : (b + 1) * SIDE].reshape(AREA, LANES) for b in range(count)]
        else:
            bands_c[i - 2, 1 : 1 + rows, :, HALF:] = mark
            bands_c[i - 2, 1 : 1 + rows, :, 0:channels] = values
            count = rows // SIDE
            pixels = bands_c[i - 2, 1 : 1 + rows]
            blocks = [pixels.reshape(-1, LANES)]
        both = dot(jnp.concatenate(blocks, axis=0).astype(BF16), wkv[...]).astype(BF16)
        kv_edge[i] = both.reshape(count, AREA, 2 * LANES)

    keys = [
        [kv_edge[0, 1], kv[0, 1], kv_edge[0, 2], kv[0, 2]],
        [kv[3, 1], kv_edge[1, 1], kv[3, 2], kv_edge[1, 2]],
        [kv_edge[2, 1], kv_edge[2, 2], kv[1, 0], kv[2, 0]],
        [kv[1, 3], kv[2, 3], kv_edge[3, 1], kv_edge[3, 2]],
    ]
    places = [((0, 1), (0, 2)), ((3, 1), (3, 2)), ((1, 0), (2, 0)), ((1, 3), (2, 3))]
    quadrants = [((1, 0), (1, 1)), ((0, 0), (0, 1)), ((0, 1), (1, 1)), ((0, 0), (1, 0))]
    units = [
        ([query[at] for at in places[i]], quadrants[i], jnp.concatenate(keys[i], axis=0))
        for i in range(4)
    ]
    mixed = attention(units, bias, head_dim, channels)

    for i, (taps, source) in enumerate((((0, 1, 2), SHIFT - 1), ((6, 7, 8), 0))):
        pieces = [bands_r[i, source, SHIFT - 1 + t : SHIFT - 1 + t + cols] for t in range(3)]
        weights = jnp.concatenate([wc[t * LANES : (t + 1) * LANES] for t in taps], axis=0)
        fixes[i] = dot(jnp.concatenate(pieces, axis=1).astype(BF16), weights)
    for i, (taps, source) in enumerate((((0, 3, 6), SHIFT - 1), ((2, 5, 8), 0))):
        pieces = [bands_c[i, t : t + rows, source] for t in range(3)]
        weights = jnp.concatenate([wc[t * LANES : (t + 1) * LANES] for t in taps], axis=0)
        fixes[2 + i] = dot(jnp.concatenate(pieces, axis=1).astype(BF16), weights)

    gain2, spread = gain2_ref[...], spread_matrix(channels)
    for group in range(2):
        raw = jnp.concatenate([mixed[2 * group], mixed[2 * group + 1]], axis=0)
        parts = [
            corrected(base, fixes, at, channels)
            for at in (*places[2 * group], *places[2 * group + 1])
        ]
        out_edge[group] = finish(
            raw, jnp.concatenate(parts, axis=0), spread, wp, gain2, fc1_ref, fc2_ref, channels
        )


def corrected(base, fixes, at, channels):
    br, bc = at
    block = base[at].reshape(SIDE, SIDE, channels)
    y = lax.broadcasted_iota(jnp.int32, (SIDE, SIDE, 1), 0)
    x = lax.broadcasted_iota(jnp.int32, (SIDE, SIDE, 1), 1)
    if br in (0, 3):
        fix = fixes[0 if br == 0 else 1, bc * SIDE : (bc + 1) * SIDE]
        block = block + jnp.where(y == (0 if br == 0 else SIDE - 1), fix[None], 0.0)
    if bc in (0, 3):
        fix = fixes[2 if bc == 0 else 3, br * SIDE : (br + 1) * SIDE]
        block = block + jnp.where(x == (0 if bc == 0 else SIDE - 1), fix[:, None], 0.0)
    return block.reshape(AREA, channels)


def corner_kernel(
    left_ref, right_ref, gain1_ref, gain2_ref, fc1_ref, fc2_ref,
    bias, query, kv, base, wkv, wp, wc, kv_edge, fixes, out_mid, out_edge,
    out_ref,
    normed,
):
    channels = left_ref.shape[2]
    head_dim = channels // HEADS
    row, last_row = lax.axis_index("row"), lax.axis_size("row") - 1
    col, last_col = lax.axis_index("col"), lax.axis_size("col") - 1
    gain1 = gain1_ref[...]
    out_row = [(row == 0).astype(F32), (row == last_row).astype(F32)]
    out_col = [(col == 0).astype(F32), (col == last_col).astype(F32)]
    for i in range(4):
        ref = (left_ref, right_ref)[i % 2]
        inside = (1.0 - out_row[i // 2]) * (1.0 - out_col[i % 2])
        mark = marks(channels, out_row[i // 2] + out_col[i % 2])
        normed[i, :, HALF:] = jnp.broadcast_to(mark, (AREA, HALF))
        values = ref[i // 2 * SIDE : (i // 2 + 1) * SIDE].astype(F32)
        normed[i, :, 0:channels] = layer_norm(values.reshape(AREA, channels), gain1 * inside)
    corner = dot(normed[...].reshape(-1, LANES).astype(BF16), wkv[...]).astype(BF16)
    corner = [corner[i * AREA : (i + 1) * AREA] for i in range(4)]
    keys = [
        [corner[0], kv_edge[2, 0], kv_edge[0, 0], kv[0, 0]],
        [kv_edge[0, 3], kv[0, 3], corner[1], kv_edge[3, 0]],
        [kv_edge[2, 3], corner[2], kv[3, 0], kv_edge[1, 0]],
        [kv[3, 3], kv_edge[1, 3], kv_edge[3, 3], corner[3]],
    ]
    places = [(0, 0), (0, 3), (3, 0), (3, 3)]
    quadrants = [(1, 1), (1, 0), (0, 1), (0, 0)]
    units = [
        ([query[places[i]]], [quadrants[i]], jnp.concatenate(keys[i], axis=0)) for i in range(4)
    ]
    mixed = attention(units, bias, head_dim, channels)

    parts = []
    for i, (tap, y, x) in enumerate(((0, 7, 7), (2, 7, 0), (6, 0, 7), (8, 0, 0))):
        start = y * SIDE
        term = dot(normed[i, start : start + SIDE].astype(BF16), wc[tap * LANES : (tap + 1) * LANES])
        term = term[x : x + 1]
        pixel = lax.broadcasted_iota(jnp.int32, (AREA, 1), 0)
        at = (SIDE - 1 - y) * SIDE + SIDE - 1 - x
        block = corrected(base, fixes, places[i], channels)
        parts.append(block + jnp.where(pixel == at, term, 0.0))
    out_corner = finish(
        jnp.concatenate(mixed, axis=0), jnp.concatenate(parts, axis=0), spread_matrix(channels), wp,
        gain2_ref[...], fc1_ref, fc2_ref, channels,
    )

    def piece(source, i):
        return source[i * AREA : (i + 1) * AREA].reshape(SIDE, SIDE, channels)

    bands = [
        [piece(out_corner, 0), piece(out_edge.at[0], 0), piece(out_edge.at[0], 1), piece(out_corner, 1)],
        [piece(out_edge.at[1], 0), piece(out_mid, 0), piece(out_mid, 1), piece(out_edge.at[1], 2)],
        [piece(out_edge.at[1], 1), piece(out_mid, 2), piece(out_mid, 3), piece(out_edge.at[1], 3)],
        [piece(out_corner, 2), piece(out_edge.at[0], 2), piece(out_edge.at[0], 3), piece(out_corner, 3)],
    ]
    for br, band in enumerate(bands):
        out_ref[br * SIDE : (br + 1) * SIDE] = jnp.concatenate(band, axis=1).astype(BF16)


def exchange(low, high, axis):
    count = lax.axis_size(axis)
    before = lax.ppermute(high, axis, [(i, (i + 1) % count) for i in range(count)])
    after = lax.ppermute(low, axis, [((i + 1) % count, i) for i in range(count)])
    return before, after


def call(kernel, name, outs, scratch, flops, operands, in_hbm=()):
    vmem = pl.BlockSpec(memory_space=pltpu.VMEM)
    hbm = pl.BlockSpec(memory_space=pltpu.HBM)
    return pl.pallas_call(
        kernel,
        out_shape=[out if isinstance(out, jax.ShapeDtypeStruct) else pltpu.VMEM(*out) for out in outs],
        in_specs=[hbm if i in in_hbm else vmem for i in range(len(operands))],
        out_specs=[vmem] * len(outs),
        scratch_shapes=[pltpu.VMEM(*s) if isinstance(s, tuple) else s for s in scratch],
        cost_estimate=pl.CostEstimate(flops=flops, bytes_accessed=4_000_000, transcendentals=1_000_000),
        compiler_params=pltpu.CompilerParams(vmem_limit_bytes=24 * 1024 * 1024),
        name=name,
    )(*[pltpu.with_memory_space_constraint(x, pltpu.HBM) if i in in_hbm else x for i, x in enumerate(operands)])


def on_device(
    image, norm1_gain, norm2_gain, qkv_weight, proj_weight, rel_table, conv_weight, fc1_weight,
    fc2_weight,
):
    rows, cols, channels = image.shape
    blocks_r, blocks_c = rows // SIDE, cols // SIDE
    gain1, gain2, fc2, table = norm1_gain[None], norm2_gain[None], fc2_weight.T, rel_table.T
    band, column = ((SHIFT, cols, channels), BF16), ((rows, SHIFT, channels), BF16)
    tile, first_rows, last_rows, first_cols, last_cols = call(
        cut_kernel,
        "cut_halo",
        [(image.shape, BF16), band, band, column, column],
        [pltpu.SemaphoreType.DMA(())],
        1_000_000,
        (image,),
        (0,),
    )
    top, bottom = exchange(first_rows, last_rows, "row")
    left, right = exchange(first_cols, last_cols, "col")
    fetched = (table, gain1, gain2, qkv_weight, proj_weight, conv_weight, fc1_weight, fc2)
    bias, query, kv, base, wkv, wp, wc, out_mid = call(
        own_kernel,
        "own_tile",
        [
            ((HEADS, 2, 2, AREA, WIN * WIN), F32),
            ((blocks_r, blocks_c, AREA, LANES), BF16),
            ((blocks_r, blocks_c, AREA, 2 * LANES), BF16),
            ((blocks_r, blocks_c, AREA, channels), F32),
            ((LANES, 2 * LANES), BF16),
            ((LANES, channels), BF16),
            ((9 * LANES, channels), BF16),
            ((4 * AREA, channels), F32),
        ],
        [
            ((8, 1024), F32),
            ((4, 8 * WIN, 128), F32),
            ((LANES, LANES), BF16),
            ((rows + 2, cols + 2 * SHIFT, LANES), F32),
            ((3, rows + 2, cols, LANES), BF16),
            *[(x.shape, x.dtype) for x in fetched],
            pltpu.SemaphoreType.DMA((len(fetched),)),
        ],
        2_000_000_000,
        (tile, gain1, gain2, qkv_weight, proj_weight, table, conv_weight, fc1_weight, fc2),
        range(1, 9),
    )
    first = jnp.concatenate([top[:, :SHIFT], bottom[:, :SHIFT]])
    last = jnp.concatenate([top[:, cols - SHIFT :], bottom[:, cols - SHIFT :]])
    left_corner, right_corner = exchange(first, last, "col")
    kv_edge, fixes, out_edge = call(
        edge_kernel,
        "edge_windows",
        [
            ((4, blocks_c, AREA, 2 * LANES), BF16),
            ((4, cols, channels), F32),
            ((2, 4 * AREA, channels), F32),
        ],
        [((2, SHIFT, cols + 2 * SHIFT, LANES), F32), ((2, rows + 2, SHIFT, LANES), F32)],
        2_000_000_000,
        (top, bottom, left, right, gain1, gain2, fc1_weight, fc2, bias, query, kv, base, wkv, wp, wc),
    )
    (out,) = call(
        corner_kernel,
        "corner_windows",
        [jax.ShapeDtypeStruct(image.shape, BF16)],
        [((4, AREA, LANES), F32)],
        1_000_000_000,
        (left_corner, right_corner, gain1, gain2, fc1_weight, fc2, bias, query, kv, base, wkv, wp, wc,
         kv_edge, fixes, out_mid, out_edge),
    )
    return out


def solution(mesh):
    placed = (P("row", "col", None), P(), P(), P(), P(), P(), P(), P(), P())
    return jax.shard_map(
        on_device, mesh=mesh, in_specs=placed, out_specs=P("row", "col", None), check_vma=False
    )
```

```python
import math

import jax
import jax.numpy as jnp
from jax import lax
from jax.experimental import pallas as pl
from jax.experimental.pallas import tpu as pltpu
from jax.sharding import PartitionSpec as P

HEADS = 6
WIN = 16
SHIFT = 8
SIDE = 8
AREA = SIDE * SIDE
LANES = 256
HALF = LANES // 2
F32 = jnp.float32
BF16 = jnp.bfloat16
LOG2E = math.log2(math.e)
MASKED = -4.0e9


def layer_norm(values, norm_gain):
    centre = jnp.mean(values, axis=-1, keepdims=True)
    values = values - centre
    spread = jnp.mean(values * values, axis=-1, keepdims=True)
    return values * lax.rsqrt(spread + 1e-05) * norm_gain


def dot(a, b):
    return jnp.dot(a, b, preferred_element_type=F32)


def dot_nt(a, b):
    return lax.dot_general(a, b, (((1,), (1,)), ((), ())), preferred_element_type=F32)


def one_hot(condition):
    return jnp.where(condition, 1.0, 0.0).astype(BF16)


def gelu(x):
    size = jnp.abs(x)
    t = 1.0 / (1.0 + (0.3275911 * math.sqrt(0.5)) * size)
    poly = 0.5 * 1.061405429
    for factor in (-1.453152027, 1.421413741, -0.284496736, 0.254829592):
        poly = poly * t + 0.5 * factor
    tail = poly * t * jnp.exp2(size * size * (-0.5 * LOG2E))
    return jnp.maximum(x, 0.0) - size * tail


def lanes_of(width=LANES):
    return lax.broadcasted_iota(jnp.int32, (1, width), 1)


def marks(channels, outside):
    half = lanes_of()[:, HALF:]
    return jnp.where(half == channels + 1, 1.0, 0.0) + jnp.where(half == channels, outside, 0.0)


def expand_bias(table_ref, padded, strip, bias):
    span = 2 * WIN - 1
    padded[...] = jnp.zeros_like(padded)
    padded[0:HEADS, 0 : span * span] = table_ref[...] * LOG2E
    table = padded[...]
    width = padded.shape[1]
    shifted = jnp.concatenate(
        [table if px == 0 else pltpu.roll(table, width - px, 1) for px in range(WIN)], axis=0
    )
    high = shifted.astype(BF16)
    low = (shifted - high.astype(F32)).astype(BF16)
    entry = lax.broadcasted_iota(jnp.int32, (width, 512), 0)
    place = lax.broadcasted_iota(jnp.int32, (1, 512), 1)
    column = lax.div(place, 256) * SIDE + lax.rem(place, SIDE)
    wanted = (span - 1 - lax.div(lax.rem(place, 256), SIDE)) * span + WIN - 1 - column
    picked = dot(jnp.concatenate([high, low], axis=0), one_hot(entry == wanted))
    half = 8 * WIN
    picked = picked[:half] + picked[half:]
    for tile in range(4):
        strip[tile] = picked[:, 128 * tile : 128 * (tile + 1)]
    for head in range(HEADS):
        for half in range(2):
            rows = jnp.concatenate(
                [strip[2 * half + t, pl.ds(head, WIN, stride=8), :] for t in range(2)], axis=1
            )
            for py in range(WIN):
                start = (WIN - 1 - py) * SIDE
                rolled = (rows if start == 0 else pltpu.roll(rows, 256 - start, 1))[:, 0:128]
                lanes = slice(128 * half, 128 * (half + 1))
                place = slice(py % SIDE * SIDE, (py % SIDE + 1) * SIDE)
                bias[head, py // SIDE, 0, place, lanes] = rolled[:SIDE]
                bias[head, py // SIDE, 1, place, lanes] = rolled[SIDE:]


def scores_of(blocks, keys, head_dim, channels):
    lane = lanes_of()
    part = jnp.concatenate(blocks, axis=0)
    own = [(lane >= h * head_dim) & (lane < (h + 1) * head_dim) for h in range(HEADS)]
    stacked = jnp.concatenate(
        [part * one_hot(own[h] | (lane == channels)) for h in range(HEADS)], axis=0
    )
    return dot_nt(stacked, keys)


def mix(scores, part_bias, values, head_dim, channels):
    lane = lanes_of()
    count = scores.shape[0] // HEADS
    scores = scores.reshape(HEADS, count, WIN * WIN) + part_bias
    scores = scores - jnp.max(scores, axis=-1, keepdims=True)
    soft = jnp.exp2(scores).astype(BF16).reshape(HEADS * count, WIN * WIN)
    mixed = dot(soft, values)
    result = mixed[0:count]
    for h in range(1, HEADS):
        mine = (lane >= h * head_dim) & (lane < (h + 1) * head_dim) | (lane == channels + h)
        result = jnp.where(mine, mixed[h * count : (h + 1) * count], result)
    return result


def attention(units, bias, head_dim, channels):
    def scores_at(unit):
        return scores_of(unit[0], unit[2][:, :LANES], head_dim, channels)

    ahead = scores_at(units[0])
    for i, unit in enumerate(units):
        scores, ahead = ahead, scores_at(units[i + 1]) if i + 1 < len(units) else None
        part_bias = jnp.concatenate([bias[:, hy, hx] for hy, hx in unit[1]], axis=1)
        yield mix(scores, part_bias, unit[2][:, LANES:], head_dim, channels)


def spread_matrix(channels):
    head_dim = channels // HEADS
    sum_row = lax.broadcasted_iota(jnp.int32, (HALF, LANES), 0) + HALF - channels
    lane_wide = lax.broadcasted_iota(jnp.int32, (HALF, LANES), 1)
    return one_hot(
        (sum_row >= 0) & (lane_wide >= sum_row * head_dim) & (lane_wide < (sum_row + 1) * head_dim)
        & (lane_wide < channels)
    )


def finish(raw, base, spread, wp, gain2, fc1, fc2, channels):
    half = lanes_of()[:, HALF:]
    is_sum = (half >= channels) & (half < channels + HEADS)
    inverse = jnp.where(is_sum, 1.0 / raw[:, HALF:], 0.0)
    high = inverse.astype(BF16)
    low = (inverse - high.astype(F32)).astype(BF16)
    heads_out = (raw * (dot(high, spread) + dot(low, spread))).astype(BF16)
    state1 = base + dot(heads_out, wp[...]).astype(BF16).astype(F32)
    normed2 = layer_norm(state1, gain2).astype(BF16)
    hidden = gelu(dot(normed2, fc1[...])).astype(BF16)
    return state1 + dot_nt(hidden, fc2[...])


def cut_kernel(image_hbm, image_ref, top, bottom, left, right, sem):
    rows, cols, _ = image_ref.shape
    fetch = pltpu.make_async_copy(image_hbm, image_ref, sem)
    fetch.start()
    fetch.wait()
    top[...] = image_ref[:SHIFT]
    bottom[...] = image_ref[rows - SHIFT :]
    for r in range(0, rows, SIDE):
        band = image_ref[r : r + SIDE].astype(F32)
        left[r : r + SIDE] = band[:, :SHIFT].astype(BF16)
        right[r : r + SIDE] = band[:, cols - SHIFT :].astype(BF16)


def own_kernel(
    image_ref, gain1_hbm, qkv_hbm, proj_hbm, table_hbm, conv_hbm,
    bias, query, kv, base, wkv, wp, wc,
    padded, strip, wq, normed, shifted,
    table_ref, gain1_ref, qkv_ref, proj_ref, conv_ref, sems,
):
    rows, cols, channels = image_ref.shape
    head_dim = channels // HEADS
    flag_lane, one_lane = channels, channels + 1
    blocks_r, blocks_c = rows // SIDE, cols // SIDE
    fetches = [
        pltpu.make_async_copy(source, target, sems.at[i])
        for i, (source, target) in enumerate(
            ((gain1_hbm, gain1_ref), (qkv_hbm, qkv_ref), (table_hbm, table_ref), (proj_hbm, proj_ref),
             (conv_hbm, conv_ref))
        )
    ]
    for fetch in fetches:
        fetch.start()

    for ref in (wq, wkv, wp, wc):
        ref[...] = jnp.zeros_like(ref)
    special = lax.broadcasted_iota(jnp.int32, (16, LANES), 0) + 176
    lanes16 = lax.broadcasted_iota(jnp.int32, (16, LANES), 1)
    wq[176:192, :] = one_hot((special == one_lane) & (lanes16 == flag_lane))
    wkv[176:192, 0:LANES] = jnp.where(
        (special == flag_lane) & (lanes16 == flag_lane), MASKED, 0.0
    ).astype(BF16)
    wkv[176:192, LANES:] = one_hot(
        (special == one_lane) & (lanes16 >= channels) & (lanes16 < channels + HEADS)
    )
    normed[...] = jnp.zeros_like(normed)
    normed[1 : 1 + rows, SHIFT : SHIFT + cols, HALF:] = jnp.broadcast_to(
        marks(channels, 0.0)[None], (rows, cols, HALF)
    )

    fetches[0].wait()
    gain1 = gain1_ref[...]
    for r in range(0, rows, SIDE):
        inner = (slice(1 + r, 1 + r + SIDE), slice(SHIFT, SHIFT + cols))
        normed[(*inner, slice(0, channels))] = layer_norm(image_ref[r : r + SIDE].astype(F32), gain1)

    for fetch in fetches[1:]:
        fetch.wait()
    wq[0:channels, 0:channels] = qkv_ref[:, 0:channels]
    wkv[0:channels, 0:channels] = qkv_ref[:, channels : 2 * channels]
    wkv[0:channels, LANES : LANES + channels] = qkv_ref[:, 2 * channels :]
    wp[0:channels, :] = proj_ref[...]
    for tap in range(9):
        wc[tap * LANES : tap * LANES + channels, :] = conv_ref[tap // 3, tap % 3]

    scale = head_dim**-0.5 * LOG2E
    for br in range(blocks_r):
        inner = (slice(1 + br * SIDE, 1 + (br + 1) * SIDE), slice(SHIFT, SHIFT + cols))
        pixels = normed[inner].astype(BF16).reshape(-1, LANES)
        q = (dot(pixels, wq[...]) * scale).reshape(SIDE, cols, LANES)
        both = dot(pixels, wkv[...]).reshape(SIDE, cols, 2 * LANES)
        for bc in range(blocks_c):
            part = slice(bc * SIDE, (bc + 1) * SIDE)
            query[br, bc] = q[:, part].reshape(AREA, LANES).astype(BF16)
            kv[br, bc] = both[:, part].reshape(AREA, 2 * LANES).astype(BF16)
    expand_bias(table_ref, padded, strip, bias)

    for tap in range(3):
        c0 = SHIFT - 1 + tap
        for r in range(0, rows + 2, SIDE):
            stop = min(r + SIDE, rows + 2)
            shifted[tap, r:stop] = normed[r:stop, c0 : c0 + cols].astype(BF16)
    for br in range(blocks_r):
        r = br * SIDE
        taps = [
            shifted[tap % 3, r + tap // 3 : r + tap // 3 + SIDE].reshape(-1, LANES) for tap in range(9)
        ]
        summed = dot(jnp.concatenate(taps, axis=1), wc[...]).reshape(SIDE, cols, channels)
        summed = summed + image_ref[r : r + SIDE].astype(F32)
        for bc in range(blocks_c):
            base[br, bc] = summed[:, bc * SIDE : (bc + 1) * SIDE].reshape(AREA, channels)


def edge_kernel(
    top_ref, bottom_ref, left_ref, right_ref, gain1_ref, gain2_ref, fc1_ref, fc2_ref,
    bias, query, kv, base, wkv, wp, wc,
    kv_edge, fixes, out_edge, out_mid,
    bands_r, bands_c,
):
    cols, channels = top_ref.shape[1:]
    rows = left_ref.shape[0]
    head_dim = channels // HEADS
    row, last_row = lax.axis_index("row"), lax.axis_size("row") - 1
    col, last_col = lax.axis_index("col"), lax.axis_size("col") - 1
    gain1 = gain1_ref[...]
    outside = [(row == 0).astype(F32), (row == last_row).astype(F32),
               (col == 0).astype(F32), (col == last_col).astype(F32)]

    bands_r[...] = jnp.zeros_like(bands_r)
    bands_c[...] = jnp.zeros_like(bands_c)
    for i, ref in enumerate((top_ref, bottom_ref, left_ref, right_ref)):
        mark = jnp.broadcast_to(marks(channels, outside[i])[None], (*ref.shape[:2], HALF))
        values = layer_norm(ref[...].astype(F32), gain1 * (1.0 - outside[i]))
        if i < 2:
            bands_r[i, :, SHIFT : SHIFT + cols, HALF:] = mark
            bands_r[i, :, SHIFT : SHIFT + cols, 0:channels] = values
            pixels = bands_r[i, :, SHIFT : SHIFT + cols]
            count = cols // SIDE
            blocks = [pixels[:, b * SIDE : (b + 1) * SIDE].reshape(AREA, LANES) for b in range(count)]
        else:
            bands_c[i - 2, 1 : 1 + rows, :, HALF:] = mark
            bands_c[i - 2, 1 : 1 + rows, :, 0:channels] = values
            count = rows // SIDE
            pixels = bands_c[i - 2, 1 : 1 + rows]
            blocks = [pixels.reshape(-1, LANES)]
        both = dot(jnp.concatenate(blocks, axis=0).astype(BF16), wkv[...]).astype(BF16)
        kv_edge[i] = both.reshape(count, AREA, 2 * LANES)

    keys = [
        [kv_edge[0, 1], kv[0, 1], kv_edge[0, 2], kv[0, 2]],
        [kv[3, 1], kv_edge[1, 1], kv[3, 2], kv_edge[1, 2]],
        [kv_edge[2, 1], kv_edge[2, 2], kv[1, 0], kv[2, 0]],
        [kv[1, 3], kv[2, 3], kv_edge[3, 1], kv_edge[3, 2]],
    ]
    places = [((0, 1), (0, 2)), ((3, 1), (3, 2)), ((1, 0), (2, 0)), ((1, 3), (2, 3))]
    quadrants = [((1, 0), (1, 1)), ((0, 0), (0, 1)), ((0, 1), (1, 1)), ((0, 0), (1, 0))]
    middle = jnp.concatenate([kv[at] for at in ((1, 1), (2, 1), (1, 2), (2, 2))], axis=0)
    units = [
        ([query[1, 1], query[1, 2]], [(0, 0), (0, 1)], middle),
        ([query[2, 1], query[2, 2]], [(1, 0), (1, 1)], middle),
    ]
    units += [
        ([query[at] for at in places[i]], quadrants[i], jnp.concatenate(keys[i], axis=0))
        for i in range(4)
    ]
    gain2, spread = gain2_ref[...], spread_matrix(channels)
    mixed_mid, mixed = [], []
    for i, result in enumerate(attention(units, bias, head_dim, channels)):
        (mixed_mid if i < 2 else mixed).append(result)
        if i == 2:
            mid_base = [base[at] for at in ((1, 1), (1, 2), (2, 1), (2, 2))]
            out_mid[...] = finish(
                jnp.concatenate(mixed_mid, axis=0), jnp.concatenate(mid_base, axis=0), spread, wp, gain2,
                fc1_ref, fc2_ref, channels,
            )

    for i, (taps, source) in enumerate((((0, 1, 2), SHIFT - 1), ((6, 7, 8), 0))):
        pieces = [bands_r[i, source, SHIFT - 1 + t : SHIFT - 1 + t + cols] for t in range(3)]
        weights = jnp.concatenate([wc[t * LANES : (t + 1) * LANES] for t in taps], axis=0)
        fixes[i] = dot(jnp.concatenate(pieces, axis=1).astype(BF16), weights)
    for i, (taps, source) in enumerate((((0, 3, 6), SHIFT - 1), ((2, 5, 8), 0))):
        pieces = [bands_c[i, t : t + rows, source] for t in range(3)]
        weights = jnp.concatenate([wc[t * LANES : (t + 1) * LANES] for t in taps], axis=0)
        fixes[2 + i] = dot(jnp.concatenate(pieces, axis=1).astype(BF16), weights)

    for group in range(2):
        raw = jnp.concatenate([mixed[2 * group], mixed[2 * group + 1]], axis=0)
        parts = [
            corrected(base, fixes, at, channels)
            for at in (*places[2 * group], *places[2 * group + 1])
        ]
        out_edge[group] = finish(
            raw, jnp.concatenate(parts, axis=0), spread, wp, gain2, fc1_ref, fc2_ref, channels
        )


def corrected(base, fixes, at, channels):
    br, bc = at
    block = base[at].reshape(SIDE, SIDE, channels)
    y = lax.broadcasted_iota(jnp.int32, (SIDE, SIDE, 1), 0)
    x = lax.broadcasted_iota(jnp.int32, (SIDE, SIDE, 1), 1)
    if br in (0, 3):
        fix = fixes[0 if br == 0 else 1, bc * SIDE : (bc + 1) * SIDE]
        block = block + jnp.where(y == (0 if br == 0 else SIDE - 1), fix[None], 0.0)
    if bc in (0, 3):
        fix = fixes[2 if bc == 0 else 3, br * SIDE : (br + 1) * SIDE]
        block = block + jnp.where(x == (0 if bc == 0 else SIDE - 1), fix[:, None], 0.0)
    return block.reshape(AREA, channels)


def corner_kernel(
    left_ref, right_ref, gain1_ref, gain2_ref, fc1_ref, fc2_ref,
    bias, query, kv, base, wkv, wp, wc, kv_edge, fixes, out_mid, out_edge,
    out_ref,
    normed,
):
    channels = left_ref.shape[2]
    head_dim = channels // HEADS
    row, last_row = lax.axis_index("row"), lax.axis_size("row") - 1
    col, last_col = lax.axis_index("col"), lax.axis_size("col") - 1
    gain1 = gain1_ref[...]
    out_row = [(row == 0).astype(F32), (row == last_row).astype(F32)]
    out_col = [(col == 0).astype(F32), (col == last_col).astype(F32)]
    for i in range(4):
        ref = (left_ref, right_ref)[i % 2]
        inside = (1.0 - out_row[i // 2]) * (1.0 - out_col[i % 2])
        mark = marks(channels, out_row[i // 2] + out_col[i % 2])
        normed[i, :, HALF:] = jnp.broadcast_to(mark, (AREA, HALF))
        values = ref[i // 2 * SIDE : (i // 2 + 1) * SIDE].astype(F32)
        normed[i, :, 0:channels] = layer_norm(values.reshape(AREA, channels), gain1 * inside)
    corner = dot(normed[...].reshape(-1, LANES).astype(BF16), wkv[...]).astype(BF16)
    corner = [corner[i * AREA : (i + 1) * AREA] for i in range(4)]
    keys = [
        [corner[0], kv_edge[2, 0], kv_edge[0, 0], kv[0, 0]],
        [kv_edge[0, 3], kv[0, 3], corner[1], kv_edge[3, 0]],
        [kv_edge[2, 3], corner[2], kv[3, 0], kv_edge[1, 0]],
        [kv[3, 3], kv_edge[1, 3], kv_edge[3, 3], corner[3]],
    ]
    places = [(0, 0), (0, 3), (3, 0), (3, 3)]
    quadrants = [(1, 1), (1, 0), (0, 1), (0, 0)]
    units = [
        ([query[places[i]]], [quadrants[i]], jnp.concatenate(keys[i], axis=0)) for i in range(4)
    ]
    mixed = list(attention(units, bias, head_dim, channels))

    parts = []
    for i, (tap, y, x) in enumerate(((0, 7, 7), (2, 7, 0), (6, 0, 7), (8, 0, 0))):
        start = y * SIDE
        term = dot(normed[i, start : start + SIDE].astype(BF16), wc[tap * LANES : (tap + 1) * LANES])
        term = term[x : x + 1]
        pixel = lax.broadcasted_iota(jnp.int32, (AREA, 1), 0)
        at = (SIDE - 1 - y) * SIDE + SIDE - 1 - x
        block = corrected(base, fixes, places[i], channels)
        parts.append(block + jnp.where(pixel == at, term, 0.0))
    out_corner = finish(
        jnp.concatenate(mixed, axis=0), jnp.concatenate(parts, axis=0), spread_matrix(channels), wp,
        gain2_ref[...], fc1_ref, fc2_ref, channels,
    )

    def piece(source, i):
        return source[i * AREA : (i + 1) * AREA].reshape(SIDE, SIDE, channels)

    bands = [
        [piece(out_corner, 0), piece(out_edge.at[0], 0), piece(out_edge.at[0], 1), piece(out_corner, 1)],
        [piece(out_edge.at[1], 0), piece(out_mid, 0), piece(out_mid, 1), piece(out_edge.at[1], 2)],
        [piece(out_edge.at[1], 1), piece(out_mid, 2), piece(out_mid, 3), piece(out_edge.at[1], 3)],
        [piece(out_corner, 2), piece(out_edge.at[0], 2), piece(out_edge.at[0], 3), piece(out_corner, 3)],
    ]
    for br, band in enumerate(bands):
        out_ref[br * SIDE : (br + 1) * SIDE] = jnp.concatenate(band, axis=1).astype(BF16)


def exchange(low, high, axis):
    count = lax.axis_size(axis)
    before = lax.ppermute(high, axis, [(i, (i + 1) % count) for i in range(count)])
    after = lax.ppermute(low, axis, [((i + 1) % count, i) for i in range(count)])
    return before, after


def call(kernel, name, outs, scratch, flops, operands, in_hbm=()):
    vmem = pl.BlockSpec(memory_space=pltpu.VMEM)
    hbm = pl.BlockSpec(memory_space=pltpu.HBM)
    return pl.pallas_call(
        kernel,
        out_shape=[out if isinstance(out, jax.ShapeDtypeStruct) else pltpu.VMEM(*out) for out in outs],
        in_specs=[hbm if i in in_hbm else vmem for i in range(len(operands))],
        out_specs=[vmem] * len(outs),
        scratch_shapes=[pltpu.VMEM(*s) if isinstance(s, tuple) else s for s in scratch],
        cost_estimate=pl.CostEstimate(flops=flops, bytes_accessed=4_000_000, transcendentals=1_000_000),
        compiler_params=pltpu.CompilerParams(vmem_limit_bytes=24 * 1024 * 1024),
        name=name,
    )(*[pltpu.with_memory_space_constraint(x, pltpu.HBM) if i in in_hbm else x for i, x in enumerate(operands)])


def on_device(
    image, norm1_gain, norm2_gain, qkv_weight, proj_weight, rel_table, conv_weight, fc1_weight,
    fc2_weight,
):
    rows, cols, channels = image.shape
    blocks_r, blocks_c = rows // SIDE, cols // SIDE
    gain1, gain2, fc2, table = norm1_gain[None], norm2_gain[None], fc2_weight.T, rel_table.T
    band, column = ((SHIFT, cols, channels), BF16), ((rows, SHIFT, channels), BF16)
    tile, first_rows, last_rows, first_cols, last_cols = call(
        cut_kernel,
        "cut_halo",
        [(image.shape, BF16), band, band, column, column],
        [pltpu.SemaphoreType.DMA(())],
        1_000_000,
        (image,),
        (0,),
    )
    top, bottom = exchange(first_rows, last_rows, "row")
    left, right = exchange(first_cols, last_cols, "col")
    fetched = (table, gain1, qkv_weight, proj_weight, conv_weight)
    bias, query, kv, base, wkv, wp, wc = call(
        own_kernel,
        "own_tile",
        [
            ((HEADS, 2, 2, AREA, WIN * WIN), F32),
            ((blocks_r, blocks_c, AREA, LANES), BF16),
            ((blocks_r, blocks_c, AREA, 2 * LANES), BF16),
            ((blocks_r, blocks_c, AREA, channels), F32),
            ((LANES, 2 * LANES), BF16),
            ((LANES, channels), BF16),
            ((9 * LANES, channels), BF16),
        ],
        [
            ((8, 1024), F32),
            ((4, 8 * WIN, 128), F32),
            ((LANES, LANES), BF16),
            ((rows + 2, cols + 2 * SHIFT, LANES), F32),
            ((3, rows + 2, cols, LANES), BF16),
            *[(x.shape, x.dtype) for x in fetched],
            pltpu.SemaphoreType.DMA((len(fetched),)),
        ],
        2_000_000_000,
        (tile, gain1, qkv_weight, proj_weight, table, conv_weight),
        range(1, 6),
    )
    first = jnp.concatenate([top[:, :SHIFT], bottom[:, :SHIFT]])
    last = jnp.concatenate([top[:, cols - SHIFT :], bottom[:, cols - SHIFT :]])
    left_corner, right_corner = exchange(first, last, "col")
    kv_edge, fixes, out_edge, out_mid = call(
        edge_kernel,
        "edge_windows",
        [
            ((4, blocks_c, AREA, 2 * LANES), BF16),
            ((4, cols, channels), F32),
            ((2, 4 * AREA, channels), F32),
            ((4 * AREA, channels), F32),
        ],
        [((2, SHIFT, cols + 2 * SHIFT, LANES), F32), ((2, rows + 2, SHIFT, LANES), F32)],
        2_000_000_000,
        (top, bottom, left, right, gain1, gain2, fc1_weight, fc2, bias, query, kv, base, wkv, wp, wc),
    )
    (out,) = call(
        corner_kernel,
        "corner_windows",
        [jax.ShapeDtypeStruct(image.shape, BF16)],
        [((4, AREA, LANES), F32)],
        1_000_000_000,
        (left_corner, right_corner, gain1, gain2, fc1_weight, fc2, bias, query, kv, base, wkv, wp, wc,
         kv_edge, fixes, out_mid, out_edge),
    )
    return out


def solution(mesh):
    placed = (P("row", "col", None), P(), P(), P(), P(), P(), P(), P(), P())
    return jax.shard_map(
        on_device, mesh=mesh, in_specs=placed, out_specs=P("row", "col", None), check_vma=False
    )
```

```python
import math

import jax
import jax.numpy as jnp
from jax import lax
from jax.experimental import pallas as pl
from jax.experimental.pallas import tpu as pltpu
from jax.sharding import PartitionSpec as P

HEADS = 6
WIN = 16
SHIFT = 8
SIDE = 8
AREA = SIDE * SIDE
LANES = 256
HALF = LANES // 2
F32 = jnp.float32
BF16 = jnp.bfloat16
LOG2E = math.log2(math.e)
MASKED = -4.0e9


def layer_norm(values, norm_gain):
    centre = jnp.mean(values, axis=-1, keepdims=True)
    values = values - centre
    spread = jnp.mean(values * values, axis=-1, keepdims=True)
    return values * lax.rsqrt(spread + 1e-05) * norm_gain


def dot(a, b):
    return jnp.dot(a, b, preferred_element_type=F32)


def dot_nt(a, b):
    return lax.dot_general(a, b, (((1,), (1,)), ((), ())), preferred_element_type=F32)


def one_hot(condition):
    return jnp.where(condition, 1.0, 0.0).astype(BF16)


def gelu(x):
    size = jnp.abs(x)
    t = 1.0 / (1.0 + (0.3275911 * math.sqrt(0.5)) * size)
    poly = 0.5 * 1.061405429
    for factor in (-1.453152027, 1.421413741, -0.284496736, 0.254829592):
        poly = poly * t + 0.5 * factor
    tail = poly * t * jnp.exp2(size * size * (-0.5 * LOG2E))
    return jnp.maximum(x, 0.0) - size * tail


def lanes_of(width=LANES):
    return lax.broadcasted_iota(jnp.int32, (1, width), 1)


def marks(channels, outside):
    half = lanes_of()[:, HALF:]
    return jnp.where(half == channels + 1, 1.0, 0.0) + jnp.where(half == channels, outside, 0.0)


def expand_bias(table_ref, padded, strip, bias):
    span = 2 * WIN - 1
    padded[...] = jnp.zeros_like(padded)
    padded[0:HEADS, 0 : span * span] = table_ref[...] * LOG2E
    table = padded[...]
    width = padded.shape[1]
    shifted = jnp.concatenate(
        [table if px == 0 else pltpu.roll(table, width - px, 1) for px in range(WIN)], axis=0
    )
    high = shifted.astype(BF16)
    low = (shifted - high.astype(F32)).astype(BF16)
    entry = lax.broadcasted_iota(jnp.int32, (width, 512), 0)
    place = lax.broadcasted_iota(jnp.int32, (1, 512), 1)
    column = lax.div(place, 256) * SIDE + lax.rem(place, SIDE)
    wanted = (span - 1 - lax.div(lax.rem(place, 256), SIDE)) * span + WIN - 1 - column
    picked = dot(jnp.concatenate([high, low], axis=0), one_hot(entry == wanted))
    half = 8 * WIN
    picked = picked[:half] + picked[half:]
    for tile in range(4):
        strip[tile] = picked[:, 128 * tile : 128 * (tile + 1)]
    for head in range(HEADS):
        for half in range(2):
            rows = jnp.concatenate(
                [strip[2 * half + t, pl.ds(head, WIN, stride=8), :] for t in range(2)], axis=1
            )
            for py in range(WIN):
                start = (WIN - 1 - py) * SIDE
                rolled = (rows if start == 0 else pltpu.roll(rows, 256 - start, 1))[:, 0:128]
                lanes = slice(128 * half, 128 * (half + 1))
                place = slice(py % SIDE * SIDE, (py % SIDE + 1) * SIDE)
                bias[head, py // SIDE, 0, place, lanes] = rolled[:SIDE]
                bias[head, py // SIDE, 1, place, lanes] = rolled[SIDE:]


def scores_of(blocks, keys, head_dim, channels):
    lane = lanes_of()
    part = jnp.concatenate(blocks, axis=0)
    own = [(lane >= h * head_dim) & (lane < (h + 1) * head_dim) for h in range(HEADS)]
    stacked = jnp.concatenate(
        [part * one_hot(own[h] | (lane == channels)) for h in range(HEADS)], axis=0
    )
    return dot_nt(stacked, keys)


def mix(scores, part_bias, values, head_dim, channels):
    lane = lanes_of()
    count = scores.shape[0] // HEADS
    scores = scores.reshape(HEADS, count, WIN * WIN) + part_bias
    scores = scores - jnp.max(scores, axis=-1, keepdims=True)
    weights = jnp.exp2(scores)
    total = jnp.sum(weights, axis=-1, keepdims=True)
    mixed = dot(weights.astype(BF16).reshape(HEADS * count, WIN * WIN), values)
    result, divisor = mixed[0:count], jnp.broadcast_to(total[0], (count, LANES))
    for h in range(1, HEADS):
        mine = (lane >= h * head_dim) & (lane < (h + 1) * head_dim)
        result = jnp.where(mine, mixed[h * count : (h + 1) * count], result)
        divisor = jnp.where(mine, total[h], divisor)
    return (result / divisor).astype(BF16)


def attention(units, bias, head_dim, channels):
    def scores_at(unit):
        return scores_of(unit[0], unit[2][:, :LANES], head_dim, channels)

    ahead = scores_at(units[0])
    for i, unit in enumerate(units):
        scores, ahead = ahead, scores_at(units[i + 1]) if i + 1 < len(units) else None
        part_bias = jnp.concatenate([bias[:, hy, hx] for hy, hx in unit[1]], axis=1)
        yield mix(scores, part_bias, unit[2][:, LANES:], head_dim, channels)


def finish(heads_out, base, wp, gain2, fc1, fc2, channels):
    state1 = base + dot(heads_out, wp[...]).astype(BF16).astype(F32)
    normed2 = layer_norm(state1, gain2).astype(BF16)
    hidden = gelu(dot(normed2, fc1[...])).astype(BF16)
    return state1 + dot_nt(hidden, fc2[...])


def cut_kernel(image_hbm, image_ref, top, bottom, left, right, sem):
    rows, cols, _ = image_ref.shape
    fetch = pltpu.make_async_copy(image_hbm, image_ref, sem)
    fetch.start()
    fetch.wait()
    top[...] = image_ref[:SHIFT]
    bottom[...] = image_ref[rows - SHIFT :]
    for r in range(0, rows, SIDE):
        band = image_ref[r : r + SIDE].astype(F32)
        left[r : r + SIDE] = band[:, :SHIFT].astype(BF16)
        right[r : r + SIDE] = band[:, cols - SHIFT :].astype(BF16)


def own_kernel(
    image_ref, gain1_hbm, qkv_hbm, proj_hbm, table_hbm, conv_hbm,
    bias, query, kv, base, wkv, wp, wc,
    padded, strip, wq, normed, shifted,
    table_ref, gain1_ref, qkv_ref, proj_ref, conv_ref, sems,
):
    rows, cols, channels = image_ref.shape
    head_dim = channels // HEADS
    flag_lane, one_lane = channels, channels + 1
    blocks_r, blocks_c = rows // SIDE, cols // SIDE
    fetches = [
        pltpu.make_async_copy(source, target, sems.at[i])
        for i, (source, target) in enumerate(
            ((gain1_hbm, gain1_ref), (qkv_hbm, qkv_ref), (table_hbm, table_ref), (proj_hbm, proj_ref),
             (conv_hbm, conv_ref))
        )
    ]
    for fetch in fetches:
        fetch.start()

    for ref in (wq, wkv, wp, wc):
        ref[...] = jnp.zeros_like(ref)
    special = lax.broadcasted_iota(jnp.int32, (16, LANES), 0) + 176
    lanes16 = lax.broadcasted_iota(jnp.int32, (16, LANES), 1)
    wq[176:192, :] = one_hot((special == one_lane) & (lanes16 == flag_lane))
    wkv[176:192, 0:LANES] = jnp.where(
        (special == flag_lane) & (lanes16 == flag_lane), MASKED, 0.0
    ).astype(BF16)
    normed[...] = jnp.zeros_like(normed)
    normed[1 : 1 + rows, SHIFT : SHIFT + cols, HALF:] = jnp.broadcast_to(
        marks(channels, 0.0)[None], (rows, cols, HALF)
    )

    fetches[0].wait()
    gain1 = gain1_ref[...]
    for r in range(0, rows, SIDE):
        inner = (slice(1 + r, 1 + r + SIDE), slice(SHIFT, SHIFT + cols))
        normed[(*inner, slice(0, channels))] = layer_norm(image_ref[r : r + SIDE].astype(F32), gain1)

    for fetch in fetches[1:]:
        fetch.wait()
    wq[0:channels, 0:channels] = qkv_ref[:, 0:channels]
    wkv[0:channels, 0:channels] = qkv_ref[:, channels : 2 * channels]
    wkv[0:channels, LANES : LANES + channels] = qkv_ref[:, 2 * channels :]
    wp[0:channels, :] = proj_ref[...]
    for tap in range(9):
        wc[tap * LANES : tap * LANES + channels, :] = conv_ref[tap // 3, tap % 3]

    scale = head_dim**-0.5 * LOG2E
    for br in range(blocks_r):
        inner = (slice(1 + br * SIDE, 1 + (br + 1) * SIDE), slice(SHIFT, SHIFT + cols))
        pixels = normed[inner].astype(BF16).reshape(-1, LANES)
        q = (dot(pixels, wq[...]) * scale).reshape(SIDE, cols, LANES)
        both = dot(pixels, wkv[...]).reshape(SIDE, cols, 2 * LANES)
        for bc in range(blocks_c):
            part = slice(bc * SIDE, (bc + 1) * SIDE)
            query[br, bc] = q[:, part].reshape(AREA, LANES).astype(BF16)
            kv[br, bc] = both[:, part].reshape(AREA, 2 * LANES).astype(BF16)
    expand_bias(table_ref, padded, strip, bias)

    for tap in range(3):
        c0 = SHIFT - 1 + tap
        for r in range(0, rows + 2, SIDE):
            stop = min(r + SIDE, rows + 2)
            shifted[tap, r:stop] = normed[r:stop, c0 : c0 + cols].astype(BF16)
    for br in range(blocks_r):
        r = br * SIDE
        taps = [
            shifted[tap % 3, r + tap // 3 : r + tap // 3 + SIDE].reshape(-1, LANES) for tap in range(9)
        ]
        summed = dot(jnp.concatenate(taps, axis=1), wc[...]).reshape(SIDE, cols, channels)
        summed = summed + image_ref[r : r + SIDE].astype(F32)
        for bc in range(blocks_c):
            base[br, bc] = summed[:, bc * SIDE : (bc + 1) * SIDE].reshape(AREA, channels)


def edge_kernel(
    top_ref, bottom_ref, left_ref, right_ref, gain1_ref, gain2_ref, fc1_ref, fc2_ref,
    bias, query, kv, base, wkv, wp, wc,
    kv_edge, corner_base, out_edge, out_mid,
    bands_r, bands_c, fixes,
):
    cols, channels = top_ref.shape[1:]
    rows = left_ref.shape[0]
    head_dim = channels // HEADS
    row, last_row = lax.axis_index("row"), lax.axis_size("row") - 1
    col, last_col = lax.axis_index("col"), lax.axis_size("col") - 1
    gain1 = gain1_ref[...]
    outside = [(row == 0).astype(F32), (row == last_row).astype(F32),
               (col == 0).astype(F32), (col == last_col).astype(F32)]

    bands_r[...] = jnp.zeros_like(bands_r)
    bands_c[...] = jnp.zeros_like(bands_c)
    for i, ref in enumerate((top_ref, bottom_ref, left_ref, right_ref)):
        mark = jnp.broadcast_to(marks(channels, outside[i])[None], (*ref.shape[:2], HALF))
        values = layer_norm(ref[...].astype(F32), gain1 * (1.0 - outside[i]))
        if i < 2:
            bands_r[i, :, SHIFT : SHIFT + cols, HALF:] = mark
            bands_r[i, :, SHIFT : SHIFT + cols, 0:channels] = values
            pixels = bands_r[i, :, SHIFT : SHIFT + cols]
            count = cols // SIDE
            blocks = [pixels[:, b * SIDE : (b + 1) * SIDE].reshape(AREA, LANES) for b in range(count)]
        else:
            bands_c[i - 2, 1 : 1 + rows, :, HALF:] = mark
            bands_c[i - 2, 1 : 1 + rows, :, 0:channels] = values
            count = rows // SIDE
            pixels = bands_c[i - 2, 1 : 1 + rows]
            blocks = [pixels.reshape(-1, LANES)]
        both = dot(jnp.concatenate(blocks, axis=0).astype(BF16), wkv[...]).astype(BF16)
        kv_edge[i] = both.reshape(count, AREA, 2 * LANES)

    keys = [
        [kv_edge[0, 1], kv[0, 1], kv_edge[0, 2], kv[0, 2]],
        [kv[3, 1], kv_edge[1, 1], kv[3, 2], kv_edge[1, 2]],
        [kv_edge[2, 1], kv_edge[2, 2], kv[1, 0], kv[2, 0]],
        [kv[1, 3], kv[2, 3], kv_edge[3, 1], kv_edge[3, 2]],
    ]
    places = [((0, 1), (0, 2)), ((3, 1), (3, 2)), ((1, 0), (2, 0)), ((1, 3), (2, 3))]
    quadrants = [((1, 0), (1, 1)), ((0, 0), (0, 1)), ((0, 1), (1, 1)), ((0, 0), (1, 0))]
    middle = jnp.concatenate([kv[at] for at in ((1, 1), (2, 1), (1, 2), (2, 2))], axis=0)
    units = [
        ([query[1, 1], query[1, 2]], [(0, 0), (0, 1)], middle),
        ([query[2, 1], query[2, 2]], [(1, 0), (1, 1)], middle),
    ]
    units += [
        ([query[at] for at in places[i]], quadrants[i], jnp.concatenate(keys[i], axis=0))
        for i in range(4)
    ]
    gain2 = gain2_ref[...]
    mixed_mid, mixed = [], []
    for i, result in enumerate(attention(units, bias, head_dim, channels)):
        (mixed_mid if i < 2 else mixed).append(result)
        if i == 2:
            mid_base = [base[at] for at in ((1, 1), (1, 2), (2, 1), (2, 2))]
            out_mid[...] = finish(
                jnp.concatenate(mixed_mid, axis=0), jnp.concatenate(mid_base, axis=0), wp, gain2,
                fc1_ref, fc2_ref, channels,
            )

    for i, (taps, source) in enumerate((((0, 1, 2), SHIFT - 1), ((6, 7, 8), 0))):
        pieces = [bands_r[i, source, SHIFT - 1 + t : SHIFT - 1 + t + cols] for t in range(3)]
        weights = jnp.concatenate([wc[t * LANES : (t + 1) * LANES] for t in taps], axis=0)
        fixes[i] = dot(jnp.concatenate(pieces, axis=1).astype(BF16), weights)
    for i, (taps, source) in enumerate((((0, 3, 6), SHIFT - 1), ((2, 5, 8), 0))):
        pieces = [bands_c[i, t : t + rows, source] for t in range(3)]
        weights = jnp.concatenate([wc[t * LANES : (t + 1) * LANES] for t in taps], axis=0)
        fixes[2 + i] = dot(jnp.concatenate(pieces, axis=1).astype(BF16), weights)

    for i, at in enumerate(((0, 0), (0, 3), (3, 0), (3, 3))):
        corner_base[i] = corrected(base, fixes, at, channels)
    for group in range(2):
        raw = jnp.concatenate([mixed[2 * group], mixed[2 * group + 1]], axis=0)
        parts = [
            corrected(base, fixes, at, channels)
            for at in (*places[2 * group], *places[2 * group + 1])
        ]
        out_edge[group] = finish(
            raw, jnp.concatenate(parts, axis=0), wp, gain2, fc1_ref, fc2_ref, channels
        )


def corrected(base, fixes, at, channels):
    br, bc = at
    block = base[at].reshape(SIDE, SIDE, channels)
    y = lax.broadcasted_iota(jnp.int32, (SIDE, SIDE, 1), 0)
    x = lax.broadcasted_iota(jnp.int32, (SIDE, SIDE, 1), 1)
    if br in (0, 3):
        fix = fixes[0 if br == 0 else 1, bc * SIDE : (bc + 1) * SIDE]
        block = block + jnp.where(y == (0 if br == 0 else SIDE - 1), fix[None], 0.0)
    if bc in (0, 3):
        fix = fixes[2 if bc == 0 else 3, br * SIDE : (br + 1) * SIDE]
        block = block + jnp.where(x == (0 if bc == 0 else SIDE - 1), fix[:, None], 0.0)
    return block.reshape(AREA, channels)


def corner_kernel(
    left_ref, right_ref, gain1_ref, gain2_ref, fc1_ref, fc2_ref,
    bias, query, kv, wkv, wp, wc, kv_edge, corner_base, out_mid, out_edge,
    out_hbm,
    normed, out_ref, sems,
):
    rows, _, channels = out_ref.shape
    head_dim = channels // HEADS

    def finish_bands(which, corners):
        def piece(source, i):
            return source[i * AREA : (i + 1) * AREA]

        for br in which:
            if br in (0, 3):
                i = 0 if br == 0 else 2
                band = [corners[i], piece(out_edge.at[0], i), piece(out_edge.at[0], i + 1), corners[i + 1]]
            else:
                i = br - 1
                band = [piece(out_edge.at[1], i), piece(out_mid, 2 * i), piece(out_mid, 2 * i + 1),
                        piece(out_edge.at[1], i + 2)]
            band = [part.reshape(SIDE, SIDE, channels) for part in band]
            out_ref[br * SIDE : (br + 1) * SIDE] = jnp.concatenate(band, axis=1).astype(BF16)

    finish_bands((1, 2), None)
    inner = slice(SIDE, rows - SIDE)
    writes = [pltpu.make_async_copy(out_ref.at[inner], out_hbm.at[inner], sems.at[0])]
    writes[0].start()
    row, last_row = lax.axis_index("row"), lax.axis_size("row") - 1
    col, last_col = lax.axis_index("col"), lax.axis_size("col") - 1
    gain1 = gain1_ref[...]
    out_row = [(row == 0).astype(F32), (row == last_row).astype(F32)]
    out_col = [(col == 0).astype(F32), (col == last_col).astype(F32)]
    for i in range(4):
        ref = (left_ref, right_ref)[i % 2]
        inside = (1.0 - out_row[i // 2]) * (1.0 - out_col[i % 2])
        mark = marks(channels, out_row[i // 2] + out_col[i % 2])
        normed[i, :, HALF:] = jnp.broadcast_to(mark, (AREA, HALF))
        values = ref[i // 2 * SIDE : (i // 2 + 1) * SIDE].astype(F32)
        normed[i, :, 0:channels] = layer_norm(values.reshape(AREA, channels), gain1 * inside)
    corner = dot(normed[...].reshape(-1, LANES).astype(BF16), wkv[...]).astype(BF16)
    corner = [corner[i * AREA : (i + 1) * AREA] for i in range(4)]
    keys = [
        [corner[0], kv_edge[2, 0], kv_edge[0, 0], kv[0, 0]],
        [kv_edge[0, 3], kv[0, 3], corner[1], kv_edge[3, 0]],
        [kv_edge[2, 3], corner[2], kv[3, 0], kv_edge[1, 0]],
        [kv[3, 3], kv_edge[1, 3], kv_edge[3, 3], corner[3]],
    ]
    places = [(0, 0), (0, 3), (3, 0), (3, 3)]
    quadrants = [(1, 1), (1, 0), (0, 1), (0, 0)]
    units = [
        ([query[places[i]]], [quadrants[i]], jnp.concatenate(keys[i], axis=0)) for i in range(4)
    ]
    mixed = list(attention(units, bias, head_dim, channels))

    parts = []
    for i, (tap, y, x) in enumerate(((0, 7, 7), (2, 7, 0), (6, 0, 7), (8, 0, 0))):
        start = y * SIDE
        term = dot(normed[i, start : start + SIDE].astype(BF16), wc[tap * LANES : (tap + 1) * LANES])
        term = term[x : x + 1]
        pixel = lax.broadcasted_iota(jnp.int32, (AREA, 1), 0)
        at = (SIDE - 1 - y) * SIDE + SIDE - 1 - x
        parts.append(corner_base[i] + jnp.where(pixel == at, term, 0.0))
    out_corner = finish(
        jnp.concatenate(mixed, axis=0), jnp.concatenate(parts, axis=0), wp, gain2_ref[...], fc1_ref, fc2_ref, channels,
    )

    finish_bands((0, 3), [out_corner[i * AREA : (i + 1) * AREA] for i in range(4)])
    writes[0].wait()
    for r in (0, rows - SIDE):
        at = slice(r, r + SIDE)
        write = pltpu.make_async_copy(out_ref.at[at], out_hbm.at[at], sems.at[1 if r == 0 else 2])
        write.start()
        writes.append(write)
    writes[1].wait()
    writes[2].wait()


def exchange(low, high, axis):
    count = lax.axis_size(axis)
    before = lax.ppermute(high, axis, [(i, (i + 1) % count) for i in range(count)])
    after = lax.ppermute(low, axis, [((i + 1) % count, i) for i in range(count)])
    return before, after


def call(kernel, name, outs, scratch, flops, operands, in_hbm=()):
    vmem = pl.BlockSpec(memory_space=pltpu.VMEM)
    hbm = pl.BlockSpec(memory_space=pltpu.HBM)
    return pl.pallas_call(
        kernel,
        out_shape=[out if isinstance(out, jax.ShapeDtypeStruct) else pltpu.VMEM(*out) for out in outs],
        in_specs=[hbm if i in in_hbm else vmem for i in range(len(operands))],
        out_specs=[hbm if isinstance(out, jax.ShapeDtypeStruct) else vmem for out in outs],
        scratch_shapes=[pltpu.VMEM(*s) if isinstance(s, tuple) else s for s in scratch],
        cost_estimate=pl.CostEstimate(flops=flops, bytes_accessed=4_000_000, transcendentals=1_000_000),
        compiler_params=pltpu.CompilerParams(vmem_limit_bytes=24 * 1024 * 1024),
        name=name,
    )(*[pltpu.with_memory_space_constraint(x, pltpu.HBM) if i in in_hbm else x for i, x in enumerate(operands)])


def on_device(
    image, norm1_gain, norm2_gain, qkv_weight, proj_weight, rel_table, conv_weight, fc1_weight,
    fc2_weight,
):
    rows, cols, channels = image.shape
    blocks_r, blocks_c = rows // SIDE, cols // SIDE
    gain1, gain2, fc2, table = norm1_gain[None], norm2_gain[None], fc2_weight.T, rel_table.T
    band, column = ((SHIFT, cols, channels), BF16), ((rows, SHIFT, channels), BF16)
    tile, first_rows, last_rows, first_cols, last_cols = call(
        cut_kernel,
        "cut_halo",
        [(image.shape, BF16), band, band, column, column],
        [pltpu.SemaphoreType.DMA(())],
        1_000_000,
        (image,),
        (0,),
    )
    top, bottom = exchange(first_rows, last_rows, "row")
    left, right = exchange(first_cols, last_cols, "col")
    fetched = (table, gain1, qkv_weight, proj_weight, conv_weight)
    bias, query, kv, base, wkv, wp, wc = call(
        own_kernel,
        "own_tile",
        [
            ((HEADS, 2, 2, AREA, WIN * WIN), F32),
            ((blocks_r, blocks_c, AREA, LANES), BF16),
            ((blocks_r, blocks_c, AREA, 2 * LANES), BF16),
            ((blocks_r, blocks_c, AREA, channels), F32),
            ((LANES, 2 * LANES), BF16),
            ((LANES, channels), BF16),
            ((9 * LANES, channels), BF16),
        ],
        [
            ((8, 1024), F32),
            ((4, 8 * WIN, 128), F32),
            ((LANES, LANES), BF16),
            ((rows + 2, cols + 2 * SHIFT, LANES), F32),
            ((3, rows + 2, cols, LANES), BF16),
            *[(x.shape, x.dtype) for x in fetched],
            pltpu.SemaphoreType.DMA((len(fetched),)),
        ],
        2_000_000_000,
        (tile, gain1, qkv_weight, proj_weight, table, conv_weight),
        range(1, 6),
    )
    first = jnp.concatenate([top[:, :SHIFT], bottom[:, :SHIFT]])
    last = jnp.concatenate([top[:, cols - SHIFT :], bottom[:, cols - SHIFT :]])
    left_corner, right_corner = exchange(first, last, "col")
    kv_edge, corner_base, out_edge, out_mid = call(
        edge_kernel,
        "edge_windows",
        [
            ((4, blocks_c, AREA, 2 * LANES), BF16),
            ((4, AREA, channels), F32),
            ((2, 4 * AREA, channels), F32),
            ((4 * AREA, channels), F32),
        ],
        [
            ((2, SHIFT, cols + 2 * SHIFT, LANES), F32),
            ((2, rows + 2, SHIFT, LANES), F32),
            ((4, cols, channels), F32),
        ],
        2_000_000_000,
        (top, bottom, left, right, gain1, gain2, fc1_weight, fc2, bias, query, kv, base, wkv, wp, wc),
    )
    (out,) = call(
        corner_kernel,
        "corner_windows",
        [jax.ShapeDtypeStruct(image.shape, BF16)],
        [((4, AREA, LANES), F32), (image.shape, BF16), pltpu.SemaphoreType.DMA((3,))],
        1_000_000_000,
        (left_corner, right_corner, gain1, gain2, fc1_weight, fc2, bias, query, kv, wkv, wp, wc,
         kv_edge, corner_base, out_mid, out_edge),
    )
    return out


def solution(mesh):
    placed = (P("row", "col", None), P(), P(), P(), P(), P(), P(), P(), P())
    return jax.shard_map(
        on_device, mesh=mesh, in_specs=placed, out_specs=P("row", "col", None), check_vma=False
    )
```

```python
import math

import jax
import jax.numpy as jnp
from jax import lax
from jax.experimental import pallas as pl
from jax.experimental.pallas import tpu as pltpu
from jax.sharding import PartitionSpec as P

HEADS = 6
WIN = 16
SHIFT = 8
SIDE = 8
AREA = SIDE * SIDE
LANES = 256
HALF = LANES // 2
F32 = jnp.float32
BF16 = jnp.bfloat16
LOG2E = math.log2(math.e)
MASKED = -4.0e9


def layer_norm(values, norm_gain):
    centre = jnp.mean(values, axis=-1, keepdims=True)
    values = values - centre
    spread = jnp.mean(values * values, axis=-1, keepdims=True)
    return values * lax.rsqrt(spread + 1e-05) * norm_gain


def layer_norm_padded(values, norm_gain, channels):
    centre = jnp.sum(values, axis=-1, keepdims=True) * (1.0 / channels)
    values = jnp.where(lanes_of() < channels, values - centre, 0.0)
    spread = jnp.sum(values * values, axis=-1, keepdims=True) * (1.0 / channels)
    return values * lax.rsqrt(spread + 1e-05) * norm_gain


def dot(a, b):
    return jnp.dot(a, b, preferred_element_type=F32)


def dot_nt(a, b):
    return lax.dot_general(a, b, (((1,), (1,)), ((), ())), preferred_element_type=F32)


def one_hot(condition):
    return jnp.where(condition, 1.0, 0.0).astype(BF16)


def gelu(x):
    size = jnp.abs(x)
    t = 1.0 / (1.0 + (0.3275911 * math.sqrt(0.5)) * size)
    poly = 0.5 * 1.061405429
    for factor in (-1.453152027, 1.421413741, -0.284496736, 0.254829592):
        poly = poly * t + 0.5 * factor
    tail = poly * t * jnp.exp2(size * size * (-0.5 * LOG2E))
    return jnp.maximum(x, 0.0) - size * tail


def lanes_of(width=LANES):
    return lax.broadcasted_iota(jnp.int32, (1, width), 1)


def marks(channels, outside):
    half = lanes_of()[:, HALF:]
    return jnp.where(half == channels + 1, 1.0, 0.0) + jnp.where(half == channels, outside, 0.0)


def expand_bias(table_ref, padded, strip, bias):
    span = 2 * WIN - 1
    padded[...] = jnp.zeros_like(padded)
    padded[0:HEADS, 0 : span * span] = table_ref[...] * LOG2E
    table = padded[...]
    width = padded.shape[1]
    shifted = jnp.concatenate(
        [table if px == 0 else pltpu.roll(table, width - px, 1) for px in range(WIN)], axis=0
    )
    high = shifted.astype(BF16)
    low = (shifted - high.astype(F32)).astype(BF16)
    entry = lax.broadcasted_iota(jnp.int32, (width, 512), 0)
    place = lax.broadcasted_iota(jnp.int32, (1, 512), 1)
    column = lax.div(place, 256) * SIDE + lax.rem(place, SIDE)
    wanted = (span - 1 - lax.div(lax.rem(place, 256), SIDE)) * span + WIN - 1 - column
    picked = dot(jnp.concatenate([high, low], axis=0), one_hot(entry == wanted))
    half = 8 * WIN
    picked = picked[:half] + picked[half:]
    for tile in range(4):
        strip[tile] = picked[:, 128 * tile : 128 * (tile + 1)]
    for head in range(HEADS):
        for half in range(2):
            rows = jnp.concatenate(
                [strip[2 * half + t, pl.ds(head, WIN, stride=8), :] for t in range(2)], axis=1
            )
            for py in range(WIN):
                start = (WIN - 1 - py) * SIDE
                rolled = (rows if start == 0 else pltpu.roll(rows, 256 - start, 1))[:, 0:128]
                lanes = slice(128 * half, 128 * (half + 1))
                place = slice(py % SIDE * SIDE, (py % SIDE + 1) * SIDE)
                bias[head, py // SIDE, 0, place, lanes] = rolled[:SIDE]
                bias[head, py // SIDE, 1, place, lanes] = rolled[SIDE:]


def scores_of(blocks, keys, head_dim, channels):
    lane = lanes_of()
    part = jnp.concatenate(blocks, axis=0)
    own = [(lane >= h * head_dim) & (lane < (h + 1) * head_dim) for h in range(HEADS)]
    stacked = jnp.concatenate(
        [part * one_hot(own[h] | (lane == channels)) for h in range(HEADS)], axis=0
    )
    return dot_nt(stacked, keys)


def mix(scores, part_bias, values, head_dim, channels):
    lane = lanes_of()
    count = scores.shape[0] // HEADS
    scores = scores.reshape(HEADS, count, WIN * WIN) + part_bias
    scores = scores - jnp.max(scores, axis=-1, keepdims=True)
    weights = jnp.exp2(scores)
    total = jnp.sum(weights, axis=-1, keepdims=True)
    mixed = dot(weights.astype(BF16).reshape(HEADS * count, WIN * WIN), values)
    result, divisor = mixed[0:count], jnp.broadcast_to(total[0], (count, LANES))
    for h in range(1, HEADS):
        mine = (lane >= h * head_dim) & (lane < (h + 1) * head_dim)
        result = jnp.where(mine, mixed[h * count : (h + 1) * count], result)
        divisor = jnp.where(mine, total[h], divisor)
    return (result / divisor).astype(BF16)


def attention(units, bias, head_dim, channels):
    def scores_at(unit):
        return scores_of(unit[0], unit[2][:, :LANES], head_dim, channels)

    ahead = scores_at(units[0])
    for i, unit in enumerate(units):
        scores, ahead = ahead, scores_at(units[i + 1]) if i + 1 < len(units) else None
        part_bias = jnp.concatenate([bias[:, hy, hx] for hy, hx in unit[1]], axis=1)
        yield mix(scores, part_bias, unit[2][:, LANES:], head_dim, channels)


def finish(heads_out, base, wp, gain2, w1, w2, channels):
    state1 = base + dot(heads_out, wp[...]).astype(BF16).astype(F32)
    normed2 = layer_norm_padded(state1, gain2, channels).astype(BF16)
    hidden = gelu(dot(normed2, w1[...])).astype(BF16)
    return state1 + dot(hidden, w2[...])


def cut_kernel(image_hbm, image_ref, top, bottom, left, right, sem):
    rows, cols, _ = image_ref.shape
    fetch = pltpu.make_async_copy(image_hbm, image_ref, sem)
    fetch.start()
    fetch.wait()
    top[...] = image_ref[:SHIFT]
    bottom[...] = image_ref[rows - SHIFT :]
    for r in range(0, rows, SIDE):
        band = image_ref[r : r + SIDE].astype(F32)
        left[r : r + SIDE] = band[:, :SHIFT].astype(BF16)
        right[r : r + SIDE] = band[:, cols - SHIFT :].astype(BF16)


def own_kernel(
    image_ref, gain1_hbm, gain2_hbm, qkv_hbm, proj_hbm, table_hbm, conv_hbm, fc1_hbm, fc2_hbm,
    bias, query, kv, base, wkv, wp, wc, w1, w2, g2,
    padded, strip, wq, normed, shifted,
    table_ref, gain1_ref, gain2_ref, qkv_ref, proj_ref, conv_ref, fc1_ref, fc2_ref, sems,
):
    rows, cols, channels = image_ref.shape
    head_dim = channels // HEADS
    flag_lane, one_lane = channels, channels + 1
    blocks_r, blocks_c = rows // SIDE, cols // SIDE
    fetches = [
        pltpu.make_async_copy(source, target, sems.at[i])
        for i, (source, target) in enumerate(
            ((gain1_hbm, gain1_ref), (qkv_hbm, qkv_ref), (table_hbm, table_ref), (proj_hbm, proj_ref),
             (conv_hbm, conv_ref), (gain2_hbm, gain2_ref), (fc1_hbm, fc1_ref), (fc2_hbm, fc2_ref))
        )
    ]
    for fetch in fetches:
        fetch.start()

    for ref in (wq, wkv, wp, wc, w1, w2, g2):
        ref[...] = jnp.zeros_like(ref)
    special = lax.broadcasted_iota(jnp.int32, (16, LANES), 0) + 176
    lanes16 = lax.broadcasted_iota(jnp.int32, (16, LANES), 1)
    wq[176:192, :] = one_hot((special == one_lane) & (lanes16 == flag_lane))
    wkv[176:192, 0:LANES] = jnp.where(
        (special == flag_lane) & (lanes16 == flag_lane), MASKED, 0.0
    ).astype(BF16)
    normed[...] = jnp.zeros_like(normed)
    normed[1 : 1 + rows, SHIFT : SHIFT + cols, HALF:] = jnp.broadcast_to(
        marks(channels, 0.0)[None], (rows, cols, HALF)
    )

    fetches[0].wait()
    gain1 = gain1_ref[...]
    for r in range(0, rows, SIDE):
        inner = (slice(1 + r, 1 + r + SIDE), slice(SHIFT, SHIFT + cols))
        normed[(*inner, slice(0, channels))] = layer_norm(image_ref[r : r + SIDE].astype(F32), gain1)

    for fetch in fetches[1:]:
        fetch.wait()
    wq[0:channels, 0:channels] = qkv_ref[:, 0:channels]
    wkv[0:channels, 0:channels] = qkv_ref[:, channels : 2 * channels]
    wkv[0:channels, LANES : LANES + channels] = qkv_ref[:, 2 * channels :]
    wp[0:channels, 0:channels] = proj_ref[...]
    w1[0:channels, 0 : fc1_ref.shape[1]] = fc1_ref[...]
    w2[0 : fc2_ref.shape[1], 0:channels] = fc2_ref[...].astype(F32).T.astype(BF16)
    g2[:, 0:channels] = gain2_ref[...]
    for tap in range(9):
        wc[tap * LANES : tap * LANES + channels, 0:channels] = conv_ref[tap // 3, tap % 3]

    scale = head_dim**-0.5 * LOG2E
    for br in range(blocks_r):
        inner = (slice(1 + br * SIDE, 1 + (br + 1) * SIDE), slice(SHIFT, SHIFT + cols))
        pixels = normed[inner].astype(BF16).reshape(-1, LANES)
        q = (dot(pixels, wq[...]) * scale).reshape(SIDE, cols, LANES)
        both = dot(pixels, wkv[...]).reshape(SIDE, cols, 2 * LANES)
        for bc in range(blocks_c):
            part = slice(bc * SIDE, (bc + 1) * SIDE)
            query[br, bc] = q[:, part].reshape(AREA, LANES).astype(BF16)
            kv[br, bc] = both[:, part].reshape(AREA, 2 * LANES).astype(BF16)
    expand_bias(table_ref, padded, strip, bias)

    for tap in range(3):
        c0 = SHIFT - 1 + tap
        for r in range(0, rows + 2, SIDE):
            stop = min(r + SIDE, rows + 2)
            shifted[tap, r:stop] = normed[r:stop, c0 : c0 + cols].astype(BF16)
    for br in range(blocks_r):
        r = br * SIDE
        taps = [
            shifted[tap % 3, r + tap // 3 : r + tap // 3 + SIDE].reshape(-1, LANES) for tap in range(9)
        ]
        summed = dot(jnp.concatenate(taps, axis=1), wc[...])[:, :channels].reshape(SIDE, cols, channels)
        summed = summed + image_ref[r : r + SIDE].astype(F32)
        for bc in range(blocks_c):
            base[br, bc, :, HALF:] = jnp.zeros((AREA, HALF), F32)
            base[br, bc, :, 0:channels] = summed[:, bc * SIDE : (bc + 1) * SIDE].reshape(AREA, channels)


def edge_kernel(
    top_ref, bottom_ref, left_ref, right_ref, gain1_ref,
    bias, query, kv, base, wkv, wp, wc, w1, w2, g2,
    kv_edge, corner_base, out_edge, out_mid,
    bands_r, bands_c, fixes,
):
    cols, channels = top_ref.shape[1:]
    rows = left_ref.shape[0]
    head_dim = channels // HEADS
    row, last_row = lax.axis_index("row"), lax.axis_size("row") - 1
    col, last_col = lax.axis_index("col"), lax.axis_size("col") - 1
    gain1 = gain1_ref[...]
    outside = [(row == 0).astype(F32), (row == last_row).astype(F32),
               (col == 0).astype(F32), (col == last_col).astype(F32)]

    bands_r[...] = jnp.zeros_like(bands_r)
    bands_c[...] = jnp.zeros_like(bands_c)
    for i, ref in enumerate((top_ref, bottom_ref, left_ref, right_ref)):
        mark = jnp.broadcast_to(marks(channels, outside[i])[None], (*ref.shape[:2], HALF))
        values = layer_norm(ref[...].astype(F32), gain1 * (1.0 - outside[i]))
        if i < 2:
            bands_r[i, :, SHIFT : SHIFT + cols, HALF:] = mark
            bands_r[i, :, SHIFT : SHIFT + cols, 0:channels] = values
            pixels = bands_r[i, :, SHIFT : SHIFT + cols]
            count = cols // SIDE
            blocks = [pixels[:, b * SIDE : (b + 1) * SIDE].reshape(AREA, LANES) for b in range(count)]
        else:
            bands_c[i - 2, 1 : 1 + rows, :, HALF:] = mark
            bands_c[i - 2, 1 : 1 + rows, :, 0:channels] = values
            count = rows // SIDE
            pixels = bands_c[i - 2, 1 : 1 + rows]
            blocks = [pixels.reshape(-1, LANES)]
        both = dot(jnp.concatenate(blocks, axis=0).astype(BF16), wkv[...]).astype(BF16)
        kv_edge[i] = both.reshape(count, AREA, 2 * LANES)

    keys = [
        [kv_edge[0, 1], kv[0, 1], kv_edge[0, 2], kv[0, 2]],
        [kv[3, 1], kv_edge[1, 1], kv[3, 2], kv_edge[1, 2]],
        [kv_edge[2, 1], kv_edge[2, 2], kv[1, 0], kv[2, 0]],
        [kv[1, 3], kv[2, 3], kv_edge[3, 1], kv_edge[3, 2]],
    ]
    places = [((0, 1), (0, 2)), ((3, 1), (3, 2)), ((1, 0), (2, 0)), ((1, 3), (2, 3))]
    quadrants = [((1, 0), (1, 1)), ((0, 0), (0, 1)), ((0, 1), (1, 1)), ((0, 0), (1, 0))]
    middle = jnp.concatenate([kv[at] for at in ((1, 1), (2, 1), (1, 2), (2, 2))], axis=0)
    units = [
        ([query[1, 1], query[1, 2]], [(0, 0), (0, 1)], middle),
        ([query[2, 1], query[2, 2]], [(1, 0), (1, 1)], middle),
    ]
    units += [
        ([query[at] for at in places[i]], quadrants[i], jnp.concatenate(keys[i], axis=0))
        for i in range(4)
    ]
    for i, (taps, source) in enumerate((((0, 1, 2), SHIFT - 1), ((6, 7, 8), 0))):
        pieces = [bands_r[i, source, SHIFT - 1 + t : SHIFT - 1 + t + cols] for t in range(3)]
        weights = jnp.concatenate([wc[t * LANES : (t + 1) * LANES] for t in taps], axis=0)
        fixes[i] = dot(jnp.concatenate(pieces, axis=1).astype(BF16), weights)
    for i, (taps, source) in enumerate((((0, 3, 6), SHIFT - 1), ((2, 5, 8), 0))):
        pieces = [bands_c[i, t : t + rows, source] for t in range(3)]
        weights = jnp.concatenate([wc[t * LANES : (t + 1) * LANES] for t in taps], axis=0)
        fixes[2 + i] = dot(jnp.concatenate(pieces, axis=1).astype(BF16), weights)

    gain2, done = g2[...], []
    for i, result in enumerate(attention(units, bias, head_dim, channels)):
        done.append(result)
        if i % 2 == 0:
            continue
        if i == 1:
            parts = [base[at] for at in ((1, 1), (1, 2), (2, 1), (2, 2))]
        else:
            parts = [corrected(base, fixes, at) for at in (*places[i - 3], *places[i - 2])]
        out = finish(
            jnp.concatenate(done[-2:], axis=0), jnp.concatenate(parts, axis=0), wp, gain2, w1, w2, channels
        )
        if i == 1:
            out_mid[...] = out
        else:
            out_edge[i // 2 - 1] = out
    for i, at in enumerate(((0, 0), (0, 3), (3, 0), (3, 3))):
        corner_base[i] = corrected(base, fixes, at)


def corrected(base, fixes, at):
    br, bc = at
    block = base[at].reshape(SIDE, SIDE, LANES)
    y = lax.broadcasted_iota(jnp.int32, (SIDE, SIDE, 1), 0)
    x = lax.broadcasted_iota(jnp.int32, (SIDE, SIDE, 1), 1)
    if br in (0, 3):
        fix = fixes[0 if br == 0 else 1, bc * SIDE : (bc + 1) * SIDE]
        block = block + jnp.where(y == (0 if br == 0 else SIDE - 1), fix[None], 0.0)
    if bc in (0, 3):
        fix = fixes[2 if bc == 0 else 3, br * SIDE : (br + 1) * SIDE]
        block = block + jnp.where(x == (0 if bc == 0 else SIDE - 1), fix[:, None], 0.0)
    return block.reshape(AREA, LANES)


def corner_kernel(
    left_ref, right_ref, gain1_ref,
    bias, query, kv, wkv, wp, wc, w1, w2, g2, kv_edge, corner_base, out_mid, out_edge,
    out_hbm,
    normed, out_ref, sems,
):
    rows, _, channels = out_ref.shape
    head_dim = channels // HEADS

    def finish_bands(which, corners):
        def piece(source, i):
            return source[i * AREA : (i + 1) * AREA]

        for br in which:
            if br in (0, 3):
                i = 0 if br == 0 else 2
                band = [corners[0], piece(out_edge.at[0], i), piece(out_edge.at[0], i + 1), corners[1]]
            else:
                i = br - 1
                band = [piece(out_edge.at[1], i), piece(out_mid, 2 * i), piece(out_mid, 2 * i + 1),
                        piece(out_edge.at[1], i + 2)]
            band = [part[:, :channels].reshape(SIDE, SIDE, channels) for part in band]
            out_ref[br * SIDE : (br + 1) * SIDE] = jnp.concatenate(band, axis=1).astype(BF16)

    finish_bands((1, 2), None)
    inner = slice(SIDE, rows - SIDE)
    writes = [pltpu.make_async_copy(out_ref.at[inner], out_hbm.at[inner], sems.at[0])]
    writes[0].start()
    row, last_row = lax.axis_index("row"), lax.axis_size("row") - 1
    col, last_col = lax.axis_index("col"), lax.axis_size("col") - 1
    gain1 = gain1_ref[...]
    out_row = [(row == 0).astype(F32), (row == last_row).astype(F32)]
    out_col = [(col == 0).astype(F32), (col == last_col).astype(F32)]
    for i in range(4):
        ref = (left_ref, right_ref)[i % 2]
        inside = (1.0 - out_row[i // 2]) * (1.0 - out_col[i % 2])
        mark = marks(channels, out_row[i // 2] + out_col[i % 2])
        normed[i, :, HALF:] = jnp.broadcast_to(mark, (AREA, HALF))
        values = ref[i // 2 * SIDE : (i // 2 + 1) * SIDE].astype(F32)
        normed[i, :, 0:channels] = layer_norm(values.reshape(AREA, channels), gain1 * inside)
    corner = dot(normed[...].reshape(-1, LANES).astype(BF16), wkv[...]).astype(BF16)
    corner = [corner[i * AREA : (i + 1) * AREA] for i in range(4)]
    keys = [
        [corner[0], kv_edge[2, 0], kv_edge[0, 0], kv[0, 0]],
        [kv_edge[0, 3], kv[0, 3], corner[1], kv_edge[3, 0]],
        [kv_edge[2, 3], corner[2], kv[3, 0], kv_edge[1, 0]],
        [kv[3, 3], kv_edge[1, 3], kv_edge[3, 3], corner[3]],
    ]
    places = [(0, 0), (0, 3), (3, 0), (3, 3)]
    quadrants = [(1, 1), (1, 0), (0, 1), (0, 0)]
    units = [
        ([query[places[i]]], [quadrants[i]], jnp.concatenate(keys[i], axis=0)) for i in range(4)
    ]
    parts = []
    for i, (tap, y, x) in enumerate(((0, 7, 7), (2, 7, 0), (6, 0, 7), (8, 0, 0))):
        start = y * SIDE
        term = dot(normed[i, start : start + SIDE].astype(BF16), wc[tap * LANES : (tap + 1) * LANES])
        term = term[x : x + 1]
        pixel = lax.broadcasted_iota(jnp.int32, (AREA, 1), 0)
        at = (SIDE - 1 - y) * SIDE + SIDE - 1 - x
        parts.append(corner_base[i] + jnp.where(pixel == at, term, 0.0))
    done = []
    for i, result in enumerate(attention(units, bias, head_dim, channels)):
        done.append(result)
        if i % 2 == 0:
            continue
        out = finish(
            jnp.concatenate(done[-2:], axis=0), jnp.concatenate(parts[i - 1 : i + 1], axis=0), wp, g2[...],
            w1, w2, channels,
        )
        finish_bands((0,) if i == 1 else (3,), [out[:AREA], out[AREA:]])
    writes[0].wait()
    for r in (0, rows - SIDE):
        at = slice(r, r + SIDE)
        write = pltpu.make_async_copy(out_ref.at[at], out_hbm.at[at], sems.at[1 if r == 0 else 2])
        write.start()
        writes.append(write)
    writes[1].wait()
    writes[2].wait()


def exchange(low, high, axis):
    count = lax.axis_size(axis)
    before = lax.ppermute(high, axis, [(i, (i + 1) % count) for i in range(count)])
    after = lax.ppermute(low, axis, [((i + 1) % count, i) for i in range(count)])
    return before, after


def call(kernel, name, outs, scratch, flops, operands, in_hbm=()):
    vmem = pl.BlockSpec(memory_space=pltpu.VMEM)
    hbm = pl.BlockSpec(memory_space=pltpu.HBM)
    return pl.pallas_call(
        kernel,
        out_shape=[out if isinstance(out, jax.ShapeDtypeStruct) else pltpu.VMEM(*out) for out in outs],
        in_specs=[hbm if i in in_hbm else vmem for i in range(len(operands))],
        out_specs=[hbm if isinstance(out, jax.ShapeDtypeStruct) else vmem for out in outs],
        scratch_shapes=[pltpu.VMEM(*s) if isinstance(s, tuple) else s for s in scratch],
        cost_estimate=pl.CostEstimate(flops=flops, bytes_accessed=4_000_000, transcendentals=1_000_000),
        compiler_params=pltpu.CompilerParams(vmem_limit_bytes=24 * 1024 * 1024),
        name=name,
    )(*[pltpu.with_memory_space_constraint(x, pltpu.HBM) if i in in_hbm else x for i, x in enumerate(operands)])


def on_device(
    image, norm1_gain, norm2_gain, qkv_weight, proj_weight, rel_table, conv_weight, fc1_weight,
    fc2_weight,
):
    rows, cols, channels = image.shape
    blocks_r, blocks_c = rows // SIDE, cols // SIDE
    gain1, gain2, fc2, table = norm1_gain[None], norm2_gain[None], fc2_weight.T, rel_table.T
    band, column = ((SHIFT, cols, channels), BF16), ((rows, SHIFT, channels), BF16)
    tile, first_rows, last_rows, first_cols, last_cols = call(
        cut_kernel,
        "cut_halo",
        [(image.shape, BF16), band, band, column, column],
        [pltpu.SemaphoreType.DMA(())],
        1_000_000,
        (image,),
        (0,),
    )
    top, bottom = exchange(first_rows, last_rows, "row")
    left, right = exchange(first_cols, last_cols, "col")
    fetched = (table, gain1, gain2, qkv_weight, proj_weight, conv_weight, fc1_weight, fc2)
    hidden = -(-fc1_weight.shape[1] // 128) * 128
    bias, query, kv, base, wkv, wp, wc, w1, w2, g2 = call(
        own_kernel,
        "own_tile",
        [
            ((HEADS, 2, 2, AREA, WIN * WIN), F32),
            ((blocks_r, blocks_c, AREA, LANES), BF16),
            ((blocks_r, blocks_c, AREA, 2 * LANES), BF16),
            ((blocks_r, blocks_c, AREA, LANES), F32),
            ((LANES, 2 * LANES), BF16),
            ((LANES, LANES), BF16),
            ((9 * LANES, LANES), BF16),
            ((LANES, hidden), BF16),
            ((hidden, LANES), BF16),
            ((1, LANES), F32),
        ],
        [
            ((8, 1024), F32),
            ((4, 8 * WIN, 128), F32),
            ((LANES, LANES), BF16),
            ((rows + 2, cols + 2 * SHIFT, LANES), F32),
            ((3, rows + 2, cols, LANES), BF16),
            *[(x.shape, x.dtype) for x in fetched],
            pltpu.SemaphoreType.DMA((len(fetched),)),
        ],
        2_000_000_000,
        (tile, gain1, gain2, qkv_weight, proj_weight, table, conv_weight, fc1_weight, fc2),
        range(1, 9),
    )
    first = jnp.concatenate([top[:, :SHIFT], bottom[:, :SHIFT]])
    last = jnp.concatenate([top[:, cols - SHIFT :], bottom[:, cols - SHIFT :]])
    left_corner, right_corner = exchange(first, last, "col")
    kv_edge, corner_base, out_edge, out_mid = call(
        edge_kernel,
        "edge_windows",
        [
            ((4, blocks_c, AREA, 2 * LANES), BF16),
            ((4, AREA, LANES), F32),
            ((2, 4 * AREA, LANES), F32),
            ((4 * AREA, LANES), F32),
        ],
        [
            ((2, SHIFT, cols + 2 * SHIFT, LANES), F32),
            ((2, rows + 2, SHIFT, LANES), F32),
            ((4, cols, LANES), F32),
        ],
        2_000_000_000,
        (top, bottom, left, right, gain1, bias, query, kv, base, wkv, wp, wc, w1, w2, g2),
    )
    (out,) = call(
        corner_kernel,
        "corner_windows",
        [jax.ShapeDtypeStruct(image.shape, BF16)],
        [((4, AREA, LANES), F32), (image.shape, BF16), pltpu.SemaphoreType.DMA((3,))],
        1_000_000_000,
        (left_corner, right_corner, gain1, bias, query, kv, wkv, wp, wc, w1, w2, g2,
         kv_edge, corner_base, out_mid, out_edge),
    )
    return out


def solution(mesh):
    placed = (P("row", "col", None), P(), P(), P(), P(), P(), P(), P(), P())
    return jax.shard_map(
        on_device, mesh=mesh, in_specs=placed, out_specs=P("row", "col", None), check_vma=False
    )
```

```python
import math

import jax
import jax.numpy as jnp
from jax import lax
from jax.experimental import pallas as pl
from jax.experimental.pallas import tpu as pltpu
from jax.sharding import PartitionSpec as P

HEADS = 6
WIN = 16
SHIFT = 8
SIDE = 8
AREA = SIDE * SIDE
LANES = 256
HALF = LANES // 2
F32 = jnp.float32
BF16 = jnp.bfloat16
LOG2E = math.log2(math.e)
MASKED = -4.0e9


def weave(tasks, width):
    waiting, active = list(tasks), []
    while waiting or active:
        while waiting and len(active) < width:
            active.append(waiting.pop(0))
        for task in list(active):
            try:
                next(task)
            except StopIteration:
                active.remove(task)


def layer_norm(values, norm_gain):
    centre = jnp.mean(values, axis=-1, keepdims=True)
    values = values - centre
    spread = jnp.mean(values * values, axis=-1, keepdims=True)
    return values * lax.rsqrt(spread + 1e-05) * norm_gain


def layer_norm_padded(values, norm_gain, channels):
    centre = jnp.sum(values, axis=-1, keepdims=True) * (1.0 / channels)
    values = jnp.where(lanes_of() < channels, values - centre, 0.0)
    spread = jnp.sum(values * values, axis=-1, keepdims=True) * (1.0 / channels)
    return values * lax.rsqrt(spread + 1e-05) * norm_gain


def dot(a, b):
    return jnp.dot(a, b, preferred_element_type=F32)


def dot_nt(a, b):
    return lax.dot_general(a, b, (((1,), (1,)), ((), ())), preferred_element_type=F32)


def one_hot(condition):
    return jnp.where(condition, 1.0, 0.0).astype(BF16)


def gelu(x):
    size = jnp.abs(x)
    t = 1.0 / (1.0 + (0.3275911 * math.sqrt(0.5)) * size)
    poly = 0.5 * 1.061405429
    for factor in (-1.453152027, 1.421413741, -0.284496736, 0.254829592):
        poly = poly * t + 0.5 * factor
    tail = poly * t * jnp.exp2(size * size * (-0.5 * LOG2E))
    return jnp.maximum(x, 0.0) - size * tail


def lanes_of(width=LANES):
    return lax.broadcasted_iota(jnp.int32, (1, width), 1)


def marks(channels, outside):
    half = lanes_of()[:, HALF:]
    return jnp.where(half == channels + 1, 1.0, 0.0) + jnp.where(half == channels, outside, 0.0)


def expand_bias(table_ref, padded, strip, bias):
    span = 2 * WIN - 1
    padded[...] = jnp.zeros_like(padded)
    padded[0:HEADS, 0 : span * span] = table_ref[...] * LOG2E
    table = padded[...]
    width = padded.shape[1]
    shifted = jnp.concatenate(
        [table if px == 0 else pltpu.roll(table, width - px, 1) for px in range(WIN)], axis=0
    )
    high = shifted.astype(BF16)
    low = (shifted - high.astype(F32)).astype(BF16)
    yield
    entry = lax.broadcasted_iota(jnp.int32, (width, 512), 0)
    place = lax.broadcasted_iota(jnp.int32, (1, 512), 1)
    column = lax.div(place, 256) * SIDE + lax.rem(place, SIDE)
    wanted = (span - 1 - lax.div(lax.rem(place, 256), SIDE)) * span + WIN - 1 - column
    picked = dot(jnp.concatenate([high, low], axis=0), one_hot(entry == wanted))
    yield
    half = 8 * WIN
    picked = picked[:half] + picked[half:]
    for tile in range(4):
        strip[tile] = picked[:, 128 * tile : 128 * (tile + 1)]
    for head in range(HEADS):
        yield
        for half in range(2):
            rows = jnp.concatenate(
                [strip[2 * half + t, pl.ds(head, WIN, stride=8), :] for t in range(2)], axis=1
            )
            for py in range(WIN):
                start = (WIN - 1 - py) * SIDE
                rolled = (rows if start == 0 else pltpu.roll(rows, 256 - start, 1))[:, 0:128]
                lanes = slice(128 * half, 128 * (half + 1))
                place = slice(py % SIDE * SIDE, (py % SIDE + 1) * SIDE)
                bias[head, py // SIDE, 0, place, lanes] = rolled[:SIDE]
                bias[head, py // SIDE, 1, place, lanes] = rolled[SIDE:]


def scores_of(blocks, keys, head_dim, channels):
    lane = lanes_of()
    part = jnp.concatenate(blocks, axis=0)
    own = [(lane >= h * head_dim) & (lane < (h + 1) * head_dim) for h in range(HEADS)]
    stacked = jnp.concatenate(
        [part * one_hot(own[h] | (lane == channels)) for h in range(HEADS)], axis=0
    )
    return dot_nt(stacked, keys)


def attend(unit, bias, head_dim, channels, put):
    lane = lanes_of()
    blocks, quadrants, pair = unit
    pair = pair()
    scores = scores_of(blocks, pair[:, :LANES], head_dim, channels)
    count = scores.shape[0] // HEADS
    yield
    part_bias = jnp.concatenate([bias[:, hy, hx] for hy, hx in quadrants], axis=1)
    scores = scores.reshape(HEADS, count, WIN * WIN) + part_bias
    scores = scores - jnp.max(scores, axis=-1, keepdims=True)
    weights = jnp.exp2(scores)
    total = jnp.sum(weights, axis=-1, keepdims=True)
    weights = weights.astype(BF16).reshape(HEADS * count, WIN * WIN)
    yield
    mixed = dot(weights, pair[:, LANES:])
    yield
    result, divisor = mixed[0:count], jnp.broadcast_to(total[0], (count, LANES))
    for h in range(1, HEADS):
        mine = (lane >= h * head_dim) & (lane < (h + 1) * head_dim)
        result = jnp.where(mine, mixed[h * count : (h + 1) * count], result)
        divisor = jnp.where(mine, total[h], divisor)
    put((result / divisor).astype(BF16))


def finish(heads_out, base, wp, gain2, w1, w2, channels, put):
    attended = dot(heads_out, wp[...])
    yield
    state1 = base() + attended.astype(BF16).astype(F32)
    normed2 = layer_norm_padded(state1, gain2, channels).astype(BF16)
    yield
    hidden = dot(normed2, w1[...])
    yield
    hidden = gelu(hidden).astype(BF16)
    yield
    put(state1 + dot(hidden, w2[...]))


def after(ready, make):
    while not ready():
        yield
    yield from make()


def cut_kernel(image_hbm, image_ref, top, bottom, left, right, sem):
    rows, cols, _ = image_ref.shape
    fetch = pltpu.make_async_copy(image_hbm, image_ref, sem)
    fetch.start()
    fetch.wait()
    top[...] = image_ref[:SHIFT]
    bottom[...] = image_ref[rows - SHIFT :]
    for r in range(0, rows, SIDE):
        band = image_ref[r : r + SIDE].astype(F32)
        left[r : r + SIDE] = band[:, :SHIFT].astype(BF16)
        right[r : r + SIDE] = band[:, cols - SHIFT :].astype(BF16)


def own_kernel(
    image_ref, gain1_hbm, gain2_hbm, qkv_hbm, proj_hbm, table_hbm, conv_hbm, fc1_hbm, fc2_hbm,
    bias, query, kv, base, wkv, wp, wc, w1, w2, g2,
    padded, strip, wq, normed, shifted,
    table_ref, gain1_ref, gain2_ref, qkv_ref, proj_ref, conv_ref, fc1_ref, fc2_ref, sems,
):
    rows, cols, channels = image_ref.shape
    head_dim = channels // HEADS
    flag_lane, one_lane = channels, channels + 1
    blocks_r, blocks_c = rows // SIDE, cols // SIDE
    fetches = [
        pltpu.make_async_copy(source, target, sems.at[i])
        for i, (source, target) in enumerate(
            ((gain1_hbm, gain1_ref), (qkv_hbm, qkv_ref), (table_hbm, table_ref), (proj_hbm, proj_ref),
             (conv_hbm, conv_ref), (gain2_hbm, gain2_ref), (fc1_hbm, fc1_ref), (fc2_hbm, fc2_ref))
        )
    ]
    for fetch in fetches:
        fetch.start()

    for ref in (wq, wkv, wp, wc, w1, w2, g2):
        ref[...] = jnp.zeros_like(ref)
    special = lax.broadcasted_iota(jnp.int32, (16, LANES), 0) + 176
    lanes16 = lax.broadcasted_iota(jnp.int32, (16, LANES), 1)
    wq[176:192, :] = one_hot((special == one_lane) & (lanes16 == flag_lane))
    wkv[176:192, 0:LANES] = jnp.where(
        (special == flag_lane) & (lanes16 == flag_lane), MASKED, 0.0
    ).astype(BF16)
    normed[...] = jnp.zeros_like(normed)
    normed[1 : 1 + rows, SHIFT : SHIFT + cols, HALF:] = jnp.broadcast_to(
        marks(channels, 0.0)[None], (rows, cols, HALF)
    )

    fetches[0].wait()
    gain1 = gain1_ref[...]
    scale = head_dim**-0.5 * LOG2E

    def weights():
        for fetch in fetches[1:]:
            fetch.wait()
        wq[0:channels, 0:channels] = qkv_ref[:, 0:channels]
        wkv[0:channels, 0:channels] = qkv_ref[:, channels : 2 * channels]
        wkv[0:channels, LANES : LANES + channels] = qkv_ref[:, 2 * channels :]
        wp[0:channels, 0:channels] = proj_ref[...]
        w1[0:channels, 0 : fc1_ref.shape[1]] = fc1_ref[...]
        w2[0 : fc2_ref.shape[1], 0:channels] = fc2_ref[...].astype(F32).T.astype(BF16)
        g2[:, 0:channels] = gain2_ref[...]
        for tap in range(9):
            wc[tap * LANES : tap * LANES + channels, 0:channels] = conv_ref[tap // 3, tap % 3]

    def norm(br):
        r = br * SIDE
        inner = (slice(1 + r, 1 + r + SIDE), slice(SHIFT, SHIFT + cols))
        normed[(*inner, slice(0, channels))] = layer_norm(image_ref[r : r + SIDE].astype(F32), gain1)

    def project(br):
        inner = (slice(1 + br * SIDE, 1 + (br + 1) * SIDE), slice(SHIFT, SHIFT + cols))
        pixels = normed[inner].astype(BF16).reshape(-1, LANES)
        q = dot(pixels, wq[...])
        yield
        both = dot(pixels, wkv[...]).reshape(SIDE, cols, 2 * LANES)
        q = (q * scale).reshape(SIDE, cols, LANES)
        for bc in range(blocks_c):
            part = slice(bc * SIDE, (bc + 1) * SIDE)
            query[br, bc] = q[:, part].reshape(AREA, LANES).astype(BF16)
        yield
        for bc in range(blocks_c):
            part = slice(bc * SIDE, (bc + 1) * SIDE)
            kv[br, bc] = both[:, part].reshape(AREA, 2 * LANES).astype(BF16)

    def convolve(br):
        r = br * SIDE
        for tap in range(3):
            c0 = SHIFT - 1 + tap
            start = 0 if br == 0 else r + 2
            shifted[tap, start : r + SIDE + 2] = normed[start : r + SIDE + 2, c0 : c0 + cols].astype(BF16)
        yield
        taps = [
            shifted[tap % 3, r + tap // 3 : r + tap // 3 + SIDE].reshape(-1, LANES) for tap in range(9)
        ]
        summed = dot(jnp.concatenate(taps, axis=1), wc[...])
        yield
        summed = summed[:, :channels].reshape(SIDE, cols, channels)
        summed = summed + image_ref[r : r + SIDE].astype(F32)
        for bc in range(blocks_c):
            base[br, bc, :, HALF:] = jnp.zeros((AREA, HALF), F32)
            base[br, bc, :, 0:channels] = summed[:, bc * SIDE : (bc + 1) * SIDE].reshape(AREA, channels)

    for br in range(blocks_r):
        norm(br)
    weights()
    tasks = [expand_bias(table_ref, padded, strip, bias)]
    for br in range(blocks_r):
        tasks += [project(br), convolve(br)]
    weave(tasks, 3)


def edge_kernel(
    top_ref, bottom_ref, left_ref, right_ref, gain1_ref,
    bias, query, kv, base, wkv, wp, wc, w1, w2, g2,
    kv_edge, corner_base, out_edge, out_mid,
    bands_r, bands_c, fixes,
):
    cols, channels = top_ref.shape[1:]
    rows = left_ref.shape[0]
    head_dim = channels // HEADS
    row, last_row = lax.axis_index("row"), lax.axis_size("row") - 1
    col, last_col = lax.axis_index("col"), lax.axis_size("col") - 1
    gain1 = gain1_ref[...]
    outside = [(row == 0).astype(F32), (row == last_row).astype(F32),
               (col == 0).astype(F32), (col == last_col).astype(F32)]

    bands_r[...] = jnp.zeros_like(bands_r)
    bands_c[...] = jnp.zeros_like(bands_c)
    sides = []

    def band(i):
        ref = (top_ref, bottom_ref, left_ref, right_ref)[i]
        mark = jnp.broadcast_to(marks(channels, outside[i])[None], (*ref.shape[:2], HALF))
        values = layer_norm(ref[...].astype(F32), gain1 * (1.0 - outside[i]))
        if i < 2:
            bands_r[i, :, SHIFT : SHIFT + cols, HALF:] = mark
            bands_r[i, :, SHIFT : SHIFT + cols, 0:channels] = values
            pixels = bands_r[i, :, SHIFT : SHIFT + cols]
            count = cols // SIDE
            blocks = [pixels[:, b * SIDE : (b + 1) * SIDE].reshape(AREA, LANES) for b in range(count)]
        else:
            bands_c[i - 2, 1 : 1 + rows, :, HALF:] = mark
            bands_c[i - 2, 1 : 1 + rows, :, 0:channels] = values
            count = rows // SIDE
            blocks = [bands_c[i - 2, 1 : 1 + rows].reshape(-1, LANES)]
        pixels = jnp.concatenate(blocks, axis=0).astype(BF16)
        yield
        both = dot(pixels, wkv[...])
        yield
        kv_edge[i] = both.astype(BF16).reshape(count, AREA, 2 * LANES)
        sides.append(i)

    keys = [
        lambda: [kv_edge[0, 1], kv[0, 1], kv_edge[0, 2], kv[0, 2]],
        lambda: [kv[3, 1], kv_edge[1, 1], kv[3, 2], kv_edge[1, 2]],
        lambda: [kv_edge[2, 1], kv_edge[2, 2], kv[1, 0], kv[2, 0]],
        lambda: [kv[1, 3], kv[2, 3], kv_edge[3, 1], kv_edge[3, 2]],
        lambda: [kv[1, 1], kv[2, 1], kv[1, 2], kv[2, 2]],
    ]
    places = [((0, 1), (0, 2)), ((3, 1), (3, 2)), ((1, 0), (2, 0)), ((1, 3), (2, 3))]
    places += [((1, 1), (1, 2)), ((2, 1), (2, 2))]
    quadrants = [((1, 0), (1, 1)), ((0, 0), (0, 1)), ((0, 1), (1, 1)), ((0, 0), (1, 0))]
    quadrants += [((0, 0), (0, 1)), ((1, 0), (1, 1))]
    done = {}

    def unit(i):
        def put(result):
            done[i] = result

        window = keys[min(i, 4)]
        parts = ([query[at] for at in places[i]], quadrants[i], lambda: jnp.concatenate(window(), axis=0))
        make = lambda: attend(parts, bias, head_dim, channels, put)
        return after(lambda: i >= 4 or i in sides, make)

    def tail(i):
        def put(out):
            if i == 4:
                out_mid[...] = out
            else:
                out_edge[i // 2] = out

        def part(at):
            return base[at] if i == 4 else corrected(base, fixes, at)

        def make():
            return finish(
                jnp.concatenate([done[i], done[i + 1]], axis=0),
                lambda: jnp.concatenate([part(at) for at in (*places[i], *places[i + 1])], axis=0),
                wp, g2[...], w1, w2, channels, put,
            )

        return after(lambda: i in done and i + 1 in done, make)

    def fix(i):
        taps = ((0, 1, 2), (6, 7, 8), (0, 3, 6), (2, 5, 8))[i]
        source = (SHIFT - 1, 0)[i % 2]
        if i < 2:
            pieces = [bands_r[i, source, SHIFT - 1 + t : SHIFT - 1 + t + cols] for t in range(3)]
        else:
            pieces = [bands_c[i - 2, t : t + rows, source] for t in range(3)]
        weights = jnp.concatenate([wc[t * LANES : (t + 1) * LANES] for t in taps], axis=0)
        fixes[i] = dot(jnp.concatenate(pieces, axis=1).astype(BF16), weights)
        yield

    def corners():
        for i, at in enumerate(((0, 0), (0, 3), (3, 0), (3, 3))):
            corner_base[i] = corrected(base, fixes, at)
            yield

    weave(
        [unit(4), band(0), band(1), unit(5), band(2), band(3), unit(0), fix(0), unit(1), fix(1), tail(4),
         unit(2), fix(2), unit(3), fix(3), tail(0), corners(), tail(2)],
        3,
    )


def corrected(base, fixes, at):
    br, bc = at
    block = base[at].reshape(SIDE, SIDE, LANES)
    y = lax.broadcasted_iota(jnp.int32, (SIDE, SIDE, 1), 0)
    x = lax.broadcasted_iota(jnp.int32, (SIDE, SIDE, 1), 1)
    if br in (0, 3):
        fix = fixes[0 if br == 0 else 1, bc * SIDE : (bc + 1) * SIDE]
        block = block + jnp.where(y == (0 if br == 0 else SIDE - 1), fix[None], 0.0)
    if bc in (0, 3):
        fix = fixes[2 if bc == 0 else 3, br * SIDE : (br + 1) * SIDE]
        block = block + jnp.where(x == (0 if bc == 0 else SIDE - 1), fix[:, None], 0.0)
    return block.reshape(AREA, LANES)


def corner_kernel(
    left_ref, right_ref, gain1_ref,
    bias, query, kv, wkv, wp, wc, w1, w2, g2, kv_edge, corner_base, out_mid, out_edge,
    out_hbm,
    normed, out_ref, sems,
):
    rows, _, channels = out_ref.shape
    head_dim = channels // HEADS

    def finish_bands(which, corners):
        def piece(source, i):
            return source[i * AREA : (i + 1) * AREA]

        for br in which:
            if br in (0, 3):
                i = 0 if br == 0 else 2
                band = [corners[0], piece(out_edge.at[0], i), piece(out_edge.at[0], i + 1), corners[1]]
            else:
                i = br - 1
                band = [piece(out_edge.at[1], i), piece(out_mid, 2 * i), piece(out_mid, 2 * i + 1),
                        piece(out_edge.at[1], i + 2)]
            band = [part[:, :channels].reshape(SIDE, SIDE, channels) for part in band]
            out_ref[br * SIDE : (br + 1) * SIDE] = jnp.concatenate(band, axis=1).astype(BF16)

    finish_bands((1, 2), None)
    inner = slice(SIDE, rows - SIDE)
    writes = [pltpu.make_async_copy(out_ref.at[inner], out_hbm.at[inner], sems.at[0])]
    writes[0].start()
    row, last_row = lax.axis_index("row"), lax.axis_size("row") - 1
    col, last_col = lax.axis_index("col"), lax.axis_size("col") - 1
    gain1 = gain1_ref[...]
    out_row = [(row == 0).astype(F32), (row == last_row).astype(F32)]
    out_col = [(col == 0).astype(F32), (col == last_col).astype(F32)]
    corner, done = {}, {}

    def project(pair):
        for i in (2 * pair, 2 * pair + 1):
            ref = (left_ref, right_ref)[i % 2]
            inside = (1.0 - out_row[i // 2]) * (1.0 - out_col[i % 2])
            mark = marks(channels, out_row[i // 2] + out_col[i % 2])
            normed[i, :, HALF:] = jnp.broadcast_to(mark, (AREA, HALF))
            values = ref[i // 2 * SIDE : (i // 2 + 1) * SIDE].astype(F32)
            normed[i, :, 0:channels] = layer_norm(values.reshape(AREA, channels), gain1 * inside)
        yield
        both = dot(normed[2 * pair : 2 * pair + 2].reshape(-1, LANES).astype(BF16), wkv[...])
        yield
        both = both.astype(BF16)
        corner[2 * pair], corner[2 * pair + 1] = both[:AREA], both[AREA:]

    keys = [
        lambda: [corner[0], kv_edge[2, 0], kv_edge[0, 0], kv[0, 0]],
        lambda: [kv_edge[0, 3], kv[0, 3], corner[1], kv_edge[3, 0]],
        lambda: [kv_edge[2, 3], corner[2], kv[3, 0], kv_edge[1, 0]],
        lambda: [kv[3, 3], kv_edge[1, 3], kv_edge[3, 3], corner[3]],
    ]
    places = [(0, 0), (0, 3), (3, 0), (3, 3)]
    quadrants = [(1, 1), (1, 0), (0, 1), (0, 0)]

    def unit(i):
        def put(result):
            done[i] = result

        parts = ([query[places[i]]], [quadrants[i]], lambda: jnp.concatenate(keys[i](), axis=0))
        return after(lambda: i in corner, lambda: attend(parts, bias, head_dim, channels, put))

    def whole(i):
        tap, y, x = ((0, 7, 7), (2, 7, 0), (6, 0, 7), (8, 0, 0))[i]
        start = y * SIDE
        term = dot(normed[i, start : start + SIDE].astype(BF16), wc[tap * LANES : (tap + 1) * LANES])
        term = term[x : x + 1]
        pixel = lax.broadcasted_iota(jnp.int32, (AREA, 1), 0)
        at = (SIDE - 1 - y) * SIDE + SIDE - 1 - x
        return corner_base[i] + jnp.where(pixel == at, term, 0.0)

    def tail(i):
        def put(out):
            finish_bands((0,) if i == 0 else (3,), [out[:AREA], out[AREA:]])

        def make():
            return finish(
                jnp.concatenate([done[i], done[i + 1]], axis=0),
                lambda: jnp.concatenate([whole(i), whole(i + 1)], axis=0),
                wp, g2[...], w1, w2, channels, put,
            )

        return after(lambda: i in done and i + 1 in done, make)

    weave([project(0), project(1), unit(0), unit(1), unit(2), unit(3), tail(0), tail(2)], 4)
    writes[0].wait()
    for r in (0, rows - SIDE):
        at = slice(r, r + SIDE)
        write = pltpu.make_async_copy(out_ref.at[at], out_hbm.at[at], sems.at[1 if r == 0 else 2])
        write.start()
        writes.append(write)
    writes[1].wait()
    writes[2].wait()


def exchange(low, high, axis):
    count = lax.axis_size(axis)
    before = lax.ppermute(high, axis, [(i, (i + 1) % count) for i in range(count)])
    after = lax.ppermute(low, axis, [((i + 1) % count, i) for i in range(count)])
    return before, after


def call(kernel, name, outs, scratch, flops, operands, in_hbm=()):
    vmem = pl.BlockSpec(memory_space=pltpu.VMEM)
    hbm = pl.BlockSpec(memory_space=pltpu.HBM)
    return pl.pallas_call(
        kernel,
        out_shape=[out if isinstance(out, jax.ShapeDtypeStruct) else pltpu.VMEM(*out) for out in outs],
        in_specs=[hbm if i in in_hbm else vmem for i in range(len(operands))],
        out_specs=[hbm if isinstance(out, jax.ShapeDtypeStruct) else vmem for out in outs],
        scratch_shapes=[pltpu.VMEM(*s) if isinstance(s, tuple) else s for s in scratch],
        cost_estimate=pl.CostEstimate(flops=flops, bytes_accessed=4_000_000, transcendentals=1_000_000),
        compiler_params=pltpu.CompilerParams(vmem_limit_bytes=24 * 1024 * 1024),
        name=name,
    )(*[pltpu.with_memory_space_constraint(x, pltpu.HBM) if i in in_hbm else x for i, x in enumerate(operands)])


def on_device(
    image, norm1_gain, norm2_gain, qkv_weight, proj_weight, rel_table, conv_weight, fc1_weight,
    fc2_weight,
):
    rows, cols, channels = image.shape
    blocks_r, blocks_c = rows // SIDE, cols // SIDE
    gain1, gain2, fc2, table = norm1_gain[None], norm2_gain[None], fc2_weight.T, rel_table.T
    band, column = ((SHIFT, cols, channels), BF16), ((rows, SHIFT, channels), BF16)
    tile, first_rows, last_rows, first_cols, last_cols = call(
        cut_kernel,
        "cut_halo",
        [(image.shape, BF16), band, band, column, column],
        [pltpu.SemaphoreType.DMA(())],
        1_000_000,
        (image,),
        (0,),
    )
    top, bottom = exchange(first_rows, last_rows, "row")
    left, right = exchange(first_cols, last_cols, "col")
    fetched = (table, gain1, gain2, qkv_weight, proj_weight, conv_weight, fc1_weight, fc2)
    hidden = -(-fc1_weight.shape[1] // 128) * 128
    bias, query, kv, base, wkv, wp, wc, w1, w2, g2 = call(
        own_kernel,
        "own_tile",
        [
            ((HEADS, 2, 2, AREA, WIN * WIN), F32),
            ((blocks_r, blocks_c, AREA, LANES), BF16),
            ((blocks_r, blocks_c, AREA, 2 * LANES), BF16),
            ((blocks_r, blocks_c, AREA, LANES), F32),
            ((LANES, 2 * LANES), BF16),
            ((LANES, LANES), BF16),
            ((9 * LANES, LANES), BF16),
            ((LANES, hidden), BF16),
            ((hidden, LANES), BF16),
            ((1, LANES), F32),
        ],
        [
            ((8, 1024), F32),
            ((4, 8 * WIN, 128), F32),
            ((LANES, LANES), BF16),
            ((rows + 2, cols + 2 * SHIFT, LANES), F32),
            ((3, rows + 2, cols, LANES), BF16),
            *[(x.shape, x.dtype) for x in fetched],
            pltpu.SemaphoreType.DMA((len(fetched),)),
        ],
        2_000_000_000,
        (tile, gain1, gain2, qkv_weight, proj_weight, table, conv_weight, fc1_weight, fc2),
        range(1, 9),
    )
    first = jnp.concatenate([top[:, :SHIFT], bottom[:, :SHIFT]])
    last = jnp.concatenate([top[:, cols - SHIFT :], bottom[:, cols - SHIFT :]])
    left_corner, right_corner = exchange(first, last, "col")
    kv_edge, corner_base, out_edge, out_mid = call(
        edge_kernel,
        "edge_windows",
        [
            ((4, blocks_c, AREA, 2 * LANES), BF16),
            ((4, AREA, LANES), F32),
            ((2, 4 * AREA, LANES), F32),
            ((4 * AREA, LANES), F32),
        ],
        [
            ((2, SHIFT, cols + 2 * SHIFT, LANES), F32),
            ((2, rows + 2, SHIFT, LANES), F32),
            ((4, cols, LANES), F32),
        ],
        2_000_000_000,
        (top, bottom, left, right, gain1, bias, query, kv, base, wkv, wp, wc, w1, w2, g2),
    )
    (out,) = call(
        corner_kernel,
        "corner_windows",
        [jax.ShapeDtypeStruct(image.shape, BF16)],
        [((4, AREA, LANES), F32), (image.shape, BF16), pltpu.SemaphoreType.DMA((3,))],
        1_000_000_000,
        (left_corner, right_corner, gain1, bias, query, kv, wkv, wp, wc, w1, w2, g2,
         kv_edge, corner_base, out_mid, out_edge),
    )
    return out


def solution(mesh):
    placed = (P("row", "col", None), P(), P(), P(), P(), P(), P(), P(), P())
    return jax.shard_map(
        on_device, mesh=mesh, in_specs=placed, out_specs=P("row", "col", None), check_vma=False
    )
```

```python
import math

import jax
import jax.numpy as jnp
from jax import lax
from jax.experimental import pallas as pl
from jax.experimental.pallas import tpu as pltpu
from jax.sharding import PartitionSpec as P

HEADS = 6
WIN = 16
SHIFT = 8
SIDE = 8
AREA = SIDE * SIDE
LANES = 256
HALF = LANES // 2
F32 = jnp.float32
BF16 = jnp.bfloat16
LOG2E = math.log2(math.e)
MASKED = -4.0e9


def weave(tasks, width):
    waiting, active = list(tasks), []
    while waiting or active:
        while waiting and len(active) < width:
            active.append(waiting.pop(0))
        for task in list(active):
            try:
                next(task)
            except StopIteration:
                active.remove(task)


def layer_norm(values, norm_gain):
    centre = jnp.mean(values, axis=-1, keepdims=True)
    values = values - centre
    spread = jnp.mean(values * values, axis=-1, keepdims=True)
    return values * lax.rsqrt(spread + 1e-05) * norm_gain


def layer_norm_padded(values, norm_gain, channels):
    centre = jnp.sum(values, axis=-1, keepdims=True) * (1.0 / channels)
    values = jnp.where(lanes_of() < channels, values - centre, 0.0)
    spread = jnp.sum(values * values, axis=-1, keepdims=True) * (1.0 / channels)
    return values * lax.rsqrt(spread + 1e-05) * norm_gain


def dot(a, b):
    return jnp.dot(a, b, preferred_element_type=F32)


def dot_nt(a, b):
    return lax.dot_general(a, b, (((1,), (1,)), ((), ())), preferred_element_type=F32)


def one_hot(condition):
    return jnp.where(condition, 1.0, 0.0).astype(BF16)


def gelu(x):
    square = jnp.minimum(x * x, 25.0)
    poly = -5.58203231240273e-08
    for factor in (2.777085437695777e-06, -4.707012890217347e-05, -5.859274357446709e-05,
                   0.036366718434813275, 0.7978721905787034):
        poly = poly * square + factor
    half = 0.5 * x
    return half + half * jnp.tanh(x * poly)


def lanes_of(width=LANES):
    return lax.broadcasted_iota(jnp.int32, (1, width), 1)


def marks(channels, outside):
    half = lanes_of()[:, HALF:]
    return jnp.where(half == channels + 1, 1.0, 0.0) + jnp.where(half == channels, outside, 0.0)


def expand_bias(table_ref, padded, strip, bias):
    span = 2 * WIN - 1
    padded[...] = jnp.zeros_like(padded)
    padded[0:HEADS, 0 : span * span] = table_ref[...] * LOG2E
    table = padded[...]
    width = padded.shape[1]
    shifted = jnp.concatenate(
        [table if px == 0 else pltpu.roll(table, width - px, 1) for px in range(WIN)], axis=0
    )
    high = shifted.astype(BF16)
    low = (shifted - high.astype(F32)).astype(BF16)
    yield
    entry = lax.broadcasted_iota(jnp.int32, (width, 512), 0)
    place = lax.broadcasted_iota(jnp.int32, (1, 512), 1)
    column = lax.div(place, 256) * SIDE + lax.rem(place, SIDE)
    wanted = (span - 1 - lax.div(lax.rem(place, 256), SIDE)) * span + WIN - 1 - column
    picked = dot(jnp.concatenate([high, low], axis=0), one_hot(entry == wanted))
    yield
    half = 8 * WIN
    picked = picked[:half] + picked[half:]
    for tile in range(4):
        strip[tile] = picked[:, 128 * tile : 128 * (tile + 1)]
    for head in range(HEADS):
        yield
        for half in range(2):
            rows = jnp.concatenate(
                [strip[2 * half + t, pl.ds(head, WIN, stride=8), :] for t in range(2)], axis=1
            )
            for py in range(WIN):
                start = (WIN - 1 - py) * SIDE
                rolled = (rows if start == 0 else pltpu.roll(rows, 256 - start, 1))[:, 0:128]
                lanes = slice(128 * half, 128 * (half + 1))
                place = slice(py % SIDE * SIDE, (py % SIDE + 1) * SIDE)
                bias[head, py // SIDE, 0, place, lanes] = rolled[:SIDE]
                bias[head, py // SIDE, 1, place, lanes] = rolled[SIDE:]


def scores_of(blocks, keys, head_dim, channels):
    lane = lanes_of()
    part = jnp.concatenate(blocks, axis=0)
    own = [(lane >= h * head_dim) & (lane < (h + 1) * head_dim) for h in range(HEADS)]
    stacked = jnp.concatenate(
        [part * one_hot(own[h] | (lane == channels)) for h in range(HEADS)], axis=0
    )
    return dot_nt(stacked, keys)


def attend(unit, bias, head_dim, channels, put):
    lane = lanes_of()
    blocks, quadrants, pair = unit
    pair = pair()
    scores = scores_of(blocks, pair[:, :LANES], head_dim, channels)
    count = scores.shape[0] // HEADS
    yield
    part_bias = jnp.concatenate([bias[:, hy, hx] for hy, hx in quadrants], axis=1)
    scores = scores.reshape(HEADS, count, WIN * WIN) + part_bias
    scores = scores - jnp.max(scores, axis=-1, keepdims=True)
    weights = jnp.exp2(scores)
    total = jnp.sum(weights, axis=-1, keepdims=True)
    weights = weights.astype(BF16).reshape(HEADS * count, WIN * WIN)
    yield
    mixed = dot(weights, pair[:, LANES:])
    yield
    result, divisor = mixed[0:count], jnp.broadcast_to(total[0], (count, LANES))
    for h in range(1, HEADS):
        mine = (lane >= h * head_dim) & (lane < (h + 1) * head_dim)
        result = jnp.where(mine, mixed[h * count : (h + 1) * count], result)
        divisor = jnp.where(mine, total[h], divisor)
    put((result / divisor).astype(BF16))


def finish(heads_out, base, wp, gain2, w1, w2, channels, put):
    attended = dot(heads_out, wp[...])
    yield
    state1 = base() + attended.astype(BF16).astype(F32)
    normed2 = layer_norm_padded(state1, gain2, channels).astype(BF16)
    yield
    hidden = dot(normed2, w1[...])
    yield
    hidden = gelu(hidden).astype(BF16)
    yield
    put(state1 + dot(hidden, w2[...]))


def after(ready, make):
    while not ready():
        yield
    yield from make()


def cut_kernel(image_hbm, image_ref, top, bottom, left, right, sem):
    rows, cols, _ = image_ref.shape
    fetch = pltpu.make_async_copy(image_hbm, image_ref, sem)
    fetch.start()
    fetch.wait()
    top[...] = image_ref[:SHIFT]
    bottom[...] = image_ref[rows - SHIFT :]
    for r in range(0, rows, SIDE):
        band = image_ref[r : r + SIDE].astype(F32)
        left[r : r + SIDE] = band[:, :SHIFT].astype(BF16)
        right[r : r + SIDE] = band[:, cols - SHIFT :].astype(BF16)


def own_kernel(
    image_ref, gain1_hbm, gain2_hbm, qkv_hbm, proj_hbm, table_hbm, conv_hbm, fc1_hbm, fc2_hbm,
    bias, query, kv, normed, wkv, wp, wc, w1, w2, g2,
    padded, strip, wq,
    table_ref, gain1_ref, gain2_ref, qkv_ref, proj_ref, conv_ref, fc1_ref, fc2_ref, sems,
):
    rows, cols, channels = image_ref.shape
    head_dim = channels // HEADS
    flag_lane, one_lane = channels, channels + 1
    blocks_r, blocks_c = rows // SIDE, cols // SIDE
    fetches = [
        pltpu.make_async_copy(source, target, sems.at[i])
        for i, (source, target) in enumerate(
            ((gain1_hbm, gain1_ref), (qkv_hbm, qkv_ref), (table_hbm, table_ref), (proj_hbm, proj_ref),
             (conv_hbm, conv_ref), (gain2_hbm, gain2_ref), (fc1_hbm, fc1_ref), (fc2_hbm, fc2_ref))
        )
    ]
    for fetch in fetches:
        fetch.start()

    for ref in (wq, wkv, wp, wc, w1, w2, g2):
        ref[...] = jnp.zeros_like(ref)
    special = lax.broadcasted_iota(jnp.int32, (16, LANES), 0) + 176
    lanes16 = lax.broadcasted_iota(jnp.int32, (16, LANES), 1)
    wq[176:192, :] = one_hot((special == one_lane) & (lanes16 == flag_lane))
    wkv[176:192, 0:LANES] = jnp.where(
        (special == flag_lane) & (lanes16 == flag_lane), MASKED, 0.0
    ).astype(BF16)
    normed[:, :, HALF:] = jnp.broadcast_to(marks(channels, 0.0)[None], (rows, cols, HALF))

    fetches[0].wait()
    gain1 = gain1_ref[...]
    scale = head_dim**-0.5 * LOG2E

    def weights():
        for fetch in fetches[1:]:
            fetch.wait()
        wq[0:channels, 0:channels] = qkv_ref[:, 0:channels]
        wkv[0:channels, 0:channels] = qkv_ref[:, channels : 2 * channels]
        wkv[0:channels, LANES : LANES + channels] = qkv_ref[:, 2 * channels :]
        wp[0:channels, 0:channels] = proj_ref[...]
        w1[0:channels, 0 : fc1_ref.shape[1]] = fc1_ref[...]
        w2[0 : fc2_ref.shape[1], 0:channels] = fc2_ref[...].astype(F32).T.astype(BF16)
        g2[:, 0:channels] = gain2_ref[...]
        for tap in range(9):
            wc[tap * LANES : tap * LANES + channels, 0:channels] = conv_ref[tap // 3, tap % 3]

    def norm(br):
        at = slice(br * SIDE, (br + 1) * SIDE)
        normed[at, :, 0:channels] = layer_norm(image_ref[at].astype(F32), gain1)

    def project(br):
        pixels = normed[br * SIDE : (br + 1) * SIDE].astype(BF16).reshape(-1, LANES)
        q = dot(pixels, wq[...])
        yield
        both = dot(pixels, wkv[...]).reshape(SIDE, cols, 2 * LANES)
        q = (q * scale).reshape(SIDE, cols, LANES)
        for bc in range(blocks_c):
            part = slice(bc * SIDE, (bc + 1) * SIDE)
            query[br, bc] = q[:, part].reshape(AREA, LANES).astype(BF16)
        yield
        for bc in range(blocks_c):
            part = slice(bc * SIDE, (bc + 1) * SIDE)
            kv[br, bc] = both[:, part].reshape(AREA, 2 * LANES).astype(BF16)

    for br in range(blocks_r):
        norm(br)
    weights()
    tasks = [expand_bias(table_ref, padded, strip, bias)]
    for br in range(blocks_r):
        tasks.append(project(br))
    weave(tasks, 3)


def edge_kernel(
    image_ref, top_ref, bottom_ref, left_ref, right_ref, gain1_ref,
    bias, query, kv, normed, wkv, wp, wc, w1, w2, g2,
    kv_edge, corner_base, out_edge, out_mid,
    halo, base, shifted,
):
    cols, channels = top_ref.shape[1:]
    rows = left_ref.shape[0]
    head_dim = channels // HEADS
    row, last_row = lax.axis_index("row"), lax.axis_size("row") - 1
    col, last_col = lax.axis_index("col"), lax.axis_size("col") - 1
    gain1 = gain1_ref[...]
    outside = [(row == 0).astype(F32), (row == last_row).astype(F32),
               (col == 0).astype(F32), (col == last_col).astype(F32)]

    for r in (0, SHIFT + rows):
        for c in (0, SHIFT + cols):
            halo[r : r + SHIFT, c : c + SHIFT] = jnp.zeros((SHIFT, SHIFT, LANES), F32)
    sides = []

    def band(i):
        ref = (top_ref, bottom_ref, left_ref, right_ref)[i]
        start = (0, SHIFT + (rows if i < 2 else cols))[i % 2]
        inner = slice(SHIFT, SHIFT + (cols if i < 2 else rows))
        outer = slice(start, start + SHIFT)
        place = (outer, inner) if i < 2 else (inner, outer)
        mark = jnp.broadcast_to(marks(channels, outside[i])[None], (*ref.shape[:2], HALF))
        halo[(*place, slice(HALF, LANES))] = mark
        halo[(*place, slice(0, channels))] = layer_norm(ref[...].astype(F32), gain1 * (1.0 - outside[i]))
        pixels = halo[place]
        if i < 2:
            blocks = [pixels[:, b * SIDE : (b + 1) * SIDE].reshape(AREA, LANES) for b in range(cols // SIDE)]
        else:
            blocks = [pixels.reshape(-1, LANES)]
        pixels = jnp.concatenate(blocks, axis=0).astype(BF16)
        yield
        both = dot(pixels, wkv[...])
        yield
        kv_edge[i] = both.astype(BF16).reshape(-1, AREA, 2 * LANES)
        sides.append(i)

    def tile():
        for r in range(0, rows, SIDE):
            halo[SHIFT + r : SHIFT + r + SIDE, SHIFT : SHIFT + cols] = normed[r : r + SIDE]
            yield

    def convolve(br):
        r = br * SIDE
        for tap in range(3):
            c0 = SHIFT - 1 + tap
            start, stop = 0 if br == 0 else r + 2, r + SIDE + 2
            shifted[tap, start:stop] = halo[
                SHIFT - 1 + start : SHIFT - 1 + stop, c0 : c0 + cols
            ].astype(BF16)
        yield
        taps = [
            shifted[tap % 3, r + tap // 3 : r + tap // 3 + SIDE].reshape(-1, LANES) for tap in range(9)
        ]
        summed = dot(jnp.concatenate(taps, axis=1), wc[...])
        yield
        summed = summed[:, :channels].reshape(SIDE, cols, channels)
        summed = summed + image_ref[r : r + SIDE].astype(F32)
        for bc in range(cols // SIDE):
            part = summed[:, bc * SIDE : (bc + 1) * SIDE].reshape(AREA, channels)
            if (br, bc) in corners:
                ref = corner_base.at[corners.index((br, bc))]
            else:
                ref = base.at[br, bc]
            ref[:, HALF:] = jnp.zeros((AREA, HALF), F32)
            ref[:, 0:channels] = part

    corners = [(0, 0), (0, 3), (3, 0), (3, 3)]
    keys = [
        lambda: [kv_edge[0, 1], kv[0, 1], kv_edge[0, 2], kv[0, 2]],
        lambda: [kv[3, 1], kv_edge[1, 1], kv[3, 2], kv_edge[1, 2]],
        lambda: [kv_edge[2, 1], kv_edge[2, 2], kv[1, 0], kv[2, 0]],
        lambda: [kv[1, 3], kv[2, 3], kv_edge[3, 1], kv_edge[3, 2]],
        lambda: [kv[1, 1], kv[2, 1], kv[1, 2], kv[2, 2]],
    ]
    places = [((0, 1), (0, 2)), ((3, 1), (3, 2)), ((1, 0), (2, 0)), ((1, 3), (2, 3))]
    places += [((1, 1), (1, 2)), ((2, 1), (2, 2))]
    quadrants = [((1, 0), (1, 1)), ((0, 0), (0, 1)), ((0, 1), (1, 1)), ((0, 0), (1, 0))]
    quadrants += [((0, 0), (0, 1)), ((1, 0), (1, 1))]
    done = {}

    def unit(i):
        def put(result):
            done[i] = result

        window = keys[min(i, 4)]
        parts = ([query[at] for at in places[i]], quadrants[i], lambda: jnp.concatenate(window(), axis=0))
        make = lambda: attend(parts, bias, head_dim, channels, put)
        return after(lambda: i >= 4 or i in sides, make)

    def tail(i):
        def put(out):
            if i == 4:
                out_mid[...] = out
            else:
                out_edge[i // 2] = out

        def make():
            return finish(
                jnp.concatenate([done[i], done[i + 1]], axis=0),
                lambda: jnp.concatenate([base[at] for at in (*places[i], *places[i + 1])], axis=0),
                wp, g2[...], w1, w2, channels, put,
            )

        return after(lambda: i in done and i + 1 in done, make)

    weave(
        [unit(4), band(0), band(1), unit(5), band(2), band(3), tile(), unit(0), convolve(0), unit(1),
         convolve(1), unit(2), convolve(2), unit(3), convolve(3), tail(4), tail(0), tail(2)],
        3,
    )


def corner_kernel(
    left_ref, right_ref, gain1_ref,
    bias, query, kv, wkv, wp, wc, w1, w2, g2, kv_edge, corner_base, out_mid, out_edge,
    out_hbm,
    normed, out_ref, sems,
):
    rows, _, channels = out_ref.shape
    head_dim = channels // HEADS

    def finish_bands(which, corners):
        def piece(source, i):
            return source[i * AREA : (i + 1) * AREA]

        for br in which:
            if br in (0, 3):
                i = 0 if br == 0 else 2
                band = [corners[0], piece(out_edge.at[0], i), piece(out_edge.at[0], i + 1), corners[1]]
            else:
                i = br - 1
                band = [piece(out_edge.at[1], i), piece(out_mid, 2 * i), piece(out_mid, 2 * i + 1),
                        piece(out_edge.at[1], i + 2)]
            band = [part[:, :channels].reshape(SIDE, SIDE, channels) for part in band]
            out_ref[br * SIDE : (br + 1) * SIDE] = jnp.concatenate(band, axis=1).astype(BF16)

    finish_bands((1, 2), None)
    inner = slice(SIDE, rows - SIDE)
    writes = [pltpu.make_async_copy(out_ref.at[inner], out_hbm.at[inner], sems.at[0])]
    writes[0].start()
    row, last_row = lax.axis_index("row"), lax.axis_size("row") - 1
    col, last_col = lax.axis_index("col"), lax.axis_size("col") - 1
    gain1 = gain1_ref[...]
    out_row = [(row == 0).astype(F32), (row == last_row).astype(F32)]
    out_col = [(col == 0).astype(F32), (col == last_col).astype(F32)]
    corner, done = {}, {}

    def project(pair):
        for i in (2 * pair, 2 * pair + 1):
            ref = (left_ref, right_ref)[i % 2]
            inside = (1.0 - out_row[i // 2]) * (1.0 - out_col[i % 2])
            mark = marks(channels, out_row[i // 2] + out_col[i % 2])
            normed[i, :, HALF:] = jnp.broadcast_to(mark, (AREA, HALF))
            values = ref[i // 2 * SIDE : (i // 2 + 1) * SIDE].astype(F32)
            normed[i, :, 0:channels] = layer_norm(values.reshape(AREA, channels), gain1 * inside)
        yield
        both = dot(normed[2 * pair : 2 * pair + 2].reshape(-1, LANES).astype(BF16), wkv[...])
        yield
        both = both.astype(BF16)
        corner[2 * pair], corner[2 * pair + 1] = both[:AREA], both[AREA:]

    keys = [
        lambda: [corner[0], kv_edge[2, 0], kv_edge[0, 0], kv[0, 0]],
        lambda: [kv_edge[0, 3], kv[0, 3], corner[1], kv_edge[3, 0]],
        lambda: [kv_edge[2, 3], corner[2], kv[3, 0], kv_edge[1, 0]],
        lambda: [kv[3, 3], kv_edge[1, 3], kv_edge[3, 3], corner[3]],
    ]
    places = [(0, 0), (0, 3), (3, 0), (3, 3)]
    quadrants = [(1, 1), (1, 0), (0, 1), (0, 0)]

    def unit(i):
        def put(result):
            done[i] = result

        parts = ([query[places[i]]], [quadrants[i]], lambda: jnp.concatenate(keys[i](), axis=0))
        return after(lambda: i in corner, lambda: attend(parts, bias, head_dim, channels, put))

    def whole(i):
        tap, y, x = ((0, 7, 7), (2, 7, 0), (6, 0, 7), (8, 0, 0))[i]
        start = y * SIDE
        term = dot(normed[i, start : start + SIDE].astype(BF16), wc[tap * LANES : (tap + 1) * LANES])
        term = term[x : x + 1]
        pixel = lax.broadcasted_iota(jnp.int32, (AREA, 1), 0)
        at = (SIDE - 1 - y) * SIDE + SIDE - 1 - x
        return corner_base[i] + jnp.where(pixel == at, term, 0.0)

    def tail(i):
        def put(out):
            finish_bands((0,) if i == 0 else (3,), [out[:AREA], out[AREA:]])

        def make():
            return finish(
                jnp.concatenate([done[i], done[i + 1]], axis=0),
                lambda: jnp.concatenate([whole(i), whole(i + 1)], axis=0),
                wp, g2[...], w1, w2, channels, put,
            )

        return after(lambda: i in done and i + 1 in done, make)

    weave([project(0), project(1), unit(0), unit(1), unit(2), unit(3), tail(0), tail(2)], 4)
    writes[0].wait()
    for r in (0, rows - SIDE):
        at = slice(r, r + SIDE)
        write = pltpu.make_async_copy(out_ref.at[at], out_hbm.at[at], sems.at[1 if r == 0 else 2])
        write.start()
        writes.append(write)
    writes[1].wait()
    writes[2].wait()


def exchange(low, high, axis):
    count = lax.axis_size(axis)
    before = lax.ppermute(high, axis, [(i, (i + 1) % count) for i in range(count)])
    after = lax.ppermute(low, axis, [((i + 1) % count, i) for i in range(count)])
    return before, after


def call(kernel, name, outs, scratch, flops, operands, in_hbm=()):
    vmem = pl.BlockSpec(memory_space=pltpu.VMEM)
    hbm = pl.BlockSpec(memory_space=pltpu.HBM)
    return pl.pallas_call(
        kernel,
        out_shape=[out if isinstance(out, jax.ShapeDtypeStruct) else pltpu.VMEM(*out) for out in outs],
        in_specs=[hbm if i in in_hbm else vmem for i in range(len(operands))],
        out_specs=[hbm if isinstance(out, jax.ShapeDtypeStruct) else vmem for out in outs],
        scratch_shapes=[pltpu.VMEM(*s) if isinstance(s, tuple) else s for s in scratch],
        cost_estimate=pl.CostEstimate(flops=flops, bytes_accessed=4_000_000, transcendentals=1_000_000),
        compiler_params=pltpu.CompilerParams(vmem_limit_bytes=24 * 1024 * 1024),
        name=name,
    )(*[pltpu.with_memory_space_constraint(x, pltpu.HBM) if i in in_hbm else x for i, x in enumerate(operands)])


def on_device(
    image, norm1_gain, norm2_gain, qkv_weight, proj_weight, rel_table, conv_weight, fc1_weight,
    fc2_weight,
):
    rows, cols, channels = image.shape
    blocks_r, blocks_c = rows // SIDE, cols // SIDE
    gain1, gain2, fc2, table = norm1_gain[None], norm2_gain[None], fc2_weight.T, rel_table.T
    band, column = ((SHIFT, cols, channels), BF16), ((rows, SHIFT, channels), BF16)
    tile, first_rows, last_rows, first_cols, last_cols = call(
        cut_kernel,
        "cut_halo",
        [(image.shape, BF16), band, band, column, column],
        [pltpu.SemaphoreType.DMA(())],
        1_000_000,
        (image,),
        (0,),
    )
    top, bottom = exchange(first_rows, last_rows, "row")
    left, right = exchange(first_cols, last_cols, "col")
    fetched = (table, gain1, gain2, qkv_weight, proj_weight, conv_weight, fc1_weight, fc2)
    hidden = -(-fc1_weight.shape[1] // 128) * 128
    bias, query, kv, normed, wkv, wp, wc, w1, w2, g2 = call(
        own_kernel,
        "own_tile",
        [
            ((HEADS, 2, 2, AREA, WIN * WIN), F32),
            ((blocks_r, blocks_c, AREA, LANES), BF16),
            ((blocks_r, blocks_c, AREA, 2 * LANES), BF16),
            ((rows, cols, LANES), F32),
            ((LANES, 2 * LANES), BF16),
            ((LANES, LANES), BF16),
            ((9 * LANES, LANES), BF16),
            ((LANES, hidden), BF16),
            ((hidden, LANES), BF16),
            ((1, LANES), F32),
        ],
        [
            ((8, 1024), F32),
            ((4, 8 * WIN, 128), F32),
            ((LANES, LANES), BF16),
            *[(x.shape, x.dtype) for x in fetched],
            pltpu.SemaphoreType.DMA((len(fetched),)),
        ],
        2_000_000_000,
        (tile, gain1, gain2, qkv_weight, proj_weight, table, conv_weight, fc1_weight, fc2),
        range(1, 9),
    )
    first = jnp.concatenate([top[:, :SHIFT], bottom[:, :SHIFT]])
    last = jnp.concatenate([top[:, cols - SHIFT :], bottom[:, cols - SHIFT :]])
    left_corner, right_corner = exchange(first, last, "col")
    kv_edge, corner_base, out_edge, out_mid = call(
        edge_kernel,
        "edge_windows",
        [
            ((4, blocks_c, AREA, 2 * LANES), BF16),
            ((4, AREA, LANES), F32),
            ((2, 4 * AREA, LANES), F32),
            ((4 * AREA, LANES), F32),
        ],
        [
            ((rows + 2 * SHIFT, cols + 2 * SHIFT, LANES), F32),
            ((blocks_r, blocks_c, AREA, LANES), F32),
            ((3, rows + 2, cols, LANES), BF16),
        ],
        2_000_000_000,
        (tile, top, bottom, left, right, gain1, bias, query, kv, normed, wkv, wp, wc, w1, w2, g2),
    )
    (out,) = call(
        corner_kernel,
        "corner_windows",
        [jax.ShapeDtypeStruct(image.shape, BF16)],
        [((4, AREA, LANES), F32), (image.shape, BF16), pltpu.SemaphoreType.DMA((3,))],
        1_000_000_000,
        (left_corner, right_corner, gain1, bias, query, kv, wkv, wp, wc, w1, w2, g2,
         kv_edge, corner_base, out_mid, out_edge),
    )
    return out


def solution(mesh):
    placed = (P("row", "col", None), P(), P(), P(), P(), P(), P(), P(), P())
    return jax.shard_map(
        on_device, mesh=mesh, in_specs=placed, out_specs=P("row", "col", None), check_vma=False
    )
```

```python
import math

import jax
import jax.numpy as jnp
from jax import lax
from jax.experimental import pallas as pl
from jax.experimental.pallas import tpu as pltpu
from jax.sharding import PartitionSpec as P

HEADS = 6
WIN = 16
SHIFT = 8
SIDE = 8
AREA = SIDE * SIDE
LANES = 256
HALF = LANES // 2
F32 = jnp.float32
BF16 = jnp.bfloat16
LOG2E = math.log2(math.e)
MASKED = -4.0e9


def weave(tasks, width):
    waiting, active = list(tasks), []
    while waiting or active:
        while waiting and len(active) < width:
            active.append(waiting.pop(0))
        for task in list(active):
            try:
                next(task)
            except StopIteration:
                active.remove(task)


def layer_norm(values, norm_gain):
    centre = jnp.mean(values, axis=-1, keepdims=True)
    values = values - centre
    spread = jnp.mean(values * values, axis=-1, keepdims=True)
    return values * lax.rsqrt(spread + 1e-05) * norm_gain


def layer_norm_padded(values, norm_gain, channels):
    centre = jnp.sum(values, axis=-1, keepdims=True) * (1.0 / channels)
    values = jnp.where(lanes_of() < channels, values - centre, 0.0)
    spread = jnp.sum(values * values, axis=-1, keepdims=True) * (1.0 / channels)
    return values * lax.rsqrt(spread + 1e-05) * norm_gain


def dot(a, b):
    return jnp.dot(a, b, preferred_element_type=F32)


def dot_nt(a, b):
    return lax.dot_general(a, b, (((1,), (1,)), ((), ())), preferred_element_type=F32)


def one_hot(condition):
    return jnp.where(condition, 1.0, 0.0).astype(BF16)


def gelu(x):
    square = jnp.minimum(x * x, 25.0)
    poly = -5.58203231240273e-08
    for factor in (2.777085437695777e-06, -4.707012890217347e-05, -5.859274357446709e-05,
                   0.036366718434813275, 0.7978721905787034):
        poly = poly * square + factor
    half = 0.5 * x
    return half + half * jnp.tanh(x * poly)


def lanes_of(width=LANES):
    return lax.broadcasted_iota(jnp.int32, (1, width), 1)


def marks(channels, outside):
    half = lanes_of()[:, HALF:]
    return jnp.where(half == channels + 1, 1.0, 0.0) + jnp.where(half == channels, outside, 0.0)


def expand_bias(table_ref, padded, strip, bias):
    span = 2 * WIN - 1
    padded[...] = jnp.zeros_like(padded)
    padded[0:HEADS, 0 : span * span] = table_ref[...] * LOG2E
    table = padded[...]
    width = padded.shape[1]
    shifted = jnp.concatenate(
        [table if px == 0 else pltpu.roll(table, width - px, 1) for px in range(WIN)], axis=0
    )
    high = shifted.astype(BF16)
    low = (shifted - high.astype(F32)).astype(BF16)
    yield
    entry = lax.broadcasted_iota(jnp.int32, (width, 512), 0)
    place = lax.broadcasted_iota(jnp.int32, (1, 512), 1)
    column = lax.div(place, 256) * SIDE + lax.rem(place, SIDE)
    wanted = (span - 1 - lax.div(lax.rem(place, 256), SIDE)) * span + WIN - 1 - column
    picked = dot(jnp.concatenate([high, low], axis=0), one_hot(entry == wanted))
    yield
    half = 8 * WIN
    picked = picked[:half] + picked[half:]
    for tile in range(4):
        strip[tile] = picked[:, 128 * tile : 128 * (tile + 1)]
    for head in range(HEADS):
        yield
        for half in range(2):
            rows = jnp.concatenate(
                [strip[2 * half + t, pl.ds(head, WIN, stride=8), :] for t in range(2)], axis=1
            )
            for py in range(WIN):
                start = (WIN - 1 - py) * SIDE
                rolled = (rows if start == 0 else pltpu.roll(rows, 256 - start, 1))[:, 0:128]
                lanes = slice(128 * half, 128 * (half + 1))
                place = slice(py % SIDE * SIDE, (py % SIDE + 1) * SIDE)
                bias[head, py // SIDE, 0, place, lanes] = rolled[:SIDE]
                bias[head, py // SIDE, 1, place, lanes] = rolled[SIDE:]


def scores_of(blocks, keys, head_dim, channels):
    lane = lanes_of()
    part = jnp.concatenate(blocks, axis=0)
    own = [(lane >= h * head_dim) & (lane < (h + 1) * head_dim) for h in range(HEADS)]
    stacked = jnp.concatenate(
        [part * one_hot(own[h] | (lane == channels)) for h in range(HEADS)], axis=0
    )
    return dot_nt(stacked, keys)


def attend(unit, bias, head_dim, channels, put):
    lane = lanes_of()
    blocks, quadrants, pair = unit
    pair = pair()
    scores = scores_of(blocks, pair[:, :LANES], head_dim, channels)
    count = scores.shape[0] // HEADS
    yield
    part_bias = jnp.concatenate([bias[:, hy, hx] for hy, hx in quadrants], axis=1)
    scores = scores.reshape(HEADS, count, WIN * WIN) + part_bias
    scores = scores - jnp.max(scores, axis=-1, keepdims=True)
    weights = jnp.exp2(scores).astype(BF16).reshape(HEADS * count, WIN * WIN)
    yield
    mixed = dot(weights, pair[:, LANES:])
    total = dot(weights, jnp.ones((WIN * WIN, HALF), BF16))
    yield
    result, low, high = mixed[0:count], total[0:count], total[0:count]
    for h in range(1, HEADS):
        rows = slice(h * count, (h + 1) * count)
        mine = (lane >= h * head_dim) & (lane < (h + 1) * head_dim)
        result = jnp.where(mine, mixed[rows], result)
        if h * head_dim < HALF:
            low = jnp.where(mine[:, :HALF], total[rows], low)
        if (h + 1) * head_dim > HALF:
            high = jnp.where(mine[:, HALF:], total[rows], high)
    put((result / jnp.concatenate([low, high], axis=1)).astype(BF16))


def finish(heads_out, base, wp, gain2, w1, w2, channels, put):
    attended = dot(heads_out, wp[...])
    yield
    state1 = base() + attended.astype(BF16).astype(F32)
    normed2 = layer_norm_padded(state1, gain2, channels).astype(BF16)
    yield
    hidden = dot(normed2, w1[...])
    yield
    hidden = gelu(hidden).astype(BF16)
    yield
    put(state1 + dot(hidden, w2[...]))


def after(ready, make):
    while not ready():
        yield
    yield from make()


def cut_kernel(image_hbm, image_ref, top, bottom, left, right, sem):
    rows, cols, _ = image_ref.shape
    fetch = pltpu.make_async_copy(image_hbm, image_ref, sem)
    fetch.start()
    fetch.wait()
    top[...] = image_ref[:SHIFT]
    bottom[...] = image_ref[rows - SHIFT :]
    for r in range(0, rows, SIDE):
        band = image_ref[r : r + SIDE].astype(F32)
        left[r : r + SIDE] = band[:, :SHIFT].astype(BF16)
        right[r : r + SIDE] = band[:, cols - SHIFT :].astype(BF16)


def own_kernel(
    image_ref, gain1_hbm, gain2_hbm, qkv_hbm, proj_hbm, table_hbm, conv_hbm, fc1_hbm, fc2_hbm,
    bias, query, kv, base, wkv, wp, wc, w1, w2, g2,
    padded, strip, wq, normed, shifted,
    table_ref, gain1_ref, gain2_ref, qkv_ref, proj_ref, conv_ref, fc1_ref, fc2_ref, sems,
):
    rows, cols, channels = image_ref.shape
    head_dim = channels // HEADS
    flag_lane, one_lane = channels, channels + 1
    blocks_r, blocks_c = rows // SIDE, cols // SIDE
    fetches = [
        pltpu.make_async_copy(source, target, sems.at[i])
        for i, (source, target) in enumerate(
            ((gain1_hbm, gain1_ref), (qkv_hbm, qkv_ref), (table_hbm, table_ref), (proj_hbm, proj_ref),
             (conv_hbm, conv_ref), (gain2_hbm, gain2_ref), (fc1_hbm, fc1_ref), (fc2_hbm, fc2_ref))
        )
    ]
    for fetch in fetches:
        fetch.start()

    for ref in (wq, wkv, wp, wc, w1, w2, g2):
        ref[...] = jnp.zeros_like(ref)
    special = lax.broadcasted_iota(jnp.int32, (16, LANES), 0) + 176
    lanes16 = lax.broadcasted_iota(jnp.int32, (16, LANES), 1)
    wq[176:192, :] = one_hot((special == one_lane) & (lanes16 == flag_lane))
    wkv[176:192, 0:LANES] = jnp.where(
        (special == flag_lane) & (lanes16 == flag_lane), MASKED, 0.0
    ).astype(BF16)
    normed[...] = jnp.zeros_like(normed)
    normed[1 : 1 + rows, SHIFT : SHIFT + cols, HALF:] = jnp.broadcast_to(
        marks(channels, 0.0)[None], (rows, cols, HALF)
    )

    fetches[0].wait()
    gain1 = gain1_ref[...]
    scale = head_dim**-0.5 * LOG2E

    def weights():
        for fetch in fetches[1:]:
            fetch.wait()
        wq[0:channels, 0:channels] = qkv_ref[:, 0:channels]
        wkv[0:channels, 0:channels] = qkv_ref[:, channels : 2 * channels]
        wkv[0:channels, LANES : LANES + channels] = qkv_ref[:, 2 * channels :]
        wp[0:channels, 0:channels] = proj_ref[...]
        w1[0:channels, 0 : fc1_ref.shape[1]] = fc1_ref[...]
        w2[0 : fc2_ref.shape[1], 0:channels] = fc2_ref[...].astype(F32).T.astype(BF16)
        g2[:, 0:channels] = gain2_ref[...]
        for tap in range(9):
            wc[tap * LANES : tap * LANES + channels, 0:channels] = conv_ref[tap // 3, tap % 3]

    def norm(br):
        r = br * SIDE
        inner = (slice(1 + r, 1 + r + SIDE), slice(SHIFT, SHIFT + cols))
        normed[(*inner, slice(0, channels))] = layer_norm(image_ref[r : r + SIDE].astype(F32), gain1)

    def project(br):
        inner = (slice(1 + br * SIDE, 1 + (br + 1) * SIDE), slice(SHIFT, SHIFT + cols))
        pixels = normed[inner].astype(BF16).reshape(-1, LANES)
        q = dot(pixels, wq[...])
        yield
        both = dot(pixels, wkv[...]).reshape(SIDE, cols, 2 * LANES)
        q = (q * scale).reshape(SIDE, cols, LANES)
        for bc in range(blocks_c):
            part = slice(bc * SIDE, (bc + 1) * SIDE)
            query[br, bc] = q[:, part].reshape(AREA, LANES).astype(BF16)
        yield
        for bc in range(blocks_c):
            part = slice(bc * SIDE, (bc + 1) * SIDE)
            kv[br, bc] = both[:, part].reshape(AREA, 2 * LANES).astype(BF16)

    def convolve(br):
        r = br * SIDE
        for tap in range(3):
            c0 = SHIFT - 1 + tap
            start = 0 if br == 0 else r + 2
            shifted[tap, start : r + SIDE + 2] = normed[start : r + SIDE + 2, c0 : c0 + cols].astype(BF16)
        yield
        taps = [
            shifted[tap % 3, r + tap // 3 : r + tap // 3 + SIDE].reshape(-1, LANES) for tap in range(9)
        ]
        summed = dot(jnp.concatenate(taps, axis=1), wc[...])
        yield
        summed = summed[:, :channels].reshape(SIDE, cols, channels)
        summed = summed + image_ref[r : r + SIDE].astype(F32)
        for bc in range(blocks_c):
            base[br, bc, :, HALF:] = jnp.zeros((AREA, HALF), F32)
            base[br, bc, :, 0:channels] = summed[:, bc * SIDE : (bc + 1) * SIDE].reshape(AREA, channels)

    for br in range(blocks_r):
        norm(br)
    weights()
    tasks = [expand_bias(table_ref, padded, strip, bias)]
    for br in range(blocks_r):
        tasks += [project(br), convolve(br)]
    weave(tasks, 3)


def edge_kernel(
    top_ref, bottom_ref, left_ref, right_ref, gain1_ref,
    bias, query, kv, base, wkv, wp, wc, w1, w2, g2,
    kv_edge, corner_base, out_edge, out_mid,
    bands_r, bands_c, fixes,
):
    cols, channels = top_ref.shape[1:]
    rows = left_ref.shape[0]
    head_dim = channels // HEADS
    row, last_row = lax.axis_index("row"), lax.axis_size("row") - 1
    col, last_col = lax.axis_index("col"), lax.axis_size("col") - 1
    gain1 = gain1_ref[...]
    outside = [(row == 0).astype(F32), (row == last_row).astype(F32),
               (col == 0).astype(F32), (col == last_col).astype(F32)]

    bands_r[...] = jnp.zeros_like(bands_r)
    bands_c[...] = jnp.zeros_like(bands_c)
    sides = []

    def band(i):
        ref = (top_ref, bottom_ref, left_ref, right_ref)[i]
        mark = jnp.broadcast_to(marks(channels, outside[i])[None], (*ref.shape[:2], HALF))
        values = layer_norm(ref[...].astype(F32), gain1 * (1.0 - outside[i]))
        if i < 2:
            bands_r[i, :, SHIFT : SHIFT + cols, HALF:] = mark
            bands_r[i, :, SHIFT : SHIFT + cols, 0:channels] = values
            pixels = bands_r[i, :, SHIFT : SHIFT + cols]
            count = cols // SIDE
            blocks = [pixels[:, b * SIDE : (b + 1) * SIDE].reshape(AREA, LANES) for b in range(count)]
        else:
            bands_c[i - 2, 1 : 1 + rows, :, HALF:] = mark
            bands_c[i - 2, 1 : 1 + rows, :, 0:channels] = values
            count = rows // SIDE
            blocks = [bands_c[i - 2, 1 : 1 + rows].reshape(-1, LANES)]
        pixels = jnp.concatenate(blocks, axis=0).astype(BF16)
        yield
        both = dot(pixels, wkv[...])
        yield
        kv_edge[i] = both.astype(BF16).reshape(count, AREA, 2 * LANES)
        sides.append(i)

    keys = [
        lambda: [kv_edge[0, 1], kv[0, 1], kv_edge[0, 2], kv[0, 2]],
        lambda: [kv[3, 1], kv_edge[1, 1], kv[3, 2], kv_edge[1, 2]],
        lambda: [kv_edge[2, 1], kv_edge[2, 2], kv[1, 0], kv[2, 0]],
        lambda: [kv[1, 3], kv[2, 3], kv_edge[3, 1], kv_edge[3, 2]],
        lambda: [kv[1, 1], kv[2, 1], kv[1, 2], kv[2, 2]],
    ]
    places = [((0, 1), (0, 2)), ((3, 1), (3, 2)), ((1, 0), (2, 0)), ((1, 3), (2, 3))]
    places += [((1, 1), (1, 2)), ((2, 1), (2, 2))]
    quadrants = [((1, 0), (1, 1)), ((0, 0), (0, 1)), ((0, 1), (1, 1)), ((0, 0), (1, 0))]
    quadrants += [((0, 0), (0, 1)), ((1, 0), (1, 1))]
    done = {}

    def unit(i):
        def put(result):
            done[i] = result

        window = keys[min(i, 4)]
        parts = ([query[at] for at in places[i]], quadrants[i], lambda: jnp.concatenate(window(), axis=0))
        make = lambda: attend(parts, bias, head_dim, channels, put)
        return after(lambda: i >= 4 or i in sides, make)

    def tail(i):
        def put(out):
            if i == 4:
                out_mid[...] = out
            else:
                out_edge[i // 2] = out

        def part(at):
            return base[at] if i == 4 else corrected(base, fixes, at)

        def make():
            return finish(
                jnp.concatenate([done[i], done[i + 1]], axis=0),
                lambda: jnp.concatenate([part(at) for at in (*places[i], *places[i + 1])], axis=0),
                wp, g2[...], w1, w2, channels, put,
            )

        return after(lambda: i in done and i + 1 in done, make)

    def fix(i):
        taps = ((0, 1, 2), (6, 7, 8), (0, 3, 6), (2, 5, 8))[i]
        source = (SHIFT - 1, 0)[i % 2]
        if i < 2:
            pieces = [bands_r[i, source, SHIFT - 1 + t : SHIFT - 1 + t + cols] for t in range(3)]
        else:
            pieces = [bands_c[i - 2, t : t + rows, source] for t in range(3)]
        weights = jnp.concatenate([wc[t * LANES : (t + 1) * LANES] for t in taps], axis=0)
        fixes[i] = dot(jnp.concatenate(pieces, axis=1).astype(BF16), weights)
        yield

    def corners():
        for i, at in enumerate(((0, 0), (0, 3), (3, 0), (3, 3))):
            corner_base[i] = corrected(base, fixes, at)
            yield

    weave(
        [unit(4), band(0), band(1), unit(5), band(2), band(3), unit(0), fix(0), unit(1), fix(1), tail(4),
         unit(2), fix(2), unit(3), fix(3), tail(0), corners(), tail(2)],
        3,
    )


def corrected(base, fixes, at):
    br, bc = at
    block = base[at].reshape(SIDE, SIDE, LANES)
    y = lax.broadcasted_iota(jnp.int32, (SIDE, SIDE, 1), 0)
    x = lax.broadcasted_iota(jnp.int32, (SIDE, SIDE, 1), 1)
    if br in (0, 3):
        fix = fixes[0 if br == 0 else 1, bc * SIDE : (bc + 1) * SIDE]
        block = block + jnp.where(y == (0 if br == 0 else SIDE - 1), fix[None], 0.0)
    if bc in (0, 3):
        fix = fixes[2 if bc == 0 else 3, br * SIDE : (br + 1) * SIDE]
        block = block + jnp.where(x == (0 if bc == 0 else SIDE - 1), fix[:, None], 0.0)
    return block.reshape(AREA, LANES)


def corner_kernel(
    left_ref, right_ref, gain1_ref,
    bias, query, kv, wkv, wp, wc, w1, w2, g2, kv_edge, corner_base, out_mid, out_edge,
    out_hbm,
    normed, out_ref, sems,
):
    rows, _, channels = out_ref.shape
    head_dim = channels // HEADS

    def finish_bands(which, corners):
        def piece(source, i):
            return source[i * AREA : (i + 1) * AREA]

        for br in which:
            if br in (0, 3):
                i = 0 if br == 0 else 2
                band = [corners[0], piece(out_edge.at[0], i), piece(out_edge.at[0], i + 1), corners[1]]
            else:
                i = br - 1
                band = [piece(out_edge.at[1], i), piece(out_mid, 2 * i), piece(out_mid, 2 * i + 1),
                        piece(out_edge.at[1], i + 2)]
            band = [part[:, :channels].reshape(SIDE, SIDE, channels) for part in band]
            out_ref[br * SIDE : (br + 1) * SIDE] = jnp.concatenate(band, axis=1).astype(BF16)

    finish_bands((1, 2), None)
    inner = slice(SIDE, rows - SIDE)
    writes = [pltpu.make_async_copy(out_ref.at[inner], out_hbm.at[inner], sems.at[0])]
    writes[0].start()
    row, last_row = lax.axis_index("row"), lax.axis_size("row") - 1
    col, last_col = lax.axis_index("col"), lax.axis_size("col") - 1
    gain1 = gain1_ref[...]
    out_row = [(row == 0).astype(F32), (row == last_row).astype(F32)]
    out_col = [(col == 0).astype(F32), (col == last_col).astype(F32)]
    corner, done = {}, {}

    def project(pair):
        for i in (2 * pair, 2 * pair + 1):
            ref = (left_ref, right_ref)[i % 2]
            inside = (1.0 - out_row[i // 2]) * (1.0 - out_col[i % 2])
            mark = marks(channels, out_row[i // 2] + out_col[i % 2])
            normed[i, :, HALF:] = jnp.broadcast_to(mark, (AREA, HALF))
            values = ref[i // 2 * SIDE : (i // 2 + 1) * SIDE].astype(F32)
            normed[i, :, 0:channels] = layer_norm(values.reshape(AREA, channels), gain1 * inside)
        yield
        both = dot(normed[2 * pair : 2 * pair + 2].reshape(-1, LANES).astype(BF16), wkv[...])
        yield
        both = both.astype(BF16)
        corner[2 * pair], corner[2 * pair + 1] = both[:AREA], both[AREA:]

    keys = [
        lambda: [corner[0], kv_edge[2, 0], kv_edge[0, 0], kv[0, 0]],
        lambda: [kv_edge[0, 3], kv[0, 3], corner[1], kv_edge[3, 0]],
        lambda: [kv_edge[2, 3], corner[2], kv[3, 0], kv_edge[1, 0]],
        lambda: [kv[3, 3], kv_edge[1, 3], kv_edge[3, 3], corner[3]],
    ]
    places = [(0, 0), (0, 3), (3, 0), (3, 3)]
    quadrants = [(1, 1), (1, 0), (0, 1), (0, 0)]

    def unit(i):
        def put(result):
            done[i] = result

        parts = ([query[places[i]]], [quadrants[i]], lambda: jnp.concatenate(keys[i](), axis=0))
        return after(lambda: i in corner, lambda: attend(parts, bias, head_dim, channels, put))

    def whole(i):
        tap, y, x = ((0, 7, 7), (2, 7, 0), (6, 0, 7), (8, 0, 0))[i]
        start = y * SIDE
        term = dot(normed[i, start : start + SIDE].astype(BF16), wc[tap * LANES : (tap + 1) * LANES])
        term = term[x : x + 1]
        pixel = lax.broadcasted_iota(jnp.int32, (AREA, 1), 0)
        at = (SIDE - 1 - y) * SIDE + SIDE - 1 - x
        return corner_base[i] + jnp.where(pixel == at, term, 0.0)

    def tail(i):
        def put(out):
            finish_bands((0,) if i == 0 else (3,), [out[:AREA], out[AREA:]])

        def make():
            return finish(
                jnp.concatenate([done[i], done[i + 1]], axis=0),
                lambda: jnp.concatenate([whole(i), whole(i + 1)], axis=0),
                wp, g2[...], w1, w2, channels, put,
            )

        return after(lambda: i in done and i + 1 in done, make)

    weave([project(0), project(1), unit(0), unit(1), unit(2), unit(3), tail(0), tail(2)], 4)
    writes[0].wait()
    for r in (0, rows - SIDE):
        at = slice(r, r + SIDE)
        write = pltpu.make_async_copy(out_ref.at[at], out_hbm.at[at], sems.at[1 if r == 0 else 2])
        write.start()
        writes.append(write)
    writes[1].wait()
    writes[2].wait()


def exchange(low, high, axis):
    count = lax.axis_size(axis)
    before = lax.ppermute(high, axis, [(i, (i + 1) % count) for i in range(count)])
    after = lax.ppermute(low, axis, [((i + 1) % count, i) for i in range(count)])
    return before, after


def call(kernel, name, outs, scratch, flops, operands, in_hbm=()):
    vmem = pl.BlockSpec(memory_space=pltpu.VMEM)
    hbm = pl.BlockSpec(memory_space=pltpu.HBM)
    return pl.pallas_call(
        kernel,
        out_shape=[out if isinstance(out, jax.ShapeDtypeStruct) else pltpu.VMEM(*out) for out in outs],
        in_specs=[hbm if i in in_hbm else vmem for i in range(len(operands))],
        out_specs=[hbm if isinstance(out, jax.ShapeDtypeStruct) else vmem for out in outs],
        scratch_shapes=[pltpu.VMEM(*s) if isinstance(s, tuple) else s for s in scratch],
        cost_estimate=pl.CostEstimate(flops=flops, bytes_accessed=4_000_000, transcendentals=1_000_000),
        compiler_params=pltpu.CompilerParams(vmem_limit_bytes=24 * 1024 * 1024),
        name=name,
    )(*[pltpu.with_memory_space_constraint(x, pltpu.HBM) if i in in_hbm else x for i, x in enumerate(operands)])


def on_device(
    image, norm1_gain, norm2_gain, qkv_weight, proj_weight, rel_table, conv_weight, fc1_weight,
    fc2_weight,
):
    rows, cols, channels = image.shape
    blocks_r, blocks_c = rows // SIDE, cols // SIDE
    gain1, gain2, fc2, table = norm1_gain[None], norm2_gain[None], fc2_weight.T, rel_table.T
    band, column = ((SHIFT, cols, channels), BF16), ((rows, SHIFT, channels), BF16)
    tile, first_rows, last_rows, first_cols, last_cols = call(
        cut_kernel,
        "cut_halo",
        [(image.shape, BF16), band, band, column, column],
        [pltpu.SemaphoreType.DMA(())],
        1_000_000,
        (image,),
        (0,),
    )
    top, bottom = exchange(first_rows, last_rows, "row")
    left, right = exchange(first_cols, last_cols, "col")
    fetched = (table, gain1, gain2, qkv_weight, proj_weight, conv_weight, fc1_weight, fc2)
    hidden = -(-fc1_weight.shape[1] // 128) * 128
    bias, query, kv, base, wkv, wp, wc, w1, w2, g2 = call(
        own_kernel,
        "own_tile",
        [
            ((HEADS, 2, 2, AREA, WIN * WIN), F32),
            ((blocks_r, blocks_c, AREA, LANES), BF16),
            ((blocks_r, blocks_c, AREA, 2 * LANES), BF16),
            ((blocks_r, blocks_c, AREA, LANES), F32),
            ((LANES, 2 * LANES), BF16),
            ((LANES, LANES), BF16),
            ((9 * LANES, LANES), BF16),
            ((LANES, hidden), BF16),
            ((hidden, LANES), BF16),
            ((1, LANES), F32),
        ],
        [
            ((8, 1024), F32),
            ((4, 8 * WIN, 128), F32),
            ((LANES, LANES), BF16),
            ((rows + 2, cols + 2 * SHIFT, LANES), F32),
            ((3, rows + 2, cols, LANES), BF16),
            *[(x.shape, x.dtype) for x in fetched],
            pltpu.SemaphoreType.DMA((len(fetched),)),
        ],
        2_000_000_000,
        (tile, gain1, gain2, qkv_weight, proj_weight, table, conv_weight, fc1_weight, fc2),
        range(1, 9),
    )
    first = jnp.concatenate([top[:, :SHIFT], bottom[:, :SHIFT]])
    last = jnp.concatenate([top[:, cols - SHIFT :], bottom[:, cols - SHIFT :]])
    left_corner, right_corner = exchange(first, last, "col")
    kv_edge, corner_base, out_edge, out_mid = call(
        edge_kernel,
        "edge_windows",
        [
            ((4, blocks_c, AREA, 2 * LANES), BF16),
            ((4, AREA, LANES), F32),
            ((2, 4 * AREA, LANES), F32),
            ((4 * AREA, LANES), F32),
        ],
        [
            ((2, SHIFT, cols + 2 * SHIFT, LANES), F32),
            ((2, rows + 2, SHIFT, LANES), F32),
            ((4, cols, LANES), F32),
        ],
        2_000_000_000,
        (top, bottom, left, right, gain1, bias, query, kv, base, wkv, wp, wc, w1, w2, g2),
    )
    (out,) = call(
        corner_kernel,
        "corner_windows",
        [jax.ShapeDtypeStruct(image.shape, BF16)],
        [((4, AREA, LANES), F32), (image.shape, BF16), pltpu.SemaphoreType.DMA((3,))],
        1_000_000_000,
        (left_corner, right_corner, gain1, bias, query, kv, wkv, wp, wc, w1, w2, g2,
         kv_edge, corner_base, out_mid, out_edge),
    )
    return out


def solution(mesh):
    placed = (P("row", "col", None), P(), P(), P(), P(), P(), P(), P(), P())
    return jax.shard_map(
        on_device, mesh=mesh, in_specs=placed, out_specs=P("row", "col", None), check_vma=False
    )
```

```python
import math

import jax
import jax.numpy as jnp
from jax import lax
from jax.experimental import pallas as pl
from jax.experimental.pallas import tpu as pltpu
from jax.sharding import PartitionSpec as P

HEADS = 6
WIN = 16
SHIFT = 8
SIDE = 8
AREA = SIDE * SIDE
LANES = 256
HALF = LANES // 2
F32 = jnp.float32
BF16 = jnp.bfloat16
LOG2E = math.log2(math.e)
MASKED = -4.0e9


def weave(tasks, width):
    waiting, active = list(tasks), []
    while waiting or active:
        while waiting and len(active) < width:
            active.append(waiting.pop(0))
        for task in list(active):
            try:
                next(task)
            except StopIteration:
                active.remove(task)


def layer_norm(values, norm_gain):
    centre = jnp.mean(values, axis=-1, keepdims=True)
    values = values - centre
    spread = jnp.mean(values * values, axis=-1, keepdims=True)
    return values * lax.rsqrt(spread + 1e-05) * norm_gain


def layer_norm_padded(values, norm_gain, channels):
    centre = jnp.sum(values, axis=-1, keepdims=True) * (1.0 / channels)
    values = jnp.where(lanes_of() < channels, values - centre, 0.0)
    spread = jnp.sum(values * values, axis=-1, keepdims=True) * (1.0 / channels)
    return values * lax.rsqrt(spread + 1e-05) * norm_gain


def dot(a, b):
    return jnp.dot(a, b, preferred_element_type=F32)


def dot_nt(a, b):
    return lax.dot_general(a, b, (((1,), (1,)), ((), ())), preferred_element_type=F32)


def one_hot(condition):
    return jnp.where(condition, 1.0, 0.0).astype(BF16)


def gelu(x):
    square = jnp.minimum(x * x, 25.0)
    poly = -5.58203231240273e-08
    for factor in (2.777085437695777e-06, -4.707012890217347e-05, -5.859274357446709e-05,
                   0.036366718434813275, 0.7978721905787034):
        poly = poly * square + factor
    half = 0.5 * x
    return half + half * jnp.tanh(x * poly)


def lanes_of(width=LANES):
    return lax.broadcasted_iota(jnp.int32, (1, width), 1)


def marks(channels, outside):
    half = lanes_of()[:, HALF:]
    return jnp.where(half == channels + 1, 1.0, 0.0) + jnp.where(half == channels, outside, 0.0)


def expand_bias(table_ref, padded, strip, bias):
    span = 2 * WIN - 1
    padded[...] = jnp.zeros_like(padded)
    padded[0:HEADS, 0 : span * span] = table_ref[...] * LOG2E
    table = padded[...]
    width = padded.shape[1]
    shifted = jnp.concatenate(
        [table if px == 0 else pltpu.roll(table, width - px, 1) for px in range(WIN)], axis=0
    )
    high = shifted.astype(BF16)
    low = (shifted - high.astype(F32)).astype(BF16)
    yield
    entry = lax.broadcasted_iota(jnp.int32, (width, 512), 0)
    place = lax.broadcasted_iota(jnp.int32, (1, 512), 1)
    column = lax.div(place, 256) * SIDE + lax.rem(place, SIDE)
    wanted = (span - 1 - lax.div(lax.rem(place, 256), SIDE)) * span + WIN - 1 - column
    picked = dot(jnp.concatenate([high, low], axis=0), one_hot(entry == wanted))
    yield
    half = 8 * WIN
    picked = picked[:half] + picked[half:]
    for tile in range(4):
        strip[tile] = picked[:, 128 * tile : 128 * (tile + 1)]
    for head in range(HEADS):
        yield
        for half in range(2):
            rows = jnp.concatenate(
                [strip[2 * half + t, pl.ds(head, WIN, stride=8), :] for t in range(2)], axis=1
            )
            for py in range(WIN):
                start = (WIN - 1 - py) * SIDE
                rolled = (rows if start == 0 else pltpu.roll(rows, 256 - start, 1))[:, 0:128]
                lanes = slice(128 * half, 128 * (half + 1))
                place = slice(py % SIDE * SIDE, (py % SIDE + 1) * SIDE)
                bias[head, py // SIDE, 0, place, lanes] = rolled[:SIDE]
                bias[head, py // SIDE, 1, place, lanes] = rolled[SIDE:]


def by_head(part, head_dim, flag):
    lane = lanes_of()
    own = [(lane >= h * head_dim) & (lane < (h + 1) * head_dim) for h in range(HEADS)]
    return jnp.concatenate([part * one_hot(own[h] | (lane == flag)) for h in range(HEADS)], axis=0)


def softmax(scores, part_bias):
    scores = scores + part_bias
    scores = scores - jnp.max(scores, axis=-1, keepdims=True)
    weights = jnp.exp2(scores)
    return weights.astype(BF16), jnp.sum(weights, axis=-1, keepdims=True)


def attend(unit, bias, head_dim, channels, put):
    lane = lanes_of()
    blocks, quadrants, pair = unit
    pair = pair()
    part = jnp.concatenate(blocks, axis=0)
    count = part.shape[0]
    scores = dot_nt(by_head(part, head_dim, channels), pair[:, :LANES])
    yield
    part_bias = jnp.concatenate([bias[:, hy, hx] for hy, hx in quadrants], axis=1)
    weights, total = softmax(scores.reshape(HEADS, count, WIN * WIN), part_bias)
    weights = weights.reshape(HEADS * count, WIN * WIN)
    yield
    mixed = dot(weights, pair[:, LANES:])
    yield
    result, divisor = mixed[0:count], jnp.broadcast_to(total[0], (count, LANES))
    for h in range(1, HEADS):
        mine = (lane >= h * head_dim) & (lane < (h + 1) * head_dim)
        result = jnp.where(mine, mixed[h * count : (h + 1) * count], result)
        divisor = jnp.where(mine, total[h], divisor)
    put((result / divisor).astype(BF16))


def finish(heads_out, base, wp, gain2, w1, w2, channels, put):
    attended = dot(heads_out, wp[...])
    yield
    state1 = base() + attended.astype(BF16).astype(F32)
    normed2 = layer_norm_padded(state1, gain2, channels).astype(BF16)
    yield
    hidden = dot(normed2, w1[...])
    yield
    hidden = gelu(hidden).astype(BF16)
    yield
    put(state1 + dot(hidden, w2[...]))


def after(ready, make):
    while not ready():
        yield
    yield from make()


def cut_kernel(
    image_hbm, gain1_hbm, table_hbm, qkv_hbm, image_ref, gain1_ref, table_ref, qkv_ref,
    top, bottom, left, right, sems,
):
    rows, cols, _ = image_ref.shape
    fetches = [
        pltpu.make_async_copy(source, target, sems.at[i])
        for i, (source, target) in enumerate(
            ((image_hbm, image_ref), (gain1_hbm, gain1_ref), (table_hbm, table_ref), (qkv_hbm, qkv_ref))
        )
    ]
    for fetch in fetches:
        fetch.start()
    for fetch in fetches:
        fetch.wait()
    top[...] = image_ref[:SHIFT]
    bottom[...] = image_ref[rows - SHIFT :]
    for r in range(0, rows, SIDE):
        band = image_ref[r : r + SIDE].astype(F32)
        left[r : r + SIDE] = band[:, :SHIFT].astype(BF16)
        right[r : r + SIDE] = band[:, cols - SHIFT :].astype(BF16)


def own_kernel(
    image_ref, gain1_ref, table_ref, qkv_ref, gain2_hbm, proj_hbm, conv_hbm, fc1_hbm, fc2_hbm,
    bias, query, kv, base, own_x, wkv, wp, wc, w1, w2, g2,
    padded, strip, wq, normed, shifted,
    gain2_ref, proj_ref, conv_ref, fc1_ref, fc2_ref, sems,
):
    rows, cols, channels = image_ref.shape
    head_dim = channels // HEADS
    flag_lane, one_lane = channels, channels + 1
    blocks_r, blocks_c = rows // SIDE, cols // SIDE
    fetches = [
        pltpu.make_async_copy(source, target, sems.at[i])
        for i, (source, target) in enumerate(
            ((conv_hbm, conv_ref), (proj_hbm, proj_ref), (gain2_hbm, gain2_ref), (fc1_hbm, fc1_ref),
             (fc2_hbm, fc2_ref))
        )
    ]
    for fetch in fetches:
        fetch.start()

    for ref in (wq, wkv, wp, wc, w1, w2, g2):
        ref[...] = jnp.zeros_like(ref)
    special = lax.broadcasted_iota(jnp.int32, (16, LANES), 0) + 176
    lanes16 = lax.broadcasted_iota(jnp.int32, (16, LANES), 1)
    wq[176:192, :] = one_hot((special == one_lane) & (lanes16 == flag_lane))
    wkv[176:192, 0:LANES] = jnp.where(
        (special == flag_lane) & (lanes16 == flag_lane), MASKED, 0.0
    ).astype(BF16)
    normed[...] = jnp.zeros_like(normed)
    normed[1 : 1 + rows, SHIFT : SHIFT + cols, HALF:] = jnp.broadcast_to(
        marks(channels, 0.0)[None], (rows, cols, HALF)
    )

    gain1 = gain1_ref[...]
    scale = head_dim**-0.5 * LOG2E

    wq[0:channels, 0:channels] = qkv_ref[:, 0:channels]
    wkv[0:channels, 0:channels] = qkv_ref[:, channels : 2 * channels]
    wkv[0:channels, LANES : LANES + channels] = qkv_ref[:, 2 * channels :]

    def weights():
        for fetch in fetches:
            fetch.wait()
        wp[0:channels, 0:channels] = proj_ref[...]
        w1[0:channels, 0 : fc1_ref.shape[1]] = fc1_ref[...]
        w2[0 : fc2_ref.shape[1], 0:channels] = fc2_ref[...].astype(F32).T.astype(BF16)
        g2[:, 0:channels] = gain2_ref[...]
        for tap in range(9):
            wc[tap * LANES : tap * LANES + channels, 0:channels] = conv_ref[tap // 3, tap % 3]
        yield

    def norm(br):
        r = br * SIDE
        inner = (slice(1 + r, 1 + r + SIDE), slice(SHIFT, SHIFT + cols))
        normed[(*inner, slice(0, channels))] = layer_norm(image_ref[r : r + SIDE].astype(F32), gain1)

    def project(br):
        inner = (slice(1 + br * SIDE, 1 + (br + 1) * SIDE), slice(SHIFT, SHIFT + cols))
        pixels = normed[inner].astype(BF16).reshape(-1, LANES)
        q = dot(pixels, wq[...])
        yield
        both = dot(pixels, wkv[...]).reshape(SIDE, cols, 2 * LANES)
        q = (q * scale).reshape(SIDE, cols, LANES)
        for bc in range(blocks_c):
            part = slice(bc * SIDE, (bc + 1) * SIDE)
            query[br, bc] = q[:, part].reshape(AREA, LANES).astype(BF16)
        yield
        for bc in range(blocks_c):
            part = slice(bc * SIDE, (bc + 1) * SIDE)
            kv[br, bc] = both[:, part].reshape(AREA, 2 * LANES).astype(BF16)

    def convolve(br):
        r = br * SIDE
        for tap in range(3):
            c0 = SHIFT - 1 + tap
            start = 0 if br == 0 else r + 2
            shifted[tap, start : r + SIDE + 2] = normed[start : r + SIDE + 2, c0 : c0 + cols].astype(BF16)
        yield
        taps = [
            shifted[tap % 3, r + tap // 3 : r + tap // 3 + SIDE].reshape(-1, LANES) for tap in range(9)
        ]
        summed = dot(jnp.concatenate(taps, axis=1), wc[...])
        yield
        summed = summed[:, :channels].reshape(SIDE, cols, channels)
        summed = summed + image_ref[r : r + SIDE].astype(F32)
        for bc in range(blocks_c):
            base[br, bc, :, HALF:] = jnp.zeros((AREA, HALF), F32)
            base[br, bc, :, 0:channels] = summed[:, bc * SIDE : (bc + 1) * SIDE].reshape(AREA, channels)

    for br in range(blocks_r):
        norm(br)
    for i, (br, bc) in enumerate(((0, 0), (0, 3), (3, 0), (3, 3))):
        at = (slice(1 + br * SIDE, 1 + (br + 1) * SIDE), slice(SHIFT + bc * SIDE, SHIFT + (bc + 1) * SIDE))
        own_x[i] = normed[at].reshape(AREA, LANES).astype(BF16)
    tasks = [expand_bias(table_ref, padded, strip, bias), *[project(br) for br in range(blocks_r)]]
    tasks += [weights(), *[convolve(br) for br in range(blocks_r)]]
    weave(tasks, 3)


def edge_kernel(
    top_ref, bottom_ref, left_ref, right_ref, gain1_ref,
    bias, query, kv, base, own_x, wkv, wp, wc, w1, w2, g2,
    corner_base, corner_x, corner_q, folded, out_edge, out_mid,
    bands_r, bands_c, fixes, kv_edge,
):
    cols, channels = top_ref.shape[1:]
    rows = left_ref.shape[0]
    head_dim = channels // HEADS
    row, last_row = lax.axis_index("row"), lax.axis_size("row") - 1
    col, last_col = lax.axis_index("col"), lax.axis_size("col") - 1
    gain1 = gain1_ref[...]
    outside = [(row == 0).astype(F32), (row == last_row).astype(F32),
               (col == 0).astype(F32), (col == last_col).astype(F32)]

    bands_r[...] = jnp.zeros_like(bands_r)
    bands_c[...] = jnp.zeros_like(bands_c)
    sides = []

    def band(i):
        ref = (top_ref, bottom_ref, left_ref, right_ref)[i]
        mark = jnp.broadcast_to(marks(channels, outside[i])[None], (*ref.shape[:2], HALF))
        values = layer_norm(ref[...].astype(F32), gain1 * (1.0 - outside[i]))
        if i < 2:
            bands_r[i, :, SHIFT : SHIFT + cols, HALF:] = mark
            bands_r[i, :, SHIFT : SHIFT + cols, 0:channels] = values
            pixels = bands_r[i, :, SHIFT : SHIFT + cols]
            count = cols // SIDE
            blocks = [pixels[:, b * SIDE : (b + 1) * SIDE].reshape(AREA, LANES) for b in range(count)]
        else:
            bands_c[i - 2, 1 : 1 + rows, :, HALF:] = mark
            bands_c[i - 2, 1 : 1 + rows, :, 0:channels] = values
            count = rows // SIDE
            blocks = [bands_c[i - 2, 1 : 1 + rows].reshape(-1, LANES)]
        pixels = jnp.concatenate(blocks, axis=0).astype(BF16)
        yield
        both = dot(pixels, wkv[...])
        yield
        kv_edge[i] = both.astype(BF16).reshape(count, AREA, 2 * LANES)
        sides.append(i)

    keys = [
        lambda: [kv_edge[0, 1], kv[0, 1], kv_edge[0, 2], kv[0, 2]],
        lambda: [kv[3, 1], kv_edge[1, 1], kv[3, 2], kv_edge[1, 2]],
        lambda: [kv_edge[2, 1], kv_edge[2, 2], kv[1, 0], kv[2, 0]],
        lambda: [kv[1, 3], kv[2, 3], kv_edge[3, 1], kv_edge[3, 2]],
        lambda: [kv[1, 1], kv[2, 1], kv[1, 2], kv[2, 2]],
    ]
    places = [((0, 1), (0, 2)), ((3, 1), (3, 2)), ((1, 0), (2, 0)), ((1, 3), (2, 3))]
    places += [((1, 1), (1, 2)), ((2, 1), (2, 2))]
    quadrants = [((1, 0), (1, 1)), ((0, 0), (0, 1)), ((0, 1), (1, 1)), ((0, 0), (1, 0))]
    quadrants += [((0, 0), (0, 1)), ((1, 0), (1, 1))]
    done = {}

    def unit(i):
        def put(result):
            done[i] = result

        window = keys[min(i, 4)]
        parts = ([query[at] for at in places[i]], quadrants[i], lambda: jnp.concatenate(window(), axis=0))
        make = lambda: attend(parts, bias, head_dim, channels, put)
        return after(lambda: i >= 4 or i in sides, make)

    def tail(i):
        def put(out):
            if i == 4:
                out_mid[...] = out
            else:
                out_edge[i // 2] = out

        def part(at):
            return base[at] if i == 4 else corrected(base, fixes, at)

        def make():
            return finish(
                jnp.concatenate([done[i], done[i + 1]], axis=0),
                lambda: jnp.concatenate([part(at) for at in (*places[i], *places[i + 1])], axis=0),
                wp, g2[...], w1, w2, channels, put,
            )

        return after(lambda: i in done and i + 1 in done, make)

    def fix(i):
        taps = ((0, 1, 2), (6, 7, 8), (0, 3, 6), (2, 5, 8))[i]
        source = (SHIFT - 1, 0)[i % 2]
        if i < 2:
            pieces = [bands_r[i, source, SHIFT - 1 + t : SHIFT - 1 + t + cols] for t in range(3)]
        else:
            pieces = [bands_c[i - 2, t : t + rows, source] for t in range(3)]
        weights = jnp.concatenate([wc[t * LANES : (t + 1) * LANES] for t in taps], axis=0)
        fixes[i] = dot(jnp.concatenate(pieces, axis=1).astype(BF16), weights)
        yield

    def corners():
        tops = [bands_r[i, :, SHIFT + c : SHIFT + c + SIDE] for i in range(2) for c in (0, cols - SIDE)]
        lefts = [bands_c[i, 1 + r : 1 + r + SIDE] for r in (0, rows - SIDE) for i in range(2)]
        for i, at in enumerate(((0, 0), (0, 3), (3, 0), (3, 3))):
            corner_base[i] = corrected(base, fixes, at)
            slots = ((1, 2, 3), (3, 0, 1), (0, 3, 2), (2, 1, 0))[i]
            corner_x[i, slots[0]] = lefts[i].reshape(AREA, LANES).astype(BF16)
            corner_x[i, slots[1]] = tops[i].reshape(AREA, LANES).astype(BF16)
            corner_x[i, slots[2]] = own_x[i]
            yield
            corner_q[i] = dot_nt(by_head(query[at], head_dim, channels), wkv[:, :LANES]).astype(BF16)
            yield
        lane = lanes_of()
        for h in range(HEADS):
            mine = one_hot((lane >= h * head_dim) & (lane < (h + 1) * head_dim))
            folded[h * LANES : (h + 1) * LANES] = dot(wkv[:, LANES:] * mine, wp[...]).astype(BF16)
            yield

    weave(
        [unit(4), band(0), band(1), unit(5), band(2), band(3), unit(0), fix(0), unit(1), fix(1), tail(4),
         unit(2), fix(2), unit(3), fix(3), tail(0), corners(), tail(2)],
        3,
    )


def corrected(base, fixes, at):
    br, bc = at
    block = base[at].reshape(SIDE, SIDE, LANES)
    y = lax.broadcasted_iota(jnp.int32, (SIDE, SIDE, 1), 0)
    x = lax.broadcasted_iota(jnp.int32, (SIDE, SIDE, 1), 1)
    if br in (0, 3):
        fix = fixes[0 if br == 0 else 1, bc * SIDE : (bc + 1) * SIDE]
        block = block + jnp.where(y == (0 if br == 0 else SIDE - 1), fix[None], 0.0)
    if bc in (0, 3):
        fix = fixes[2 if bc == 0 else 3, br * SIDE : (br + 1) * SIDE]
        block = block + jnp.where(x == (0 if bc == 0 else SIDE - 1), fix[:, None], 0.0)
    return block.reshape(AREA, LANES)


def corner_kernel(
    left_ref, right_ref, gain1_ref,
    bias, corner_x, corner_q, folded, wc, w1, w2, g2, corner_base, out_mid, out_edge,
    out_hbm,
    normed, out_ref, sems,
):
    rows, _, channels = out_ref.shape
    head_dim = channels // HEADS

    def finish_bands(which, corners):
        def piece(source, i):
            return source[i * AREA : (i + 1) * AREA]

        for br in which:
            if br in (0, 3):
                i = 0 if br == 0 else 2
                band = [corners[0], piece(out_edge.at[0], i), piece(out_edge.at[0], i + 1), corners[1]]
            else:
                i = br - 1
                band = [piece(out_edge.at[1], i), piece(out_mid, 2 * i), piece(out_mid, 2 * i + 1),
                        piece(out_edge.at[1], i + 2)]
            band = [part[:, :channels].reshape(SIDE, SIDE, channels) for part in band]
            out_ref[br * SIDE : (br + 1) * SIDE] = jnp.concatenate(band, axis=1).astype(BF16)

    finish_bands((1, 2), None)
    inner = slice(SIDE, rows - SIDE)
    writes = [pltpu.make_async_copy(out_ref.at[inner], out_hbm.at[inner], sems.at[0])]
    writes[0].start()
    row, last_row = lax.axis_index("row"), lax.axis_size("row") - 1
    col, last_col = lax.axis_index("col"), lax.axis_size("col") - 1
    gain1 = gain1_ref[...]
    out_row = [(row == 0).astype(F32), (row == last_row).astype(F32)]
    out_col = [(col == 0).astype(F32), (col == last_col).astype(F32)]
    corner, done = {}, {}

    def norm(i):
        ref = (left_ref, right_ref)[i % 2]
        inside = (1.0 - out_row[i // 2]) * (1.0 - out_col[i % 2])
        mark = marks(channels, out_row[i // 2] + out_col[i % 2])
        normed[i, :, HALF:] = jnp.broadcast_to(mark, (AREA, HALF))
        values = ref[i // 2 * SIDE : (i // 2 + 1) * SIDE].astype(F32)
        normed[i, :, 0:channels] = layer_norm(values.reshape(AREA, channels), gain1 * inside)
        corner[i] = normed[i].astype(BF16)

    def unit(i):
        norm(i)
        yield
        slot = (0, 2, 1, 3)[i]
        blocks = [corner[i] if b == slot else corner_x[i, b] for b in range(4)]
        pixels = jnp.concatenate(blocks, axis=0)
        scores = dot_nt(corner_q[i], pixels).reshape(HEADS, AREA, WIN * WIN)
        yield
        weights, total = softmax(scores, bias[:, 1 - i // 2, 1 - i % 2])
        yield
        mixed = dot(weights.reshape(HEADS * AREA, WIN * WIN), pixels).reshape(HEADS, AREA, LANES)
        yield
        mixed = (mixed / total).astype(BF16)
        done[i] = jnp.concatenate([mixed[h] for h in range(HEADS)], axis=1)

    def whole(i):
        tap, y, x = ((0, 7, 7), (2, 7, 0), (6, 0, 7), (8, 0, 0))[i]
        start = y * SIDE
        term = dot(normed[i, start : start + SIDE].astype(BF16), wc[tap * LANES : (tap + 1) * LANES])
        term = term[x : x + 1]
        pixel = lax.broadcasted_iota(jnp.int32, (AREA, 1), 0)
        at = (SIDE - 1 - y) * SIDE + SIDE - 1 - x
        return corner_base[i] + jnp.where(pixel == at, term, 0.0)

    def tail(i):
        def put(out):
            finish_bands((0,) if i == 0 else (3,), [out[:AREA], out[AREA:]])

        def make():
            return finish(
                jnp.concatenate([done[i], done[i + 1]], axis=0),
                lambda: jnp.concatenate([whole(i), whole(i + 1)], axis=0),
                folded, g2[...], w1, w2, channels, put,
            )

        return after(lambda: i in done and i + 1 in done, make)

    weave([unit(0), unit(1), unit(2), unit(3), tail(0), tail(2)], 4)
    writes[0].wait()
    for r in (0, rows - SIDE):
        at = slice(r, r + SIDE)
        write = pltpu.make_async_copy(out_ref.at[at], out_hbm.at[at], sems.at[1 if r == 0 else 2])
        write.start()
        writes.append(write)
    writes[1].wait()
    writes[2].wait()


def exchange(low, high, axis):
    count = lax.axis_size(axis)
    before = lax.ppermute(high, axis, [(i, (i + 1) % count) for i in range(count)])
    after = lax.ppermute(low, axis, [((i + 1) % count, i) for i in range(count)])
    return before, after


def call(kernel, name, outs, scratch, flops, operands, in_hbm=()):
    vmem = pl.BlockSpec(memory_space=pltpu.VMEM)
    hbm = pl.BlockSpec(memory_space=pltpu.HBM)
    return pl.pallas_call(
        kernel,
        out_shape=[out if isinstance(out, jax.ShapeDtypeStruct) else pltpu.VMEM(*out) for out in outs],
        in_specs=[hbm if i in in_hbm else vmem for i in range(len(operands))],
        out_specs=[hbm if isinstance(out, jax.ShapeDtypeStruct) else vmem for out in outs],
        scratch_shapes=[pltpu.VMEM(*s) if isinstance(s, tuple) else s for s in scratch],
        cost_estimate=pl.CostEstimate(flops=flops, bytes_accessed=4_000_000, transcendentals=1_000_000),
        compiler_params=pltpu.CompilerParams(vmem_limit_bytes=24 * 1024 * 1024),
        name=name,
    )(*[pltpu.with_memory_space_constraint(x, pltpu.HBM) if i in in_hbm else x for i, x in enumerate(operands)])


def on_device(
    image, norm1_gain, norm2_gain, qkv_weight, proj_weight, rel_table, conv_weight, fc1_weight,
    fc2_weight,
):
    rows, cols, channels = image.shape
    blocks_r, blocks_c = rows // SIDE, cols // SIDE
    gain1, gain2, fc2, table = norm1_gain[None], norm2_gain[None], fc2_weight.T, rel_table.T
    band, column = ((SHIFT, cols, channels), BF16), ((rows, SHIFT, channels), BF16)
    tile, gain1, table, qkv_weight, first_rows, last_rows, first_cols, last_cols = call(
        cut_kernel,
        "cut_halo",
        [(image.shape, BF16), (gain1.shape, F32), (table.shape, F32), (qkv_weight.shape, BF16),
         band, band, column, column],
        [pltpu.SemaphoreType.DMA((4,))],
        1_000_000,
        (image, gain1, table, qkv_weight),
        range(4),
    )
    top, bottom = exchange(first_rows, last_rows, "row")
    left, right = exchange(first_cols, last_cols, "col")
    fetched = (gain2, proj_weight, conv_weight, fc1_weight, fc2)
    hidden = -(-fc1_weight.shape[1] // 128) * 128
    bias, query, kv, base, own_x, wkv, wp, wc, w1, w2, g2 = call(
        own_kernel,
        "own_tile",
        [
            ((HEADS, 2, 2, AREA, WIN * WIN), F32),
            ((blocks_r, blocks_c, AREA, LANES), BF16),
            ((blocks_r, blocks_c, AREA, 2 * LANES), BF16),
            ((blocks_r, blocks_c, AREA, LANES), F32),
            ((4, AREA, LANES), BF16),
            ((LANES, 2 * LANES), BF16),
            ((LANES, LANES), BF16),
            ((9 * LANES, LANES), BF16),
            ((LANES, hidden), BF16),
            ((hidden, LANES), BF16),
            ((1, LANES), F32),
        ],
        [
            ((8, 1024), F32),
            ((4, 8 * WIN, 128), F32),
            ((LANES, LANES), BF16),
            ((rows + 2, cols + 2 * SHIFT, LANES), F32),
            ((3, rows + 2, cols, LANES), BF16),
            *[(x.shape, x.dtype) for x in fetched],
            pltpu.SemaphoreType.DMA((len(fetched),)),
        ],
        2_000_000_000,
        (tile, gain1, table, qkv_weight, gain2, proj_weight, conv_weight, fc1_weight, fc2),
        range(4, 9),
    )
    first = jnp.concatenate([top[:, :SHIFT], bottom[:, :SHIFT]])
    last = jnp.concatenate([top[:, cols - SHIFT :], bottom[:, cols - SHIFT :]])
    left_corner, right_corner = exchange(first, last, "col")
    corner_base, corner_x, corner_q, folded, out_edge, out_mid = call(
        edge_kernel,
        "edge_windows",
        [
            ((4, AREA, LANES), F32),
            ((4, 4, AREA, LANES), BF16),
            ((4, HEADS * AREA, LANES), BF16),
            ((HEADS * LANES, LANES), BF16),
            ((2, 4 * AREA, LANES), F32),
            ((4 * AREA, LANES), F32),
        ],
        [
            ((2, SHIFT, cols + 2 * SHIFT, LANES), F32),
            ((2, rows + 2, SHIFT, LANES), F32),
            ((4, cols, LANES), F32),
            ((4, blocks_c, AREA, 2 * LANES), BF16),
        ],
        2_000_000_000,
        (top, bottom, left, right, gain1, bias, query, kv, base, own_x, wkv, wp, wc, w1, w2, g2),
    )
    (out,) = call(
        corner_kernel,
        "corner_windows",
        [jax.ShapeDtypeStruct(image.shape, BF16)],
        [((4, AREA, LANES), F32), (image.shape, BF16), pltpu.SemaphoreType.DMA((3,))],
        1_000_000_000,
        (left_corner, right_corner, gain1, bias, corner_x, corner_q, folded, wc, w1, w2, g2,
         corner_base, out_mid, out_edge),
    )
    return out


def solution(mesh):
    placed = (P("row", "col", None), P(), P(), P(), P(), P(), P(), P(), P())
    return jax.shard_map(
        on_device, mesh=mesh, in_specs=placed, out_specs=P("row", "col", None), check_vma=False
    )
```

```python
import math

import jax
import jax.numpy as jnp
from jax import lax
from jax.experimental import pallas as pl
from jax.experimental.pallas import tpu as pltpu
from jax.sharding import PartitionSpec as P

HEADS = 6
WIN = 16
SHIFT = 8
SIDE = 8
AREA = SIDE * SIDE
LANES = 256
HALF = LANES // 2
F32 = jnp.float32
BF16 = jnp.bfloat16
LOG2E = math.log2(math.e)
MASKED = -4.0e9


def weave(tasks, width):
    waiting, active = list(tasks), []
    while waiting or active:
        while waiting and len(active) < width:
            active.append(waiting.pop(0))
        for task in list(active):
            try:
                next(task)
            except StopIteration:
                active.remove(task)


def layer_norm(values, norm_gain):
    centre = jnp.mean(values, axis=-1, keepdims=True)
    values = values - centre
    spread = jnp.mean(values * values, axis=-1, keepdims=True)
    return values * lax.rsqrt(spread + 1e-05) * norm_gain


def layer_norm_padded(values, norm_gain, channels):
    centre = jnp.sum(values, axis=-1, keepdims=True) * (1.0 / channels)
    values = jnp.where(lanes_of() < channels, values - centre, 0.0)
    spread = jnp.sum(values * values, axis=-1, keepdims=True) * (1.0 / channels)
    return values * lax.rsqrt(spread + 1e-05) * norm_gain


def dot(a, b):
    return jnp.dot(a, b, preferred_element_type=F32)


def dot_nt(a, b):
    return lax.dot_general(a, b, (((1,), (1,)), ((), ())), preferred_element_type=F32)


def one_hot(condition):
    return jnp.where(condition, 1.0, 0.0).astype(BF16)


def gelu(x):
    square = jnp.minimum(x * x, 25.0)
    poly = -5.58203231240273e-08
    for factor in (2.777085437695777e-06, -4.707012890217347e-05, -5.859274357446709e-05,
                   0.036366718434813275, 0.7978721905787034):
        poly = poly * square + factor
    half = 0.5 * x
    return half + half * jnp.tanh(x * poly)


def lanes_of(width=LANES):
    return lax.broadcasted_iota(jnp.int32, (1, width), 1)


def marks(channels, outside):
    half = lanes_of()[:, HALF:]
    return jnp.where(half == channels + 1, 1.0, 0.0) + jnp.where(half == channels, outside, 0.0)


def expand_bias(table_ref, padded, strip, bias):
    span = 2 * WIN - 1
    padded[...] = jnp.zeros_like(padded)
    padded[0:HEADS, 0 : span * span] = table_ref[...] * LOG2E
    table = padded[...]
    width = padded.shape[1]
    shifted = jnp.concatenate(
        [table if px == 0 else pltpu.roll(table, width - px, 1) for px in range(WIN)], axis=0
    )
    high = shifted.astype(BF16)
    low = (shifted - high.astype(F32)).astype(BF16)
    yield
    entry = lax.broadcasted_iota(jnp.int32, (width, 512), 0)
    place = lax.broadcasted_iota(jnp.int32, (1, 512), 1)
    column = lax.div(place, 256) * SIDE + lax.rem(place, SIDE)
    wanted = (span - 1 - lax.div(lax.rem(place, 256), SIDE)) * span + WIN - 1 - column
    picked = dot(jnp.concatenate([high, low], axis=0), one_hot(entry == wanted))
    yield
    half = 8 * WIN
    picked = picked[:half] + picked[half:]
    for tile in range(4):
        strip[tile] = picked[:, 128 * tile : 128 * (tile + 1)]
    for head in range(HEADS):
        yield
        for half in range(2):
            rows = jnp.concatenate(
                [strip[2 * half + t, pl.ds(head, WIN, stride=8), :] for t in range(2)], axis=1
            )
            for py in range(WIN):
                start = (WIN - 1 - py) * SIDE
                rolled = (rows if start == 0 else pltpu.roll(rows, 256 - start, 1))[:, 0:128]
                lanes = slice(128 * half, 128 * (half + 1))
                place = slice(py % SIDE * SIDE, (py % SIDE + 1) * SIDE)
                bias[head, py // SIDE, 0, place, lanes] = rolled[:SIDE]
                bias[head, py // SIDE, 1, place, lanes] = rolled[SIDE:]


def scores_of(blocks, keys, head_dim, channels):
    lane = lanes_of()
    part = jnp.concatenate(blocks, axis=0)
    own = [(lane >= h * head_dim) & (lane < (h + 1) * head_dim) for h in range(HEADS)]
    stacked = jnp.concatenate(
        [part * one_hot(own[h] | (lane == channels)) for h in range(HEADS)], axis=0
    )
    return dot_nt(stacked, keys)


def attend(unit, bias, head_dim, channels, put):
    lane = lanes_of()
    blocks, quadrants, pair = unit
    pair = pair()
    scores = scores_of(blocks, pair[:, :LANES], head_dim, channels)
    count = scores.shape[0] // HEADS
    yield
    part_bias = jnp.concatenate([bias[:, hy, hx] for hy, hx in quadrants], axis=1)
    scores = scores.reshape(HEADS, count, WIN * WIN) + part_bias
    scores = scores - jnp.max(scores, axis=-1, keepdims=True)
    weights = jnp.exp2(scores)
    total = jnp.sum(weights, axis=-1, keepdims=True)
    weights = weights.astype(BF16).reshape(HEADS * count, WIN * WIN)
    yield
    mixed = dot(weights, pair[:, LANES:])
    yield
    result, divisor = mixed[0:count], jnp.broadcast_to(total[0], (count, LANES))
    for h in range(1, HEADS):
        mine = (lane >= h * head_dim) & (lane < (h + 1) * head_dim)
        result = jnp.where(mine, mixed[h * count : (h + 1) * count], result)
        divisor = jnp.where(mine, total[h], divisor)
    put((result / divisor).astype(BF16))


def finish(heads_out, base, wp, gain2, w1, w2, channels, put):
    attended = dot(heads_out, wp[...])
    yield
    state1 = base() + attended.astype(BF16).astype(F32)
    normed2 = layer_norm_padded(state1, gain2, channels).astype(BF16)
    yield
    hidden = dot(normed2, w1[...])
    yield
    hidden = gelu(hidden).astype(BF16)
    yield
    put(state1 + dot(hidden, w2[...]))


def after(ready, make):
    while not ready():
        yield
    yield from make()


def pack(pixels, spare):
    rows, cols, channels = pixels.shape
    spare[...] = jnp.zeros_like(spare)
    spare[:, :, 0:channels] = pixels
    rest = spare[:, :, HALF:]
    second = pltpu.roll(rest[:, cols // 2 :].reshape(-1, HALF), HALF // 2, 1)
    both = rest[:, : cols // 2] + second.reshape(rows, cols // 2, HALF)
    return jnp.concatenate([spare[:, :, :HALF], both], axis=1).astype(BF16)


def unpack(main, rest, turned, channels):
    if turned:
        rest = pltpu.roll(rest.reshape(-1, HALF), HALF // 2, 1).reshape(rest.shape)
    return jnp.concatenate([main, rest], axis=2)[:, :, :channels]


def cut_kernel(
    image_hbm, gain1_hbm, table_hbm, qkv_hbm, image_ref, gain1_ref, table_ref, qkv_ref,
    top, bottom, left, right, spare, sems,
):
    rows, cols, _ = image_ref.shape
    fetches = [
        pltpu.make_async_copy(source, target, sems.at[i])
        for i, (source, target) in enumerate(
            ((image_hbm, image_ref), (gain1_hbm, gain1_ref), (table_hbm, table_ref), (qkv_hbm, qkv_ref))
        )
    ]
    for fetch in fetches:
        fetch.start()
    for fetch in fetches:
        fetch.wait()
    top[...] = pack(image_ref[:SHIFT].astype(F32), spare.at[0])
    bottom[...] = pack(image_ref[rows - SHIFT :].astype(F32), spare.at[1])
    for r in range(0, rows, SIDE):
        band = image_ref[r : r + SIDE].astype(F32)
        left[r : r + SIDE] = band[:, :SHIFT].astype(BF16)
        right[r : r + SIDE] = band[:, cols - SHIFT :].astype(BF16)


def own_kernel(
    image_ref, gain1_ref, table_ref, qkv_ref, gain2_hbm, proj_hbm, conv_hbm, fc1_hbm, fc2_hbm,
    bias, query, kv, normed, wkv, wp, wc, w1, w2, g2,
    padded, strip, wq,
    gain2_ref, proj_ref, conv_ref, fc1_ref, fc2_ref, sems,
):
    rows, cols, channels = image_ref.shape
    head_dim = channels // HEADS
    flag_lane, one_lane = channels, channels + 1
    blocks_r, blocks_c = rows // SIDE, cols // SIDE
    fetches = [
        pltpu.make_async_copy(source, target, sems.at[i])
        for i, (source, target) in enumerate(
            ((conv_hbm, conv_ref), (proj_hbm, proj_ref), (gain2_hbm, gain2_ref), (fc1_hbm, fc1_ref),
             (fc2_hbm, fc2_ref))
        )
    ]
    for fetch in fetches:
        fetch.start()

    for ref in (wq, wkv, wp, wc, w1, w2, g2):
        ref[...] = jnp.zeros_like(ref)
    special = lax.broadcasted_iota(jnp.int32, (16, LANES), 0) + 176
    lanes16 = lax.broadcasted_iota(jnp.int32, (16, LANES), 1)
    wq[176:192, :] = one_hot((special == one_lane) & (lanes16 == flag_lane))
    wkv[176:192, 0:LANES] = jnp.where(
        (special == flag_lane) & (lanes16 == flag_lane), MASKED, 0.0
    ).astype(BF16)
    normed[:, :, HALF:] = jnp.broadcast_to(marks(channels, 0.0)[None], (rows, cols, HALF))

    gain1 = gain1_ref[...]
    scale = head_dim**-0.5 * LOG2E

    wq[0:channels, 0:channels] = qkv_ref[:, 0:channels]
    wkv[0:channels, 0:channels] = qkv_ref[:, channels : 2 * channels]
    wkv[0:channels, LANES : LANES + channels] = qkv_ref[:, 2 * channels :]

    def weights():
        for fetch in fetches:
            fetch.wait()
        wp[0:channels, 0:channels] = proj_ref[...]
        w1[0:channels, 0 : fc1_ref.shape[1]] = fc1_ref[...]
        w2[0 : fc2_ref.shape[1], 0:channels] = fc2_ref[...].astype(F32).T.astype(BF16)
        g2[:, 0:channels] = gain2_ref[...]
        for tap in range(9):
            wc[tap * LANES : tap * LANES + channels, 0:channels] = conv_ref[tap // 3, tap % 3]

    def norm(br):
        at = slice(br * SIDE, (br + 1) * SIDE)
        normed[at, :, 0:channels] = layer_norm(image_ref[at].astype(F32), gain1)

    def project(br):
        pixels = normed[br * SIDE : (br + 1) * SIDE].astype(BF16).reshape(-1, LANES)
        q = dot(pixels, wq[...])
        yield
        both = dot(pixels, wkv[...]).reshape(SIDE, cols, 2 * LANES)
        q = (q * scale).reshape(SIDE, cols, LANES)
        for bc in range(blocks_c):
            part = slice(bc * SIDE, (bc + 1) * SIDE)
            query[br, bc] = q[:, part].reshape(AREA, LANES).astype(BF16)
        yield
        for bc in range(blocks_c):
            part = slice(bc * SIDE, (bc + 1) * SIDE)
            kv[br, bc] = both[:, part].reshape(AREA, 2 * LANES).astype(BF16)

    for br in range(blocks_r):
        norm(br)
    weave([expand_bias(table_ref, padded, strip, bias), *[project(br) for br in range(blocks_r)]], 3)
    weights()


def edge_kernel(
    image_ref, top_ref, bottom_ref, left_ref, right_ref, gain1_ref,
    bias, query, kv, normed, wkv, wp, wc, w1, w2, g2,
    kv_edge, corner_base, out_edge, out_mid,
    halo, base, shifted,
):
    rows, cols, channels = image_ref.shape
    head_dim = channels // HEADS
    row, last_row = lax.axis_index("row"), lax.axis_size("row") - 1
    col, last_col = lax.axis_index("col"), lax.axis_size("col") - 1
    gain1 = gain1_ref[...]
    outside = [(row == 0).astype(F32), (row == last_row).astype(F32),
               (col == 0).astype(F32), (col == last_col).astype(F32)]

    for r in (0, SHIFT + rows):
        for c in (0, SHIFT + cols):
            halo[r : r + SHIFT, c : c + SHIFT] = jnp.zeros((SHIFT, SHIFT, LANES), F32)
    sides = []

    def band(i):
        ref = (top_ref, bottom_ref, left_ref, right_ref)[i]
        start = (0, SHIFT + (rows if i < 2 else cols))[i % 2]
        inner = slice(SHIFT, SHIFT + (cols if i < 2 else rows))
        outer = slice(start, start + SHIFT)
        place = (outer, inner) if i < 2 else (inner, outer)
        values = ref[...].astype(F32)
        if i < 2:
            rest, half = values[:, cols:], cols // 2
            values = jnp.concatenate(
                [unpack(values[:, :half], rest, False, channels),
                 unpack(values[:, half:cols], rest, True, channels)], axis=1
            )
        mark = jnp.broadcast_to(marks(channels, outside[i])[None], (*values.shape[:2], HALF))
        halo[(*place, slice(HALF, LANES))] = mark
        halo[(*place, slice(0, channels))] = layer_norm(values, gain1 * (1.0 - outside[i]))
        pixels = halo[place]
        if i < 2:
            blocks = [pixels[:, b * SIDE : (b + 1) * SIDE].reshape(AREA, LANES) for b in range(cols // SIDE)]
        else:
            blocks = [pixels.reshape(-1, LANES)]
        pixels = jnp.concatenate(blocks, axis=0).astype(BF16)
        yield
        both = dot(pixels, wkv[...])
        yield
        kv_edge[i] = both.astype(BF16).reshape(-1, AREA, 2 * LANES)
        sides.append(i)

    def tile():
        for r in range(0, rows, SIDE):
            halo[SHIFT + r : SHIFT + r + SIDE, SHIFT : SHIFT + cols] = normed[r : r + SIDE]
            yield

    def convolve(br):
        r = br * SIDE
        for tap in range(3):
            c0 = SHIFT - 1 + tap
            start, stop = 0 if br == 0 else r + 2, r + SIDE + 2
            shifted[tap, start:stop] = halo[
                SHIFT - 1 + start : SHIFT - 1 + stop, c0 : c0 + cols
            ].astype(BF16)
        yield
        taps = [
            shifted[tap % 3, r + tap // 3 : r + tap // 3 + SIDE].reshape(-1, LANES) for tap in range(9)
        ]
        summed = dot(jnp.concatenate(taps, axis=1), wc[...])
        yield
        summed = summed[:, :channels].reshape(SIDE, cols, channels)
        summed = summed + image_ref[r : r + SIDE].astype(F32)
        for bc in range(cols // SIDE):
            part = summed[:, bc * SIDE : (bc + 1) * SIDE].reshape(AREA, channels)
            if (br, bc) in corners:
                ref = corner_base.at[corners.index((br, bc))]
            else:
                ref = base.at[br, bc]
            ref[:, HALF:] = jnp.zeros((AREA, HALF), F32)
            ref[:, 0:channels] = part

    corners = [(0, 0), (0, 3), (3, 0), (3, 3)]
    keys = [
        lambda: [kv_edge[0, 1], kv[0, 1], kv_edge[0, 2], kv[0, 2]],
        lambda: [kv[3, 1], kv_edge[1, 1], kv[3, 2], kv_edge[1, 2]],
        lambda: [kv_edge[2, 1], kv_edge[2, 2], kv[1, 0], kv[2, 0]],
        lambda: [kv[1, 3], kv[2, 3], kv_edge[3, 1], kv_edge[3, 2]],
        lambda: [kv[1, 1], kv[2, 1], kv[1, 2], kv[2, 2]],
    ]
    places = [((0, 1), (0, 2)), ((3, 1), (3, 2)), ((1, 0), (2, 0)), ((1, 3), (2, 3))]
    places += [((1, 1), (1, 2)), ((2, 1), (2, 2))]
    quadrants = [((1, 0), (1, 1)), ((0, 0), (0, 1)), ((0, 1), (1, 1)), ((0, 0), (1, 0))]
    quadrants += [((0, 0), (0, 1)), ((1, 0), (1, 1))]
    done = {}

    def unit(i):
        def put(result):
            done[i] = result

        window = keys[min(i, 4)]
        parts = ([query[at] for at in places[i]], quadrants[i], lambda: jnp.concatenate(window(), axis=0))
        make = lambda: attend(parts, bias, head_dim, channels, put)
        return after(lambda: i >= 4 or i in sides, make)

    def tail(i):
        def put(out):
            if i == 4:
                out_mid[...] = out
            else:
                out_edge[i // 2] = out

        def make():
            return finish(
                jnp.concatenate([done[i], done[i + 1]], axis=0),
                lambda: jnp.concatenate([base[at] for at in (*places[i], *places[i + 1])], axis=0),
                wp, g2[...], w1, w2, channels, put,
            )

        return after(lambda: i in done and i + 1 in done, make)

    weave(
        [unit(4), band(0), band(1), unit(5), band(2), band(3), tile(), unit(0), convolve(0), unit(1),
         convolve(1), unit(2), convolve(2), unit(3), convolve(3), tail(4), tail(0), tail(2)],
        3,
    )


def corner_kernel(
    left_ref, right_ref, gain1_ref,
    bias, query, kv, wkv, wp, wc, w1, w2, g2, kv_edge, corner_base, out_mid, out_edge,
    out_hbm,
    normed, out_ref, sems,
):
    rows, _, channels = out_ref.shape
    head_dim = channels // HEADS

    def finish_bands(which, corners):
        def piece(source, i):
            return source[i * AREA : (i + 1) * AREA]

        for br in which:
            if br in (0, 3):
                i = 0 if br == 0 else 2
                band = [corners[0], piece(out_edge.at[0], i), piece(out_edge.at[0], i + 1), corners[1]]
            else:
                i = br - 1
                band = [piece(out_edge.at[1], i), piece(out_mid, 2 * i), piece(out_mid, 2 * i + 1),
                        piece(out_edge.at[1], i + 2)]
            band = [part[:, :channels].reshape(SIDE, SIDE, channels) for part in band]
            out_ref[br * SIDE : (br + 1) * SIDE] = jnp.concatenate(band, axis=1).astype(BF16)

    finish_bands((1, 2), None)
    inner = slice(SIDE, rows - SIDE)
    writes = [pltpu.make_async_copy(out_ref.at[inner], out_hbm.at[inner], sems.at[0])]
    writes[0].start()
    row, last_row = lax.axis_index("row"), lax.axis_size("row") - 1
    col, last_col = lax.axis_index("col"), lax.axis_size("col") - 1
    gain1 = gain1_ref[...]
    out_row = [(row == 0).astype(F32), (row == last_row).astype(F32)]
    out_col = [(col == 0).astype(F32), (col == last_col).astype(F32)]
    corner, done = {}, {}

    def project(pair):
        for i in (2 * pair, 2 * pair + 1):
            ref = (left_ref, right_ref)[i % 2]
            inside = (1.0 - out_row[i // 2]) * (1.0 - out_col[i % 2])
            mark = marks(channels, out_row[i // 2] + out_col[i % 2])
            normed[i, :, HALF:] = jnp.broadcast_to(mark, (AREA, HALF))
            values = ref[i // 2 * SIDE : (i // 2 + 1) * SIDE].astype(F32)
            values = unpack(values[:, :SIDE], values[:, SIDE:], i % 2 == 0, channels)
            normed[i, :, 0:channels] = layer_norm(values.reshape(AREA, channels), gain1 * inside)
        yield
        both = dot(normed[2 * pair : 2 * pair + 2].reshape(-1, LANES).astype(BF16), wkv[...])
        yield
        both = both.astype(BF16)
        corner[2 * pair], corner[2 * pair + 1] = both[:AREA], both[AREA:]

    keys = [
        lambda: [corner[0], kv_edge[2, 0], kv_edge[0, 0], kv[0, 0]],
        lambda: [kv_edge[0, 3], kv[0, 3], corner[1], kv_edge[3, 0]],
        lambda: [kv_edge[2, 3], corner[2], kv[3, 0], kv_edge[1, 0]],
        lambda: [kv[3, 3], kv_edge[1, 3], kv_edge[3, 3], corner[3]],
    ]
    places = [(0, 0), (0, 3), (3, 0), (3, 3)]
    quadrants = [(1, 1), (1, 0), (0, 1), (0, 0)]

    def unit(i):
        def put(result):
            done[i] = result

        parts = ([query[places[i]]], [quadrants[i]], lambda: jnp.concatenate(keys[i](), axis=0))
        return after(lambda: i in corner, lambda: attend(parts, bias, head_dim, channels, put))

    def whole(i):
        tap, y, x = ((0, 7, 7), (2, 7, 0), (6, 0, 7), (8, 0, 0))[i]
        start = y * SIDE
        term = dot(normed[i, start : start + SIDE].astype(BF16), wc[tap * LANES : (tap + 1) * LANES])
        term = term[x : x + 1]
        pixel = lax.broadcasted_iota(jnp.int32, (AREA, 1), 0)
        at = (SIDE - 1 - y) * SIDE + SIDE - 1 - x
        return corner_base[i] + jnp.where(pixel == at, term, 0.0)

    def tail(i):
        def put(out):
            finish_bands((0,) if i == 0 else (3,), [out[:AREA], out[AREA:]])

        def make():
            return finish(
                jnp.concatenate([done[i], done[i + 1]], axis=0),
                lambda: jnp.concatenate([whole(i), whole(i + 1)], axis=0),
                wp, g2[...], w1, w2, channels, put,
            )

        return after(lambda: i in done and i + 1 in done, make)

    weave([project(0), project(1), unit(0), unit(1), unit(2), unit(3), tail(0), tail(2)], 4)
    writes[0].wait()
    for r in (0, rows - SIDE):
        at = slice(r, r + SIDE)
        write = pltpu.make_async_copy(out_ref.at[at], out_hbm.at[at], sems.at[1 if r == 0 else 2])
        write.start()
        writes.append(write)
    writes[1].wait()
    writes[2].wait()


def exchange(low, high, axis):
    count = lax.axis_size(axis)
    before = lax.ppermute(high, axis, [(i, (i + 1) % count) for i in range(count)])
    after = lax.ppermute(low, axis, [((i + 1) % count, i) for i in range(count)])
    return before, after


def call(kernel, name, outs, scratch, flops, operands, in_hbm=()):
    vmem = pl.BlockSpec(memory_space=pltpu.VMEM)
    hbm = pl.BlockSpec(memory_space=pltpu.HBM)
    return pl.pallas_call(
        kernel,
        out_shape=[out if isinstance(out, jax.ShapeDtypeStruct) else pltpu.VMEM(*out) for out in outs],
        in_specs=[hbm if i in in_hbm else vmem for i in range(len(operands))],
        out_specs=[hbm if isinstance(out, jax.ShapeDtypeStruct) else vmem for out in outs],
        scratch_shapes=[pltpu.VMEM(*s) if isinstance(s, tuple) else s for s in scratch],
        cost_estimate=pl.CostEstimate(flops=flops, bytes_accessed=4_000_000, transcendentals=1_000_000),
        compiler_params=pltpu.CompilerParams(vmem_limit_bytes=24 * 1024 * 1024),
        name=name,
    )(*[pltpu.with_memory_space_constraint(x, pltpu.HBM) if i in in_hbm else x for i, x in enumerate(operands)])


def on_device(
    image, norm1_gain, norm2_gain, qkv_weight, proj_weight, rel_table, conv_weight, fc1_weight,
    fc2_weight,
):
    rows, cols, channels = image.shape
    blocks_r, blocks_c = rows // SIDE, cols // SIDE
    gain1, gain2, fc2, table = norm1_gain[None], norm2_gain[None], fc2_weight.T, rel_table.T
    band, column = ((SHIFT, cols * 3 // 2, HALF), BF16), ((rows, SHIFT, channels), BF16)
    tile, gain1, table, qkv_weight, first_rows, last_rows, first_cols, last_cols = call(
        cut_kernel,
        "cut_halo",
        [(image.shape, BF16), (gain1.shape, F32), (table.shape, F32), (qkv_weight.shape, BF16),
         band, band, column, column],
        [((2, SHIFT, cols, LANES), F32), pltpu.SemaphoreType.DMA((4,))],
        1_000_000,
        (image, gain1, table, qkv_weight),
        range(4),
    )
    top, bottom = exchange(first_rows, last_rows, "row")
    left, right = exchange(first_cols, last_cols, "col")
    fetched = (gain2, proj_weight, conv_weight, fc1_weight, fc2)
    hidden = -(-fc1_weight.shape[1] // 128) * 128
    bias, query, kv, normed, wkv, wp, wc, w1, w2, g2 = call(
        own_kernel,
        "own_tile",
        [
            ((HEADS, 2, 2, AREA, WIN * WIN), F32),
            ((blocks_r, blocks_c, AREA, LANES), BF16),
            ((blocks_r, blocks_c, AREA, 2 * LANES), BF16),
            ((rows, cols, LANES), F32),
            ((LANES, 2 * LANES), BF16),
            ((LANES, LANES), BF16),
            ((9 * LANES, LANES), BF16),
            ((LANES, hidden), BF16),
            ((hidden, LANES), BF16),
            ((1, LANES), F32),
        ],
        [
            ((8, 1024), F32),
            ((4, 8 * WIN, 128), F32),
            ((LANES, LANES), BF16),
            *[(x.shape, x.dtype) for x in fetched],
            pltpu.SemaphoreType.DMA((len(fetched),)),
        ],
        2_000_000_000,
        (tile, gain1, table, qkv_weight, gain2, proj_weight, conv_weight, fc1_weight, fc2),
        range(4, 9),
    )
    def ends(start, rest):
        parts = [(start, start + SHIFT), (cols + rest, cols + rest + SHIFT)]
        return jnp.concatenate(
            [jnp.concatenate([x[:, a:b] for a, b in parts], axis=1) for x in (top, bottom)]
        )

    first, last = ends(0, 0), ends(cols - SHIFT, cols // 2 - SHIFT)
    left_corner, right_corner = exchange(first, last, "col")
    kv_edge, corner_base, out_edge, out_mid = call(
        edge_kernel,
        "edge_windows",
        [
            ((4, blocks_c, AREA, 2 * LANES), BF16),
            ((4, AREA, LANES), F32),
            ((2, 4 * AREA, LANES), F32),
            ((4 * AREA, LANES), F32),
        ],
        [
            ((rows + 2 * SHIFT, cols + 2 * SHIFT, LANES), F32),
            ((blocks_r, blocks_c, AREA, LANES), F32),
            ((3, rows + 2, cols, LANES), BF16),
        ],
        2_000_000_000,
        (tile, top, bottom, left, right, gain1, bias, query, kv, normed, wkv, wp, wc, w1, w2, g2),
    )
    (out,) = call(
        corner_kernel,
        "corner_windows",
        [jax.ShapeDtypeStruct(image.shape, BF16)],
        [((4, AREA, LANES), F32), (image.shape, BF16), pltpu.SemaphoreType.DMA((3,))],
        1_000_000_000,
        (left_corner, right_corner, gain1, bias, query, kv, wkv, wp, wc, w1, w2, g2,
         kv_edge, corner_base, out_mid, out_edge),
    )
    return out


def solution(mesh):
    placed = (P("row", "col", None), P(), P(), P(), P(), P(), P(), P(), P())
    return jax.shard_map(
        on_device, mesh=mesh, in_specs=placed, out_specs=P("row", "col", None), check_vma=False
    )
```

```python
import math

import jax
import jax.numpy as jnp
from jax import lax
from jax.experimental import pallas as pl
from jax.experimental.pallas import tpu as pltpu
from jax.sharding import PartitionSpec as P

HEADS = 6
WIN = 16
SHIFT = 8
SIDE = 8
AREA = SIDE * SIDE
LANES = 256
HALF = LANES // 2
F32 = jnp.float32
BF16 = jnp.bfloat16
LOG2E = math.log2(math.e)
MASKED = -4.0e9
CORNERS = [(0, 0), (0, 3), (3, 0), (3, 3)]


def weave(tasks, width):
    waiting, active = list(tasks), []
    while waiting or active:
        while waiting and len(active) < width:
            active.append(waiting.pop(0))
        for task in list(active):
            try:
                next(task)
            except StopIteration:
                active.remove(task)


def layer_norm(values, norm_gain):
    centre = jnp.mean(values, axis=-1, keepdims=True)
    values = values - centre
    spread = jnp.mean(values * values, axis=-1, keepdims=True)
    return values * lax.rsqrt(spread + 1e-05) * norm_gain


def layer_norm_padded(values, norm_gain, channels):
    centre = jnp.sum(values, axis=-1, keepdims=True) * (1.0 / channels)
    values = jnp.where(lanes_of() < channels, values - centre, 0.0)
    spread = jnp.sum(values * values, axis=-1, keepdims=True) * (1.0 / channels)
    return values * lax.rsqrt(spread + 1e-05) * norm_gain


def dot(a, b):
    return jnp.dot(a, b, preferred_element_type=F32)


def dot_nt(a, b):
    return lax.dot_general(a, b, (((1,), (1,)), ((), ())), preferred_element_type=F32)


def one_hot(condition):
    return jnp.where(condition, 1.0, 0.0).astype(BF16)


def gelu(x):
    square = jnp.minimum(x * x, 25.0)
    poly = -5.58203231240273e-08
    for factor in (2.777085437695777e-06, -4.707012890217347e-05, -5.859274357446709e-05,
                   0.036366718434813275, 0.7978721905787034):
        poly = poly * square + factor
    half = 0.5 * x
    return half + half * jnp.tanh(x * poly)


def lanes_of(width=LANES):
    return lax.broadcasted_iota(jnp.int32, (1, width), 1)


def marks(channels, outside):
    half = lanes_of()[:, HALF:]
    return jnp.where(half == channels + 1, 1.0, 0.0) + jnp.where(half == channels, outside, 0.0)


def expand_bias(table_ref, padded, strip, bias):
    span = 2 * WIN - 1
    padded[...] = jnp.zeros_like(padded)
    padded[0:HEADS, 0 : span * span] = table_ref[...] * LOG2E
    table = padded[...]
    width = padded.shape[1]
    shifted = jnp.concatenate(
        [table if px == 0 else pltpu.roll(table, width - px, 1) for px in range(WIN)], axis=0
    )
    high = shifted.astype(BF16)
    low = (shifted - high.astype(F32)).astype(BF16)
    yield
    entry = lax.broadcasted_iota(jnp.int32, (width, 512), 0)
    place = lax.broadcasted_iota(jnp.int32, (1, 512), 1)
    column = lax.div(place, 256) * SIDE + lax.rem(place, SIDE)
    wanted = (span - 1 - lax.div(lax.rem(place, 256), SIDE)) * span + WIN - 1 - column
    picked = dot(jnp.concatenate([high, low], axis=0), one_hot(entry == wanted))
    yield
    half = 8 * WIN
    picked = picked[:half] + picked[half:]
    for tile in range(4):
        strip[tile] = picked[:, 128 * tile : 128 * (tile + 1)]
    for head in range(HEADS):
        yield
        for half in range(2):
            rows = jnp.concatenate(
                [strip[2 * half + t, pl.ds(head, WIN, stride=8), :] for t in range(2)], axis=1
            )
            for py in range(0, WIN, 2):
                start = (WIN - 1 - py) * SIDE
                pair = [pltpu.roll(rows, 256 - start, 1)[:, 0:128]]
                start -= SIDE
                pair.append((rows if start == 0 else pltpu.roll(rows, 256 - start, 1))[:, 0:128])
                lanes = slice(128 * half, 128 * (half + 1))
                place = slice(py % SIDE * SIDE, (py % SIDE + 2) * SIDE)
                for hx in range(2):
                    part = [rolled[hx * SIDE : (hx + 1) * SIDE] for rolled in pair]
                    bias[head, py // SIDE, hx, place, lanes] = jnp.concatenate(part, axis=0).astype(BF16)


def scores_of(blocks, keys, head_dim, channels):
    lane = lanes_of()
    part = jnp.concatenate(blocks, axis=0)
    own = [(lane >= h * head_dim) & (lane < (h + 1) * head_dim) for h in range(HEADS)]
    stacked = jnp.concatenate(
        [part * one_hot(own[h] | (lane == channels)) for h in range(HEADS)], axis=0
    )
    return dot_nt(stacked, keys)


def attend(unit, bias, head_dim, channels, put):
    lane = lanes_of()
    blocks, quadrants, pair = unit
    pair = pair()
    scores = scores_of(blocks, pair[:, :LANES], head_dim, channels)
    count = scores.shape[0] // HEADS
    yield
    part_bias = jnp.concatenate([bias[:, hy, hx] for hy, hx in quadrants], axis=1).astype(F32)
    scores = scores.reshape(HEADS, count, WIN * WIN) + part_bias
    scores = scores - jnp.max(scores, axis=-1, keepdims=True)
    weights = jnp.exp2(scores)
    total = jnp.sum(weights, axis=-1, keepdims=True)
    weights = weights.astype(BF16).reshape(HEADS * count, WIN * WIN)
    yield
    mixed = dot(weights, pair[:, LANES:])
    yield
    result, divisor = mixed[0:count], jnp.broadcast_to(total[0], (count, LANES))
    for h in range(1, HEADS):
        mine = (lane >= h * head_dim) & (lane < (h + 1) * head_dim)
        result = jnp.where(mine, mixed[h * count : (h + 1) * count], result)
        divisor = jnp.where(mine, total[h], divisor)
    put((result / divisor).astype(BF16))


def finish(heads_out, base, wp, gain2, w1, w2, channels, put):
    attended = dot(heads_out, wp[...])
    yield
    state1 = base() + attended.astype(BF16).astype(F32)
    normed2 = layer_norm_padded(state1, gain2, channels).astype(BF16)
    yield
    hidden = dot(normed2, w1[...])
    yield
    hidden = gelu(hidden).astype(BF16)
    yield
    put(state1 + dot(hidden, w2[...]))


def after(ready, make):
    while not ready():
        yield
    yield from make()


def pack(pixels, spare):
    rows, cols, channels = pixels.shape
    spare[...] = jnp.zeros_like(spare)
    spare[:, :, 0:channels] = pixels
    rest = spare[:, :, HALF:]
    second = pltpu.roll(rest[:, cols // 2 :].reshape(-1, HALF), HALF // 2, 1)
    both = rest[:, : cols // 2] + second.reshape(rows, cols // 2, HALF)
    return jnp.concatenate([spare[:, :, :HALF], both], axis=1).astype(BF16)


def unpack(main, rest, turned, channels):
    if turned:
        rest = pltpu.roll(rest.reshape(-1, HALF), HALF // 2, 1).reshape(rest.shape)
    return jnp.concatenate([main, rest], axis=2)[:, :, :channels]


def cut_kernel(
    image_hbm, gain1_hbm, table_hbm, qkv_hbm, image_ref, gain1_ref, table_ref, qkv_ref,
    top, bottom, left, right, spare, sems,
):
    rows, cols, _ = image_ref.shape
    fetches = [
        pltpu.make_async_copy(source, target, sems.at[i])
        for i, (source, target) in enumerate(
            ((image_hbm, image_ref), (gain1_hbm, gain1_ref), (table_hbm, table_ref), (qkv_hbm, qkv_ref))
        )
    ]
    for fetch in fetches:
        fetch.start()
    for fetch in fetches:
        fetch.wait()
    top[...] = pack(image_ref[:SHIFT].astype(F32), spare.at[0])
    bottom[...] = pack(image_ref[rows - SHIFT :].astype(F32), spare.at[1])
    for r in range(0, rows, SIDE):
        band = image_ref[r : r + SIDE].astype(F32)
        left[r : r + SIDE] = band[:, :SHIFT].astype(BF16)
        right[r : r + SIDE] = band[:, cols - SHIFT :].astype(BF16)


def own_kernel(
    image_ref, gain1_ref, table_ref, qkv_ref, gain2_hbm, proj_hbm, conv_hbm, fc1_hbm, fc2_hbm,
    bias, query, kv, normed, q_corner, kv_corner, wkv, wp, wc, w1, w2, g2,
    padded, strip, wq, normed32,
    gain2_ref, proj_ref, conv_ref, fc1_ref, fc2_ref, sems,
):
    rows, cols, channels = image_ref.shape
    head_dim = channels // HEADS
    flag_lane, one_lane = channels, channels + 1
    blocks_r, blocks_c = rows // SIDE, cols // SIDE
    fetches = [
        pltpu.make_async_copy(source, target, sems.at[i])
        for i, (source, target) in enumerate(
            ((conv_hbm, conv_ref), (proj_hbm, proj_ref), (gain2_hbm, gain2_ref), (fc1_hbm, fc1_ref),
             (fc2_hbm, fc2_ref))
        )
    ]
    for fetch in fetches:
        fetch.start()

    for ref in (wq, wkv, wp, wc, w1, w2, g2):
        ref[...] = jnp.zeros_like(ref)
    special = lax.broadcasted_iota(jnp.int32, (16, LANES), 0) + 176
    lanes16 = lax.broadcasted_iota(jnp.int32, (16, LANES), 1)
    wq[176:192, :] = one_hot((special == one_lane) & (lanes16 == flag_lane))
    wkv[176:192, 0:LANES] = jnp.where(
        (special == flag_lane) & (lanes16 == flag_lane), MASKED, 0.0
    ).astype(BF16)
    normed32[:, :, HALF:] = jnp.broadcast_to(marks(channels, 0.0)[None], (rows, cols, HALF))

    gain1 = gain1_ref[...]
    scale = head_dim**-0.5 * LOG2E

    wq[0:channels, 0:channels] = qkv_ref[:, 0:channels]
    wkv[0:channels, 0:channels] = qkv_ref[:, channels : 2 * channels]
    wkv[0:channels, LANES : LANES + channels] = qkv_ref[:, 2 * channels :]

    def weights():
        for fetch in fetches:
            fetch.wait()
        wp[0:channels, 0:channels] = proj_ref[...]
        w1[0:channels, 0 : fc1_ref.shape[1]] = fc1_ref[...]
        w2[0 : fc2_ref.shape[1], 0:channels] = fc2_ref[...].astype(F32).T.astype(BF16)
        g2[:, 0:channels] = gain2_ref[...]
        for tap in range(9):
            wc[tap * LANES : tap * LANES + channels, 0:channels] = conv_ref[tap // 3, tap % 3]

    def norm(br):
        at = slice(br * SIDE, (br + 1) * SIDE)
        normed32[at, :, 0:channels] = layer_norm(image_ref[at].astype(F32), gain1)
        normed[at] = normed32[at].astype(BF16)

    def project(br):
        pixels = normed[br * SIDE : (br + 1) * SIDE].reshape(-1, LANES)
        q = dot(pixels, wq[...])
        yield
        both = dot(pixels, wkv[...]).reshape(SIDE, cols, 2 * LANES)
        q = (q * scale).reshape(SIDE, cols, LANES)
        for bc in range(blocks_c):
            part = slice(bc * SIDE, (bc + 1) * SIDE)
            ref = q_corner.at[CORNERS.index((br, bc))] if (br, bc) in CORNERS else query.at[br, bc]
            ref[...] = q[:, part].reshape(AREA, LANES).astype(BF16)
        yield
        for bc in range(blocks_c):
            part = slice(bc * SIDE, (bc + 1) * SIDE)
            ref = kv_corner.at[CORNERS.index((br, bc))] if (br, bc) in CORNERS else kv.at[br, bc]
            ref[...] = both[:, part].reshape(AREA, 2 * LANES).astype(BF16)

    for br in range(blocks_r):
        norm(br)
    weave([expand_bias(table_ref, padded, strip, bias), *[project(br) for br in range(blocks_r)]], 3)
    weights()


def edge_kernel(
    image_ref, top_ref, bottom_ref, left_ref, right_ref, gain1_ref,
    bias, query, kv, normed, wkv, wp, wc, w1, w2, g2,
    kv_ends, corner_base, out_edge, out_mid,
    halo, base, shifted, kv_edge,
):
    rows, cols, channels = image_ref.shape
    head_dim = channels // HEADS
    row, last_row = lax.axis_index("row"), lax.axis_size("row") - 1
    col, last_col = lax.axis_index("col"), lax.axis_size("col") - 1
    gain1 = gain1_ref[...]
    outside = [(row == 0).astype(F32), (row == last_row).astype(F32),
               (col == 0).astype(F32), (col == last_col).astype(F32)]

    for r in (0, SHIFT + rows):
        for c in (0, SHIFT + cols):
            halo[r : r + SHIFT, c : c + SHIFT] = jnp.zeros((SHIFT, SHIFT, LANES), F32)
    sides = []

    def band(i):
        ref = (top_ref, bottom_ref, left_ref, right_ref)[i]
        start = (0, SHIFT + (rows if i < 2 else cols))[i % 2]
        inner = slice(SHIFT, SHIFT + (cols if i < 2 else rows))
        outer = slice(start, start + SHIFT)
        place = (outer, inner) if i < 2 else (inner, outer)
        values = ref[...].astype(F32)
        if i < 2:
            rest, half = values[:, cols:], cols // 2
            values = jnp.concatenate(
                [unpack(values[:, :half], rest, False, channels),
                 unpack(values[:, half:cols], rest, True, channels)], axis=1
            )
        mark = jnp.broadcast_to(marks(channels, outside[i])[None], (*values.shape[:2], HALF))
        halo[(*place, slice(HALF, LANES))] = mark
        halo[(*place, slice(0, channels))] = layer_norm(values, gain1 * (1.0 - outside[i]))
        pixels = halo[place]
        if i < 2:
            blocks = [pixels[:, b * SIDE : (b + 1) * SIDE].reshape(AREA, LANES) for b in range(cols // SIDE)]
        else:
            blocks = [pixels.reshape(-1, LANES)]
        pixels = jnp.concatenate(blocks, axis=0).astype(BF16)
        yield
        both = dot(pixels, wkv[...])
        yield
        both = both.astype(BF16).reshape(-1, AREA, 2 * LANES)
        kv_edge[i] = both
        kv_ends[i, 0], kv_ends[i, 1] = both[0], both[-1]
        sides.append(i)

    def tile():
        for r in range(0, rows, SIDE):
            halo[SHIFT + r : SHIFT + r + SIDE, SHIFT : SHIFT + cols] = normed[r : r + SIDE].astype(F32)
            yield

    def convolve(br):
        r = br * SIDE
        for tap in range(3):
            c0 = SHIFT - 1 + tap
            start, stop = 0 if br == 0 else r + 2, r + SIDE + 2
            shifted[tap, start:stop] = halo[
                SHIFT - 1 + start : SHIFT - 1 + stop, c0 : c0 + cols
            ].astype(BF16)
        yield
        taps = [
            shifted[tap % 3, r + tap // 3 : r + tap // 3 + SIDE].reshape(-1, LANES) for tap in range(9)
        ]
        summed = dot(jnp.concatenate(taps, axis=1), wc[...])
        yield
        summed = summed[:, :channels].reshape(SIDE, cols, channels)
        summed = summed + image_ref[r : r + SIDE].astype(F32)
        for bc in range(cols // SIDE):
            part = summed[:, bc * SIDE : (bc + 1) * SIDE].reshape(AREA, channels)
            if (br, bc) in CORNERS:
                ref = corner_base.at[CORNERS.index((br, bc))]
            else:
                ref = base.at[br, bc]
            ref[:, HALF:] = jnp.zeros((AREA, HALF), F32)
            ref[:, 0:channels] = part

    keys = [
        lambda: [kv_edge[0, 1], kv[0, 1], kv_edge[0, 2], kv[0, 2]],
        lambda: [kv[3, 1], kv_edge[1, 1], kv[3, 2], kv_edge[1, 2]],
        lambda: [kv_edge[2, 1], kv_edge[2, 2], kv[1, 0], kv[2, 0]],
        lambda: [kv[1, 3], kv[2, 3], kv_edge[3, 1], kv_edge[3, 2]],
        lambda: [kv[1, 1], kv[2, 1], kv[1, 2], kv[2, 2]],
    ]
    places = [((0, 1), (0, 2)), ((3, 1), (3, 2)), ((1, 0), (2, 0)), ((1, 3), (2, 3))]
    places += [((1, 1), (1, 2)), ((2, 1), (2, 2))]
    quadrants = [((1, 0), (1, 1)), ((0, 0), (0, 1)), ((0, 1), (1, 1)), ((0, 0), (1, 0))]
    quadrants += [((0, 0), (0, 1)), ((1, 0), (1, 1))]
    done = {}

    def unit(i):
        def put(result):
            done[i] = result

        window = keys[min(i, 4)]
        parts = ([query[at] for at in places[i]], quadrants[i], lambda: jnp.concatenate(window(), axis=0))
        make = lambda: attend(parts, bias, head_dim, channels, put)
        return after(lambda: i >= 4 or i in sides, make)

    def tail(i):
        def put(out):
            if i == 4:
                out_mid[...] = out.astype(BF16)
            else:
                out_edge[i // 2] = out.astype(BF16)

        def make():
            return finish(
                jnp.concatenate([done[i], done[i + 1]], axis=0),
                lambda: jnp.concatenate([base[at] for at in (*places[i], *places[i + 1])], axis=0),
                wp, g2[...], w1, w2, channels, put,
            )

        return after(lambda: i in done and i + 1 in done, make)

    weave(
        [unit(4), band(0), band(1), unit(5), band(2), band(3), tile(), unit(0), convolve(0), unit(1),
         convolve(1), unit(2), convolve(2), unit(3), convolve(3), tail(4), tail(0), tail(2)],
        3,
    )


def corner_kernel(
    left_ref, right_ref, gain1_ref,
    conv_hbm, bias, query, kv, wkv, wp, w1, w2, g2, kv_edge, corner_base, out_mid, out_edge,
    out_hbm,
    normed, out_ref, taps, sems,
):
    rows, _, channels = out_ref.shape
    head_dim = channels // HEADS

    def finish_bands(which, corners):
        def piece(source, i):
            return source[i * AREA : (i + 1) * AREA]

        for br in which:
            if br in (0, 3):
                i = 0 if br == 0 else 2
                band = [corners[0], piece(out_edge.at[0], i), piece(out_edge.at[0], i + 1), corners[1]]
            else:
                i = br - 1
                band = [piece(out_edge.at[1], i), piece(out_mid, 2 * i), piece(out_mid, 2 * i + 1),
                        piece(out_edge.at[1], i + 2)]
            band = [part[:, :channels].astype(F32).reshape(SIDE, SIDE, channels) for part in band]
            out_ref[br * SIDE : (br + 1) * SIDE] = jnp.concatenate(band, axis=1).astype(BF16)

    fetches = [
        pltpu.make_async_copy(conv_hbm.at[2 * (i // 2), 2 * (i % 2)], taps.at[i], sems.at[3 + i])
        for i in range(4)
    ]
    for fetch in fetches:
        fetch.start()
    finish_bands((1, 2), None)
    inner = slice(SIDE, rows - SIDE)
    writes = [pltpu.make_async_copy(out_ref.at[inner], out_hbm.at[inner], sems.at[0])]
    writes[0].start()
    row, last_row = lax.axis_index("row"), lax.axis_size("row") - 1
    col, last_col = lax.axis_index("col"), lax.axis_size("col") - 1
    gain1 = gain1_ref[...]
    out_row = [(row == 0).astype(F32), (row == last_row).astype(F32)]
    out_col = [(col == 0).astype(F32), (col == last_col).astype(F32)]
    corner, done = {}, {}

    def project(pair):
        for i in (2 * pair, 2 * pair + 1):
            ref = (left_ref, right_ref)[i % 2]
            inside = (1.0 - out_row[i // 2]) * (1.0 - out_col[i % 2])
            mark = marks(channels, out_row[i // 2] + out_col[i % 2])
            normed[i, :, HALF:] = jnp.broadcast_to(mark, (AREA, HALF))
            values = ref[i // 2 * SIDE : (i // 2 + 1) * SIDE].astype(F32)
            values = unpack(values[:, :SIDE], values[:, SIDE:], i % 2 == 0, channels)
            normed[i, :, 0:channels] = layer_norm(values.reshape(AREA, channels), gain1 * inside)
        yield
        both = dot(normed[2 * pair : 2 * pair + 2].reshape(-1, LANES).astype(BF16), wkv[...])
        yield
        both = both.astype(BF16)
        corner[2 * pair], corner[2 * pair + 1] = both[:AREA], both[AREA:]

    keys = [
        lambda: [corner[0], kv_edge[2, 0], kv_edge[0, 0], kv[0]],
        lambda: [kv_edge[0, 1], kv[1], corner[1], kv_edge[3, 0]],
        lambda: [kv_edge[2, 1], corner[2], kv[2], kv_edge[1, 0]],
        lambda: [kv[3], kv_edge[1, 1], kv_edge[3, 1], corner[3]],
    ]
    quadrants = [(1, 1), (1, 0), (0, 1), (0, 0)]

    def unit(i):
        def put(result):
            done[i] = result

        parts = ([query[i]], [quadrants[i]], lambda: jnp.concatenate(keys[i](), axis=0))
        return after(lambda: i in corner, lambda: attend(parts, bias, head_dim, channels, put))

    def whole(i):
        y, x = ((7, 7), (7, 0), (0, 7), (0, 0))[i]
        if i == 0:
            for fetch in fetches:
                fetch.wait()
        pixels = normed[i, y * SIDE : (y + 1) * SIDE][:, :channels].astype(BF16)
        term = jnp.pad(dot(pixels, taps[i]), ((0, 0), (0, LANES - channels)))
        term = term[x : x + 1]
        pixel = lax.broadcasted_iota(jnp.int32, (AREA, 1), 0)
        at = (SIDE - 1 - y) * SIDE + SIDE - 1 - x
        return corner_base[i] + jnp.where(pixel == at, term, 0.0)

    def tail(i):
        def put(out):
            finish_bands((0,) if i == 0 else (3,), [out[:AREA], out[AREA:]])

        def make():
            return finish(
                jnp.concatenate([done[i], done[i + 1]], axis=0),
                lambda: jnp.concatenate([whole(i), whole(i + 1)], axis=0),
                wp, g2[...], w1, w2, channels, put,
            )

        return after(lambda: i in done and i + 1 in done, make)

    weave([project(0), project(1), unit(0), unit(1), unit(2), unit(3), tail(0), tail(2)], 4)
    writes[0].wait()
    for r in (0, rows - SIDE):
        at = slice(r, r + SIDE)
        write = pltpu.make_async_copy(out_ref.at[at], out_hbm.at[at], sems.at[1 if r == 0 else 2])
        write.start()
        writes.append(write)
    writes[1].wait()
    writes[2].wait()


def exchange(low, high, axis):
    count = lax.axis_size(axis)
    before = lax.ppermute(high, axis, [(i, (i + 1) % count) for i in range(count)])
    after = lax.ppermute(low, axis, [((i + 1) % count, i) for i in range(count)])
    return before, after


def call(kernel, name, outs, scratch, flops, operands, in_hbm=()):
    vmem = pl.BlockSpec(memory_space=pltpu.VMEM)
    hbm = pl.BlockSpec(memory_space=pltpu.HBM)
    return pl.pallas_call(
        kernel,
        out_shape=[out if isinstance(out, jax.ShapeDtypeStruct) else pltpu.VMEM(*out) for out in outs],
        in_specs=[hbm if i in in_hbm else vmem for i in range(len(operands))],
        out_specs=[hbm if isinstance(out, jax.ShapeDtypeStruct) else vmem for out in outs],
        scratch_shapes=[pltpu.VMEM(*s) if isinstance(s, tuple) else s for s in scratch],
        cost_estimate=pl.CostEstimate(flops=flops, bytes_accessed=4_000_000, transcendentals=1_000_000),
        compiler_params=pltpu.CompilerParams(vmem_limit_bytes=24 * 1024 * 1024),
        name=name,
    )(*[pltpu.with_memory_space_constraint(x, pltpu.HBM) if i in in_hbm else x for i, x in enumerate(operands)])


def on_device(
    image, norm1_gain, norm2_gain, qkv_weight, proj_weight, rel_table, conv_weight, fc1_weight,
    fc2_weight,
):
    rows, cols, channels = image.shape
    blocks_r, blocks_c = rows // SIDE, cols // SIDE
    gain1, gain2, fc2, table = norm1_gain[None], norm2_gain[None], fc2_weight.T, rel_table.T
    band, column = ((SHIFT, cols * 3 // 2, HALF), BF16), ((rows, SHIFT, channels), BF16)
    tile, gain1, table, qkv_weight, first_rows, last_rows, first_cols, last_cols = call(
        cut_kernel,
        "cut_halo",
        [(image.shape, BF16), (gain1.shape, F32), (table.shape, F32), (qkv_weight.shape, BF16),
         band, band, column, column],
        [((2, SHIFT, cols, LANES), F32), pltpu.SemaphoreType.DMA((4,))],
        1_000_000,
        (image, gain1, table, qkv_weight),
        range(4),
    )
    top, bottom = exchange(first_rows, last_rows, "row")
    left, right = exchange(first_cols, last_cols, "col")
    fetched = (gain2, proj_weight, conv_weight, fc1_weight, fc2)
    hidden = -(-fc1_weight.shape[1] // 128) * 128
    bias, query, kv, normed, q_corner, kv_corner, wkv, wp, wc, w1, w2, g2 = call(
        own_kernel,
        "own_tile",
        [
            ((HEADS, 2, 2, AREA, WIN * WIN), BF16),
            ((blocks_r, blocks_c, AREA, LANES), BF16),
            ((blocks_r, blocks_c, AREA, 2 * LANES), BF16),
            ((rows, cols, LANES), BF16),
            ((4, AREA, LANES), BF16),
            ((4, AREA, 2 * LANES), BF16),
            ((LANES, 2 * LANES), BF16),
            ((LANES, LANES), BF16),
            ((9 * LANES, LANES), BF16),
            ((LANES, hidden), BF16),
            ((hidden, LANES), BF16),
            ((1, LANES), F32),
        ],
        [
            ((8, 1024), F32),
            ((4, 8 * WIN, 128), F32),
            ((LANES, LANES), BF16),
            ((rows, cols, LANES), F32),
            *[(x.shape, x.dtype) for x in fetched],
            pltpu.SemaphoreType.DMA((len(fetched),)),
        ],
        2_000_000_000,
        (tile, gain1, table, qkv_weight, gain2, proj_weight, conv_weight, fc1_weight, fc2),
        range(4, 9),
    )
    def ends(start, rest):
        parts = [(start, start + SHIFT), (cols + rest, cols + rest + SHIFT)]
        return jnp.concatenate(
            [jnp.concatenate([x[:, a:b] for a, b in parts], axis=1) for x in (top, bottom)]
        )

    first, last = ends(0, 0), ends(cols - SHIFT, cols // 2 - SHIFT)
    left_corner, right_corner = exchange(first, last, "col")
    kv_ends, corner_base, out_edge, out_mid = call(
        edge_kernel,
        "edge_windows",
        [
            ((4, 2, AREA, 2 * LANES), BF16),
            ((4, AREA, LANES), F32),
            ((2, 4 * AREA, LANES), BF16),
            ((4 * AREA, LANES), BF16),
        ],
        [
            ((rows + 2 * SHIFT, cols + 2 * SHIFT, LANES), F32),
            ((blocks_r, blocks_c, AREA, LANES), F32),
            ((3, rows + 2, cols, LANES), BF16),
            ((4, blocks_c, AREA, 2 * LANES), BF16),
        ],
        2_000_000_000,
        (tile, top, bottom, left, right, gain1, bias, query, kv, normed, wkv, wp, wc, w1, w2, g2),
    )
    (out,) = call(
        corner_kernel,
        "corner_windows",
        [jax.ShapeDtypeStruct(image.shape, BF16)],
        [((4, AREA, LANES), F32), (image.shape, BF16), ((4, channels, channels), BF16),
         pltpu.SemaphoreType.DMA((7,))],
        1_000_000_000,
        (left_corner, right_corner, gain1, conv_weight, bias, q_corner, kv_corner, wkv, wp, w1, w2, g2,
         kv_ends, corner_base, out_mid, out_edge),
        (3,),
    )
    return out


def solution(mesh):
    placed = (P("row", "col", None), P(), P(), P(), P(), P(), P(), P(), P())
    return jax.shard_map(
        on_device, mesh=mesh, in_specs=placed, out_specs=P("row", "col", None), check_vma=False
    )
```

```python
import math

import jax
import jax.numpy as jnp
from jax import lax
from jax.experimental import pallas as pl
from jax.experimental.pallas import tpu as pltpu
from jax.sharding import PartitionSpec as P

HEADS = 6
WIN = 16
SHIFT = 8
SIDE = 8
AREA = SIDE * SIDE
LANES = 256
HALF = LANES // 2
F32 = jnp.float32
BF16 = jnp.bfloat16
LOG2E = math.log2(math.e)
MASKED = -4.0e9


def weave(tasks, width):
    waiting, active = list(tasks), []
    while waiting or active:
        while waiting and len(active) < width:
            active.append(waiting.pop(0))
        for task in list(active):
            try:
                next(task)
            except StopIteration:
                active.remove(task)


def layer_norm(values, norm_gain):
    centre = jnp.mean(values, axis=-1, keepdims=True)
    values = values - centre
    spread = jnp.mean(values * values, axis=-1, keepdims=True)
    return values * lax.rsqrt(spread + 1e-05) * norm_gain


def layer_norm_padded(values, norm_gain, channels):
    centre = jnp.sum(values, axis=-1, keepdims=True) * (1.0 / channels)
    values = jnp.where(lanes_of() < channels, values - centre, 0.0)
    spread = jnp.sum(values * values, axis=-1, keepdims=True) * (1.0 / channels)
    return values * lax.rsqrt(spread + 1e-05) * norm_gain


def dot(a, b):
    return jnp.dot(a, b, preferred_element_type=F32)


def dot_nt(a, b):
    return lax.dot_general(a, b, (((1,), (1,)), ((), ())), preferred_element_type=F32)


def one_hot(condition):
    return jnp.where(condition, 1.0, 0.0).astype(BF16)


def gelu(x):
    square = jnp.minimum(x * x, 25.0)
    poly = -5.58203231240273e-08
    for factor in (2.777085437695777e-06, -4.707012890217347e-05, -5.859274357446709e-05,
                   0.036366718434813275, 0.7978721905787034):
        poly = poly * square + factor
    half = 0.5 * x
    return half + half * jnp.tanh(x * poly)


def pick(index, values):
    result = jnp.int32(values[-1])
    for i in range(len(values) - 2, -1, -1):
        result = jnp.where(index == i, jnp.int32(values[i]), result)
    return result


def lanes_of(width=LANES):
    return lax.broadcasted_iota(jnp.int32, (1, width), 1)


def marks(channels, outside):
    half = lanes_of()[:, HALF:]
    return jnp.where(half == channels + 1, 1.0, 0.0) + jnp.where(half == channels, outside, 0.0)


def expand_bias(table_ref, padded, strip, bias):
    span = 2 * WIN - 1
    padded[...] = jnp.zeros_like(padded)
    padded[0:HEADS, 0 : span * span] = table_ref[...] * LOG2E
    table = padded[...]
    width = padded.shape[1]
    shifted = jnp.concatenate(
        [table if px == 0 else pltpu.roll(table, width - px, 1) for px in range(WIN)], axis=0
    )
    high = shifted.astype(BF16)
    low = (shifted - high.astype(F32)).astype(BF16)
    entry = lax.broadcasted_iota(jnp.int32, (width, 512), 0)
    place = lax.broadcasted_iota(jnp.int32, (1, 512), 1)
    column = lax.div(place, 256) * SIDE + lax.rem(place, SIDE)
    wanted = (span - 1 - lax.div(lax.rem(place, 256), SIDE)) * span + WIN - 1 - column
    picked = dot(jnp.concatenate([high, low], axis=0), one_hot(entry == wanted))
    half = 8 * WIN
    picked = picked[:half] + picked[half:]
    for tile in range(4):
        strip[tile] = picked[:, 128 * tile : 128 * (tile + 1)]

    @pl.loop(0, HEADS)
    def _(head):
        for half in range(2):
            rows = jnp.concatenate(
                [strip[2 * half + t, pl.ds(head, WIN, stride=8), :] for t in range(2)], axis=1
            )
            lanes = slice(128 * half, 128 * (half + 1))
            for py in range(WIN):
                start = (WIN - 1 - py) * SIDE
                rolled = (rows if start == 0 else pltpu.roll(rows, 256 - start, 1))[:, 0:128]
                place = slice(py % SIDE * SIDE, (py % SIDE + 1) * SIDE)
                bias[head, py // SIDE * 2, place, lanes] = rolled[:SIDE]
                bias[head, py // SIDE * 2 + 1, place, lanes] = rolled[SIDE:]


def scores_of(blocks, keys, head_dim, channels):
    lane = lanes_of()
    part = jnp.concatenate(blocks, axis=0)
    own = [(lane >= h * head_dim) & (lane < (h + 1) * head_dim) for h in range(HEADS)]
    stacked = jnp.concatenate(
        [part * one_hot(own[h] | (lane == channels)) for h in range(HEADS)], axis=0
    )
    return dot_nt(stacked, keys)


def attend(unit, bias, head_dim, channels, put):
    lane = lanes_of()
    blocks, quadrants, pair = unit
    pair = pair()
    scores = scores_of(blocks, pair[:, :LANES], head_dim, channels)
    count = scores.shape[0] // HEADS
    yield
    part_bias = jnp.concatenate([bias[:, quadrant] for quadrant in quadrants], axis=1)
    scores = scores.reshape(HEADS, count, WIN * WIN) + part_bias
    scores = scores - jnp.max(scores, axis=-1, keepdims=True)
    weights = jnp.exp2(scores)
    total = jnp.sum(weights, axis=-1, keepdims=True)
    weights = weights.astype(BF16).reshape(HEADS * count, WIN * WIN)
    yield
    mixed = dot(weights, pair[:, LANES:])
    yield
    result, divisor = mixed[0:count], jnp.broadcast_to(total[0], (count, LANES))
    for h in range(1, HEADS):
        mine = (lane >= h * head_dim) & (lane < (h + 1) * head_dim)
        result = jnp.where(mine, mixed[h * count : (h + 1) * count], result)
        divisor = jnp.where(mine, total[h], divisor)
    put((result / divisor).astype(BF16))


def finish(heads_out, base, wp, gain2, w1, w2, channels, put):
    attended = dot(heads_out, wp[...])
    yield
    state1 = base() + attended.astype(BF16).astype(F32)
    normed2 = layer_norm_padded(state1, gain2, channels).astype(BF16)
    yield
    hidden = dot(normed2, w1[...])
    yield
    hidden = gelu(hidden).astype(BF16)
    yield
    put(state1 + dot(hidden, w2[...]))


def after(ready, make):
    while not ready():
        yield
    yield from make()


def pack(pixels, spare):
    rows, cols, channels = pixels.shape
    spare[...] = jnp.zeros_like(spare)
    spare[:, :, 0:channels] = pixels
    rest = spare[:, :, HALF:]
    second = pltpu.roll(rest[:, cols // 2 :].reshape(-1, HALF), HALF // 2, 1)
    both = rest[:, : cols // 2] + second.reshape(rows, cols // 2, HALF)
    return jnp.concatenate([spare[:, :, :HALF], both], axis=1).astype(BF16)


def unpack(main, rest, turned, channels):
    if turned:
        rest = pltpu.roll(rest.reshape(-1, HALF), HALF // 2, 1).reshape(rest.shape)
    return jnp.concatenate([main, rest], axis=2)[:, :, :channels]


def cut_kernel(
    image_hbm, gain1_hbm, table_hbm, qkv_hbm, image_ref, gain1_ref, table_ref, qkv_ref,
    top, bottom, left, right, spare, sems,
):
    rows, cols, _ = image_ref.shape
    fetches = [
        pltpu.make_async_copy(source, target, sems.at[i])
        for i, (source, target) in enumerate(
            ((image_hbm, image_ref), (gain1_hbm, gain1_ref), (table_hbm, table_ref), (qkv_hbm, qkv_ref))
        )
    ]
    for fetch in fetches:
        fetch.start()
    for fetch in fetches:
        fetch.wait()
    top[...] = pack(image_ref[:SHIFT].astype(F32), spare.at[0])
    bottom[...] = pack(image_ref[rows - SHIFT :].astype(F32), spare.at[1])
    for r in range(0, rows, SIDE):
        band = image_ref[r : r + SIDE].astype(F32)
        left[r : r + SIDE] = band[:, :SHIFT].astype(BF16)
        right[r : r + SIDE] = band[:, cols - SHIFT :].astype(BF16)


def own_kernel(
    image_ref, gain1_ref, table_ref, qkv_ref, gain2_hbm, proj_hbm, conv_hbm, fc1_hbm, fc2_hbm,
    bias, query, kv, normed, wkv, wp, wc, w1, w2, g2,
    padded, strip, wq,
    gain2_ref, proj_ref, conv_ref, fc1_ref, fc2_ref, sems,
):
    rows, cols, channels = image_ref.shape
    head_dim = channels // HEADS
    flag_lane, one_lane = channels, channels + 1
    blocks_r, blocks_c = rows // SIDE, cols // SIDE
    fetches = [
        pltpu.make_async_copy(source, target, sems.at[i])
        for i, (source, target) in enumerate(
            ((conv_hbm, conv_ref), (proj_hbm, proj_ref), (gain2_hbm, gain2_ref), (fc1_hbm, fc1_ref),
             (fc2_hbm, fc2_ref))
        )
    ]
    for fetch in fetches:
        fetch.start()

    for ref in (wq, wkv, wp, wc, w1, w2, g2):
        ref[...] = jnp.zeros_like(ref)
    special = lax.broadcasted_iota(jnp.int32, (16, LANES), 0) + 176
    lanes16 = lax.broadcasted_iota(jnp.int32, (16, LANES), 1)
    wq[176:192, :] = one_hot((special == one_lane) & (lanes16 == flag_lane))
    wkv[176:192, 0:LANES] = jnp.where(
        (special == flag_lane) & (lanes16 == flag_lane), MASKED, 0.0
    ).astype(BF16)
    normed[:, :, HALF:] = jnp.broadcast_to(marks(channels, 0.0)[None], (rows, cols, HALF))

    gain1 = gain1_ref[...]
    scale = head_dim**-0.5 * LOG2E

    wq[0:channels, 0:channels] = qkv_ref[:, 0:channels]
    wkv[0:channels, 0:channels] = qkv_ref[:, channels : 2 * channels]
    wkv[0:channels, LANES : LANES + channels] = qkv_ref[:, 2 * channels :]

    def weights():
        for fetch in fetches:
            fetch.wait()
        wp[0:channels, 0:channels] = proj_ref[...]
        w1[0:channels, 0 : fc1_ref.shape[1]] = fc1_ref[...]
        w2[0 : fc2_ref.shape[1], 0:channels] = fc2_ref[...].astype(F32).T.astype(BF16)
        g2[:, 0:channels] = gain2_ref[...]
        for tap in range(9):
            wc[tap * LANES : tap * LANES + channels, 0:channels] = conv_ref[tap // 3, tap % 3]

    @pl.loop(0, blocks_r)
    def _(br):
        at = pl.ds(br * SIDE, SIDE)
        normed[at, :, 0:channels] = layer_norm(image_ref[at].astype(F32), gain1)
        pixels = normed[at].astype(BF16).reshape(-1, LANES)
        q = (dot(pixels, wq[...]) * scale).reshape(SIDE, cols, LANES)
        both = dot(pixels, wkv[...]).reshape(SIDE, cols, 2 * LANES)
        for bc in range(blocks_c):
            part = slice(bc * SIDE, (bc + 1) * SIDE)
            query[br * blocks_c + bc] = q[:, part].reshape(AREA, LANES).astype(BF16)
            kv[br * blocks_c + bc] = both[:, part].reshape(AREA, 2 * LANES).astype(BF16)

    expand_bias(table_ref, padded, strip, bias)
    weights()


def edge_kernel(
    image_ref, top_ref, bottom_ref, left_ref, right_ref, gain1_ref,
    bias, query, kv, normed, wkv, wp, wc, w1, w2, g2,
    blocks, base, out,
    halo, shifted, heads,
):
    rows, cols, channels = image_ref.shape
    head_dim = channels // HEADS
    row, last_row = lax.axis_index("row"), lax.axis_size("row") - 1
    col, last_col = lax.axis_index("col"), lax.axis_size("col") - 1
    gain1 = gain1_ref[...]
    outside = [(row == 0).astype(F32), (row == last_row).astype(F32),
               (col == 0).astype(F32), (col == last_col).astype(F32)]

    for r in (0, SHIFT + rows):
        for c in (0, SHIFT + cols):
            halo[r : r + SHIFT, c : c + SHIFT] = jnp.zeros((SHIFT, SHIFT, LANES), F32)
    def band(i):
        ref = (top_ref, bottom_ref, left_ref, right_ref)[i]
        start = (0, SHIFT + (rows if i < 2 else cols))[i % 2]
        inner = slice(SHIFT, SHIFT + (cols if i < 2 else rows))
        outer = slice(start, start + SHIFT)
        place = (outer, inner) if i < 2 else (inner, outer)
        values = ref[...].astype(F32)
        if i < 2:
            rest, half = values[:, cols:], cols // 2
            values = jnp.concatenate(
                [unpack(values[:, :half], rest, False, channels),
                 unpack(values[:, half:cols], rest, True, channels)], axis=1
            )
        mark = jnp.broadcast_to(marks(channels, outside[i])[None], (*values.shape[:2], HALF))
        halo[(*place, slice(HALF, LANES))] = mark
        halo[(*place, slice(0, channels))] = layer_norm(values, gain1 * (1.0 - outside[i]))
        pixels = halo[place]
        if i < 2:
            parts = [pixels[:, b * SIDE : (b + 1) * SIDE].reshape(AREA, LANES) for b in range(cols // SIDE)]
        else:
            parts = [pixels.reshape(-1, LANES)]
        pixels = jnp.concatenate(parts, axis=0).astype(BF16)
        yield
        both = dot(pixels, wkv[...])
        yield
        blocks[16 + 4 * i : 20 + 4 * i] = both.astype(BF16).reshape(-1, AREA, 2 * LANES)

    weave([band(i) for i in range(4)], 4)

    @pl.loop(0, rows // SIDE)
    def _(br):
        halo[pl.ds(SHIFT + br * SIDE, SIDE), SHIFT : SHIFT + cols] = normed[pl.ds(br * SIDE, SIDE)]
        blocks[pl.ds(br * 4, 4)] = kv[pl.ds(br * 4, 4)]

    @pl.loop(0, (rows + 2) // 2)
    def _(i):
        for tap in range(3):
            c0 = SHIFT - 1 + tap
            piece = halo[pl.ds(SHIFT - 1 + 2 * i, 2), c0 : c0 + cols]
            shifted[tap, pl.ds(2 * i, 2)] = piece.astype(BF16)

    slots = [[17, 13, 25, 7, 5, 5], [1, 21, 26, 11, 9, 9], [18, 14, 4, 29, 6, 6], [2, 22, 8, 30, 10, 10]]
    places = [[1, 13, 4, 7, 5, 9], [2, 14, 8, 11, 6, 10]]
    quadrants = [[2, 0, 1, 0, 0, 2], [3, 1, 3, 2, 1, 3]]

    def unit(i):
        def put(result):
            heads[i] = result

        parts = [query[pick(i, place)] for place in places]
        pair = lambda: jnp.concatenate([blocks[pick(i, slot)] for slot in slots], axis=0)
        return attend((parts, [pick(i, q) for q in quadrants], pair), bias, head_dim, channels, put)

    def convolve(br):
        r = br * SIDE
        taps = [
            shifted[tap % 3, pl.ds(r + tap // 3, SIDE)].reshape(-1, LANES) for tap in range(9)
        ]
        summed = dot(jnp.concatenate(taps, axis=1), wc[...])
        yield
        summed = summed[:, :channels].reshape(SIDE, cols, channels)
        summed = summed + image_ref[pl.ds(r, SIDE)].astype(F32)
        for bc in range(cols // SIDE):
            base[br * 4 + bc, :, HALF:] = jnp.zeros((AREA, HALF), F32)
            part = summed[:, bc * SIDE : (bc + 1) * SIDE].reshape(AREA, channels)
            base[br * 4 + bc, :, 0:channels] = part

    @pl.loop(0, 2)
    def _(i):
        weave([unit(i), convolve(2 * i), unit(i + 2), convolve(2 * i + 1), unit(i + 4)], 5)

    @pl.loop(0, 3)
    def _(i):
        def put(result):
            out[i] = result

        parts = [base[pick(2 * i + j, place)] for j in range(2) for place in places]
        raw = heads[pl.ds(2 * i, 2)].reshape(-1, LANES)
        weave([finish(raw, lambda: jnp.concatenate(parts, axis=0), wp, g2[...], w1, w2, channels, put)], 1)


def corner_kernel(
    left_ref, right_ref, gain1_ref,
    bias, query, wkv, wp, wc, w1, w2, g2, blocks, base, out_inner,
    out_hbm,
    normed, out_ref, sems,
):
    rows, _, channels = out_ref.shape
    head_dim = channels // HEADS

    def finish_bands(which, corners):
        def piece(source, i):
            return source[i * AREA : (i + 1) * AREA]

        for br in which:
            if br in (0, 3):
                i = 0 if br == 0 else 2
                band = [corners[0], piece(out_inner.at[0], i), piece(out_inner.at[0], i + 1), corners[1]]
            else:
                i = br - 1
                band = [piece(out_inner.at[1], i), piece(out_inner.at[2], 2 * i),
                        piece(out_inner.at[2], 2 * i + 1), piece(out_inner.at[1], i + 2)]
            band = [part[:, :channels].reshape(SIDE, SIDE, channels) for part in band]
            out_ref[br * SIDE : (br + 1) * SIDE] = jnp.concatenate(band, axis=1).astype(BF16)

    finish_bands((1, 2), None)
    inner = slice(SIDE, rows - SIDE)
    writes = [pltpu.make_async_copy(out_ref.at[inner], out_hbm.at[inner], sems.at[0])]
    writes[0].start()
    row, last_row = lax.axis_index("row"), lax.axis_size("row") - 1
    col, last_col = lax.axis_index("col"), lax.axis_size("col") - 1
    gain1 = gain1_ref[...]
    out_row = [(row == 0).astype(F32), (row == last_row).astype(F32)]
    out_col = [(col == 0).astype(F32), (col == last_col).astype(F32)]
    corner, done = {}, {}

    def project(pair):
        for i in (2 * pair, 2 * pair + 1):
            ref = (left_ref, right_ref)[i % 2]
            inside = (1.0 - out_row[i // 2]) * (1.0 - out_col[i % 2])
            mark = marks(channels, out_row[i // 2] + out_col[i % 2])
            normed[i, :, HALF:] = jnp.broadcast_to(mark, (AREA, HALF))
            values = ref[i // 2 * SIDE : (i // 2 + 1) * SIDE].astype(F32)
            values = unpack(values[:, :SIDE], values[:, SIDE:], i % 2 == 0, channels)
            normed[i, :, 0:channels] = layer_norm(values.reshape(AREA, channels), gain1 * inside)
        yield
        both = dot(normed[2 * pair : 2 * pair + 2].reshape(-1, LANES).astype(BF16), wkv[...])
        yield
        both = both.astype(BF16)
        corner[2 * pair], corner[2 * pair + 1] = both[:AREA], both[AREA:]

    keys = [
        lambda: [corner[0], blocks[24], blocks[16], blocks[0]],
        lambda: [blocks[19], blocks[3], corner[1], blocks[28]],
        lambda: [blocks[27], corner[2], blocks[12], blocks[20]],
        lambda: [blocks[15], blocks[23], blocks[31], corner[3]],
    ]
    places = [0, 3, 12, 15]
    quadrants = [3, 2, 1, 0]

    def unit(i):
        def put(result):
            done[i] = result

        parts = ([query[places[i]]], [quadrants[i]], lambda: jnp.concatenate(keys[i](), axis=0))
        return after(lambda: i in corner, lambda: attend(parts, bias, head_dim, channels, put))

    def whole(i):
        tap, y, x = ((0, 7, 7), (2, 7, 0), (6, 0, 7), (8, 0, 0))[i]
        start = y * SIDE
        term = dot(normed[i, start : start + SIDE].astype(BF16), wc[tap * LANES : (tap + 1) * LANES])
        term = term[x : x + 1]
        pixel = lax.broadcasted_iota(jnp.int32, (AREA, 1), 0)
        at = (SIDE - 1 - y) * SIDE + SIDE - 1 - x
        return base[places[i]] + jnp.where(pixel == at, term, 0.0)

    def tail(i):
        def put(out):
            finish_bands((0,) if i == 0 else (3,), [out[:AREA], out[AREA:]])

        def make():
            return finish(
                jnp.concatenate([done[i], done[i + 1]], axis=0),
                lambda: jnp.concatenate([whole(i), whole(i + 1)], axis=0),
                wp, g2[...], w1, w2, channels, put,
            )

        return after(lambda: i in done and i + 1 in done, make)

    weave([project(0), project(1), unit(0), unit(1), unit(2), unit(3), tail(0), tail(2)], 4)
    writes[0].wait()
    for r in (0, rows - SIDE):
        at = slice(r, r + SIDE)
        write = pltpu.make_async_copy(out_ref.at[at], out_hbm.at[at], sems.at[1 if r == 0 else 2])
        write.start()
        writes.append(write)
    writes[1].wait()
    writes[2].wait()


def exchange(low, high, axis):
    count = lax.axis_size(axis)
    before = lax.ppermute(high, axis, [(i, (i + 1) % count) for i in range(count)])
    after = lax.ppermute(low, axis, [((i + 1) % count, i) for i in range(count)])
    return before, after


def call(kernel, name, outs, scratch, flops, operands, in_hbm=()):
    vmem = pl.BlockSpec(memory_space=pltpu.VMEM)
    hbm = pl.BlockSpec(memory_space=pltpu.HBM)
    return pl.pallas_call(
        kernel,
        out_shape=[out if isinstance(out, jax.ShapeDtypeStruct) else pltpu.VMEM(*out) for out in outs],
        in_specs=[hbm if i in in_hbm else vmem for i in range(len(operands))],
        out_specs=[hbm if isinstance(out, jax.ShapeDtypeStruct) else vmem for out in outs],
        scratch_shapes=[pltpu.VMEM(*s) if isinstance(s, tuple) else s for s in scratch],
        cost_estimate=pl.CostEstimate(flops=flops, bytes_accessed=4_000_000, transcendentals=1_000_000),
        compiler_params=pltpu.CompilerParams(vmem_limit_bytes=24 * 1024 * 1024),
        name=name,
    )(*[pltpu.with_memory_space_constraint(x, pltpu.HBM) if i in in_hbm else x for i, x in enumerate(operands)])


def on_device(
    image, norm1_gain, norm2_gain, qkv_weight, proj_weight, rel_table, conv_weight, fc1_weight,
    fc2_weight,
):
    rows, cols, channels = image.shape
    blocks_r, blocks_c = rows // SIDE, cols // SIDE
    gain1, gain2, fc2, table = norm1_gain[None], norm2_gain[None], fc2_weight.T, rel_table.T
    band, column = ((SHIFT, cols * 3 // 2, HALF), BF16), ((rows, SHIFT, channels), BF16)
    tile, gain1, table, qkv_weight, first_rows, last_rows, first_cols, last_cols = call(
        cut_kernel,
        "cut_halo",
        [(image.shape, BF16), (gain1.shape, F32), (table.shape, F32), (qkv_weight.shape, BF16),
         band, band, column, column],
        [((2, SHIFT, cols, LANES), F32), pltpu.SemaphoreType.DMA((4,))],
        1_000_000,
        (image, gain1, table, qkv_weight),
        range(4),
    )
    top, bottom = exchange(first_rows, last_rows, "row")
    left, right = exchange(first_cols, last_cols, "col")
    fetched = (gain2, proj_weight, conv_weight, fc1_weight, fc2)
    hidden = -(-fc1_weight.shape[1] // 128) * 128
    bias, query, kv, normed, wkv, wp, wc, w1, w2, g2 = call(
        own_kernel,
        "own_tile",
        [
            ((HEADS, 4, AREA, WIN * WIN), F32),
            ((blocks_r * blocks_c, AREA, LANES), BF16),
            ((blocks_r * blocks_c, AREA, 2 * LANES), BF16),
            ((rows, cols, LANES), F32),
            ((LANES, 2 * LANES), BF16),
            ((LANES, LANES), BF16),
            ((9 * LANES, LANES), BF16),
            ((LANES, hidden), BF16),
            ((hidden, LANES), BF16),
            ((1, LANES), F32),
        ],
        [
            ((8, 1024), F32),
            ((4, 8 * WIN, 128), F32),
            ((LANES, LANES), BF16),
            *[(x.shape, x.dtype) for x in fetched],
            pltpu.SemaphoreType.DMA((len(fetched),)),
        ],
        2_000_000_000,
        (tile, gain1, table, qkv_weight, gain2, proj_weight, conv_weight, fc1_weight, fc2),
        range(4, 9),
    )
    def ends(start, rest):
        parts = [(start, start + SHIFT), (cols + rest, cols + rest + SHIFT)]
        return jnp.concatenate(
            [jnp.concatenate([x[:, a:b] for a, b in parts], axis=1) for x in (top, bottom)]
        )

    first, last = ends(0, 0), ends(cols - SHIFT, cols // 2 - SHIFT)
    left_corner, right_corner = exchange(first, last, "col")
    blocks, base, out_inner = call(
        edge_kernel,
        "edge_windows",
        [
            ((2 * blocks_r * blocks_c, AREA, 2 * LANES), BF16),
            ((blocks_r * blocks_c, AREA, LANES), F32),
            ((3, 4 * AREA, LANES), F32),
        ],
        [
            ((rows + 2 * SHIFT, cols + 2 * SHIFT, LANES), F32),
            ((3, rows + 2, cols, LANES), BF16),
            ((HEADS, 2 * AREA, LANES), BF16),
        ],
        2_000_000_000,
        (tile, top, bottom, left, right, gain1, bias, query, kv, normed, wkv, wp, wc, w1, w2, g2),
    )
    (out,) = call(
        corner_kernel,
        "corner_windows",
        [jax.ShapeDtypeStruct(image.shape, BF16)],
        [((4, AREA, LANES), F32), (image.shape, BF16), pltpu.SemaphoreType.DMA((3,))],
        1_000_000_000,
        (left_corner, right_corner, gain1, bias, query, wkv, wp, wc, w1, w2, g2, blocks, base, out_inner),
    )
    return out


def solution(mesh):
    placed = (P("row", "col", None), P(), P(), P(), P(), P(), P(), P(), P())
    return jax.shard_map(
        on_device, mesh=mesh, in_specs=placed, out_specs=P("row", "col", None), check_vma=False
    )
```

```python
import math

import jax
import jax.numpy as jnp
from jax import lax
from jax.experimental import pallas as pl
from jax.experimental.pallas import tpu as pltpu
from jax.sharding import PartitionSpec as P

HEADS = 6
WIN = 16
SHIFT = 8
SIDE = 8
AREA = SIDE * SIDE
LANES = 256
HALF = LANES // 2
F32 = jnp.float32
BF16 = jnp.bfloat16
LOG2E = math.log2(math.e)
MASKED = -4.0e9


def weave(tasks, width):
    waiting, active = list(tasks), []
    while waiting or active:
        while waiting and len(active) < width:
            active.append(waiting.pop(0))
        for task in list(active):
            try:
                next(task)
            except StopIteration:
                active.remove(task)


def layer_norm(values, norm_gain):
    centre = jnp.mean(values, axis=-1, keepdims=True)
    values = values - centre
    spread = jnp.mean(values * values, axis=-1, keepdims=True)
    return values * lax.rsqrt(spread + 1e-05) * norm_gain


def layer_norm_padded(values, norm_gain, channels):
    centre = jnp.sum(values, axis=-1, keepdims=True) * (1.0 / channels)
    values = jnp.where(lanes_of() < channels, values - centre, 0.0)
    spread = jnp.sum(values * values, axis=-1, keepdims=True) * (1.0 / channels)
    return values * lax.rsqrt(spread + 1e-05) * norm_gain


def dot(a, b):
    return jnp.dot(a, b, preferred_element_type=F32)


def dot_nt(a, b):
    return lax.dot_general(a, b, (((1,), (1,)), ((), ())), preferred_element_type=F32)


def one_hot(condition):
    return jnp.where(condition, 1.0, 0.0).astype(BF16)


def gelu(x):
    square = jnp.minimum(x * x, 25.0)
    poly = -5.58203231240273e-08
    for factor in (2.777085437695777e-06, -4.707012890217347e-05, -5.859274357446709e-05,
                   0.036366718434813275, 0.7978721905787034):
        poly = poly * square + factor
    half = 0.5 * x
    return half + half * jnp.tanh(x * poly)


def lanes_of(width=LANES):
    return lax.broadcasted_iota(jnp.int32, (1, width), 1)


def marks(channels, outside):
    half = lanes_of()[:, HALF:]
    return jnp.where(half == channels + 1, 1.0, 0.0) + jnp.where(half == channels, outside, 0.0)


def expand_bias(table_ref, padded, strip, bias):
    span = 2 * WIN - 1
    padded[...] = jnp.zeros_like(padded)
    padded[0:HEADS, 0 : span * span] = table_ref[...] * LOG2E
    table = padded[...]
    width = padded.shape[1]
    shifted = jnp.concatenate(
        [table if px == 0 else pltpu.roll(table, width - px, 1) for px in range(WIN)], axis=0
    )
    high = shifted.astype(BF16)
    low = (shifted - high.astype(F32)).astype(BF16)
    yield
    entry = lax.broadcasted_iota(jnp.int32, (width, 512), 0)
    place = lax.broadcasted_iota(jnp.int32, (1, 512), 1)
    column = lax.div(place, 256) * SIDE + lax.rem(place, SIDE)
    wanted = (span - 1 - lax.div(lax.rem(place, 256), SIDE)) * span + WIN - 1 - column
    picked = dot(jnp.concatenate([high, low], axis=0), one_hot(entry == wanted))
    yield
    half = 8 * WIN
    picked = picked[:half] + picked[half:]
    for tile in range(4):
        strip[tile] = picked[:, 128 * tile : 128 * (tile + 1)]
    for head in range(HEADS):
        yield
        for half in range(2):
            rows = jnp.concatenate(
                [strip[2 * half + t, pl.ds(head, WIN, stride=8), :] for t in range(2)], axis=1
            )
            for py in range(WIN):
                start = (WIN - 1 - py) * SIDE
                rolled = (rows if start == 0 else pltpu.roll(rows, 256 - start, 1))[:, 0:128]
                lanes = slice(128 * half, 128 * (half + 1))
                place = slice(py % SIDE * SIDE, (py % SIDE + 1) * SIDE)
                bias[head, py // SIDE, 0, place, lanes] = rolled[:SIDE]
                bias[head, py // SIDE, 1, place, lanes] = rolled[SIDE:]


def scores_of(blocks, keys, head_dim, channels):
    lane = lanes_of()
    part = jnp.concatenate(blocks, axis=0)
    own = [(lane >= h * head_dim) & (lane < (h + 1) * head_dim) for h in range(HEADS)]
    stacked = jnp.concatenate(
        [part * one_hot(own[h] | (lane == channels)) for h in range(HEADS)], axis=0
    )
    return dot_nt(stacked, keys)


def attend(unit, bias, head_dim, channels, put):
    lane = lanes_of()
    blocks, quadrants, pair = unit
    pair = pair()
    scores = scores_of(blocks, pair[:, :LANES], head_dim, channels)
    count = scores.shape[0] // HEADS
    yield
    part_bias = jnp.concatenate([bias[:, hy, hx] for hy, hx in quadrants], axis=1)
    scores = scores.reshape(HEADS, count, WIN * WIN) + part_bias
    scores = scores - jnp.max(scores, axis=-1, keepdims=True)
    weights = jnp.exp2(scores)
    total = jnp.sum(weights, axis=-1, keepdims=True)
    weights = weights.astype(BF16).reshape(HEADS * count, WIN * WIN)
    yield
    mixed = dot(weights, pair[:, LANES:])
    yield
    result, divisor = mixed[0:count], jnp.broadcast_to(total[0], (count, LANES))
    for h in range(1, HEADS):
        mine = (lane >= h * head_dim) & (lane < (h + 1) * head_dim)
        result = jnp.where(mine, mixed[h * count : (h + 1) * count], result)
        divisor = jnp.where(mine, total[h], divisor)
    put((result / divisor).astype(BF16))


def finish(heads_out, base, wp, gain2, w1, w2, channels, put):
    attended = dot(heads_out, wp[...])
    yield
    state1 = base() + attended.astype(BF16).astype(F32)
    normed2 = layer_norm_padded(state1, gain2, channels).astype(BF16)
    yield
    hidden = dot(normed2, w1[...])
    yield
    hidden = gelu(hidden).astype(BF16)
    yield
    put(state1 + dot(hidden, w2[...]))


def after(ready, make):
    while not ready():
        yield
    yield from make()


def pack(pixels, spare):
    rows, cols, channels = pixels.shape
    spare[...] = jnp.zeros_like(spare)
    spare[:, :, 0:channels] = pixels
    rest = spare[:, :, HALF:]
    second = pltpu.roll(rest[:, cols // 2 :].reshape(-1, HALF), HALF // 2, 1)
    both = rest[:, : cols // 2] + second.reshape(rows, cols // 2, HALF)
    return jnp.concatenate([spare[:, :, :HALF], both], axis=1).astype(BF16)


def unpack(main, rest, turned, channels):
    if turned:
        rest = pltpu.roll(rest.reshape(-1, HALF), HALF // 2, 1).reshape(rest.shape)
    return jnp.concatenate([main, rest], axis=2)[:, :, :channels]


def cut_kernel(
    image_hbm, gain1_hbm, table_hbm, qkv_hbm, image_ref, gain1_ref, table_ref, qkv_ref,
    top, bottom, left, right, spare, sems,
):
    rows, cols, _ = image_ref.shape
    fetches = [
        pltpu.make_async_copy(source, target, sems.at[i])
        for i, (source, target) in enumerate(
            ((image_hbm, image_ref), (gain1_hbm, gain1_ref), (table_hbm, table_ref), (qkv_hbm, qkv_ref))
        )
    ]
    for fetch in fetches:
        fetch.start()
    for fetch in fetches:
        fetch.wait()
    top[...] = pack(image_ref[:SHIFT].astype(F32), spare.at[0])
    bottom[...] = pack(image_ref[rows - SHIFT :].astype(F32), spare.at[1])
    for r in range(0, rows, SIDE):
        band = image_ref[r : r + SIDE].astype(F32)
        left[r : r + SIDE] = band[:, :SHIFT].astype(BF16)
        right[r : r + SIDE] = band[:, cols - SHIFT :].astype(BF16)


def own_kernel(
    image_ref, gain1_ref, table_ref, qkv_ref, gain2_hbm, proj_hbm, conv_hbm, fc1_hbm, fc2_hbm,
    bias, query, kv, normed, wkv, wp, wc, w1, w2, g2,
    padded, strip, wq,
    gain2_ref, proj_ref, conv_ref, fc1_ref, fc2_ref, sems,
):
    rows, cols, channels = image_ref.shape
    head_dim = channels // HEADS
    flag_lane, one_lane = channels, channels + 1
    blocks_r, blocks_c = rows // SIDE, cols // SIDE
    fetches = [
        pltpu.make_async_copy(source, target, sems.at[i])
        for i, (source, target) in enumerate(
            ((conv_hbm, conv_ref), (proj_hbm, proj_ref), (gain2_hbm, gain2_ref), (fc1_hbm, fc1_ref),
             (fc2_hbm, fc2_ref))
        )
    ]
    for fetch in fetches:
        fetch.start()

    for ref in (wq, wkv, wp, wc, w1, w2, g2):
        ref[...] = jnp.zeros_like(ref)
    special = lax.broadcasted_iota(jnp.int32, (16, LANES), 0) + 176
    lanes16 = lax.broadcasted_iota(jnp.int32, (16, LANES), 1)
    wq[176:192, :] = one_hot((special == one_lane) & (lanes16 == flag_lane))
    wkv[176:192, 0:LANES] = jnp.where(
        (special == flag_lane) & (lanes16 == flag_lane), MASKED, 0.0
    ).astype(BF16)
    normed[:, :, HALF:] = jnp.broadcast_to(marks(channels, 0.0)[None], (rows, cols, HALF))

    gain1 = gain1_ref[...]
    scale = head_dim**-0.5 * LOG2E

    wq[0:channels, 0:channels] = qkv_ref[:, 0:channels]
    wkv[0:channels, 0:channels] = qkv_ref[:, channels : 2 * channels]
    wkv[0:channels, LANES : LANES + channels] = qkv_ref[:, 2 * channels :]

    def weights():
        for fetch in fetches:
            fetch.wait()
        wp[0:channels, 0:channels] = proj_ref[...]
        w1[0:channels, 0 : fc1_ref.shape[1]] = fc1_ref[...]
        w2[0 : fc2_ref.shape[1], 0:channels] = fc2_ref[...].astype(F32).T.astype(BF16)
        g2[:, 0:channels] = gain2_ref[...]
        for tap in range(9):
            wc[tap * LANES : tap * LANES + channels, 0:channels] = conv_ref[tap // 3, tap % 3]
            if tap % 3 == 2:
                yield

    def norm(br):
        at = slice(br * SIDE, (br + 1) * SIDE)
        normed[at, :, 0:channels] = layer_norm(image_ref[at].astype(F32), gain1)

    def project(br):
        pixels = normed[br * SIDE : (br + 1) * SIDE].astype(BF16).reshape(-1, LANES)
        q = dot(pixels, wq[...])
        yield
        both = dot(pixels, wkv[...]).reshape(SIDE, cols, 2 * LANES)
        q = (q * scale).reshape(SIDE, cols, LANES)
        for bc in range(blocks_c):
            part = slice(bc * SIDE, (bc + 1) * SIDE)
            query[br, bc] = q[:, part].reshape(AREA, LANES).astype(BF16)
        yield
        for bc in range(blocks_c):
            part = slice(bc * SIDE, (bc + 1) * SIDE)
            kv[br, bc] = both[:, part].reshape(AREA, 2 * LANES).astype(BF16)

    for br in range(blocks_r):
        norm(br)
    tasks = [expand_bias(table_ref, padded, strip, bias), *[project(br) for br in range(blocks_r)]]
    weave([*tasks, weights()], 3)


def edge_kernel(
    image_ref, top_ref, bottom_ref, left_ref, right_ref, gain1_ref,
    bias, query, kv, normed, wkv, wp, wc, w1, w2, g2,
    kv_edge, corner_base, out_edge, out_mid,
    halo, base, shifted,
):
    rows, cols, channels = image_ref.shape
    head_dim = channels // HEADS
    row, last_row = lax.axis_index("row"), lax.axis_size("row") - 1
    col, last_col = lax.axis_index("col"), lax.axis_size("col") - 1
    gain1 = gain1_ref[...]
    outside = [(row == 0).astype(F32), (row == last_row).astype(F32),
               (col == 0).astype(F32), (col == last_col).astype(F32)]

    for r in (0, SHIFT + rows):
        for c in (0, SHIFT + cols):
            halo[r : r + SHIFT, c : c + SHIFT] = jnp.zeros((SHIFT, SHIFT, LANES), F32)
    sides = []

    def band(i):
        ref = (top_ref, bottom_ref, left_ref, right_ref)[i]
        start = (0, SHIFT + (rows if i < 2 else cols))[i % 2]
        inner = slice(SHIFT, SHIFT + (cols if i < 2 else rows))
        outer = slice(start, start + SHIFT)
        place = (outer, inner) if i < 2 else (inner, outer)
        values = ref[...].astype(F32)
        if i < 2:
            rest, half = values[:, cols:], cols // 2
            values = jnp.concatenate(
                [unpack(values[:, :half], rest, False, channels),
                 unpack(values[:, half:cols], rest, True, channels)], axis=1
            )
        mark = jnp.broadcast_to(marks(channels, outside[i])[None], (*values.shape[:2], HALF))
        halo[(*place, slice(HALF, LANES))] = mark
        halo[(*place, slice(0, channels))] = layer_norm(values, gain1 * (1.0 - outside[i]))
        pixels = halo[place]
        if i < 2:
            blocks = [pixels[:, b * SIDE : (b + 1) * SIDE].reshape(AREA, LANES) for b in range(cols // SIDE)]
        else:
            blocks = [pixels.reshape(-1, LANES)]
        pixels = jnp.concatenate(blocks, axis=0).astype(BF16)
        yield
        both = dot(pixels, wkv[...])
        yield
        kv_edge[i] = both.astype(BF16).reshape(-1, AREA, 2 * LANES)
        sides.append(i)

    def tile():
        for r in range(0, rows, SIDE):
            halo[SHIFT + r : SHIFT + r + SIDE, SHIFT : SHIFT + cols] = normed[r : r + SIDE]
            yield

    def convolve(br):
        r = br * SIDE
        for tap in range(3):
            c0 = SHIFT - 1 + tap
            start, stop = 0 if br == 0 else r + 2, r + SIDE + 2
            shifted[tap, start:stop] = halo[
                SHIFT - 1 + start : SHIFT - 1 + stop, c0 : c0 + cols
            ].astype(BF16)
        yield
        taps = [
            shifted[tap % 3, r + tap // 3 : r + tap // 3 + SIDE].reshape(-1, LANES) for tap in range(9)
        ]
        summed = dot(jnp.concatenate(taps, axis=1), wc[...])
        yield
        summed = summed[:, :channels].reshape(SIDE, cols, channels)
        summed = summed + image_ref[r : r + SIDE].astype(F32)
        for bc in range(cols // SIDE):
            part = summed[:, bc * SIDE : (bc + 1) * SIDE].reshape(AREA, channels)
            if (br, bc) in corners:
                ref = corner_base.at[corners.index((br, bc))]
            else:
                ref = base.at[br, bc]
            ref[:, HALF:] = jnp.zeros((AREA, HALF), F32)
            ref[:, 0:channels] = part

    corners = [(0, 0), (0, 3), (3, 0), (3, 3)]
    keys = [
        lambda: [kv_edge[0, 1], kv[0, 1], kv_edge[0, 2], kv[0, 2]],
        lambda: [kv[3, 1], kv_edge[1, 1], kv[3, 2], kv_edge[1, 2]],
        lambda: [kv_edge[2, 1], kv_edge[2, 2], kv[1, 0], kv[2, 0]],
        lambda: [kv[1, 3], kv[2, 3], kv_edge[3, 1], kv_edge[3, 2]],
        lambda: [kv[1, 1], kv[2, 1], kv[1, 2], kv[2, 2]],
    ]
    places = [((0, 1), (0, 2)), ((3, 1), (3, 2)), ((1, 0), (2, 0)), ((1, 3), (2, 3))]
    places += [((1, 1), (1, 2)), ((2, 1), (2, 2))]
    quadrants = [((1, 0), (1, 1)), ((0, 0), (0, 1)), ((0, 1), (1, 1)), ((0, 0), (1, 0))]
    quadrants += [((0, 0), (0, 1)), ((1, 0), (1, 1))]
    done = {}

    def unit(i):
        def put(result):
            done[i] = result

        window = keys[min(i, 4)]
        parts = ([query[at] for at in places[i]], quadrants[i], lambda: jnp.concatenate(window(), axis=0))
        make = lambda: attend(parts, bias, head_dim, channels, put)
        return after(lambda: i >= 4 or i in sides, make)

    def tail(i):
        def put(out):
            if i == 4:
                out_mid[...] = out
            else:
                out_edge[i // 2] = out

        def make():
            return finish(
                jnp.concatenate([done[i], done[i + 1]], axis=0),
                lambda: jnp.concatenate([base[at] for at in (*places[i], *places[i + 1])], axis=0),
                wp, g2[...], w1, w2, channels, put,
            )

        return after(lambda: i in done and i + 1 in done, make)

    weave(
        [unit(4), band(0), band(1), unit(5), band(2), band(3), tile(), unit(0), convolve(0), unit(1),
         convolve(1), unit(2), convolve(2), unit(3), convolve(3), tail(4), tail(0), tail(2)],
        3,
    )


def corner_kernel(
    left_ref, right_ref, gain1_ref,
    bias, query, kv, wkv, wp, wc, w1, w2, g2, kv_edge, corner_base, out_mid, out_edge,
    out_hbm,
    normed, out_ref, sems,
):
    rows, _, channels = out_ref.shape
    head_dim = channels // HEADS

    def finish_bands(which, corners):
        def piece(source, i):
            return source[i * AREA : (i + 1) * AREA]

        for br in which:
            if br in (0, 3):
                i = 0 if br == 0 else 2
                band = [corners[i], piece(out_edge.at[0], i), piece(out_edge.at[0], i + 1), corners[i + 1]]
            else:
                i = br - 1
                band = [piece(out_edge.at[1], i), piece(out_mid, 2 * i), piece(out_mid, 2 * i + 1),
                        piece(out_edge.at[1], i + 2)]
            band = [part[:, :channels].reshape(SIDE, SIDE, channels) for part in band]
            out_ref[br * SIDE : (br + 1) * SIDE] = jnp.concatenate(band, axis=1).astype(BF16)

    finish_bands((1, 2), None)
    inner = slice(SIDE, rows - SIDE)
    writes = [pltpu.make_async_copy(out_ref.at[inner], out_hbm.at[inner], sems.at[0])]
    writes[0].start()
    row, last_row = lax.axis_index("row"), lax.axis_size("row") - 1
    col, last_col = lax.axis_index("col"), lax.axis_size("col") - 1
    gain1 = gain1_ref[...]
    out_row = [(row == 0).astype(F32), (row == last_row).astype(F32)]
    out_col = [(col == 0).astype(F32), (col == last_col).astype(F32)]
    corner, done = {}, {}

    def project():
        for i in range(4):
            ref = (left_ref, right_ref)[i % 2]
            inside = (1.0 - out_row[i // 2]) * (1.0 - out_col[i % 2])
            mark = marks(channels, out_row[i // 2] + out_col[i % 2])
            normed[i, :, HALF:] = jnp.broadcast_to(mark, (AREA, HALF))
            values = ref[i // 2 * SIDE : (i // 2 + 1) * SIDE].astype(F32)
            values = unpack(values[:, :SIDE], values[:, SIDE:], i % 2 == 0, channels)
            normed[i, :, 0:channels] = layer_norm(values.reshape(AREA, channels), gain1 * inside)
        both = dot(normed[...].reshape(-1, LANES).astype(BF16), wkv[...])
        both = both.astype(BF16)
        for i in range(4):
            corner[i] = both[i * AREA : (i + 1) * AREA]

    keys = [
        lambda: [corner[0], kv_edge[2, 0], kv_edge[0, 0], kv[0, 0]],
        lambda: [kv_edge[0, 3], kv[0, 3], corner[1], kv_edge[3, 0]],
        lambda: [kv_edge[2, 3], corner[2], kv[3, 0], kv_edge[1, 0]],
        lambda: [kv[3, 3], kv_edge[1, 3], kv_edge[3, 3], corner[3]],
    ]
    places = [(0, 0), (0, 3), (3, 0), (3, 3)]
    quadrants = [(1, 1), (1, 0), (0, 1), (0, 0)]

    def unit(i):
        def put(result):
            done[i] = result

        parts = ([query[places[i]]], [quadrants[i]], lambda: jnp.concatenate(keys[i](), axis=0))
        return after(lambda: i in corner, lambda: attend(parts, bias, head_dim, channels, put))

    def whole(i):
        tap, y, x = ((0, 7, 7), (2, 7, 0), (6, 0, 7), (8, 0, 0))[i]
        start = y * SIDE
        term = dot(normed[i, start : start + SIDE].astype(BF16), wc[tap * LANES : (tap + 1) * LANES])
        term = term[x : x + 1]
        pixel = lax.broadcasted_iota(jnp.int32, (AREA, 1), 0)
        at = (SIDE - 1 - y) * SIDE + SIDE - 1 - x
        return corner_base[i] + jnp.where(pixel == at, term, 0.0)

    def tail():
        def put(out):
            finish_bands((0, 3), [out[i * AREA : (i + 1) * AREA] for i in range(4)])

        def make():
            return finish(
                jnp.concatenate([done[i] for i in range(4)], axis=0),
                lambda: jnp.concatenate([whole(i) for i in range(4)], axis=0),
                wp, g2[...], w1, w2, channels, put,
            )

        return after(lambda: len(done) == 4, make)

    project()
    weave([unit(0), unit(1), unit(2), unit(3), tail()], 2)
    writes[0].wait()
    for r in (0, rows - SIDE):
        at = slice(r, r + SIDE)
        write = pltpu.make_async_copy(out_ref.at[at], out_hbm.at[at], sems.at[1 if r == 0 else 2])
        write.start()
        writes.append(write)
    writes[1].wait()
    writes[2].wait()


def exchange(low, high, axis):
    count = lax.axis_size(axis)
    before = lax.ppermute(high, axis, [(i, (i + 1) % count) for i in range(count)])
    after = lax.ppermute(low, axis, [((i + 1) % count, i) for i in range(count)])
    return before, after


def call(kernel, name, outs, scratch, flops, operands, in_hbm=()):
    vmem = pl.BlockSpec(memory_space=pltpu.VMEM)
    hbm = pl.BlockSpec(memory_space=pltpu.HBM)
    return pl.pallas_call(
        kernel,
        out_shape=[out if isinstance(out, jax.ShapeDtypeStruct) else pltpu.VMEM(*out) for out in outs],
        in_specs=[hbm if i in in_hbm else vmem for i in range(len(operands))],
        out_specs=[hbm if isinstance(out, jax.ShapeDtypeStruct) else vmem for out in outs],
        scratch_shapes=[pltpu.VMEM(*s) if isinstance(s, tuple) else s for s in scratch],
        cost_estimate=pl.CostEstimate(flops=flops, bytes_accessed=4_000_000, transcendentals=1_000_000),
        compiler_params=pltpu.CompilerParams(vmem_limit_bytes=24 * 1024 * 1024),
        name=name,
    )(*[pltpu.with_memory_space_constraint(x, pltpu.HBM) if i in in_hbm else x for i, x in enumerate(operands)])


def on_device(
    image, norm1_gain, norm2_gain, qkv_weight, proj_weight, rel_table, conv_weight, fc1_weight,
    fc2_weight,
):
    rows, cols, channels = image.shape
    blocks_r, blocks_c = rows // SIDE, cols // SIDE
    gain1, gain2, fc2, table = norm1_gain[None], norm2_gain[None], fc2_weight.T, rel_table.T
    band, column = ((SHIFT, cols * 3 // 2, HALF), BF16), ((rows, SHIFT, channels), BF16)
    tile, gain1, table, qkv_weight, first_rows, last_rows, first_cols, last_cols = call(
        cut_kernel,
        "cut_halo",
        [(image.shape, BF16), (gain1.shape, F32), (table.shape, F32), (qkv_weight.shape, BF16),
         band, band, column, column],
        [((2, SHIFT, cols, LANES), F32), pltpu.SemaphoreType.DMA((4,))],
        1_000_000,
        (image, gain1, table, qkv_weight),
        range(4),
    )
    top, bottom = exchange(first_rows, last_rows, "row")
    left, right = exchange(first_cols, last_cols, "col")
    fetched = (gain2, proj_weight, conv_weight, fc1_weight, fc2)
    hidden = -(-fc1_weight.shape[1] // 128) * 128
    bias, query, kv, normed, wkv, wp, wc, w1, w2, g2 = call(
        own_kernel,
        "own_tile",
        [
            ((HEADS, 2, 2, AREA, WIN * WIN), F32),
            ((blocks_r, blocks_c, AREA, LANES), BF16),
            ((blocks_r, blocks_c, AREA, 2 * LANES), BF16),
            ((rows, cols, LANES), F32),
            ((LANES, 2 * LANES), BF16),
            ((LANES, LANES), BF16),
            ((9 * LANES, LANES), BF16),
            ((LANES, hidden), BF16),
            ((hidden, LANES), BF16),
            ((1, LANES), F32),
        ],
        [
            ((8, 1024), F32),
            ((4, 8 * WIN, 128), F32),
            ((LANES, LANES), BF16),
            *[(x.shape, x.dtype) for x in fetched],
            pltpu.SemaphoreType.DMA((len(fetched),)),
        ],
        2_000_000_000,
        (tile, gain1, table, qkv_weight, gain2, proj_weight, conv_weight, fc1_weight, fc2),
        range(4, 9),
    )
    def ends(start, rest):
        parts = [(start, start + SHIFT), (cols + rest, cols + rest + SHIFT)]
        return jnp.concatenate(
            [jnp.concatenate([x[:, a:b] for a, b in parts], axis=1) for x in (top, bottom)]
        )

    first, last = ends(0, 0), ends(cols - SHIFT, cols // 2 - SHIFT)
    left_corner, right_corner = exchange(first, last, "col")
    kv_edge, corner_base, out_edge, out_mid = call(
        edge_kernel,
        "edge_windows",
        [
            ((4, blocks_c, AREA, 2 * LANES), BF16),
            ((4, AREA, LANES), F32),
            ((2, 4 * AREA, LANES), F32),
            ((4 * AREA, LANES), F32),
        ],
        [
            ((rows + 2 * SHIFT, cols + 2 * SHIFT, LANES), F32),
            ((blocks_r, blocks_c, AREA, LANES), F32),
            ((3, rows + 2, cols, LANES), BF16),
        ],
        2_000_000_000,
        (tile, top, bottom, left, right, gain1, bias, query, kv, normed, wkv, wp, wc, w1, w2, g2),
    )
    (out,) = call(
        corner_kernel,
        "corner_windows",
        [jax.ShapeDtypeStruct(image.shape, BF16)],
        [((4, AREA, LANES), F32), (image.shape, BF16), pltpu.SemaphoreType.DMA((3,))],
        1_000_000_000,
        (left_corner, right_corner, gain1, bias, query, kv, wkv, wp, wc, w1, w2, g2,
         kv_edge, corner_base, out_mid, out_edge),
    )
    return out


def solution(mesh):
    placed = (P("row", "col", None), P(), P(), P(), P(), P(), P(), P(), P())
    return jax.shard_map(
        on_device, mesh=mesh, in_specs=placed, out_specs=P("row", "col", None), check_vma=False
    )
```

```python
import math

import jax
import jax.numpy as jnp
from jax import lax
from jax.experimental import pallas as pl
from jax.experimental.pallas import tpu as pltpu
from jax.sharding import PartitionSpec as P

HEADS = 6
WIN = 16
SHIFT = 8
SIDE = 8
AREA = SIDE * SIDE
LANES = 256
HALF = LANES // 2
F32 = jnp.float32
BF16 = jnp.bfloat16
LOG2E = math.log2(math.e)
MASKED = -4.0e9


def weave(tasks, width):
    waiting, active = list(tasks), []
    while waiting or active:
        while waiting and len(active) < width:
            active.append(waiting.pop(0))
        for task in list(active):
            try:
                next(task)
            except StopIteration:
                active.remove(task)


def layer_norm(values, norm_gain):
    centre = jnp.mean(values, axis=-1, keepdims=True)
    values = values - centre
    spread = jnp.mean(values * values, axis=-1, keepdims=True)
    return values * lax.rsqrt(spread + 1e-05) * norm_gain


def layer_norm_padded(values, norm_gain, channels):
    centre = jnp.sum(values, axis=-1, keepdims=True) * (1.0 / channels)
    values = jnp.where(lanes_of() < channels, values - centre, 0.0)
    spread = jnp.sum(values * values, axis=-1, keepdims=True) * (1.0 / channels)
    return values * lax.rsqrt(spread + 1e-05) * norm_gain


def dot(a, b):
    return jnp.dot(a, b, preferred_element_type=F32)


def dot_nt(a, b):
    return lax.dot_general(a, b, (((1,), (1,)), ((), ())), preferred_element_type=F32)


def one_hot(condition):
    return jnp.where(condition, 1.0, 0.0).astype(BF16)


def gelu(x):
    square = jnp.minimum(x * x, 25.0)
    poly = -5.58203231240273e-08
    for factor in (2.777085437695777e-06, -4.707012890217347e-05, -5.859274357446709e-05,
                   0.036366718434813275, 0.7978721905787034):
        poly = poly * square + factor
    half = 0.5 * x
    return half + half * jnp.tanh(x * poly)


def lanes_of(width=LANES):
    return lax.broadcasted_iota(jnp.int32, (1, width), 1)


def marks(channels, outside):
    half = lanes_of()[:, HALF:]
    return jnp.where(half == channels + 1, 1.0, 0.0) + jnp.where(half == channels, outside, 0.0)


def expand_bias(table_ref, padded, strip, bias):
    span = 2 * WIN - 1
    padded[...] = jnp.zeros_like(padded)
    padded[0:HEADS, 0 : span * span] = table_ref[...] * LOG2E
    table = padded[...]
    width = padded.shape[1]
    shifted = jnp.concatenate(
        [table if px == 0 else pltpu.roll(table, width - px, 1) for px in range(WIN)], axis=0
    )
    high = shifted.astype(BF16)
    low = (shifted - high.astype(F32)).astype(BF16)
    yield
    entry = lax.broadcasted_iota(jnp.int32, (width, 512), 0)
    place = lax.broadcasted_iota(jnp.int32, (1, 512), 1)
    column = lax.div(place, 256) * SIDE + lax.rem(place, SIDE)
    wanted = (span - 1 - lax.div(lax.rem(place, 256), SIDE)) * span + WIN - 1 - column
    picked = dot(jnp.concatenate([high, low], axis=0), one_hot(entry == wanted))
    yield
    half = 8 * WIN
    picked = picked[:half] + picked[half:]
    for tile in range(4):
        strip[tile] = picked[:, 128 * tile : 128 * (tile + 1)]
    for head in range(HEADS):
        yield
        for half in range(2):
            rows = jnp.concatenate(
                [strip[2 * half + t, pl.ds(head, WIN, stride=8), :] for t in range(2)], axis=1
            )
            for py in range(WIN):
                start = (WIN - 1 - py) * SIDE
                rolled = (rows if start == 0 else pltpu.roll(rows, 256 - start, 1))[:, 0:128]
                lanes = slice(128 * half, 128 * (half + 1))
                place = slice(py % SIDE * SIDE, (py % SIDE + 1) * SIDE)
                bias[head, py // SIDE, 0, place, lanes] = rolled[:SIDE]
                bias[head, py // SIDE, 1, place, lanes] = rolled[SIDE:]


def scores_of(blocks, keys, head_dim, channels):
    lane = lanes_of()
    part = jnp.concatenate(blocks, axis=0)
    own = [(lane >= h * head_dim) & (lane < (h + 1) * head_dim) for h in range(HEADS)]
    stacked = jnp.concatenate(
        [part * one_hot(own[h] | (lane == channels)) for h in range(HEADS)], axis=0
    )
    return dot_nt(stacked, keys)


def attend(unit, bias, head_dim, channels, put):
    lane = lanes_of()
    blocks, quadrants, pair = unit
    pair = pair()
    scores = scores_of(blocks, pair[:, :LANES], head_dim, channels)
    count = scores.shape[0] // HEADS
    yield
    part_bias = jnp.concatenate([bias[:, hy, hx] for hy, hx in quadrants], axis=1)
    scores = scores.reshape(HEADS, count, WIN * WIN) + part_bias
    scores = scores - jnp.max(scores, axis=-1, keepdims=True)
    weights = jnp.exp2(scores)
    total = jnp.sum(weights, axis=-1, keepdims=True)
    weights = weights.astype(BF16).reshape(HEADS * count, WIN * WIN)
    yield
    mixed = dot(weights, pair[:, LANES:])
    yield
    result, divisor = mixed[0:count], jnp.broadcast_to(total[0], (count, LANES))
    for h in range(1, HEADS):
        mine = (lane >= h * head_dim) & (lane < (h + 1) * head_dim)
        result = jnp.where(mine, mixed[h * count : (h + 1) * count], result)
        divisor = jnp.where(mine, total[h], divisor)
    put((result / divisor).astype(BF16))


def finish(heads_out, base, wp, gain2, w1, w2, channels, put):
    attended = dot(heads_out, wp[...])
    yield
    state1 = base() + attended.astype(BF16).astype(F32)
    normed2 = layer_norm_padded(state1, gain2, channels).astype(BF16)
    yield
    hidden = dot(normed2, w1[...])
    yield
    hidden = gelu(hidden).astype(BF16)
    yield
    put(state1 + dot(hidden, w2[...]))


def after(ready, make):
    while not ready():
        yield
    yield from make()


def pack(pixels, spare):
    rows, cols, channels = pixels.shape
    spare[...] = jnp.zeros_like(spare)
    spare[:, :, 0:channels] = pixels
    rest = spare[:, :, HALF:]
    second = pltpu.roll(rest[:, cols // 2 :].reshape(-1, HALF), HALF // 2, 1)
    both = rest[:, : cols // 2] + second.reshape(rows, cols // 2, HALF)
    return jnp.concatenate([spare[:, :, :HALF], both], axis=1).astype(BF16)


def unpack(main, rest, turned, channels):
    if turned:
        rest = pltpu.roll(rest.reshape(-1, HALF), HALF // 2, 1).reshape(rest.shape)
    return jnp.concatenate([main, rest], axis=2)[:, :, :channels]


def cut_kernel(
    image_hbm, gain1_hbm, table_hbm, qkv_hbm, image_ref, gain1_ref, table_ref, qkv_ref,
    top, bottom, left, right, spare, sems,
):
    rows, cols, _ = image_ref.shape
    fetches = [
        pltpu.make_async_copy(source, target, sems.at[i])
        for i, (source, target) in enumerate(
            ((image_hbm, image_ref), (gain1_hbm, gain1_ref), (table_hbm, table_ref), (qkv_hbm, qkv_ref))
        )
    ]
    for fetch in fetches:
        fetch.start()
    for fetch in fetches:
        fetch.wait()
    top[...] = pack(image_ref[:SHIFT].astype(F32), spare.at[0])
    bottom[...] = pack(image_ref[rows - SHIFT :].astype(F32), spare.at[1])
    for r in range(0, rows, SIDE):
        band = image_ref[r : r + SIDE].astype(F32)
        left[r : r + SIDE] = band[:, :SHIFT].astype(BF16)
        right[r : r + SIDE] = band[:, cols - SHIFT :].astype(BF16)


def own_kernel(
    image_ref, gain1_ref, table_ref, qkv_ref, gain2_hbm, proj_hbm, conv_hbm, fc1_hbm, fc2_hbm,
    bias, query, kv, normed, wkv, wp, wc, w1, w2, g2,
    padded, strip, wq,
    gain2_ref, proj_ref, conv_ref, fc1_ref, fc2_ref, sems,
):
    rows, cols, channels = image_ref.shape
    head_dim = channels // HEADS
    flag_lane, one_lane = channels, channels + 1
    blocks_r, blocks_c = rows // SIDE, cols // SIDE
    fetches = [
        pltpu.make_async_copy(source, target, sems.at[i])
        for i, (source, target) in enumerate(
            ((conv_hbm, conv_ref), (proj_hbm, proj_ref), (gain2_hbm, gain2_ref), (fc1_hbm, fc1_ref),
             (fc2_hbm, fc2_ref))
        )
    ]
    for fetch in fetches:
        fetch.start()

    for ref in (wq, wkv, wp, wc, w1, w2, g2):
        ref[...] = jnp.zeros_like(ref)
    special = lax.broadcasted_iota(jnp.int32, (16, LANES), 0) + 176
    lanes16 = lax.broadcasted_iota(jnp.int32, (16, LANES), 1)
    wq[176:192, :] = one_hot((special == one_lane) & (lanes16 == flag_lane))
    wkv[176:192, 0:LANES] = jnp.where(
        (special == flag_lane) & (lanes16 == flag_lane), MASKED, 0.0
    ).astype(BF16)
    normed[:, :, HALF:] = jnp.broadcast_to(marks(channels, 0.0)[None], (rows, cols, HALF))

    gain1 = gain1_ref[...]
    scale = head_dim**-0.5 * LOG2E

    wq[0:channels, 0:channels] = qkv_ref[:, 0:channels]
    wkv[0:channels, 0:channels] = qkv_ref[:, channels : 2 * channels]
    wkv[0:channels, LANES : LANES + channels] = qkv_ref[:, 2 * channels :]

    def weights():
        for fetch in fetches:
            fetch.wait()
        wp[0:channels, 0:channels] = proj_ref[...]
        w1[0:channels, 0 : fc1_ref.shape[1]] = fc1_ref[...]
        w2[0 : fc2_ref.shape[1], 0:channels] = fc2_ref[...].astype(F32).T.astype(BF16)
        g2[:, 0:channels] = gain2_ref[...]
        for tap in range(9):
            wc[tap * LANES : tap * LANES + channels, 0:channels] = conv_ref[tap // 3, tap % 3]
            if tap % 3 == 2:
                yield

    def norm(br):
        at = slice(br * SIDE, (br + 1) * SIDE)
        normed[at, :, 0:channels] = layer_norm(image_ref[at].astype(F32), gain1)

    def project(br):
        pixels = normed[br * SIDE : (br + 1) * SIDE].astype(BF16).reshape(-1, LANES)
        q = dot(pixels, wq[...])
        yield
        both = dot(pixels, wkv[...]).reshape(SIDE, cols, 2 * LANES)
        q = (q * scale).reshape(SIDE, cols, LANES)
        for bc in range(blocks_c):
            part = slice(bc * SIDE, (bc + 1) * SIDE)
            query[br, bc] = q[:, part].reshape(AREA, LANES).astype(BF16)
        yield
        for bc in range(blocks_c):
            part = slice(bc * SIDE, (bc + 1) * SIDE)
            kv[br, bc] = both[:, part].reshape(AREA, 2 * LANES).astype(BF16)

    for br in range(blocks_r):
        norm(br)
    tasks = [expand_bias(table_ref, padded, strip, bias), *[project(br) for br in range(blocks_r)]]
    weave([*tasks, weights()], 3)


def edge_kernel(
    image_ref, top_ref, bottom_ref, left_ref, right_ref, gain1_ref,
    bias, query, kv, normed, wkv, wp, wc, w1, w2, g2,
    kv_edge, corner_base, out_edge, out_mid,
    halo, base, shifted,
):
    rows, cols, channels = image_ref.shape
    head_dim = channels // HEADS
    row, last_row = lax.axis_index("row"), lax.axis_size("row") - 1
    col, last_col = lax.axis_index("col"), lax.axis_size("col") - 1
    gain1 = gain1_ref[...]
    outside = [(row == 0).astype(F32), (row == last_row).astype(F32),
               (col == 0).astype(F32), (col == last_col).astype(F32)]

    for r in (0, SHIFT + rows):
        for c in (0, SHIFT + cols):
            halo[r : r + SHIFT, c : c + SHIFT] = jnp.zeros((SHIFT, SHIFT, LANES), F32)
    sides = []

    def band(i):
        ref = (top_ref, bottom_ref, left_ref, right_ref)[i]
        start = (0, SHIFT + (rows if i < 2 else cols))[i % 2]
        inner = slice(SHIFT, SHIFT + (cols if i < 2 else rows))
        outer = slice(start, start + SHIFT)
        place = (outer, inner) if i < 2 else (inner, outer)
        values = ref[...].astype(F32)
        if i < 2:
            rest, half = values[:, cols:], cols // 2
            values = jnp.concatenate(
                [unpack(values[:, :half], rest, False, channels),
                 unpack(values[:, half:cols], rest, True, channels)], axis=1
            )
        mark = jnp.broadcast_to(marks(channels, outside[i])[None], (*values.shape[:2], HALF))
        halo[(*place, slice(HALF, LANES))] = mark
        halo[(*place, slice(0, channels))] = layer_norm(values, gain1 * (1.0 - outside[i]))
        pixels = halo[place]
        if i < 2:
            blocks = [pixels[:, b * SIDE : (b + 1) * SIDE].reshape(AREA, LANES) for b in range(cols // SIDE)]
        else:
            blocks = [pixels.reshape(-1, LANES)]
        pixels = jnp.concatenate(blocks, axis=0).astype(BF16)
        yield
        both = dot(pixels, wkv[...])
        yield
        kv_edge[i] = both.astype(BF16).reshape(-1, AREA, 2 * LANES)
        sides.append(i)

    def tile():
        for r in range(0, rows, SIDE):
            halo[SHIFT + r : SHIFT + r + SIDE, SHIFT : SHIFT + cols] = normed[r : r + SIDE]
            yield

    def convolve(br):
        r = br * SIDE
        for tap in range(3):
            c0 = SHIFT - 1 + tap
            start, stop = 0 if br == 0 else r + 2, r + SIDE + 2
            shifted[tap, start:stop] = halo[
                SHIFT - 1 + start : SHIFT - 1 + stop, c0 : c0 + cols
            ].astype(BF16)
        yield
        taps = [
            shifted[tap % 3, r + tap // 3 : r + tap // 3 + SIDE].reshape(-1, LANES) for tap in range(9)
        ]
        summed = dot(jnp.concatenate(taps, axis=1), wc[...])
        yield
        summed = summed[:, :channels].reshape(SIDE, cols, channels)
        summed = summed + image_ref[r : r + SIDE].astype(F32)
        for bc in range(cols // SIDE):
            part = summed[:, bc * SIDE : (bc + 1) * SIDE].reshape(AREA, channels)
            if (br, bc) in corners:
                ref = corner_base.at[corners.index((br, bc))]
            else:
                ref = base.at[br, bc]
            ref[:, HALF:] = jnp.zeros((AREA, HALF), F32)
            ref[:, 0:channels] = part

    corners = [(0, 0), (0, 3), (3, 0), (3, 3)]
    keys = [
        lambda: [kv_edge[0, 1], kv[0, 1], kv_edge[0, 2], kv[0, 2]],
        lambda: [kv[3, 1], kv_edge[1, 1], kv[3, 2], kv_edge[1, 2]],
        lambda: [kv_edge[2, 1], kv_edge[2, 2], kv[1, 0], kv[2, 0]],
        lambda: [kv[1, 3], kv[2, 3], kv_edge[3, 1], kv_edge[3, 2]],
        lambda: [kv[1, 1], kv[2, 1], kv[1, 2], kv[2, 2]],
    ]
    places = [((0, 1), (0, 2)), ((3, 1), (3, 2)), ((1, 0), (2, 0)), ((1, 3), (2, 3))]
    places += [((1, 1), (1, 2)), ((2, 1), (2, 2))]
    quadrants = [((1, 0), (1, 1)), ((0, 0), (0, 1)), ((0, 1), (1, 1)), ((0, 0), (1, 0))]
    quadrants += [((0, 0), (0, 1)), ((1, 0), (1, 1))]
    done = {}

    def unit(i):
        def put(result):
            done[i] = result

        window = keys[min(i, 4)]
        parts = ([query[at] for at in places[i]], quadrants[i], lambda: jnp.concatenate(window(), axis=0))
        make = lambda: attend(parts, bias, head_dim, channels, put)
        return after(lambda: i >= 4 or i in sides, make)

    def tail(i):
        def put(out):
            if i == 4:
                out_mid[...] = out
            else:
                out_edge[i // 2] = out

        def make():
            return finish(
                jnp.concatenate([done[i], done[i + 1]], axis=0),
                lambda: jnp.concatenate([base[at] for at in (*places[i], *places[i + 1])], axis=0),
                wp, g2[...], w1, w2, channels, put,
            )

        return after(lambda: i in done and i + 1 in done, make)

    weave(
        [unit(4), band(0), band(1), unit(5), band(2), band(3), tile(), unit(0), convolve(0), unit(1),
         convolve(1), unit(2), convolve(2), unit(3), convolve(3), tail(4), tail(0), tail(2)],
        3,
    )


def corner_kernel(
    top_ref, bottom_ref, gain1_ref,
    bias, query, kv, wkv, wp, wc, w1, w2, g2, kv_edge, corner_base, out_mid, out_edge,
    out_hbm,
    normed, out_ref, sems,
):
    rows, _, channels = out_ref.shape
    head_dim = channels // HEADS

    def finish_bands(which, corners):
        def piece(source, i):
            return source[i * AREA : (i + 1) * AREA]

        for br in which:
            if br in (0, 3):
                i = 0 if br == 0 else 2
                band = [corners[0], piece(out_edge.at[0], i), piece(out_edge.at[0], i + 1), corners[1]]
            else:
                i = br - 1
                band = [piece(out_edge.at[1], i), piece(out_mid, 2 * i), piece(out_mid, 2 * i + 1),
                        piece(out_edge.at[1], i + 2)]
            band = [part[:, :channels].reshape(SIDE, SIDE, channels) for part in band]
            out_ref[br * SIDE : (br + 1) * SIDE] = jnp.concatenate(band, axis=1).astype(BF16)

    finish_bands((1, 2), None)
    inner = slice(SIDE, rows - SIDE)
    writes = [pltpu.make_async_copy(out_ref.at[inner], out_hbm.at[inner], sems.at[0])]
    writes[0].start()
    row, last_row = lax.axis_index("row"), lax.axis_size("row") - 1
    col, last_col = lax.axis_index("col"), lax.axis_size("col") - 1
    gain1 = gain1_ref[...]
    out_row = [(row == 0).astype(F32), (row == last_row).astype(F32)]
    out_col = [(col == 0).astype(F32), (col == last_col).astype(F32)]
    corner, done = {}, {}

    def project(pair):
        for i in (2 * pair, 2 * pair + 1):
            ref = (top_ref, bottom_ref)[i // 2]
            inside = (1.0 - out_row[i // 2]) * (1.0 - out_col[i % 2])
            mark = marks(channels, out_row[i // 2] + out_col[i % 2])
            normed[i, :, HALF:] = jnp.broadcast_to(mark, (AREA, HALF))
            values = ref[...].astype(F32)[:, i % 2 * SIDE : (i % 2 + 1) * SIDE]
            normed[i, :, 0:channels] = layer_norm(values.reshape(AREA, channels), gain1 * inside)
        yield
        both = dot(normed[2 * pair : 2 * pair + 2].reshape(-1, LANES).astype(BF16), wkv[...])
        yield
        both = both.astype(BF16)
        corner[2 * pair], corner[2 * pair + 1] = both[:AREA], both[AREA:]

    keys = [
        lambda: [corner[0], kv_edge[2, 0], kv_edge[0, 0], kv[0, 0]],
        lambda: [kv_edge[0, 3], kv[0, 3], corner[1], kv_edge[3, 0]],
        lambda: [kv_edge[2, 3], corner[2], kv[3, 0], kv_edge[1, 0]],
        lambda: [kv[3, 3], kv_edge[1, 3], kv_edge[3, 3], corner[3]],
    ]
    places = [(0, 0), (0, 3), (3, 0), (3, 3)]
    quadrants = [(1, 1), (1, 0), (0, 1), (0, 0)]

    def unit(i):
        def put(result):
            done[i] = result

        parts = ([query[places[i]]], [quadrants[i]], lambda: jnp.concatenate(keys[i](), axis=0))
        return after(lambda: i in corner, lambda: attend(parts, bias, head_dim, channels, put))

    def whole(i):
        tap, y, x = ((0, 7, 7), (2, 7, 0), (6, 0, 7), (8, 0, 0))[i]
        start = y * SIDE
        term = dot(normed[i, start : start + SIDE].astype(BF16), wc[tap * LANES : (tap + 1) * LANES])
        term = term[x : x + 1]
        pixel = lax.broadcasted_iota(jnp.int32, (AREA, 1), 0)
        at = (SIDE - 1 - y) * SIDE + SIDE - 1 - x
        return corner_base[i] + jnp.where(pixel == at, term, 0.0)

    def tail(i):
        def put(out):
            finish_bands((0,) if i == 0 else (3,), [out[:AREA], out[AREA:]])

        def make():
            return finish(
                jnp.concatenate([done[i], done[i + 1]], axis=0),
                lambda: jnp.concatenate([whole(i), whole(i + 1)], axis=0),
                wp, g2[...], w1, w2, channels, put,
            )

        return after(lambda: i in done and i + 1 in done, make)

    weave([project(0), project(1), unit(0), unit(1), unit(2), unit(3), tail(0), tail(2)], 4)
    writes[0].wait()
    for r in (0, rows - SIDE):
        at = slice(r, r + SIDE)
        write = pltpu.make_async_copy(out_ref.at[at], out_hbm.at[at], sems.at[1 if r == 0 else 2])
        write.start()
        writes.append(write)
    writes[1].wait()
    writes[2].wait()


def exchange(low, high, axis):
    count = lax.axis_size(axis)
    before = lax.ppermute(high, axis, [(i, (i + 1) % count) for i in range(count)])
    after = lax.ppermute(low, axis, [((i + 1) % count, i) for i in range(count)])
    return before, after


def call(kernel, name, outs, scratch, flops, operands, in_hbm=()):
    vmem = pl.BlockSpec(memory_space=pltpu.VMEM)
    hbm = pl.BlockSpec(memory_space=pltpu.HBM)
    return pl.pallas_call(
        kernel,
        out_shape=[out if isinstance(out, jax.ShapeDtypeStruct) else pltpu.VMEM(*out) for out in outs],
        in_specs=[hbm if i in in_hbm else vmem for i in range(len(operands))],
        out_specs=[hbm if isinstance(out, jax.ShapeDtypeStruct) else vmem for out in outs],
        scratch_shapes=[pltpu.VMEM(*s) if isinstance(s, tuple) else s for s in scratch],
        cost_estimate=pl.CostEstimate(flops=flops, bytes_accessed=4_000_000, transcendentals=1_000_000),
        compiler_params=pltpu.CompilerParams(vmem_limit_bytes=24 * 1024 * 1024),
        name=name,
    )(*[pltpu.with_memory_space_constraint(x, pltpu.HBM) if i in in_hbm else x for i, x in enumerate(operands)])


def on_device(
    image, norm1_gain, norm2_gain, qkv_weight, proj_weight, rel_table, conv_weight, fc1_weight,
    fc2_weight,
):
    rows, cols, channels = image.shape
    blocks_r, blocks_c = rows // SIDE, cols // SIDE
    gain1, gain2, fc2, table = norm1_gain[None], norm2_gain[None], fc2_weight.T, rel_table.T
    band, column = ((SHIFT, cols * 3 // 2, HALF), BF16), ((rows, SHIFT, channels), BF16)
    tile, gain1, table, qkv_weight, first_rows, last_rows, first_cols, last_cols = call(
        cut_kernel,
        "cut_halo",
        [(image.shape, BF16), (gain1.shape, F32), (table.shape, F32), (qkv_weight.shape, BF16),
         band, band, column, column],
        [((2, SHIFT, cols, LANES), F32), pltpu.SemaphoreType.DMA((4,))],
        1_000_000,
        (image, gain1, table, qkv_weight),
        range(4),
    )
    left, right = exchange(first_cols, last_cols, "col")
    top, bottom = exchange(first_rows, last_rows, "row")
    fetched = (gain2, proj_weight, conv_weight, fc1_weight, fc2)
    hidden = -(-fc1_weight.shape[1] // 128) * 128
    bias, query, kv, normed, wkv, wp, wc, w1, w2, g2 = call(
        own_kernel,
        "own_tile",
        [
            ((HEADS, 2, 2, AREA, WIN * WIN), F32),
            ((blocks_r, blocks_c, AREA, LANES), BF16),
            ((blocks_r, blocks_c, AREA, 2 * LANES), BF16),
            ((rows, cols, LANES), F32),
            ((LANES, 2 * LANES), BF16),
            ((LANES, LANES), BF16),
            ((9 * LANES, LANES), BF16),
            ((LANES, hidden), BF16),
            ((hidden, LANES), BF16),
            ((1, LANES), F32),
        ],
        [
            ((8, 1024), F32),
            ((4, 8 * WIN, 128), F32),
            ((LANES, LANES), BF16),
            *[(x.shape, x.dtype) for x in fetched],
            pltpu.SemaphoreType.DMA((len(fetched),)),
        ],
        2_000_000_000,
        (tile, gain1, table, qkv_weight, gain2, proj_weight, conv_weight, fc1_weight, fc2),
        range(4, 9),
    )
    first = jnp.concatenate([left[:SHIFT], right[:SHIFT]], axis=1)
    last = jnp.concatenate([left[rows - SHIFT :], right[rows - SHIFT :]], axis=1)
    top_corner, bottom_corner = exchange(first, last, "row")
    kv_edge, corner_base, out_edge, out_mid = call(
        edge_kernel,
        "edge_windows",
        [
            ((4, blocks_c, AREA, 2 * LANES), BF16),
            ((4, AREA, LANES), F32),
            ((2, 4 * AREA, LANES), F32),
            ((4 * AREA, LANES), F32),
        ],
        [
            ((rows + 2 * SHIFT, cols + 2 * SHIFT, LANES), F32),
            ((blocks_r, blocks_c, AREA, LANES), F32),
            ((3, rows + 2, cols, LANES), BF16),
        ],
        2_000_000_000,
        (tile, top, bottom, left, right, gain1, bias, query, kv, normed, wkv, wp, wc, w1, w2, g2),
    )
    (out,) = call(
        corner_kernel,
        "corner_windows",
        [jax.ShapeDtypeStruct(image.shape, BF16)],
        [((4, AREA, LANES), F32), (image.shape, BF16), pltpu.SemaphoreType.DMA((3,))],
        1_000_000_000,
        (top_corner, bottom_corner, gain1, bias, query, kv, wkv, wp, wc, w1, w2, g2,
         kv_edge, corner_base, out_mid, out_edge),
    )
    return out


def solution(mesh):
    placed = (P("row", "col", None), P(), P(), P(), P(), P(), P(), P(), P())
    return jax.shard_map(
        on_device, mesh=mesh, in_specs=placed, out_specs=P("row", "col", None), check_vma=False
    )
```

```python
import math

import jax
import jax.numpy as jnp
from jax import lax
from jax.experimental import pallas as pl
from jax.experimental.pallas import tpu as pltpu
from jax.sharding import PartitionSpec as P

HEADS = 6
WIN = 16
SHIFT = 8
SIDE = 8
AREA = SIDE * SIDE
LANES = 256
HALF = LANES // 2
F32 = jnp.float32
BF16 = jnp.bfloat16
LOG2E = math.log2(math.e)
MASKED = -4.0e9


def weave(tasks, width):
    waiting, active = list(tasks), []
    while waiting or active:
        while waiting and len(active) < width:
            active.append(waiting.pop(0))
        for task in list(active):
            try:
                next(task)
            except StopIteration:
                active.remove(task)


def layer_norm(values, norm_gain):
    centre = jnp.mean(values, axis=-1, keepdims=True)
    values = values - centre
    spread = jnp.mean(values * values, axis=-1, keepdims=True)
    return values * lax.rsqrt(spread + 1e-05) * norm_gain


def layer_norm_padded(values, norm_gain, channels):
    centre = jnp.sum(values, axis=-1, keepdims=True) * (1.0 / channels)
    values = jnp.where(lanes_of() < channels, values - centre, 0.0)
    spread = jnp.sum(values * values, axis=-1, keepdims=True) * (1.0 / channels)
    return values * lax.rsqrt(spread + 1e-05) * norm_gain


def dot(a, b):
    return jnp.dot(a, b, preferred_element_type=F32)


def dot_nt(a, b):
    return lax.dot_general(a, b, (((1,), (1,)), ((), ())), preferred_element_type=F32)


def one_hot(condition):
    return jnp.where(condition, 1.0, 0.0).astype(BF16)


def gelu(x):
    square = jnp.minimum(x * x, 25.0)
    poly = -5.58203231240273e-08
    for factor in (2.777085437695777e-06, -4.707012890217347e-05, -5.859274357446709e-05,
                   0.036366718434813275, 0.7978721905787034):
        poly = poly * square + factor
    half = 0.5 * x
    return half + half * jnp.tanh(x * poly)


def lanes_of(width=LANES):
    return lax.broadcasted_iota(jnp.int32, (1, width), 1)


def marks(channels, outside):
    half = lanes_of()[:, HALF:]
    return jnp.where(half == channels + 1, 1.0, 0.0) + jnp.where(half == channels, outside, 0.0)


def expand_bias(table_ref, padded, strip, bias):
    span = 2 * WIN - 1
    padded[...] = jnp.zeros_like(padded)
    padded[0:HEADS, 0 : span * span] = table_ref[...] * LOG2E
    table = padded[...]
    width = padded.shape[1]
    shifted = jnp.concatenate(
        [table if px == 0 else pltpu.roll(table, width - px, 1) for px in range(WIN)], axis=0
    )
    high = shifted.astype(BF16)
    low = (shifted - high.astype(F32)).astype(BF16)
    yield
    entry = lax.broadcasted_iota(jnp.int32, (width, 512), 0)
    place = lax.broadcasted_iota(jnp.int32, (1, 512), 1)
    column = lax.div(place, 256) * SIDE + lax.rem(place, SIDE)
    wanted = (span - 1 - lax.div(lax.rem(place, 256), SIDE)) * span + WIN - 1 - column
    picked = dot(jnp.concatenate([high, low], axis=0), one_hot(entry == wanted))
    yield
    half = 8 * WIN
    picked = picked[:half] + picked[half:]
    for tile in range(4):
        strip[tile] = picked[:, 128 * tile : 128 * (tile + 1)]
    for head in range(HEADS):
        yield
        for half in range(2):
            rows = jnp.concatenate(
                [strip[2 * half + t, pl.ds(head, WIN, stride=8), :] for t in range(2)], axis=1
            )
            for py in range(WIN):
                start = (WIN - 1 - py) * SIDE
                rolled = (rows if start == 0 else pltpu.roll(rows, 256 - start, 1))[:, 0:128]
                lanes = slice(128 * half, 128 * (half + 1))
                place = slice(py % SIDE * SIDE, (py % SIDE + 1) * SIDE)
                bias[head, py // SIDE, 0, place, lanes] = rolled[:SIDE]
                bias[head, py // SIDE, 1, place, lanes] = rolled[SIDE:]


def scores_of(blocks, keys, head_dim, channels):
    lane = lanes_of()
    part = jnp.concatenate(blocks, axis=0)
    own = [(lane >= h * head_dim) & (lane < (h + 1) * head_dim) for h in range(HEADS)]
    stacked = jnp.concatenate(
        [part * one_hot(own[h] | (lane == channels)) for h in range(HEADS)], axis=0
    )
    return dot_nt(stacked, keys)


def attend(unit, bias, head_dim, channels, put):
    lane = lanes_of()
    blocks, quadrants, pair = unit
    pair = pair()
    scores = scores_of(blocks, pair[:, :LANES], head_dim, channels)
    count = scores.shape[0] // HEADS
    yield
    part_bias = jnp.concatenate([bias[:, hy, hx] for hy, hx in quadrants], axis=1)
    scores = scores.reshape(HEADS, count, WIN * WIN) + part_bias
    scores = scores - jnp.max(scores, axis=-1, keepdims=True)
    weights = jnp.exp2(scores)
    total = jnp.sum(weights, axis=-1, keepdims=True)
    weights = weights.astype(BF16).reshape(HEADS * count, WIN * WIN)
    yield
    mixed = dot(weights, pair[:, LANES:])
    yield
    result, divisor = mixed[0:count], jnp.broadcast_to(total[0], (count, LANES))
    for h in range(1, HEADS):
        mine = (lane >= h * head_dim) & (lane < (h + 1) * head_dim)
        result = jnp.where(mine, mixed[h * count : (h + 1) * count], result)
        divisor = jnp.where(mine, total[h], divisor)
    put((result / divisor).astype(BF16))


def finish(heads_out, base, wp, gain2, w1, w2, channels, put):
    attended = dot(heads_out, wp[...])
    yield
    state1 = base() + attended.astype(BF16).astype(F32)
    normed2 = layer_norm_padded(state1, gain2, channels).astype(BF16)
    yield
    hidden = dot(normed2, w1[...])
    yield
    hidden = gelu(hidden).astype(BF16)
    yield
    put(state1 + dot(hidden, w2[...]))


def after(ready, make):
    while not ready():
        yield
    yield from make()


def pack(pixels, spare):
    rows, cols, channels = pixels.shape
    spare[...] = jnp.zeros_like(spare)
    spare[:, :, 0:channels] = pixels
    rest = spare[:, :, HALF:]
    second = pltpu.roll(rest[:, cols // 2 :].reshape(-1, HALF), HALF // 2, 1)
    both = rest[:, : cols // 2] + second.reshape(rows, cols // 2, HALF)
    return jnp.concatenate([spare[:, :, :HALF], both], axis=1).astype(BF16)


def unpack(main, rest, turned, channels):
    if turned:
        rest = pltpu.roll(rest.reshape(-1, HALF), HALF // 2, 1).reshape(rest.shape)
    return jnp.concatenate([main, rest], axis=2)[:, :, :channels]


def cut_kernel(
    image_hbm, gain1_hbm, table_hbm, qkv_hbm, image_ref, gain1_ref, table_ref, qkv_ref,
    top, bottom, left, right, spare, sems,
):
    rows, cols, _ = image_ref.shape
    fetches = [
        pltpu.make_async_copy(source, target, sems.at[i])
        for i, (source, target) in enumerate(
            ((image_hbm, image_ref), (gain1_hbm, gain1_ref), (table_hbm, table_ref), (qkv_hbm, qkv_ref))
        )
    ]
    for fetch in fetches:
        fetch.start()
    for fetch in fetches:
        fetch.wait()
    top[...] = pack(image_ref[:SHIFT].astype(F32), spare.at[0])
    bottom[...] = pack(image_ref[rows - SHIFT :].astype(F32), spare.at[1])
    for r in range(0, rows, SIDE):
        band = image_ref[r : r + SIDE].astype(F32)
        left[r : r + SIDE] = band[:, :SHIFT].astype(BF16)
        right[r : r + SIDE] = band[:, cols - SHIFT :].astype(BF16)


def own_kernel(
    image_ref, gain1_ref, table_ref, qkv_ref, gain2_hbm, proj_hbm, conv_hbm, fc1_hbm, fc2_hbm,
    bias, query, kv, normed, wkv, wp, wc, w1, w2, g2,
    padded, strip, wq,
    gain2_ref, proj_ref, conv_ref, fc1_ref, fc2_ref, sems,
):
    rows, cols, channels = image_ref.shape
    head_dim = channels // HEADS
    flag_lane, one_lane = channels, channels + 1
    blocks_r, blocks_c = rows // SIDE, cols // SIDE
    fetches = [
        pltpu.make_async_copy(source, target, sems.at[i])
        for i, (source, target) in enumerate(
            ((conv_hbm, conv_ref), (proj_hbm, proj_ref), (gain2_hbm, gain2_ref), (fc1_hbm, fc1_ref),
             (fc2_hbm, fc2_ref))
        )
    ]
    for fetch in fetches:
        fetch.start()

    for ref in (wq, wkv, wp, wc, w1, w2, g2):
        ref[...] = jnp.zeros_like(ref)
    special = lax.broadcasted_iota(jnp.int32, (16, LANES), 0) + 176
    lanes16 = lax.broadcasted_iota(jnp.int32, (16, LANES), 1)
    wq[176:192, :] = one_hot((special == one_lane) & (lanes16 == flag_lane))
    wkv[176:192, 0:LANES] = jnp.where(
        (special == flag_lane) & (lanes16 == flag_lane), MASKED, 0.0
    ).astype(BF16)
    normed[:, :, HALF:] = jnp.broadcast_to(marks(channels, 0.0)[None], (rows, cols, HALF))

    gain1 = gain1_ref[...]
    scale = head_dim**-0.5 * LOG2E

    wq[0:channels, 0:channels] = qkv_ref[:, 0:channels]
    wkv[0:channels, 0:channels] = qkv_ref[:, channels : 2 * channels]
    wkv[0:channels, LANES : LANES + channels] = qkv_ref[:, 2 * channels :]

    def weights():
        for fetch in fetches:
            fetch.wait()
        wp[0:channels, 0:channels] = proj_ref[...]
        w1[0:channels, 0 : fc1_ref.shape[1]] = fc1_ref[...]
        w2[0 : fc2_ref.shape[1], 0:channels] = fc2_ref[...].astype(F32).T.astype(BF16)
        g2[:, 0:channels] = gain2_ref[...]
        for tap in range(9):
            wc[tap * LANES : tap * LANES + channels, 0:channels] = conv_ref[tap // 3, tap % 3]
            if tap % 3 == 2:
                yield

    def norm(br):
        at = slice(br * SIDE, (br + 1) * SIDE)
        normed[at, :, 0:channels] = layer_norm(image_ref[at].astype(F32), gain1)

    def project(br):
        pixels = normed[br * SIDE : (br + 1) * SIDE].astype(BF16).reshape(-1, LANES)
        q = dot(pixels, wq[...])
        yield
        both = dot(pixels, wkv[...]).reshape(SIDE, cols, 2 * LANES)
        q = (q * scale).reshape(SIDE, cols, LANES)
        for bc in range(blocks_c):
            part = slice(bc * SIDE, (bc + 1) * SIDE)
            query[br, bc] = q[:, part].reshape(AREA, LANES).astype(BF16)
        yield
        for bc in range(blocks_c):
            part = slice(bc * SIDE, (bc + 1) * SIDE)
            kv[br, bc] = both[:, part].reshape(AREA, 2 * LANES).astype(BF16)

    for br in range(blocks_r):
        norm(br)
    tasks = [expand_bias(table_ref, padded, strip, bias), *[project(br) for br in range(blocks_r)]]
    weave([*tasks, weights()], 3)


def edge_kernel(
    image_ref, top_ref, bottom_ref, left_ref, right_ref, gain1_ref,
    bias, query, kv, normed, wkv, wp, wc, w1, w2, g2,
    kv_edge, corner_base, out_edge, out_mid,
    halo, base, shifted,
):
    rows, cols, channels = image_ref.shape
    head_dim = channels // HEADS
    row, last_row = lax.axis_index("row"), lax.axis_size("row") - 1
    col, last_col = lax.axis_index("col"), lax.axis_size("col") - 1
    gain1 = gain1_ref[...]
    outside = [(row == 0).astype(F32), (row == last_row).astype(F32),
               (col == 0).astype(F32), (col == last_col).astype(F32)]

    for r in (0, SHIFT + rows):
        for c in (0, SHIFT + cols):
            halo[r : r + SHIFT, c : c + SHIFT] = jnp.zeros((SHIFT, SHIFT, LANES), F32)
    sides = []

    def band(i):
        ref = (top_ref, bottom_ref, left_ref, right_ref)[i]
        start = (0, SHIFT + (rows if i < 2 else cols))[i % 2]
        inner = slice(SHIFT, SHIFT + (cols if i < 2 else rows))
        outer = slice(start, start + SHIFT)
        place = (outer, inner) if i < 2 else (inner, outer)
        values = ref[...].astype(F32)
        if i < 2:
            rest, half = values[:, cols:], cols // 2
            values = jnp.concatenate(
                [unpack(values[:, :half], rest, False, channels),
                 unpack(values[:, half:cols], rest, True, channels)], axis=1
            )
        mark = jnp.broadcast_to(marks(channels, outside[i])[None], (*values.shape[:2], HALF))
        halo[(*place, slice(HALF, LANES))] = mark
        halo[(*place, slice(0, channels))] = layer_norm(values, gain1 * (1.0 - outside[i]))
        pixels = halo[place]
        if i < 2:
            blocks = [pixels[:, b * SIDE : (b + 1) * SIDE].reshape(AREA, LANES) for b in range(cols // SIDE)]
        else:
            blocks = [pixels.reshape(-1, LANES)]
        pixels = jnp.concatenate(blocks, axis=0).astype(BF16)
        yield
        both = dot(pixels, wkv[...])
        yield
        kv_edge[i] = both.astype(BF16).reshape(-1, AREA, 2 * LANES)
        sides.append(i)

    def tile():
        for r in range(0, rows, SIDE):
            halo[SHIFT + r : SHIFT + r + SIDE, SHIFT : SHIFT + cols] = normed[r : r + SIDE]
            yield

    def convolve(br):
        r = br * SIDE
        for tap in range(3):
            c0 = SHIFT - 1 + tap
            start, stop = 0 if br == 0 else r + 2, r + SIDE + 2
            shifted[tap, start:stop] = halo[
                SHIFT - 1 + start : SHIFT - 1 + stop, c0 : c0 + cols
            ].astype(BF16)
        yield
        taps = [
            shifted[tap % 3, r + tap // 3 : r + tap // 3 + SIDE].reshape(-1, LANES) for tap in range(9)
        ]
        summed = dot(jnp.concatenate(taps, axis=1), wc[...])
        yield
        summed = summed[:, :channels].reshape(SIDE, cols, channels)
        summed = summed + image_ref[r : r + SIDE].astype(F32)
        for bc in range(cols // SIDE):
            part = summed[:, bc * SIDE : (bc + 1) * SIDE].reshape(AREA, channels)
            if (br, bc) in corners:
                ref = corner_base.at[corners.index((br, bc))]
            else:
                ref = base.at[br, bc]
            ref[:, HALF:] = jnp.zeros((AREA, HALF), F32)
            ref[:, 0:channels] = part

    corners = [(0, 0), (0, 3), (3, 0), (3, 3)]
    keys = [
        lambda: [kv_edge[0, 1], kv[0, 1], kv_edge[0, 2], kv[0, 2]],
        lambda: [kv[3, 1], kv_edge[1, 1], kv[3, 2], kv_edge[1, 2]],
        lambda: [kv_edge[2, 1], kv_edge[2, 2], kv[1, 0], kv[2, 0]],
        lambda: [kv[1, 3], kv[2, 3], kv_edge[3, 1], kv_edge[3, 2]],
        lambda: [kv[1, 1], kv[2, 1], kv[1, 2], kv[2, 2]],
    ]
    places = [((0, 1), (0, 2)), ((3, 1), (3, 2)), ((1, 0), (2, 0)), ((1, 3), (2, 3))]
    places += [((1, 1), (1, 2)), ((2, 1), (2, 2))]
    quadrants = [((1, 0), (1, 1)), ((0, 0), (0, 1)), ((0, 1), (1, 1)), ((0, 0), (1, 0))]
    quadrants += [((0, 0), (0, 1)), ((1, 0), (1, 1))]
    done = {}

    def unit(i):
        def put(result):
            done[i] = result

        window = keys[min(i, 4)]
        parts = ([query[at] for at in places[i]], quadrants[i], lambda: jnp.concatenate(window(), axis=0))
        make = lambda: attend(parts, bias, head_dim, channels, put)
        return after(lambda: i >= 4 or i in sides, make)

    def tail(i):
        def put(out):
            if i == 4:
                out_mid[...] = out
            else:
                out_edge[i // 2] = out

        def make():
            return finish(
                jnp.concatenate([done[i], done[i + 1]], axis=0),
                lambda: jnp.concatenate([base[at] for at in (*places[i], *places[i + 1])], axis=0),
                wp, g2[...], w1, w2, channels, put,
            )

        return after(lambda: i in done and i + 1 in done, make)

    weave(
        [unit(4), band(0), band(1), unit(5), band(2), band(3), tile(), unit(0), convolve(0), unit(1),
         convolve(1), unit(2), convolve(2), unit(3), convolve(3), tail(4), tail(0), tail(2)],
        3,
    )


def corner_kernel(
    left_ref, right_ref, gain1_ref,
    bias, query, kv, wkv, wp, wc, w1, w2, g2, kv_edge, corner_base, out_mid, out_edge,
    out_hbm,
    normed, out_ref, sems,
):
    rows, _, channels = out_ref.shape
    head_dim = channels // HEADS

    def finish_bands(which, corners):
        def piece(source, i):
            return source[i * AREA : (i + 1) * AREA]

        for br in which:
            if br in (0, 3):
                i = 0 if br == 0 else 2
                band = [corners[i], piece(out_edge.at[0], i), piece(out_edge.at[0], i + 1), corners[i + 1]]
            else:
                i = br - 1
                band = [piece(out_edge.at[1], i), piece(out_mid, 2 * i), piece(out_mid, 2 * i + 1),
                        piece(out_edge.at[1], i + 2)]
            band = [part[:, :channels].reshape(SIDE, SIDE, channels) for part in band]
            out_ref[br * SIDE : (br + 1) * SIDE] = jnp.concatenate(band, axis=1).astype(BF16)

    finish_bands((1, 2), None)
    inner = slice(SIDE, rows - SIDE)
    writes = [pltpu.make_async_copy(out_ref.at[inner], out_hbm.at[inner], sems.at[0])]
    writes[0].start()
    row, last_row = lax.axis_index("row"), lax.axis_size("row") - 1
    col, last_col = lax.axis_index("col"), lax.axis_size("col") - 1
    gain1 = gain1_ref[...]
    out_row = [(row == 0).astype(F32), (row == last_row).astype(F32)]
    out_col = [(col == 0).astype(F32), (col == last_col).astype(F32)]
    corner, done = {}, {}

    def project():
        for i in range(4):
            ref = (left_ref, right_ref)[i % 2]
            inside = (1.0 - out_row[i // 2]) * (1.0 - out_col[i % 2])
            mark = marks(channels, out_row[i // 2] + out_col[i % 2])
            normed[i, :, HALF:] = jnp.broadcast_to(mark, (AREA, HALF))
            values = ref[i // 2 * SIDE : (i // 2 + 1) * SIDE].astype(F32)
            values = unpack(values[:, :SIDE], values[:, SIDE:], i % 2 == 0, channels)
            normed[i, :, 0:channels] = layer_norm(values.reshape(AREA, channels), gain1 * inside)
        both = dot(normed[...].reshape(-1, LANES).astype(BF16), wkv[...])
        both = both.astype(BF16)
        for i in range(4):
            corner[i] = both[i * AREA : (i + 1) * AREA]

    keys = [
        lambda: [corner[0], kv_edge[2, 0], kv_edge[0, 0], kv[0, 0]],
        lambda: [kv_edge[0, 3], kv[0, 3], corner[1], kv_edge[3, 0]],
        lambda: [kv_edge[2, 3], corner[2], kv[3, 0], kv_edge[1, 0]],
        lambda: [kv[3, 3], kv_edge[1, 3], kv_edge[3, 3], corner[3]],
    ]
    places = [(0, 0), (0, 3), (3, 0), (3, 3)]
    quadrants = [(1, 1), (1, 0), (0, 1), (0, 0)]

    def unit(i):
        def put(result):
            done[i] = result

        parts = ([query[places[i]]], [quadrants[i]], lambda: jnp.concatenate(keys[i](), axis=0))
        return after(lambda: i in corner, lambda: attend(parts, bias, head_dim, channels, put))

    def whole(i):
        tap, y, x = ((0, 7, 7), (2, 7, 0), (6, 0, 7), (8, 0, 0))[i]
        start = y * SIDE
        term = dot(normed[i, start : start + SIDE].astype(BF16), wc[tap * LANES : (tap + 1) * LANES])
        term = term[x : x + 1]
        pixel = lax.broadcasted_iota(jnp.int32, (AREA, 1), 0)
        at = (SIDE - 1 - y) * SIDE + SIDE - 1 - x
        return corner_base[i] + jnp.where(pixel == at, term, 0.0)

    def tail():
        def put(out):
            finish_bands((0, 3), [out[i * AREA : (i + 1) * AREA] for i in range(4)])

        def make():
            return finish(
                jnp.concatenate([done[i] for i in range(4)], axis=0),
                lambda: jnp.concatenate([whole(i) for i in range(4)], axis=0),
                wp, g2[...], w1, w2, channels, put,
            )

        return after(lambda: len(done) == 4, make)

    project()
    units = [unit(i) for i in range(4)]
    next(units[0])
    for i in range(4):
        if i < 3:
            next(units[i + 1])
        weave([units[i]], 1)
    weave([tail()], 1)
    writes[0].wait()
    for r in (0, rows - SIDE):
        at = slice(r, r + SIDE)
        write = pltpu.make_async_copy(out_ref.at[at], out_hbm.at[at], sems.at[1 if r == 0 else 2])
        write.start()
        writes.append(write)
    writes[1].wait()
    writes[2].wait()


def exchange(low, high, axis):
    count = lax.axis_size(axis)
    before = lax.ppermute(high, axis, [(i, (i + 1) % count) for i in range(count)])
    after = lax.ppermute(low, axis, [((i + 1) % count, i) for i in range(count)])
    return before, after


def call(kernel, name, outs, scratch, flops, operands, in_hbm=()):
    vmem = pl.BlockSpec(memory_space=pltpu.VMEM)
    hbm = pl.BlockSpec(memory_space=pltpu.HBM)
    return pl.pallas_call(
        kernel,
        out_shape=[out if isinstance(out, jax.ShapeDtypeStruct) else pltpu.VMEM(*out) for out in outs],
        in_specs=[hbm if i in in_hbm else vmem for i in range(len(operands))],
        out_specs=[hbm if isinstance(out, jax.ShapeDtypeStruct) else vmem for out in outs],
        scratch_shapes=[pltpu.VMEM(*s) if isinstance(s, tuple) else s for s in scratch],
        cost_estimate=pl.CostEstimate(flops=flops, bytes_accessed=4_000_000, transcendentals=1_000_000),
        compiler_params=pltpu.CompilerParams(vmem_limit_bytes=24 * 1024 * 1024),
        name=name,
    )(*[pltpu.with_memory_space_constraint(x, pltpu.HBM) if i in in_hbm else x for i, x in enumerate(operands)])


def on_device(
    image, norm1_gain, norm2_gain, qkv_weight, proj_weight, rel_table, conv_weight, fc1_weight,
    fc2_weight,
):
    rows, cols, channels = image.shape
    blocks_r, blocks_c = rows // SIDE, cols // SIDE
    gain1, gain2, fc2, table = norm1_gain[None], norm2_gain[None], fc2_weight.T, rel_table.T
    band, column = ((SHIFT, cols * 3 // 2, HALF), BF16), ((rows, SHIFT, channels), BF16)
    tile, gain1, table, qkv_weight, first_rows, last_rows, first_cols, last_cols = call(
        cut_kernel,
        "cut_halo",
        [(image.shape, BF16), (gain1.shape, F32), (table.shape, F32), (qkv_weight.shape, BF16),
         band, band, column, column],
        [((2, SHIFT, cols, LANES), F32), pltpu.SemaphoreType.DMA((4,))],
        1_000_000,
        (image, gain1, table, qkv_weight),
        range(4),
    )
    top, bottom = exchange(first_rows, last_rows, "row")
    left, right = exchange(first_cols, last_cols, "col")
    fetched = (gain2, proj_weight, conv_weight, fc1_weight, fc2)
    hidden = -(-fc1_weight.shape[1] // 128) * 128
    bias, query, kv, normed, wkv, wp, wc, w1, w2, g2 = call(
        own_kernel,
        "own_tile",
        [
            ((HEADS, 2, 2, AREA, WIN * WIN), F32),
            ((blocks_r, blocks_c, AREA, LANES), BF16),
            ((blocks_r, blocks_c, AREA, 2 * LANES), BF16),
            ((rows, cols, LANES), F32),
            ((LANES, 2 * LANES), BF16),
            ((LANES, LANES), BF16),
            ((9 * LANES, LANES), BF16),
            ((LANES, hidden), BF16),
            ((hidden, LANES), BF16),
            ((1, LANES), F32),
        ],
        [
            ((8, 1024), F32),
            ((4, 8 * WIN, 128), F32),
            ((LANES, LANES), BF16),
            *[(x.shape, x.dtype) for x in fetched],
            pltpu.SemaphoreType.DMA((len(fetched),)),
        ],
        2_000_000_000,
        (tile, gain1, table, qkv_weight, gain2, proj_weight, conv_weight, fc1_weight, fc2),
        range(4, 9),
    )
    def ends(start, rest):
        parts = [(start, start + SHIFT), (cols + rest, cols + rest + SHIFT)]
        return jnp.concatenate(
            [jnp.concatenate([x[:, a:b] for a, b in parts], axis=1) for x in (top, bottom)]
        )

    first, last = ends(0, 0), ends(cols - SHIFT, cols // 2 - SHIFT)
    left_corner, right_corner = exchange(first, last, "col")
    kv_edge, corner_base, out_edge, out_mid = call(
        edge_kernel,
        "edge_windows",
        [
            ((4, blocks_c, AREA, 2 * LANES), BF16),
            ((4, AREA, LANES), F32),
            ((2, 4 * AREA, LANES), F32),
            ((4 * AREA, LANES), F32),
        ],
        [
            ((rows + 2 * SHIFT, cols + 2 * SHIFT, LANES), F32),
            ((blocks_r, blocks_c, AREA, LANES), F32),
            ((3, rows + 2, cols, LANES), BF16),
        ],
        2_000_000_000,
        (tile, top, bottom, left, right, gain1, bias, query, kv, normed, wkv, wp, wc, w1, w2, g2),
    )
    (out,) = call(
        corner_kernel,
        "corner_windows",
        [jax.ShapeDtypeStruct(image.shape, BF16)],
        [((4, AREA, LANES), F32), (image.shape, BF16), pltpu.SemaphoreType.DMA((3,))],
        1_000_000_000,
        (left_corner, right_corner, gain1, bias, query, kv, wkv, wp, wc, w1, w2, g2,
         kv_edge, corner_base, out_mid, out_edge),
    )
    return out


def solution(mesh):
    placed = (P("row", "col", None), P(), P(), P(), P(), P(), P(), P(), P())
    return jax.shard_map(
        on_device, mesh=mesh, in_specs=placed, out_specs=P("row", "col", None), check_vma=False
    )
```

```python
import math

import jax
import jax.numpy as jnp
from jax import lax
from jax.experimental import pallas as pl
from jax.experimental.pallas import tpu as pltpu
from jax.sharding import PartitionSpec as P

HEADS = 6
WIN = 16
SHIFT = 8
SIDE = 8
AREA = SIDE * SIDE
LANES = 256
HALF = LANES // 2
F32 = jnp.float32
BF16 = jnp.bfloat16
LOG2E = math.log2(math.e)
MASKED = -4.0e9


def weave(tasks, width):
    waiting, active = list(tasks), []
    while waiting or active:
        while waiting and len(active) < width:
            active.append(waiting.pop(0))
        for task in list(active):
            try:
                next(task)
            except StopIteration:
                active.remove(task)


def layer_norm(values, norm_gain):
    centre = jnp.mean(values, axis=-1, keepdims=True)
    values = values - centre
    spread = jnp.mean(values * values, axis=-1, keepdims=True)
    return values * lax.rsqrt(spread + 1e-05) * norm_gain


def layer_norm_padded(values, norm_gain, channels):
    centre = jnp.sum(values, axis=-1, keepdims=True) * (1.0 / channels)
    values = jnp.where(lanes_of() < channels, values - centre, 0.0)
    spread = jnp.sum(values * values, axis=-1, keepdims=True) * (1.0 / channels)
    return values * lax.rsqrt(spread + 1e-05) * norm_gain


def dot(a, b):
    return jnp.dot(a, b, preferred_element_type=F32)


def dot_nt(a, b):
    return lax.dot_general(a, b, (((1,), (1,)), ((), ())), preferred_element_type=F32)


def one_hot(condition):
    return jnp.where(condition, 1.0, 0.0).astype(BF16)


def gelu(x):
    square = jnp.minimum(x * x, 25.0)
    poly = -5.58203231240273e-08
    for factor in (2.777085437695777e-06, -4.707012890217347e-05, -5.859274357446709e-05,
                   0.036366718434813275, 0.7978721905787034):
        poly = poly * square + factor
    half = 0.5 * x
    return half + half * jnp.tanh(x * poly)


def lanes_of(width=LANES):
    return lax.broadcasted_iota(jnp.int32, (1, width), 1)


def marks(channels, outside):
    half = lanes_of()[:, HALF:]
    return jnp.where(half == channels + 1, 1.0, 0.0) + jnp.where(half == channels, outside, 0.0)


def expand_bias(table_ref, padded, strip, bias):
    span = 2 * WIN - 1
    padded[...] = jnp.zeros_like(padded)
    padded[0:HEADS, 0 : span * span] = table_ref[...] * LOG2E
    table = padded[...]
    width = padded.shape[1]
    shifted = jnp.concatenate(
        [table if px == 0 else pltpu.roll(table, width - px, 1) for px in range(WIN)], axis=0
    )
    high = shifted.astype(BF16)
    low = (shifted - high.astype(F32)).astype(BF16)
    yield
    entry = lax.broadcasted_iota(jnp.int32, (width, 512), 0)
    place = lax.broadcasted_iota(jnp.int32, (1, 512), 1)
    column = lax.div(place, 256) * SIDE + lax.rem(place, SIDE)
    wanted = (span - 1 - lax.div(lax.rem(place, 256), SIDE)) * span + WIN - 1 - column
    picked = dot(jnp.concatenate([high, low], axis=0), one_hot(entry == wanted))
    yield
    half = 8 * WIN
    picked = picked[:half] + picked[half:]
    for tile in range(4):
        strip[tile] = picked[:, 128 * tile : 128 * (tile + 1)]
    for head in range(HEADS):
        yield
        for half in range(2):
            rows = jnp.concatenate(
                [strip[2 * half + t, pl.ds(head, WIN, stride=8), :] for t in range(2)], axis=1
            )
            for py in range(WIN):
                start = (WIN - 1 - py) * SIDE
                rolled = (rows if start == 0 else pltpu.roll(rows, 256 - start, 1))[:, 0:128]
                lanes = slice(128 * half, 128 * (half + 1))
                place = slice(py % SIDE * SIDE, (py % SIDE + 1) * SIDE)
                bias[head, py // SIDE, 0, place, lanes] = rolled[:SIDE]
                bias[head, py // SIDE, 1, place, lanes] = rolled[SIDE:]


def scores_of(blocks, keys, head_dim, channels):
    lane = lanes_of()
    part = jnp.concatenate(blocks, axis=0)
    own = [(lane >= h * head_dim) & (lane < (h + 1) * head_dim) for h in range(HEADS)]
    stacked = jnp.concatenate(
        [part * one_hot(own[h] | (lane == channels)) for h in range(HEADS)], axis=0
    )
    return dot_nt(stacked, keys)


def attend(unit, bias, head_dim, channels, put):
    lane = lanes_of()
    blocks, quadrants, pair = unit
    pair = pair()
    scores = scores_of(blocks, pair[:, :LANES], head_dim, channels)
    count = scores.shape[0] // HEADS
    yield
    part_bias = jnp.concatenate([bias[:, hy, hx] for hy, hx in quadrants], axis=1)
    scores = scores.reshape(HEADS, count, WIN * WIN) + part_bias
    scores = scores - jnp.max(scores, axis=-1, keepdims=True)
    weights = jnp.exp2(scores)
    total = jnp.sum(weights, axis=-1, keepdims=True)
    weights = weights.astype(BF16).reshape(HEADS * count, WIN * WIN)
    yield
    mixed = dot(weights, pair[:, LANES:])
    yield
    result, divisor = mixed[0:count], jnp.broadcast_to(total[0], (count, LANES))
    for h in range(1, HEADS):
        mine = (lane >= h * head_dim) & (lane < (h + 1) * head_dim)
        result = jnp.where(mine, mixed[h * count : (h + 1) * count], result)
        divisor = jnp.where(mine, total[h], divisor)
    put((result / divisor).astype(BF16))


def finish(heads_out, base, wp, gain2, w1, w2, channels, put):
    attended = dot(heads_out, wp[...])
    yield
    state1 = base() + attended.astype(BF16).astype(F32)
    normed2 = layer_norm_padded(state1, gain2, channels).astype(BF16)
    yield
    hidden = dot(normed2, w1[...])
    yield
    hidden = gelu(hidden).astype(BF16)
    yield
    put(state1 + dot(hidden, w2[...]))


def after(ready, make):
    while not ready():
        yield
    yield from make()


def pack(pixels, spare):
    rows, cols, channels = pixels.shape
    spare[...] = jnp.zeros_like(spare)
    spare[:, :, 0:channels] = pixels
    rest = spare[:, :, HALF:]
    second = pltpu.roll(rest[:, cols // 2 :].reshape(-1, HALF), HALF // 2, 1)
    both = rest[:, : cols // 2] + second.reshape(rows, cols // 2, HALF)
    return jnp.concatenate([spare[:, :, :HALF], both], axis=1).astype(BF16)


def unpack(main, rest, turned, channels):
    if turned:
        rest = pltpu.roll(rest.reshape(-1, HALF), HALF // 2, 1).reshape(rest.shape)
    return jnp.concatenate([main, rest], axis=2)[:, :, :channels]


def cut_kernel(
    image_hbm, gain1_hbm, table_hbm, qkv_hbm, image_ref, gain1_ref, table_ref, qkv_ref,
    top, bottom, left, right, spare, sems,
):
    rows, cols, _ = image_ref.shape
    fetches = [
        pltpu.make_async_copy(source, target, sems.at[i])
        for i, (source, target) in enumerate(
            ((image_hbm, image_ref), (gain1_hbm, gain1_ref), (table_hbm, table_ref), (qkv_hbm, qkv_ref))
        )
    ]
    for fetch in fetches:
        fetch.start()
    for fetch in fetches:
        fetch.wait()
    top[...] = pack(image_ref[:SHIFT].astype(F32), spare.at[0])
    bottom[...] = pack(image_ref[rows - SHIFT :].astype(F32), spare.at[1])
    for r in range(0, rows, SIDE):
        band = image_ref[r : r + SIDE].astype(F32)
        left[r : r + SIDE] = band[:, :SHIFT].astype(BF16)
        right[r : r + SIDE] = band[:, cols - SHIFT :].astype(BF16)


def own_kernel(
    image_ref, gain1_ref, table_ref, qkv_ref,
    bias, query, kv, normed, wkv,
    padded, strip, wq,
):
    rows, cols, channels = image_ref.shape
    head_dim = channels // HEADS
    flag_lane, one_lane = channels, channels + 1
    blocks_r, blocks_c = rows // SIDE, cols // SIDE
    for ref in (wq, wkv):
        ref[...] = jnp.zeros_like(ref)
    special = lax.broadcasted_iota(jnp.int32, (16, LANES), 0) + 176
    lanes16 = lax.broadcasted_iota(jnp.int32, (16, LANES), 1)
    wq[176:192, :] = one_hot((special == one_lane) & (lanes16 == flag_lane))
    wkv[176:192, 0:LANES] = jnp.where(
        (special == flag_lane) & (lanes16 == flag_lane), MASKED, 0.0
    ).astype(BF16)
    normed[:, :, HALF:] = jnp.broadcast_to(marks(channels, 0.0)[None], (rows, cols, HALF))

    gain1 = gain1_ref[...]
    scale = head_dim**-0.5 * LOG2E

    wq[0:channels, 0:channels] = qkv_ref[:, 0:channels]
    wkv[0:channels, 0:channels] = qkv_ref[:, channels : 2 * channels]
    wkv[0:channels, LANES : LANES + channels] = qkv_ref[:, 2 * channels :]

    def norm(br):
        at = slice(br * SIDE, (br + 1) * SIDE)
        normed[at, :, 0:channels] = layer_norm(image_ref[at].astype(F32), gain1)

    def project(br):
        pixels = normed[br * SIDE : (br + 1) * SIDE].astype(BF16).reshape(-1, LANES)
        q = dot(pixels, wq[...])
        yield
        both = dot(pixels, wkv[...]).reshape(SIDE, cols, 2 * LANES)
        q = (q * scale).reshape(SIDE, cols, LANES)
        for bc in range(blocks_c):
            part = slice(bc * SIDE, (bc + 1) * SIDE)
            query[br, bc] = q[:, part].reshape(AREA, LANES).astype(BF16)
        yield
        for bc in range(blocks_c):
            part = slice(bc * SIDE, (bc + 1) * SIDE)
            kv[br, bc] = both[:, part].reshape(AREA, 2 * LANES).astype(BF16)

    for br in range(blocks_r):
        norm(br)
    weave([expand_bias(table_ref, padded, strip, bias), *[project(br) for br in range(blocks_r)]], 3)


def edge_kernel(
    image_ref, top_ref, bottom_ref, left_ref, right_ref, gain1_ref,
    bias, query, kv, normed, wkv, gain2_hbm, proj_hbm, conv_hbm, fc1_hbm, fc2_hbm,
    kv_edge, corner_base, out_edge, out_mid, wp, wc, w1, w2, g2,
    halo, base, shifted,
    gain2_ref, proj_ref, conv_ref, fc1_ref, fc2_ref, sems,
):
    rows, cols, channels = image_ref.shape
    head_dim = channels // HEADS
    row, last_row = lax.axis_index("row"), lax.axis_size("row") - 1
    col, last_col = lax.axis_index("col"), lax.axis_size("col") - 1
    gain1 = gain1_ref[...]
    outside = [(row == 0).astype(F32), (row == last_row).astype(F32),
               (col == 0).astype(F32), (col == last_col).astype(F32)]

    fetches = [
        pltpu.make_async_copy(source, target, sems.at[i])
        for i, (source, target) in enumerate(
            ((conv_hbm, conv_ref), (proj_hbm, proj_ref), (gain2_hbm, gain2_ref), (fc1_hbm, fc1_ref),
             (fc2_hbm, fc2_ref))
        )
    ]
    for fetch in fetches:
        fetch.start()

    loaded = []

    def weights():
        for ref in (wp, wc, w1, w2, g2):
            ref[...] = jnp.zeros_like(ref)
        yield
        for fetch in fetches:
            fetch.wait()
        wp[0:channels, 0:channels] = proj_ref[...]
        w1[0:channels, 0 : fc1_ref.shape[1]] = fc1_ref[...]
        w2[0 : fc2_ref.shape[1], 0:channels] = fc2_ref[...].astype(F32).T.astype(BF16)
        g2[:, 0:channels] = gain2_ref[...]
        for tap in range(9):
            wc[tap * LANES : tap * LANES + channels, 0:channels] = conv_ref[tap // 3, tap % 3]
            if tap % 3 == 2:
                yield
        loaded.append(True)

    for r in (0, SHIFT + rows):
        for c in (0, SHIFT + cols):
            halo[r : r + SHIFT, c : c + SHIFT] = jnp.zeros((SHIFT, SHIFT, LANES), F32)
    sides = []

    def band(i):
        ref = (top_ref, bottom_ref, left_ref, right_ref)[i]
        start = (0, SHIFT + (rows if i < 2 else cols))[i % 2]
        inner = slice(SHIFT, SHIFT + (cols if i < 2 else rows))
        outer = slice(start, start + SHIFT)
        place = (outer, inner) if i < 2 else (inner, outer)
        values = ref[...].astype(F32)
        if i < 2:
            rest, half = values[:, cols:], cols // 2
            values = jnp.concatenate(
                [unpack(values[:, :half], rest, False, channels),
                 unpack(values[:, half:cols], rest, True, channels)], axis=1
            )
        mark = jnp.broadcast_to(marks(channels, outside[i])[None], (*values.shape[:2], HALF))
        halo[(*place, slice(HALF, LANES))] = mark
        halo[(*place, slice(0, channels))] = layer_norm(values, gain1 * (1.0 - outside[i]))
        pixels = halo[place]
        if i < 2:
            blocks = [pixels[:, b * SIDE : (b + 1) * SIDE].reshape(AREA, LANES) for b in range(cols // SIDE)]
        else:
            blocks = [pixels.reshape(-1, LANES)]
        pixels = jnp.concatenate(blocks, axis=0).astype(BF16)
        yield
        both = dot(pixels, wkv[...])
        yield
        kv_edge[i] = both.astype(BF16).reshape(-1, AREA, 2 * LANES)
        sides.append(i)

    def tile():
        for r in range(0, rows, SIDE):
            halo[SHIFT + r : SHIFT + r + SIDE, SHIFT : SHIFT + cols] = normed[r : r + SIDE]
            yield

    def convolve(br):
        r = br * SIDE
        for tap in range(3):
            c0 = SHIFT - 1 + tap
            start, stop = 0 if br == 0 else r + 2, r + SIDE + 2
            shifted[tap, start:stop] = halo[
                SHIFT - 1 + start : SHIFT - 1 + stop, c0 : c0 + cols
            ].astype(BF16)
        yield
        taps = [
            shifted[tap % 3, r + tap // 3 : r + tap // 3 + SIDE].reshape(-1, LANES) for tap in range(9)
        ]
        summed = dot(jnp.concatenate(taps, axis=1), wc[...])
        yield
        summed = summed[:, :channels].reshape(SIDE, cols, channels)
        summed = summed + image_ref[r : r + SIDE].astype(F32)
        for bc in range(cols // SIDE):
            part = summed[:, bc * SIDE : (bc + 1) * SIDE].reshape(AREA, channels)
            if (br, bc) in corners:
                ref = corner_base.at[corners.index((br, bc))]
            else:
                ref = base.at[br, bc]
            ref[:, HALF:] = jnp.zeros((AREA, HALF), F32)
            ref[:, 0:channels] = part

    corners = [(0, 0), (0, 3), (3, 0), (3, 3)]
    keys = [
        lambda: [kv_edge[0, 1], kv[0, 1], kv_edge[0, 2], kv[0, 2]],
        lambda: [kv[3, 1], kv_edge[1, 1], kv[3, 2], kv_edge[1, 2]],
        lambda: [kv_edge[2, 1], kv_edge[2, 2], kv[1, 0], kv[2, 0]],
        lambda: [kv[1, 3], kv[2, 3], kv_edge[3, 1], kv_edge[3, 2]],
        lambda: [kv[1, 1], kv[2, 1], kv[1, 2], kv[2, 2]],
    ]
    places = [((0, 1), (0, 2)), ((3, 1), (3, 2)), ((1, 0), (2, 0)), ((1, 3), (2, 3))]
    places += [((1, 1), (1, 2)), ((2, 1), (2, 2))]
    quadrants = [((1, 0), (1, 1)), ((0, 0), (0, 1)), ((0, 1), (1, 1)), ((0, 0), (1, 0))]
    quadrants += [((0, 0), (0, 1)), ((1, 0), (1, 1))]
    done = {}

    def unit(i):
        def put(result):
            done[i] = result

        window = keys[min(i, 4)]
        parts = ([query[at] for at in places[i]], quadrants[i], lambda: jnp.concatenate(window(), axis=0))
        make = lambda: attend(parts, bias, head_dim, channels, put)
        return after(lambda: i >= 4 or i in sides, make)

    def tail(i):
        def put(out):
            if i == 4:
                out_mid[...] = out
            else:
                out_edge[i // 2] = out

        def make():
            return finish(
                jnp.concatenate([done[i], done[i + 1]], axis=0),
                lambda: jnp.concatenate([base[at] for at in (*places[i], *places[i + 1])], axis=0),
                wp, g2[...], w1, w2, channels, put,
            )

        return after(lambda: i in done and i + 1 in done, make)

    conv = lambda br: after(lambda: bool(loaded), lambda: convolve(br))
    weave(
        [unit(4), band(0), band(1), unit(5), band(2), band(3), weights(), tile(), unit(0), conv(0), unit(1),
         conv(1), unit(2), conv(2), unit(3), conv(3), tail(4), tail(0), tail(2)],
        3,
    )


def corner_kernel(
    left_ref, right_ref, gain1_ref,
    bias, query, kv, wkv, wp, wc, w1, w2, g2, kv_edge, corner_base, out_mid, out_edge,
    out_hbm,
    normed, out_ref, sems,
):
    rows, _, channels = out_ref.shape
    head_dim = channels // HEADS

    def finish_bands(which, corners):
        def piece(source, i):
            return source[i * AREA : (i + 1) * AREA]

        for br in which:
            if br in (0, 3):
                i = 0 if br == 0 else 2
                band = [corners[0], piece(out_edge.at[0], i), piece(out_edge.at[0], i + 1), corners[1]]
            else:
                i = br - 1
                band = [piece(out_edge.at[1], i), piece(out_mid, 2 * i), piece(out_mid, 2 * i + 1),
                        piece(out_edge.at[1], i + 2)]
            band = [part[:, :channels].reshape(SIDE, SIDE, channels) for part in band]
            out_ref[br * SIDE : (br + 1) * SIDE] = jnp.concatenate(band, axis=1).astype(BF16)

    finish_bands((1, 2), None)
    inner = slice(SIDE, rows - SIDE)
    writes = [pltpu.make_async_copy(out_ref.at[inner], out_hbm.at[inner], sems.at[0])]
    writes[0].start()
    row, last_row = lax.axis_index("row"), lax.axis_size("row") - 1
    col, last_col = lax.axis_index("col"), lax.axis_size("col") - 1
    gain1 = gain1_ref[...]
    out_row = [(row == 0).astype(F32), (row == last_row).astype(F32)]
    out_col = [(col == 0).astype(F32), (col == last_col).astype(F32)]
    corner, done = {}, {}

    def project(pair):
        for i in (2 * pair, 2 * pair + 1):
            ref = (left_ref, right_ref)[i % 2]
            inside = (1.0 - out_row[i // 2]) * (1.0 - out_col[i % 2])
            mark = marks(channels, out_row[i // 2] + out_col[i % 2])
            normed[i, :, HALF:] = jnp.broadcast_to(mark, (AREA, HALF))
            values = ref[i // 2 * SIDE : (i // 2 + 1) * SIDE].astype(F32)
            values = unpack(values[:, :SIDE], values[:, SIDE:], i % 2 == 0, channels)
            normed[i, :, 0:channels] = layer_norm(values.reshape(AREA, channels), gain1 * inside)
        yield
        both = dot(normed[2 * pair : 2 * pair + 2].reshape(-1, LANES).astype(BF16), wkv[...])
        yield
        both = both.astype(BF16)
        corner[2 * pair], corner[2 * pair + 1] = both[:AREA], both[AREA:]

    keys = [
        lambda: [corner[0], kv_edge[2, 0], kv_edge[0, 0], kv[0, 0]],
        lambda: [kv_edge[0, 3], kv[0, 3], corner[1], kv_edge[3, 0]],
        lambda: [kv_edge[2, 3], corner[2], kv[3, 0], kv_edge[1, 0]],
        lambda: [kv[3, 3], kv_edge[1, 3], kv_edge[3, 3], corner[3]],
    ]
    places = [(0, 0), (0, 3), (3, 0), (3, 3)]
    quadrants = [(1, 1), (1, 0), (0, 1), (0, 0)]

    def unit(i):
        def put(result):
            done[i] = result

        parts = ([query[places[i]]], [quadrants[i]], lambda: jnp.concatenate(keys[i](), axis=0))
        return after(lambda: i in corner, lambda: attend(parts, bias, head_dim, channels, put))

    def whole(i):
        tap, y, x = ((0, 7, 7), (2, 7, 0), (6, 0, 7), (8, 0, 0))[i]
        start = y * SIDE
        term = dot(normed[i, start : start + SIDE].astype(BF16), wc[tap * LANES : (tap + 1) * LANES])
        term = term[x : x + 1]
        pixel = lax.broadcasted_iota(jnp.int32, (AREA, 1), 0)
        at = (SIDE - 1 - y) * SIDE + SIDE - 1 - x
        return corner_base[i] + jnp.where(pixel == at, term, 0.0)

    def tail(i):
        def put(out):
            finish_bands((0,) if i == 0 else (3,), [out[:AREA], out[AREA:]])

        def make():
            return finish(
                jnp.concatenate([done[i], done[i + 1]], axis=0),
                lambda: jnp.concatenate([whole(i), whole(i + 1)], axis=0),
                wp, g2[...], w1, w2, channels, put,
            )

        return after(lambda: i in done and i + 1 in done, make)

    weave([project(0), project(1), unit(0), unit(1), unit(2), unit(3), tail(0), tail(2)], 4)
    writes[0].wait()
    for r in (0, rows - SIDE):
        at = slice(r, r + SIDE)
        write = pltpu.make_async_copy(out_ref.at[at], out_hbm.at[at], sems.at[1 if r == 0 else 2])
        write.start()
        writes.append(write)
    writes[1].wait()
    writes[2].wait()


def exchange(low, high, axis):
    count = lax.axis_size(axis)
    before = lax.ppermute(high, axis, [(i, (i + 1) % count) for i in range(count)])
    after = lax.ppermute(low, axis, [((i + 1) % count, i) for i in range(count)])
    return before, after


def call(kernel, name, outs, scratch, flops, operands, in_hbm=()):
    vmem = pl.BlockSpec(memory_space=pltpu.VMEM)
    hbm = pl.BlockSpec(memory_space=pltpu.HBM)
    return pl.pallas_call(
        kernel,
        out_shape=[out if isinstance(out, jax.ShapeDtypeStruct) else pltpu.VMEM(*out) for out in outs],
        in_specs=[hbm if i in in_hbm else vmem for i in range(len(operands))],
        out_specs=[hbm if isinstance(out, jax.ShapeDtypeStruct) else vmem for out in outs],
        scratch_shapes=[pltpu.VMEM(*s) if isinstance(s, tuple) else s for s in scratch],
        cost_estimate=pl.CostEstimate(flops=flops, bytes_accessed=4_000_000, transcendentals=1_000_000),
        compiler_params=pltpu.CompilerParams(vmem_limit_bytes=24 * 1024 * 1024),
        name=name,
    )(*[pltpu.with_memory_space_constraint(x, pltpu.HBM) if i in in_hbm else x for i, x in enumerate(operands)])


def on_device(
    image, norm1_gain, norm2_gain, qkv_weight, proj_weight, rel_table, conv_weight, fc1_weight,
    fc2_weight,
):
    rows, cols, channels = image.shape
    blocks_r, blocks_c = rows // SIDE, cols // SIDE
    gain1, gain2, fc2, table = norm1_gain[None], norm2_gain[None], fc2_weight.T, rel_table.T
    band, column = ((SHIFT, cols * 3 // 2, HALF), BF16), ((rows, SHIFT, channels), BF16)
    tile, gain1, table, qkv_weight, first_rows, last_rows, first_cols, last_cols = call(
        cut_kernel,
        "cut_halo",
        [(image.shape, BF16), (gain1.shape, F32), (table.shape, F32), (qkv_weight.shape, BF16),
         band, band, column, column],
        [((2, SHIFT, cols, LANES), F32), pltpu.SemaphoreType.DMA((4,))],
        1_000_000,
        (image, gain1, table, qkv_weight),
        range(4),
    )
    top, bottom = exchange(first_rows, last_rows, "row")
    left, right = exchange(first_cols, last_cols, "col")
    fetched = (gain2, proj_weight, conv_weight, fc1_weight, fc2)
    hidden = -(-fc1_weight.shape[1] // 128) * 128
    bias, query, kv, normed, wkv = call(
        own_kernel,
        "own_tile",
        [
            ((HEADS, 2, 2, AREA, WIN * WIN), F32),
            ((blocks_r, blocks_c, AREA, LANES), BF16),
            ((blocks_r, blocks_c, AREA, 2 * LANES), BF16),
            ((rows, cols, LANES), F32),
            ((LANES, 2 * LANES), BF16),
        ],
        [
            ((8, 1024), F32),
            ((4, 8 * WIN, 128), F32),
            ((LANES, LANES), BF16),
        ],
        2_000_000_000,
        (tile, gain1, table, qkv_weight),
    )
    def ends(start, rest):
        parts = [(start, start + SHIFT), (cols + rest, cols + rest + SHIFT)]
        return jnp.concatenate(
            [jnp.concatenate([x[:, a:b] for a, b in parts], axis=1) for x in (top, bottom)]
        )

    first, last = ends(0, 0), ends(cols - SHIFT, cols // 2 - SHIFT)
    left_corner, right_corner = exchange(first, last, "col")
    kv_edge, corner_base, out_edge, out_mid, wp, wc, w1, w2, g2 = call(
        edge_kernel,
        "edge_windows",
        [
            ((4, blocks_c, AREA, 2 * LANES), BF16),
            ((4, AREA, LANES), F32),
            ((2, 4 * AREA, LANES), F32),
            ((4 * AREA, LANES), F32),
            ((LANES, LANES), BF16),
            ((9 * LANES, LANES), BF16),
            ((LANES, hidden), BF16),
            ((hidden, LANES), BF16),
            ((1, LANES), F32),
        ],
        [
            ((rows + 2 * SHIFT, cols + 2 * SHIFT, LANES), F32),
            ((blocks_r, blocks_c, AREA, LANES), F32),
            ((3, rows + 2, cols, LANES), BF16),
            *[(x.shape, x.dtype) for x in fetched],
            pltpu.SemaphoreType.DMA((len(fetched),)),
        ],
        2_000_000_000,
        (tile, top, bottom, left, right, gain1, bias, query, kv, normed, wkv, *fetched),
        range(11, 16),
    )
    (out,) = call(
        corner_kernel,
        "corner_windows",
        [jax.ShapeDtypeStruct(image.shape, BF16)],
        [((4, AREA, LANES), F32), (image.shape, BF16), pltpu.SemaphoreType.DMA((3,))],
        1_000_000_000,
        (left_corner, right_corner, gain1, bias, query, kv, wkv, wp, wc, w1, w2, g2,
         kv_edge, corner_base, out_mid, out_edge),
    )
    return out


def solution(mesh):
    placed = (P("row", "col", None), P(), P(), P(), P(), P(), P(), P(), P())
    return jax.shard_map(
        on_device, mesh=mesh, in_specs=placed, out_specs=P("row", "col", None), check_vma=False
    )
```

```python
import math

import jax
import jax.numpy as jnp
from jax import lax
from jax.experimental import pallas as pl
from jax.experimental.pallas import tpu as pltpu
from jax.sharding import PartitionSpec as P

HEADS = 6
WIN = 16
SHIFT = 8
SIDE = 8
AREA = SIDE * SIDE
LANES = 256
HALF = LANES // 2
F32 = jnp.float32
BF16 = jnp.bfloat16
LOG2E = math.log2(math.e)
MASKED = -4.0e9


def weave(tasks, width):
    waiting, active = list(tasks), []
    while waiting or active:
        while waiting and len(active) < width:
            active.append(waiting.pop(0))
        for task in list(active):
            try:
                next(task)
            except StopIteration:
                active.remove(task)


def layer_norm(values, norm_gain):
    centre = jnp.mean(values, axis=-1, keepdims=True)
    values = values - centre
    spread = jnp.mean(values * values, axis=-1, keepdims=True)
    return values * lax.rsqrt(spread + 1e-05) * norm_gain


def dot(a, b):
    return jnp.dot(a, b, preferred_element_type=F32)


def dot_nt(a, b):
    return lax.dot_general(a, b, (((1,), (1,)), ((), ())), preferred_element_type=F32)


def one_hot(condition):
    return jnp.where(condition, 1.0, 0.0).astype(BF16)


def gelu(x):
    square = jnp.minimum(x * x, 25.0)
    poly = -5.58203231240273e-08
    for factor in (2.777085437695777e-06, -4.707012890217347e-05, -5.859274357446709e-05,
                   0.036366718434813275, 0.7978721905787034):
        poly = poly * square + factor
    half = 0.5 * x
    return half + half * jnp.tanh(x * poly)


def lanes_of(width=LANES):
    return lax.broadcasted_iota(jnp.int32, (1, width), 1)


def marks(channels, outside):
    half = lanes_of()[:, HALF:]
    return jnp.where(half == channels + 1, 1.0, 0.0) + jnp.where(half == channels, outside, 0.0)


def expand_bias(table_ref, padded, strip, bias):
    span = 2 * WIN - 1
    padded[...] = jnp.zeros_like(padded)
    padded[0:HEADS, 0 : span * span] = table_ref[...] * LOG2E
    table = padded[...]
    width = padded.shape[1]
    shifted = jnp.concatenate(
        [table if px == 0 else pltpu.roll(table, width - px, 1) for px in range(WIN)], axis=0
    )
    high = shifted.astype(BF16)
    low = (shifted - high.astype(F32)).astype(BF16)
    yield
    entry = lax.broadcasted_iota(jnp.int32, (width, 512), 0)
    place = lax.broadcasted_iota(jnp.int32, (1, 512), 1)
    column = lax.div(place, 256) * SIDE + lax.rem(place, SIDE)
    wanted = (span - 1 - lax.div(lax.rem(place, 256), SIDE)) * span + WIN - 1 - column
    picked = dot(jnp.concatenate([high, low], axis=0), one_hot(entry == wanted))
    yield
    half = 8 * WIN
    picked = picked[:half] + picked[half:]
    for tile in range(4):
        strip[tile] = picked[:, 128 * tile : 128 * (tile + 1)]
    for head in range(HEADS):
        yield
        for half in range(2):
            rows = jnp.concatenate(
                [strip[2 * half + t, pl.ds(head, WIN, stride=8), :] for t in range(2)], axis=1
            )
            for py in range(WIN):
                start = (WIN - 1 - py) * SIDE
                rolled = (rows if start == 0 else pltpu.roll(rows, 256 - start, 1))[:, 0:128]
                lanes = slice(128 * half, 128 * (half + 1))
                place = slice(py % SIDE * SIDE, (py % SIDE + 1) * SIDE)
                bias[head, py // SIDE, 0, place, lanes] = rolled[:SIDE]
                bias[head, py // SIDE, 1, place, lanes] = rolled[SIDE:]


def scores_of(blocks, keys, head_dim, channels):
    lane = lanes_of()
    part = jnp.concatenate(blocks, axis=0)
    own = [(lane >= h * head_dim) & (lane < (h + 1) * head_dim) for h in range(HEADS)]
    stacked = jnp.concatenate(
        [part * one_hot(own[h] | (lane == channels)) for h in range(HEADS)], axis=0
    )
    return dot_nt(stacked, keys)


def attend(unit, bias, head_dim, channels, put):
    lane = lanes_of()
    blocks, quadrants, pair = unit
    pair = pair()
    scores = scores_of(blocks, pair[:, :LANES], head_dim, channels)
    count = scores.shape[0] // HEADS
    yield
    part_bias = jnp.concatenate([bias[:, hy, hx] for hy, hx in quadrants], axis=1)
    scores = scores.reshape(HEADS, count, WIN * WIN) + part_bias
    scores = scores - jnp.max(scores, axis=-1, keepdims=True)
    weights = jnp.exp2(scores)
    total = jnp.sum(weights, axis=-1, keepdims=True)
    weights = weights.astype(BF16).reshape(HEADS * count, WIN * WIN)
    yield
    mixed = dot(weights, pair[:, LANES:])
    yield
    result, divisor = mixed[0:count], jnp.broadcast_to(total[0], (count, LANES))
    for h in range(1, HEADS):
        mine = (lane >= h * head_dim) & (lane < (h + 1) * head_dim)
        result = jnp.where(mine, mixed[h * count : (h + 1) * count], result)
        divisor = jnp.where(mine, total[h], divisor)
    put((result / divisor).astype(BF16))


def finish(heads_out, base, wp, gain2, w1, w2, channels, put):
    attended = dot(heads_out, wp[...])
    yield
    state1 = (base() + attended.astype(BF16).astype(F32))[:, :channels]
    normed2 = layer_norm(state1, gain2).astype(BF16)
    yield
    hidden = dot(normed2, w1[...])
    yield
    hidden = gelu(hidden).astype(BF16)
    yield
    put(state1 + dot_nt(hidden, w2[...]))


def after(ready, make):
    while not ready():
        yield
    yield from make()


def pack(pixels, spare):
    rows, cols, channels = pixels.shape
    spare[...] = jnp.zeros_like(spare)
    spare[:, :, 0:channels] = pixels
    rest = spare[:, :, HALF:]
    second = pltpu.roll(rest[:, cols // 2 :].reshape(-1, HALF), HALF // 2, 1)
    both = rest[:, : cols // 2] + second.reshape(rows, cols // 2, HALF)
    return jnp.concatenate([spare[:, :, :HALF], both], axis=1).astype(BF16)


def unpack(main, rest, turned, channels):
    if turned:
        rest = pltpu.roll(rest.reshape(-1, HALF), HALF // 2, 1).reshape(rest.shape)
    return jnp.concatenate([main, rest], axis=2)[:, :, :channels]


def cut_kernel(
    image_hbm, gain1_hbm, table_hbm, qkv_hbm, image_ref, gain1_ref, table_ref, qkv_ref,
    top, bottom, left, right, spare, sems,
):
    rows, cols, _ = image_ref.shape
    fetches = [
        pltpu.make_async_copy(source, target, sems.at[i])
        for i, (source, target) in enumerate(
            ((image_hbm, image_ref), (gain1_hbm, gain1_ref), (table_hbm, table_ref), (qkv_hbm, qkv_ref))
        )
    ]
    for fetch in fetches:
        fetch.start()
    for fetch in fetches:
        fetch.wait()
    top[...] = pack(image_ref[:SHIFT].astype(F32), spare.at[0])
    bottom[...] = pack(image_ref[rows - SHIFT :].astype(F32), spare.at[1])
    for r in range(0, rows, SIDE):
        band = image_ref[r : r + SIDE].astype(F32)
        left[r : r + SIDE] = band[:, :SHIFT].astype(BF16)
        right[r : r + SIDE] = band[:, cols - SHIFT :].astype(BF16)


def own_kernel(
    image_ref, gain1_ref, table_ref, qkv_ref, proj_hbm, conv_hbm,
    bias, query, kv, normed, wkv, wp, wc,
    padded, strip, wq,
    proj_ref, conv_ref, sems,
):
    rows, cols, channels = image_ref.shape
    head_dim = channels // HEADS
    flag_lane, one_lane = channels, channels + 1
    blocks_r, blocks_c = rows // SIDE, cols // SIDE
    fetches = [
        pltpu.make_async_copy(source, target, sems.at[i])
        for i, (source, target) in enumerate(
            ((conv_hbm, conv_ref), (proj_hbm, proj_ref))
        )
    ]
    for fetch in fetches:
        fetch.start()

    for ref in (wq, wkv, wp, wc):
        ref[...] = jnp.zeros_like(ref)
    special = lax.broadcasted_iota(jnp.int32, (16, LANES), 0) + 176
    lanes16 = lax.broadcasted_iota(jnp.int32, (16, LANES), 1)
    wq[176:192, :] = one_hot((special == one_lane) & (lanes16 == flag_lane))
    wkv[176:192, 0:LANES] = jnp.where(
        (special == flag_lane) & (lanes16 == flag_lane), MASKED, 0.0
    ).astype(BF16)
    normed[:, :, HALF:] = jnp.broadcast_to(marks(channels, 0.0)[None], (rows, cols, HALF))

    gain1 = gain1_ref[...]
    scale = head_dim**-0.5 * LOG2E

    wq[0:channels, 0:channels] = qkv_ref[:, 0:channels]
    wkv[0:channels, 0:channels] = qkv_ref[:, channels : 2 * channels]
    wkv[0:channels, LANES : LANES + channels] = qkv_ref[:, 2 * channels :]

    def weights():
        for fetch in fetches:
            fetch.wait()
        wp[0:channels, 0:channels] = proj_ref[...]
        for tap in range(9):
            wc[tap * LANES : tap * LANES + channels, 0:channels] = conv_ref[tap // 3, tap % 3]
            if tap % 3 == 2:
                yield

    def norm(br):
        at = slice(br * SIDE, (br + 1) * SIDE)
        normed[at, :, 0:channels] = layer_norm(image_ref[at].astype(F32), gain1)

    def project(br):
        pixels = normed[br * SIDE : (br + 1) * SIDE].astype(BF16).reshape(-1, LANES)
        q = dot(pixels, wq[...])
        yield
        both = dot(pixels, wkv[...]).reshape(SIDE, cols, 2 * LANES)
        q = (q * scale).reshape(SIDE, cols, LANES)
        for bc in range(blocks_c):
            part = slice(bc * SIDE, (bc + 1) * SIDE)
            query[br, bc] = q[:, part].reshape(AREA, LANES).astype(BF16)
        yield
        for bc in range(blocks_c):
            part = slice(bc * SIDE, (bc + 1) * SIDE)
            kv[br, bc] = both[:, part].reshape(AREA, 2 * LANES).astype(BF16)

    for br in range(blocks_r):
        norm(br)
    tasks = [expand_bias(table_ref, padded, strip, bias), *[project(br) for br in range(blocks_r)]]
    weave([*tasks, weights()], 3)


def edge_kernel(
    image_ref, top_ref, bottom_ref, left_ref, right_ref, gain1_ref,
    bias, query, kv, normed, wkv, wp, wc, w1, w2, g2,
    kv_edge, corner_base, out_edge, out_mid,
    halo, base, shifted,
):
    rows, cols, channels = image_ref.shape
    head_dim = channels // HEADS
    row, last_row = lax.axis_index("row"), lax.axis_size("row") - 1
    col, last_col = lax.axis_index("col"), lax.axis_size("col") - 1
    gain1 = gain1_ref[...]
    outside = [(row == 0).astype(F32), (row == last_row).astype(F32),
               (col == 0).astype(F32), (col == last_col).astype(F32)]

    for r in (0, SHIFT + rows):
        for c in (0, SHIFT + cols):
            halo[r : r + SHIFT, c : c + SHIFT] = jnp.zeros((SHIFT, SHIFT, LANES), F32)
    sides = []

    def band(i):
        ref = (top_ref, bottom_ref, left_ref, right_ref)[i]
        start = (0, SHIFT + (rows if i < 2 else cols))[i % 2]
        inner = slice(SHIFT, SHIFT + (cols if i < 2 else rows))
        outer = slice(start, start + SHIFT)
        place = (outer, inner) if i < 2 else (inner, outer)
        values = ref[...].astype(F32)
        if i < 2:
            rest, half = values[:, cols:], cols // 2
            values = jnp.concatenate(
                [unpack(values[:, :half], rest, False, channels),
                 unpack(values[:, half:cols], rest, True, channels)], axis=1
            )
        mark = jnp.broadcast_to(marks(channels, outside[i])[None], (*values.shape[:2], HALF))
        halo[(*place, slice(HALF, LANES))] = mark
        halo[(*place, slice(0, channels))] = layer_norm(values, gain1 * (1.0 - outside[i]))
        pixels = halo[place]
        if i < 2:
            blocks = [pixels[:, b * SIDE : (b + 1) * SIDE].reshape(AREA, LANES) for b in range(cols // SIDE)]
        else:
            blocks = [pixels.reshape(-1, LANES)]
        pixels = jnp.concatenate(blocks, axis=0).astype(BF16)
        yield
        both = dot(pixels, wkv[...])
        yield
        kv_edge[i] = both.astype(BF16).reshape(-1, AREA, 2 * LANES)
        sides.append(i)

    def tile():
        for r in range(0, rows, SIDE):
            halo[SHIFT + r : SHIFT + r + SIDE, SHIFT : SHIFT + cols] = normed[r : r + SIDE]
            yield

    def convolve(br):
        r = br * SIDE
        for tap in range(3):
            c0 = SHIFT - 1 + tap
            start, stop = 0 if br == 0 else r + 2, r + SIDE + 2
            shifted[tap, start:stop] = halo[
                SHIFT - 1 + start : SHIFT - 1 + stop, c0 : c0 + cols
            ].astype(BF16)
        yield
        taps = [
            shifted[tap % 3, r + tap // 3 : r + tap // 3 + SIDE].reshape(-1, LANES) for tap in range(9)
        ]
        summed = dot(jnp.concatenate(taps, axis=1), wc[...])
        yield
        summed = summed[:, :channels].reshape(SIDE, cols, channels)
        summed = summed + image_ref[r : r + SIDE].astype(F32)
        for bc in range(cols // SIDE):
            part = summed[:, bc * SIDE : (bc + 1) * SIDE].reshape(AREA, channels)
            if (br, bc) in corners:
                ref = corner_base.at[corners.index((br, bc))]
            else:
                ref = base.at[br, bc]
            ref[:, HALF:] = jnp.zeros((AREA, HALF), F32)
            ref[:, 0:channels] = part

    corners = [(0, 0), (0, 3), (3, 0), (3, 3)]
    keys = [
        lambda: [kv_edge[0, 1], kv[0, 1], kv_edge[0, 2], kv[0, 2]],
        lambda: [kv[3, 1], kv_edge[1, 1], kv[3, 2], kv_edge[1, 2]],
        lambda: [kv_edge[2, 1], kv_edge[2, 2], kv[1, 0], kv[2, 0]],
        lambda: [kv[1, 3], kv[2, 3], kv_edge[3, 1], kv_edge[3, 2]],
        lambda: [kv[1, 1], kv[2, 1], kv[1, 2], kv[2, 2]],
    ]
    places = [((0, 1), (0, 2)), ((3, 1), (3, 2)), ((1, 0), (2, 0)), ((1, 3), (2, 3))]
    places += [((1, 1), (1, 2)), ((2, 1), (2, 2))]
    quadrants = [((1, 0), (1, 1)), ((0, 0), (0, 1)), ((0, 1), (1, 1)), ((0, 0), (1, 0))]
    quadrants += [((0, 0), (0, 1)), ((1, 0), (1, 1))]
    done = {}

    def unit(i):
        def put(result):
            done[i] = result

        window = keys[min(i, 4)]
        parts = ([query[at] for at in places[i]], quadrants[i], lambda: jnp.concatenate(window(), axis=0))
        make = lambda: attend(parts, bias, head_dim, channels, put)
        return after(lambda: i >= 4 or i in sides, make)

    def tail(i):
        def put(out):
            if i == 4:
                out_mid[...] = out
            else:
                out_edge[i // 2] = out

        def make():
            return finish(
                jnp.concatenate([done[i], done[i + 1]], axis=0),
                lambda: jnp.concatenate([base[at] for at in (*places[i], *places[i + 1])], axis=0),
                wp, g2[...], w1, w2, channels, put,
            )

        return after(lambda: i in done and i + 1 in done, make)

    weave(
        [unit(4), band(0), band(1), unit(5), band(2), band(3), tile(), unit(0), convolve(0), unit(1),
         convolve(1), unit(2), convolve(2), unit(3), convolve(3), tail(4), tail(0), tail(2)],
        3,
    )


def corner_kernel(
    left_ref, right_ref, gain1_ref,
    bias, query, kv, wkv, wp, wc, w1, w2, g2, kv_edge, corner_base, out_mid, out_edge,
    out_hbm,
    normed, out_ref, sems,
):
    rows, _, channels = out_ref.shape
    head_dim = channels // HEADS

    def finish_bands(which, corners):
        def piece(source, i):
            return source[i * AREA : (i + 1) * AREA]

        for br in which:
            if br in (0, 3):
                i = 0 if br == 0 else 2
                band = [corners[0], piece(out_edge.at[0], i), piece(out_edge.at[0], i + 1), corners[1]]
            else:
                i = br - 1
                band = [piece(out_edge.at[1], i), piece(out_mid, 2 * i), piece(out_mid, 2 * i + 1),
                        piece(out_edge.at[1], i + 2)]
            band = [part[:, :channels].reshape(SIDE, SIDE, channels) for part in band]
            out_ref[br * SIDE : (br + 1) * SIDE] = jnp.concatenate(band, axis=1).astype(BF16)

    finish_bands((1, 2), None)
    inner = slice(SIDE, rows - SIDE)
    writes = [pltpu.make_async_copy(out_ref.at[inner], out_hbm.at[inner], sems.at[0])]
    writes[0].start()
    row, last_row = lax.axis_index("row"), lax.axis_size("row") - 1
    col, last_col = lax.axis_index("col"), lax.axis_size("col") - 1
    gain1 = gain1_ref[...]
    out_row = [(row == 0).astype(F32), (row == last_row).astype(F32)]
    out_col = [(col == 0).astype(F32), (col == last_col).astype(F32)]
    corner, done = {}, {}

    def project(pair):
        for i in (2 * pair, 2 * pair + 1):
            ref = (left_ref, right_ref)[i % 2]
            inside = (1.0 - out_row[i // 2]) * (1.0 - out_col[i % 2])
            mark = marks(channels, out_row[i // 2] + out_col[i % 2])
            normed[i, :, HALF:] = jnp.broadcast_to(mark, (AREA, HALF))
            values = ref[i // 2 * SIDE : (i // 2 + 1) * SIDE].astype(F32)
            values = unpack(values[:, :SIDE], values[:, SIDE:], i % 2 == 0, channels)
            normed[i, :, 0:channels] = layer_norm(values.reshape(AREA, channels), gain1 * inside)
        yield
        both = dot(normed[2 * pair : 2 * pair + 2].reshape(-1, LANES).astype(BF16), wkv[...])
        yield
        both = both.astype(BF16)
        corner[2 * pair], corner[2 * pair + 1] = both[:AREA], both[AREA:]

    keys = [
        lambda: [corner[0], kv_edge[2, 0], kv_edge[0, 0], kv[0, 0]],
        lambda: [kv_edge[0, 3], kv[0, 3], corner[1], kv_edge[3, 0]],
        lambda: [kv_edge[2, 3], corner[2], kv[3, 0], kv_edge[1, 0]],
        lambda: [kv[3, 3], kv_edge[1, 3], kv_edge[3, 3], corner[3]],
    ]
    places = [(0, 0), (0, 3), (3, 0), (3, 3)]
    quadrants = [(1, 1), (1, 0), (0, 1), (0, 0)]

    def unit(i):
        def put(result):
            done[i] = result

        parts = ([query[places[i]]], [quadrants[i]], lambda: jnp.concatenate(keys[i](), axis=0))
        return after(lambda: i in corner, lambda: attend(parts, bias, head_dim, channels, put))

    def whole(i):
        tap, y, x = ((0, 7, 7), (2, 7, 0), (6, 0, 7), (8, 0, 0))[i]
        start = y * SIDE
        term = dot(normed[i, start : start + SIDE].astype(BF16), wc[tap * LANES : (tap + 1) * LANES])
        term = term[x : x + 1]
        pixel = lax.broadcasted_iota(jnp.int32, (AREA, 1), 0)
        at = (SIDE - 1 - y) * SIDE + SIDE - 1 - x
        return corner_base[i] + jnp.where(pixel == at, term, 0.0)

    def tail(i):
        def put(out):
            finish_bands((0,) if i == 0 else (3,), [out[:AREA], out[AREA:]])

        def make():
            return finish(
                jnp.concatenate([done[i], done[i + 1]], axis=0),
                lambda: jnp.concatenate([whole(i), whole(i + 1)], axis=0),
                wp, g2[...], w1, w2, channels, put,
            )

        return after(lambda: i in done and i + 1 in done, make)

    weave([project(0), project(1), unit(0), unit(1), unit(2), unit(3), tail(0), tail(2)], 4)
    writes[0].wait()
    for r in (0, rows - SIDE):
        at = slice(r, r + SIDE)
        write = pltpu.make_async_copy(out_ref.at[at], out_hbm.at[at], sems.at[1 if r == 0 else 2])
        write.start()
        writes.append(write)
    writes[1].wait()
    writes[2].wait()


def exchange(low, high, axis):
    count = lax.axis_size(axis)
    before = lax.ppermute(high, axis, [(i, (i + 1) % count) for i in range(count)])
    after = lax.ppermute(low, axis, [((i + 1) % count, i) for i in range(count)])
    return before, after


def call(kernel, name, outs, scratch, flops, operands, in_hbm=()):
    vmem = pl.BlockSpec(memory_space=pltpu.VMEM)
    hbm = pl.BlockSpec(memory_space=pltpu.HBM)
    return pl.pallas_call(
        kernel,
        out_shape=[out if isinstance(out, jax.ShapeDtypeStruct) else pltpu.VMEM(*out) for out in outs],
        in_specs=[hbm if i in in_hbm else vmem for i in range(len(operands))],
        out_specs=[hbm if isinstance(out, jax.ShapeDtypeStruct) else vmem for out in outs],
        scratch_shapes=[pltpu.VMEM(*s) if isinstance(s, tuple) else s for s in scratch],
        cost_estimate=pl.CostEstimate(flops=flops, bytes_accessed=4_000_000, transcendentals=1_000_000),
        compiler_params=pltpu.CompilerParams(vmem_limit_bytes=24 * 1024 * 1024),
        name=name,
    )(*[pltpu.with_memory_space_constraint(x, pltpu.HBM) if i in in_hbm else x for i, x in enumerate(operands)])


def on_device(
    image, norm1_gain, norm2_gain, qkv_weight, proj_weight, rel_table, conv_weight, fc1_weight,
    fc2_weight,
):
    rows, cols, channels = image.shape
    blocks_r, blocks_c = rows // SIDE, cols // SIDE
    gain1, gain2, fc2, table = norm1_gain[None], norm2_gain[None], fc2_weight.T, rel_table.T
    band, column = ((SHIFT, cols * 3 // 2, HALF), BF16), ((rows, SHIFT, channels), BF16)
    tile, gain1, table, qkv_weight, first_rows, last_rows, first_cols, last_cols = call(
        cut_kernel,
        "cut_halo",
        [(image.shape, BF16), (gain1.shape, F32), (table.shape, F32), (qkv_weight.shape, BF16),
         band, band, column, column],
        [((2, SHIFT, cols, LANES), F32), pltpu.SemaphoreType.DMA((4,))],
        1_000_000,
        (image, gain1, table, qkv_weight),
        range(4),
    )
    top, bottom = exchange(first_rows, last_rows, "row")
    left, right = exchange(first_cols, last_cols, "col")
    fetched = (proj_weight, conv_weight)
    bias, query, kv, normed, wkv, wp, wc = call(
        own_kernel,
        "own_tile",
        [
            ((HEADS, 2, 2, AREA, WIN * WIN), F32),
            ((blocks_r, blocks_c, AREA, LANES), BF16),
            ((blocks_r, blocks_c, AREA, 2 * LANES), BF16),
            ((rows, cols, LANES), F32),
            ((LANES, 2 * LANES), BF16),
            ((LANES, LANES), BF16),
            ((9 * LANES, LANES), BF16),
        ],
        [
            ((8, 1024), F32),
            ((4, 8 * WIN, 128), F32),
            ((LANES, LANES), BF16),
            *[(x.shape, x.dtype) for x in fetched],
            pltpu.SemaphoreType.DMA((len(fetched),)),
        ],
        2_000_000_000,
        (tile, gain1, table, qkv_weight, proj_weight, conv_weight),
        range(4, 6),
    )
    def ends(start, rest):
        parts = [(start, start + SHIFT), (cols + rest, cols + rest + SHIFT)]
        return jnp.concatenate(
            [jnp.concatenate([x[:, a:b] for a, b in parts], axis=1) for x in (top, bottom)]
        )

    first, last = ends(0, 0), ends(cols - SHIFT, cols // 2 - SHIFT)
    left_corner, right_corner = exchange(first, last, "col")
    kv_edge, corner_base, out_edge, out_mid = call(
        edge_kernel,
        "edge_windows",
        [
            ((4, blocks_c, AREA, 2 * LANES), BF16),
            ((4, AREA, LANES), F32),
            ((2, 4 * AREA, channels), F32),
            ((4 * AREA, channels), F32),
        ],
        [
            ((rows + 2 * SHIFT, cols + 2 * SHIFT, LANES), F32),
            ((blocks_r, blocks_c, AREA, LANES), F32),
            ((3, rows + 2, cols, LANES), BF16),
        ],
        2_000_000_000,
        (tile, top, bottom, left, right, gain1, bias, query, kv, normed, wkv, wp, wc, fc1_weight, fc2, gain2),
    )
    (out,) = call(
        corner_kernel,
        "corner_windows",
        [jax.ShapeDtypeStruct(image.shape, BF16)],
        [((4, AREA, LANES), F32), (image.shape, BF16), pltpu.SemaphoreType.DMA((3,))],
        1_000_000_000,
        (left_corner, right_corner, gain1, bias, query, kv, wkv, wp, wc, fc1_weight, fc2, gain2,
         kv_edge, corner_base, out_mid, out_edge),
    )
    return out


def solution(mesh):
    placed = (P("row", "col", None), P(), P(), P(), P(), P(), P(), P(), P())
    return jax.shard_map(
        on_device, mesh=mesh, in_specs=placed, out_specs=P("row", "col", None), check_vma=False
    )
```

```python
import math

import jax
import jax.numpy as jnp
from jax import lax
from jax.experimental import pallas as pl
from jax.experimental.pallas import tpu as pltpu
from jax.sharding import PartitionSpec as P

HEADS = 6
WIN = 16
SHIFT = 8
SIDE = 8
AREA = SIDE * SIDE
LANES = 256
HALF = LANES // 2
F32 = jnp.float32
BF16 = jnp.bfloat16
LOG2E = math.log2(math.e)
MASKED = -4.0e9


def weave(tasks, width):
    waiting, active = list(tasks), []
    while waiting or active:
        while waiting and len(active) < width:
            active.append(waiting.pop(0))
        for task in list(active):
            try:
                next(task)
            except StopIteration:
                active.remove(task)


def layer_norm(values, norm_gain):
    centre = jnp.mean(values, axis=-1, keepdims=True)
    values = values - centre
    spread = jnp.mean(values * values, axis=-1, keepdims=True)
    return values * lax.rsqrt(spread + 1e-05) * norm_gain


def dot(a, b):
    return jnp.dot(a, b, preferred_element_type=F32)


def dot_nt(a, b):
    return lax.dot_general(a, b, (((1,), (1,)), ((), ())), preferred_element_type=F32)


def one_hot(condition):
    return jnp.where(condition, 1.0, 0.0).astype(BF16)


def gelu(x):
    square = jnp.minimum(x * x, 25.0)
    poly = -5.58203231240273e-08
    for factor in (2.777085437695777e-06, -4.707012890217347e-05, -5.859274357446709e-05,
                   0.036366718434813275, 0.7978721905787034):
        poly = poly * square + factor
    half = 0.5 * x
    return half + half * jnp.tanh(x * poly)


def lanes_of(width=LANES):
    return lax.broadcasted_iota(jnp.int32, (1, width), 1)


def marks(channels, outside):
    half = lanes_of()[:, HALF:]
    return jnp.where(half == channels + 1, 1.0, 0.0) + jnp.where(half == channels, outside, 0.0)


def expand_bias(table_ref, padded, strip, bias):
    span = 2 * WIN - 1
    padded[...] = jnp.zeros_like(padded)
    padded[0:HEADS, 0 : span * span] = table_ref[...] * LOG2E
    table = padded[...]
    width = padded.shape[1]
    shifted = jnp.concatenate(
        [table if px == 0 else pltpu.roll(table, width - px, 1) for px in range(WIN)], axis=0
    )
    high = shifted.astype(BF16)
    low = (shifted - high.astype(F32)).astype(BF16)
    yield
    entry = lax.broadcasted_iota(jnp.int32, (width, 512), 0)
    place = lax.broadcasted_iota(jnp.int32, (1, 512), 1)
    column = lax.div(place, 256) * SIDE + lax.rem(place, SIDE)
    wanted = (span - 1 - lax.div(lax.rem(place, 256), SIDE)) * span + WIN - 1 - column
    picked = dot(jnp.concatenate([high, low], axis=0), one_hot(entry == wanted))
    yield
    half = 8 * WIN
    picked = picked[:half] + picked[half:]
    for tile in range(4):
        strip[tile] = picked[:, 128 * tile : 128 * (tile + 1)]
    for head in range(HEADS):
        yield
        for half in range(2):
            rows = jnp.concatenate(
                [strip[2 * half + t, pl.ds(head, WIN, stride=8), :] for t in range(2)], axis=1
            )
            for py in range(WIN):
                start = (WIN - 1 - py) * SIDE
                rolled = (rows if start == 0 else pltpu.roll(rows, 256 - start, 1))[:, 0:128]
                lanes = slice(128 * half, 128 * (half + 1))
                place = slice(py % SIDE * SIDE, (py % SIDE + 1) * SIDE)
                bias[head, py // SIDE, 0, place, lanes] = rolled[:SIDE]
                bias[head, py // SIDE, 1, place, lanes] = rolled[SIDE:]


def scores_of(blocks, keys, head_dim, channels):
    lane = lanes_of()
    part = jnp.concatenate(blocks, axis=0)
    own = [(lane >= h * head_dim) & (lane < (h + 1) * head_dim) for h in range(HEADS)]
    stacked = jnp.concatenate(
        [part * one_hot(own[h] | (lane == channels)) for h in range(HEADS)], axis=0
    )
    return dot_nt(stacked, keys)


def attend(unit, bias, head_dim, channels, put):
    lane = lanes_of()
    blocks, quadrants, pair = unit
    pair = pair()
    scores = scores_of(blocks, pair[:, :LANES], head_dim, channels)
    count = scores.shape[0] // HEADS
    yield
    part_bias = jnp.concatenate([bias[:, hy, hx] for hy, hx in quadrants], axis=1)
    scores = scores.reshape(HEADS, count, WIN * WIN) + part_bias
    scores = scores - jnp.max(scores, axis=-1, keepdims=True)
    weights = jnp.exp2(scores)
    total = jnp.sum(weights, axis=-1, keepdims=True)
    weights = weights.astype(BF16).reshape(HEADS * count, WIN * WIN)
    yield
    mixed = dot(weights, pair[:, LANES:])
    yield
    result, divisor = mixed[0:count], jnp.broadcast_to(total[0], (count, LANES))
    for h in range(1, HEADS):
        mine = (lane >= h * head_dim) & (lane < (h + 1) * head_dim)
        result = jnp.where(mine, mixed[h * count : (h + 1) * count], result)
        divisor = jnp.where(mine, total[h], divisor)
    put((result / divisor).astype(BF16))


def finish(heads_out, base, wp, gain2, w1, w2, channels, put):
    attended = dot(heads_out, wp[...])
    yield
    state1 = (base() + attended.astype(BF16).astype(F32))[:, :channels]
    normed2 = layer_norm(state1, gain2).astype(BF16)
    yield
    hidden = dot(normed2, w1[...])
    yield
    hidden = gelu(hidden).astype(BF16)
    yield
    put(state1 + dot_nt(hidden, w2[...]))


def after(ready, make):
    while not ready():
        yield
    yield from make()


def pack(pixels, spare):
    rows, cols, channels = pixels.shape
    spare[...] = jnp.zeros_like(spare)
    spare[:, :, 0:channels] = pixels
    rest = spare[:, :, HALF:]
    second = pltpu.roll(rest[:, cols // 2 :].reshape(-1, HALF), HALF // 2, 1)
    both = rest[:, : cols // 2] + second.reshape(rows, cols // 2, HALF)
    return jnp.concatenate([spare[:, :, :HALF], both], axis=1).astype(BF16)


def unpack(main, rest, turned, channels):
    if turned:
        rest = pltpu.roll(rest.reshape(-1, HALF), HALF // 2, 1).reshape(rest.shape)
    return jnp.concatenate([main, rest], axis=2)[:, :, :channels]


def cut_kernel(
    image_hbm, gain1_hbm, table_hbm, qkv_hbm, image_ref, gain1_ref, table_ref, qkv_ref,
    top, bottom, left, right, spare, sems,
):
    rows, cols, _ = image_ref.shape
    fetches = [
        pltpu.make_async_copy(source, target, sems.at[i])
        for i, (source, target) in enumerate(
            ((image_hbm, image_ref), (gain1_hbm, gain1_ref), (table_hbm, table_ref), (qkv_hbm, qkv_ref))
        )
    ]
    for fetch in fetches:
        fetch.start()
    for fetch in fetches:
        fetch.wait()
    top[...] = pack(image_ref[:SHIFT].astype(F32), spare.at[0])
    bottom[...] = pack(image_ref[rows - SHIFT :].astype(F32), spare.at[1])
    for r in range(0, rows, SIDE):
        band = image_ref[r : r + SIDE].astype(F32)
        left[r : r + SIDE] = band[:, :SHIFT].astype(BF16)
        right[r : r + SIDE] = band[:, cols - SHIFT :].astype(BF16)


def own_kernel(
    image_ref, gain1_ref, table_ref, qkv_ref, proj_hbm, conv_hbm,
    bias, query, kv, normed, wkv, wp, wc,
    padded, strip, wq,
    proj_ref, conv_ref, sems,
):
    rows, cols, channels = image_ref.shape
    head_dim = channels // HEADS
    flag_lane, one_lane = channels, channels + 1
    blocks_r, blocks_c = rows // SIDE, cols // SIDE
    fetches = [
        pltpu.make_async_copy(source, target, sems.at[i])
        for i, (source, target) in enumerate(
            ((conv_hbm, conv_ref), (proj_hbm, proj_ref))
        )
    ]
    for fetch in fetches:
        fetch.start()

    for ref in (wq, wkv, wp, wc):
        for r in range(0, ref.shape[0], LANES):
            edge = slice(r + channels // 16 * 16, r + LANES)
            ref[edge] = jnp.zeros_like(ref[edge])
        for c in range(HALF, ref.shape[1], LANES):
            ref[:, c : c + HALF] = jnp.zeros((ref.shape[0], HALF), BF16)
    special = lax.broadcasted_iota(jnp.int32, (16, LANES), 0) + 176
    lanes16 = lax.broadcasted_iota(jnp.int32, (16, LANES), 1)
    wq[176:192, :] = one_hot((special == one_lane) & (lanes16 == flag_lane))
    wkv[176:192, 0:LANES] = jnp.where(
        (special == flag_lane) & (lanes16 == flag_lane), MASKED, 0.0
    ).astype(BF16)
    normed[:, :, HALF:] = jnp.broadcast_to(marks(channels, 0.0)[None], (rows, cols, HALF))

    gain1 = gain1_ref[...]
    scale = head_dim**-0.5 * LOG2E

    wq[0:channels, 0:channels] = qkv_ref[:, 0:channels]
    wkv[0:channels, 0:channels] = qkv_ref[:, channels : 2 * channels]
    wkv[0:channels, LANES : LANES + channels] = qkv_ref[:, 2 * channels :]

    def weights():
        for fetch in fetches:
            fetch.wait()
        wp[0:channels, 0:channels] = proj_ref[...]
        for tap in range(9):
            wc[tap * LANES : tap * LANES + channels, 0:channels] = conv_ref[tap // 3, tap % 3]
            if tap % 3 == 2:
                yield

    def norm(br):
        at = slice(br * SIDE, (br + 1) * SIDE)
        normed[at, :, 0:channels] = layer_norm(image_ref[at].astype(F32), gain1)

    def project(br):
        pixels = normed[br * SIDE : (br + 1) * SIDE].astype(BF16).reshape(-1, LANES)
        q = dot(pixels, wq[...])
        yield
        both = dot(pixels, wkv[...]).reshape(SIDE, cols, 2 * LANES)
        q = (q * scale).reshape(SIDE, cols, LANES)
        for bc in range(blocks_c):
            part = slice(bc * SIDE, (bc + 1) * SIDE)
            query[br, bc] = q[:, part].reshape(AREA, LANES).astype(BF16)
        yield
        for bc in range(blocks_c):
            part = slice(bc * SIDE, (bc + 1) * SIDE)
            kv[br, bc] = both[:, part].reshape(AREA, 2 * LANES).astype(BF16)

    for br in range(blocks_r):
        norm(br)
    tasks = [expand_bias(table_ref, padded, strip, bias), *[project(br) for br in range(blocks_r)]]
    weave([*tasks, weights()], 3)


def edge_kernel(
    image_ref, top_ref, bottom_ref, left_ref, right_ref, gain1_ref,
    bias, query, kv, normed, wkv, wp, wc, w1, w2, g2,
    kv_edge, corner_base, out_edge, out_mid,
    halo, base, shifted,
):
    rows, cols, channels = image_ref.shape
    head_dim = channels // HEADS
    row, last_row = lax.axis_index("row"), lax.axis_size("row") - 1
    col, last_col = lax.axis_index("col"), lax.axis_size("col") - 1
    gain1 = gain1_ref[...]
    outside = [(row == 0).astype(F32), (row == last_row).astype(F32),
               (col == 0).astype(F32), (col == last_col).astype(F32)]

    for r in (0, SHIFT + rows):
        for c in (0, SHIFT + cols):
            halo[r : r + SHIFT, c : c + SHIFT] = jnp.zeros((SHIFT, SHIFT, LANES), F32)
    sides = []

    def band(i):
        ref = (top_ref, bottom_ref, left_ref, right_ref)[i]
        start = (0, SHIFT + (rows if i < 2 else cols))[i % 2]
        inner = slice(SHIFT, SHIFT + (cols if i < 2 else rows))
        outer = slice(start, start + SHIFT)
        place = (outer, inner) if i < 2 else (inner, outer)
        values = ref[...].astype(F32)
        if i < 2:
            rest, half = values[:, cols:], cols // 2
            values = jnp.concatenate(
                [unpack(values[:, :half], rest, False, channels),
                 unpack(values[:, half:cols], rest, True, channels)], axis=1
            )
        mark = jnp.broadcast_to(marks(channels, outside[i])[None], (*values.shape[:2], HALF))
        halo[(*place, slice(HALF, LANES))] = mark
        halo[(*place, slice(0, channels))] = layer_norm(values, gain1 * (1.0 - outside[i]))
        pixels = halo[place]
        if i < 2:
            blocks = [pixels[:, b * SIDE : (b + 1) * SIDE].reshape(AREA, LANES) for b in range(cols // SIDE)]
        else:
            blocks = [pixels.reshape(-1, LANES)]
        pixels = jnp.concatenate(blocks, axis=0).astype(BF16)
        yield
        both = dot(pixels, wkv[...])
        yield
        kv_edge[i] = both.astype(BF16).reshape(-1, AREA, 2 * LANES)
        sides.append(i)

    def tile():
        for r in range(0, rows, SIDE):
            halo[SHIFT + r : SHIFT + r + SIDE, SHIFT : SHIFT + cols] = normed[r : r + SIDE]
            yield

    def convolve(br):
        r = br * SIDE
        for tap in range(3):
            c0 = SHIFT - 1 + tap
            start, stop = 0 if br == 0 else r + 2, r + SIDE + 2
            shifted[tap, start:stop] = halo[
                SHIFT - 1 + start : SHIFT - 1 + stop, c0 : c0 + cols
            ].astype(BF16)
        yield
        taps = [
            shifted[tap % 3, r + tap // 3 : r + tap // 3 + SIDE].reshape(-1, LANES) for tap in range(9)
        ]
        summed = dot(jnp.concatenate(taps, axis=1), wc[...])
        yield
        summed = summed[:, :channels].reshape(SIDE, cols, channels)
        summed = summed + image_ref[r : r + SIDE].astype(F32)
        for bc in range(cols // SIDE):
            part = summed[:, bc * SIDE : (bc + 1) * SIDE].reshape(AREA, channels)
            if (br, bc) in corners:
                ref = corner_base.at[corners.index((br, bc))]
            else:
                ref = base.at[br, bc]
            ref[:, HALF:] = jnp.zeros((AREA, HALF), F32)
            ref[:, 0:channels] = part

    corners = [(0, 0), (0, 3), (3, 0), (3, 3)]
    keys = [
        lambda: [kv_edge[0, 1], kv[0, 1], kv_edge[0, 2], kv[0, 2]],
        lambda: [kv[3, 1], kv_edge[1, 1], kv[3, 2], kv_edge[1, 2]],
        lambda: [kv_edge[2, 1], kv_edge[2, 2], kv[1, 0], kv[2, 0]],
        lambda: [kv[1, 3], kv[2, 3], kv_edge[3, 1], kv_edge[3, 2]],
        lambda: [kv[1, 1], kv[2, 1], kv[1, 2], kv[2, 2]],
    ]
    places = [((0, 1), (0, 2)), ((3, 1), (3, 2)), ((1, 0), (2, 0)), ((1, 3), (2, 3))]
    places += [((1, 1), (1, 2)), ((2, 1), (2, 2))]
    quadrants = [((1, 0), (1, 1)), ((0, 0), (0, 1)), ((0, 1), (1, 1)), ((0, 0), (1, 0))]
    quadrants += [((0, 0), (0, 1)), ((1, 0), (1, 1))]
    done = {}

    def unit(i):
        def put(result):
            done[i] = result

        window = keys[min(i, 4)]
        parts = ([query[at] for at in places[i]], quadrants[i], lambda: jnp.concatenate(window(), axis=0))
        make = lambda: attend(parts, bias, head_dim, channels, put)
        return after(lambda: i >= 4 or i in sides, make)

    def tail(i):
        def put(out):
            if i == 4:
                out_mid[...] = out
            else:
                out_edge[i // 2] = out

        def make():
            return finish(
                jnp.concatenate([done[i], done[i + 1]], axis=0),
                lambda: jnp.concatenate([base[at] for at in (*places[i], *places[i + 1])], axis=0),
                wp, g2[...], w1, w2, channels, put,
            )

        return after(lambda: i in done and i + 1 in done, make)

    weave(
        [unit(4), band(0), band(1), unit(5), band(2), band(3), tile(), unit(0), convolve(0), unit(1),
         convolve(1), unit(2), convolve(2), unit(3), convolve(3), tail(4), tail(0), tail(2)],
        3,
    )


def corner_kernel(
    left_ref, right_ref, gain1_ref,
    bias, query, kv, wkv, wp, wc, w1, w2, g2, kv_edge, corner_base, out_mid, out_edge,
    out_hbm,
    normed, out_ref, sems,
):
    rows, _, channels = out_ref.shape
    head_dim = channels // HEADS

    def finish_bands(which, corners):
        def piece(source, i):
            return source[i * AREA : (i + 1) * AREA]

        for br in which:
            if br in (0, 3):
                i = 0 if br == 0 else 2
                band = [corners[0], piece(out_edge.at[0], i), piece(out_edge.at[0], i + 1), corners[1]]
            else:
                i = br - 1
                band = [piece(out_edge.at[1], i), piece(out_mid, 2 * i), piece(out_mid, 2 * i + 1),
                        piece(out_edge.at[1], i + 2)]
            band = [part[:, :channels].reshape(SIDE, SIDE, channels) for part in band]
            out_ref[br * SIDE : (br + 1) * SIDE] = jnp.concatenate(band, axis=1).astype(BF16)

    finish_bands((1, 2), None)
    inner = slice(SIDE, rows - SIDE)
    writes = [pltpu.make_async_copy(out_ref.at[inner], out_hbm.at[inner], sems.at[0])]
    writes[0].start()
    row, last_row = lax.axis_index("row"), lax.axis_size("row") - 1
    col, last_col = lax.axis_index("col"), lax.axis_size("col") - 1
    gain1 = gain1_ref[...]
    out_row = [(row == 0).astype(F32), (row == last_row).astype(F32)]
    out_col = [(col == 0).astype(F32), (col == last_col).astype(F32)]
    corner, done = {}, {}

    def project(pair):
        for i in (2 * pair, 2 * pair + 1):
            ref = (left_ref, right_ref)[i % 2]
            inside = (1.0 - out_row[i // 2]) * (1.0 - out_col[i % 2])
            mark = marks(channels, out_row[i // 2] + out_col[i % 2])
            normed[i, :, HALF:] = jnp.broadcast_to(mark, (AREA, HALF))
            values = ref[i // 2 * SIDE : (i // 2 + 1) * SIDE].astype(F32)
            values = unpack(values[:, :SIDE], values[:, SIDE:], i % 2 == 0, channels)
            normed[i, :, 0:channels] = layer_norm(values.reshape(AREA, channels), gain1 * inside)
        yield
        both = dot(normed[2 * pair : 2 * pair + 2].reshape(-1, LANES).astype(BF16), wkv[...])
        yield
        both = both.astype(BF16)
        corner[2 * pair], corner[2 * pair + 1] = both[:AREA], both[AREA:]

    keys = [
        lambda: [corner[0], kv_edge[2, 0], kv_edge[0, 0], kv[0, 0]],
        lambda: [kv_edge[0, 3], kv[0, 3], corner[1], kv_edge[3, 0]],
        lambda: [kv_edge[2, 3], corner[2], kv[3, 0], kv_edge[1, 0]],
        lambda: [kv[3, 3], kv_edge[1, 3], kv_edge[3, 3], corner[3]],
    ]
    places = [(0, 0), (0, 3), (3, 0), (3, 3)]
    quadrants = [(1, 1), (1, 0), (0, 1), (0, 0)]

    def unit(i):
        def put(result):
            done[i] = result

        parts = ([query[places[i]]], [quadrants[i]], lambda: jnp.concatenate(keys[i](), axis=0))
        return after(lambda: i in corner, lambda: attend(parts, bias, head_dim, channels, put))

    def whole(i):
        tap, y, x = ((0, 7, 7), (2, 7, 0), (6, 0, 7), (8, 0, 0))[i]
        start = y * SIDE
        term = dot(normed[i, start : start + SIDE].astype(BF16), wc[tap * LANES : (tap + 1) * LANES])
        term = term[x : x + 1]
        pixel = lax.broadcasted_iota(jnp.int32, (AREA, 1), 0)
        at = (SIDE - 1 - y) * SIDE + SIDE - 1 - x
        return corner_base[i] + jnp.where(pixel == at, term, 0.0)

    def tail(i):
        def put(out):
            finish_bands((0,) if i == 0 else (3,), [out[:AREA], out[AREA:]])

        def make():
            return finish(
                jnp.concatenate([done[i], done[i + 1]], axis=0),
                lambda: jnp.concatenate([whole(i), whole(i + 1)], axis=0),
                wp, g2[...], w1, w2, channels, put,
            )

        return after(lambda: i in done and i + 1 in done, make)

    weave([project(0), project(1), unit(0), unit(1), unit(2), unit(3), tail(0), tail(2)], 4)
    writes[0].wait()
    for r in (0, rows - SIDE):
        at = slice(r, r + SIDE)
        write = pltpu.make_async_copy(out_ref.at[at], out_hbm.at[at], sems.at[1 if r == 0 else 2])
        write.start()
        writes.append(write)
    writes[1].wait()
    writes[2].wait()


def exchange(low, high, axis):
    count = lax.axis_size(axis)
    before = lax.ppermute(high, axis, [(i, (i + 1) % count) for i in range(count)])
    after = lax.ppermute(low, axis, [((i + 1) % count, i) for i in range(count)])
    return before, after


def call(kernel, name, outs, scratch, flops, operands, in_hbm=()):
    vmem = pl.BlockSpec(memory_space=pltpu.VMEM)
    hbm = pl.BlockSpec(memory_space=pltpu.HBM)
    return pl.pallas_call(
        kernel,
        out_shape=[out if isinstance(out, jax.ShapeDtypeStruct) else pltpu.VMEM(*out) for out in outs],
        in_specs=[hbm if i in in_hbm else vmem for i in range(len(operands))],
        out_specs=[hbm if isinstance(out, jax.ShapeDtypeStruct) else vmem for out in outs],
        scratch_shapes=[pltpu.VMEM(*s) if isinstance(s, tuple) else s for s in scratch],
        cost_estimate=pl.CostEstimate(flops=flops, bytes_accessed=4_000_000, transcendentals=1_000_000),
        compiler_params=pltpu.CompilerParams(vmem_limit_bytes=24 * 1024 * 1024),
        name=name,
    )(*[pltpu.with_memory_space_constraint(x, pltpu.HBM) if i in in_hbm else x for i, x in enumerate(operands)])


def on_device(
    image, norm1_gain, norm2_gain, qkv_weight, proj_weight, rel_table, conv_weight, fc1_weight,
    fc2_weight,
):
    rows, cols, channels = image.shape
    blocks_r, blocks_c = rows // SIDE, cols // SIDE
    gain1, gain2, fc2, table = norm1_gain[None], norm2_gain[None], fc2_weight.T, rel_table.T
    band, column = ((SHIFT, cols * 3 // 2, HALF), BF16), ((rows, SHIFT, channels), BF16)
    tile, gain1, table, qkv_weight, first_rows, last_rows, first_cols, last_cols = call(
        cut_kernel,
        "cut_halo",
        [(image.shape, BF16), (gain1.shape, F32), (table.shape, F32), (qkv_weight.shape, BF16),
         band, band, column, column],
        [((2, SHIFT, cols, LANES), F32), pltpu.SemaphoreType.DMA((4,))],
        1_000_000,
        (image, gain1, table, qkv_weight),
        range(4),
    )
    top, bottom = exchange(first_rows, last_rows, "row")
    left, right = exchange(first_cols, last_cols, "col")
    fetched = (proj_weight, conv_weight)
    bias, query, kv, normed, wkv, wp, wc = call(
        own_kernel,
        "own_tile",
        [
            ((HEADS, 2, 2, AREA, WIN * WIN), F32),
            ((blocks_r, blocks_c, AREA, LANES), BF16),
            ((blocks_r, blocks_c, AREA, 2 * LANES), BF16),
            ((rows, cols, LANES), F32),
            ((LANES, 2 * LANES), BF16),
            ((LANES, LANES), BF16),
            ((9 * LANES, LANES), BF16),
        ],
        [
            ((8, 1024), F32),
            ((4, 8 * WIN, 128), F32),
            ((LANES, LANES), BF16),
            *[(x.shape, x.dtype) for x in fetched],
            pltpu.SemaphoreType.DMA((len(fetched),)),
        ],
        2_000_000_000,
        (tile, gain1, table, qkv_weight, proj_weight, conv_weight),
        range(4, 6),
    )
    def ends(start, rest):
        parts = [(start, start + SHIFT), (cols + rest, cols + rest + SHIFT)]
        return jnp.concatenate(
            [jnp.concatenate([x[:, a:b] for a, b in parts], axis=1) for x in (top, bottom)]
        )

    first, last = ends(0, 0), ends(cols - SHIFT, cols // 2 - SHIFT)
    left_corner, right_corner = exchange(first, last, "col")
    kv_edge, corner_base, out_edge, out_mid = call(
        edge_kernel,
        "edge_windows",
        [
            ((4, blocks_c, AREA, 2 * LANES), BF16),
            ((4, AREA, LANES), F32),
            ((2, 4 * AREA, channels), F32),
            ((4 * AREA, channels), F32),
        ],
        [
            ((rows + 2 * SHIFT, cols + 2 * SHIFT, LANES), F32),
            ((blocks_r, blocks_c, AREA, LANES), F32),
            ((3, rows + 2, cols, LANES), BF16),
        ],
        2_000_000_000,
        (tile, top, bottom, left, right, gain1, bias, query, kv, normed, wkv, wp, wc, fc1_weight, fc2, gain2),
    )
    (out,) = call(
        corner_kernel,
        "corner_windows",
        [jax.ShapeDtypeStruct(image.shape, BF16)],
        [((4, AREA, LANES), F32), (image.shape, BF16), pltpu.SemaphoreType.DMA((3,))],
        1_000_000_000,
        (left_corner, right_corner, gain1, bias, query, kv, wkv, wp, wc, fc1_weight, fc2, gain2,
         kv_edge, corner_base, out_mid, out_edge),
    )
    return out


def solution(mesh):
    placed = (P("row", "col", None), P(), P(), P(), P(), P(), P(), P(), P())
    return jax.shard_map(
        on_device, mesh=mesh, in_specs=placed, out_specs=P("row", "col", None), check_vma=False
    )
```
